32 devices in a mesh: clip: 8 (over z, x), chan: 4 (over y, core).
Axes of the slice: x: 2, y: 2, z: 4, core: 2. Of those that a mesh axis runs over, the one named last changes fastest.
Arguments:
- frames_in: bfloat16 [6272, 2048], P('clip'), may hold values from -10 to 10
- boundary: int32 [16, 8], P('clip'), may hold values from 0 to 1, as said below
- w_reduce: bfloat16 [2, 2048, 512], P(None, None, 'chan'), may hold values from -0.125 to 0.125
- gain_inner: float32 [2, 2, 512], P(None, None, 'chan'), may hold values from 0.1 to 1.9
- bias_inner: float32 [2, 2, 512], P(None, None, 'chan'), may hold values from -3 to 3
- w_conv: bfloat16 [2, 9, 512, 512], P(None, None, None, 'chan'), may hold values from -0.09375 to 0.09375
- w_expand: bfloat16 [2, 512, 2048], P(None, 'chan'), may hold values from -0.25 to 0.25
- gain_outer: float32 [2, 2048], replicated, may hold values from 0.1 to 1.9
- bias_outer: float32 [2, 2048], replicated, may hold values from -3 to 3
- depth_kernels: float32 [3, 9, 512], P(None, None, 'chan'), may hold values from -2 to 2
- gate_bias: float32 [512], P('chan'), may hold values from -3 to 3
- cotangent: bfloat16 [6272, 2048], P('clip'), may hold values from -7 to 7
Outputs:
- activations: bfloat16 [6272, 2048], P('clip', 'chan')
- input_grad: float32 [6272, 2048], P('clip', 'chan')
- grad_reduce: float32 [2, 2048, 512], P(None, None, 'chan')
- grad_gain_inner: float32 [2, 2, 512], P(None, None, 'chan')
- grad_bias_inner: float32 [2, 2, 512], P(None, None, 'chan')
- grad_conv: float32 [2, 9, 512, 512], P(None, None, None, 'chan')
- grad_expand: float32 [2, 512, 2048], P(None, 'chan')
- grad_gain_outer: float32 [2, 2048], P(None, 'chan')
- grad_bias_outer: float32 [2, 2048], P(None, 'chan')
- grad_kernels: float32 [3, 9, 512], P(None, None, 'chan')
- grad_gate_bias: float32 [512], P('chan')
The draws below stay inside these ranges and needn't reach their ends.
Inputs may be any that keep to these rules, and one draw needn't show every extreme that they name: `boundary`: each row of 8 entries has a 1 at its last segment and at exactly one earlier segment, where the first packed video ends; 0 elsewhere.
All inputs are finite; a program needn't handle non-finite values.
Results may differ from the reference program's by a relative error of at most 0.03.
Values may be sent and summed in bfloat16 or wider, within the bound.
A program may use at most 192 MiB of HBM per device.

```python
import jax
import jax.numpy as jnp
from jax import lax

C = 2048
I = 512
SEG = 8
SIDE = 7
CLIPS = 16
TOKENS = 6272


def draw_frames_in(key, part):
    key = jax.random.fold_in(key, 11)
    noise_key = jax.random.fold_in(key, 0)
    clip_of = jnp.arange(TOKENS) // (SEG * SIDE * SIDE)
    level = 0.5 + 1.5 * clip_of.astype(jnp.float32) / max(CLIPS - 1, 1)
    values = jnp.clip(jax.random.normal(noise_key, (TOKENS, C), jnp.float32), -5.0, 5.0)
    return (values * level[:, None]).astype(jnp.bfloat16)


def draw_boundary(key, part):
    key = jax.random.fold_in(key, 23)
    split_at = jax.random.randint(key, (CLIPS, 1), 0, SEG - 1)
    places = jnp.arange(SEG)[None, :]
    return ((places == split_at) | (places == SEG - 1)).astype(jnp.int32)


def draw_cotangent(key, part):
    key = jax.random.fold_in(key, 37)
    noise_key, offset_key = jax.random.split(key, 2)
    clip_of = jnp.arange(TOKENS) // (SEG * SIDE * SIDE)
    ramp = -1.0 + 2.0 * jnp.arange(CLIPS).astype(jnp.float32) / max(CLIPS - 1, 1)
    jitter = jnp.clip(jax.random.normal(offset_key, (CLIPS, C), jnp.float32), -2.0, 2.0)
    offset = 1.5 * ramp[:, None] + jitter
    noise = jnp.clip(jax.random.normal(noise_key, (TOKENS, C), jnp.float32), -4.0, 4.0)
    values = jnp.clip(noise + offset[clip_of], -7.0, 7.0)
    return values.astype(jnp.bfloat16)


def block_scale(stream_key, shape, shards, least, largest):
    loudness = 1.0
    for position, parts in shards:
        heights = jax.random.uniform(jax.random.fold_in(jax.random.fold_in(stream_key, 6), position), (parts,), jnp.float32, least / len(shards), largest / len(shards))
        loudness = loudness * jnp.repeat(jnp.exp(heights), shape[position] // parts).reshape((-1,) + (1,) * (len(shape) - 1 - position))
    return loudness


def bell_draw(own_key, shape, width, most, cuts=(), kind=jnp.bfloat16):
    level = block_scale(own_key, shape, cuts, -0.22, 0.18) if cuts else 1.0
    array = jax.random.normal(own_key, shape, jnp.float32) * width * level
    return jnp.minimum(jnp.maximum(array, -most), most).astype(kind)


def setup_inputs(seed: int = 0) -> dict:
    key_of = jax.random.split(jax.random.key(seed), 13)
    return {
        "frames_in": draw_frames_in(jax.random.fold_in(key_of[12], 71), 0),
        "boundary": draw_boundary(jax.random.fold_in(key_of[12], 71), 0),
        "w_reduce": bell_draw(key_of[2], (2, C, I), C ** -0.5, 0.125, ((2, 4),)),
        "gain_inner": jnp.clip(1.0 + 0.18 * jax.random.normal(key_of[3], (2, 2, I), jnp.float32), 0.1, 1.9),
        "bias_inner": bell_draw(key_of[4], (2, 2, I), 0.5, 3.0, ((2, 4),), jnp.float32),
        "w_conv": bell_draw(key_of[5], (2, 9, I, I), (9 * I) ** -0.5, 0.09375, ((3, 4),)),
        "w_expand": bell_draw(key_of[6], (2, I, C), I ** -0.5, 0.25, ((1, 4),)),
        "gain_outer": jnp.clip(1.0 + 0.18 * jax.random.normal(key_of[7], (2, C), jnp.float32), 0.1, 1.9),
        "bias_outer": bell_draw(key_of[8], (2, C), 0.5, 3.0, (), jnp.float32),
        "depth_kernels": bell_draw(key_of[9], (3, 9, I), 0.3, 2.0, ((2, 4),), jnp.float32),
        "gate_bias": bell_draw(key_of[10], (I,), 0.5, 3.0, ((0, 4),), jnp.float32),
        "cotangent": draw_cotangent(jax.random.fold_in(key_of[12], 71), 0),
    }


epsilon = 1e-05

@jax.custom_vjp
def low(v):
    return lax.optimization_barrier(v.astype(jnp.bfloat16)).astype(jnp.float32)

@jax.custom_vjp
def low_back(v):
    return v

def low_keep(v):
    return (low(v), None)

def low_pass(kept, grad):
    return (grad,)

def back_keep(v):
    return (v, None)

def back_low(kept, grad):
    return (low(grad),)
low.defvjp(low_keep, low_pass)
low_back.defvjp(back_keep, back_low)

def framed(values):
    return values.reshape(-1, SIDE, SIDE, values.shape[-1])

def shifted(frame_grid, row_step, col_step, dilation):
    padded = jnp.pad(frame_grid, ((0, 0), (dilation, dilation), (dilation, dilation), (0, 0)))
    return padded[:, dilation + row_step:dilation + row_step + SIDE, dilation + col_step:dilation + col_step + SIDE, :]

def depthwise(values, kernel, dilation):
    frame_grid = framed(values)
    running = jnp.zeros_like(frame_grid)
    for tap_index in range(9):
        running = running + shifted(frame_grid, (tap_index // 3 - 1) * dilation, (tap_index % 3 - 1) * dilation, dilation) * kernel[tap_index]
    return running.reshape(values.shape)

def patch_rows(values):
    frame_grid = framed(values)
    pieces = [shifted(frame_grid, tap_index // 3 - 1, tap_index % 3 - 1, 1) for tap_index in range(9)]
    return jnp.concatenate(pieces, axis=-1).reshape(values.shape[0], 9 * values.shape[1])

def neighbours(values, boundary):
    clip_count = boundary.shape[0]
    frame_grid = values.reshape(clip_count, SEG, SIDE * SIDE, values.shape[-1])
    stop_mask = (boundary == 1)[:, :, None, None]
    start_mask = jnp.concatenate([jnp.ones_like(stop_mask[:, :1]), stop_mask[:, :-1]], axis=1)
    after_seg = jnp.concatenate([frame_grid[:, 1:], frame_grid[:, -1:]], axis=1)
    before = jnp.concatenate([frame_grid[:, :1], frame_grid[:, :-1]], axis=1)
    later_seg = jnp.where(stop_mask, frame_grid, after_seg)
    earlier = jnp.where(start_mask, frame_grid, before)
    return (later_seg.reshape(values.shape), earlier.reshape(values.shape))

def temporal(values, kernels, gate_vec, boundary, short_range):
    later_seg, earlier = neighbours(values, boundary)
    if short_range:
        return values + depthwise(later_seg - earlier, kernels[0], 1)
    change = later_seg - values
    logits = depthwise(change, kernels[1], 1) + depthwise(change, kernels[2], 2) + gate_vec
    return values + values * jax.nn.sigmoid(logits)

def highest(left, right):
    return jnp.dot(left, right, precision=lax.Precision.HIGHEST)

def normalize(values, gain_vec, bias_vec):
    mean_val = lax.optimization_barrier(jnp.mean(values, axis=0))
    spread = lax.optimization_barrier(jnp.mean(values * values, axis=0)) - mean_val * mean_val
    return (values - mean_val) * lax.rsqrt(spread + epsilon) * gain_vec + bias_vec

def residual_block(inputs, boundary, w_red, gain_pair, bias_pair, w_cv, w_ex, gain_out, bias_out, kernels, gate_vec, short_range):
    reduced = low_back(highest(inputs, w_red))
    hidden = jax.nn.gelu(normalize(reduced, gain_pair[0], bias_pair[0]))
    mixed_act = low(temporal(hidden, kernels, gate_vec, boundary, short_range))
    conv_out = low_back(highest(patch_rows(mixed_act), w_cv.reshape(-1, w_cv.shape[-1])))
    inner_act = low(jax.nn.gelu(normalize(conv_out, gain_pair[1], bias_pair[1])))
    expanded = low_back(highest(inner_act, w_ex))
    return low(jax.nn.gelu(normalize(expanded, gain_out, bias_out) + inputs))

def reference(frames_in, boundary, w_reduce, gain_inner, bias_inner, w_conv, w_expand, gain_outer, bias_outer, depth_kernels, gate_bias, cotangent):
    floats = tuple((item.astype(jnp.float32) for item in (frames_in, w_reduce, gain_inner, bias_inner, w_conv, w_expand, gain_outer, bias_outer, depth_kernels, gate_bias)))

    def forward(inputs, w_red, gain_in, bias_in, w_cv, w_ex, gain_out, bias_out, kernels, gate_vec):
        first_out = residual_block(inputs, boundary, w_red[0], gain_in[0], bias_in[0], w_cv[0], w_ex[0], gain_out[0], bias_out[0], kernels, gate_vec, True)
        return residual_block(first_out, boundary, w_red[1], gain_in[1], bias_in[1], w_cv[1], w_ex[1], gain_out[1], bias_out[1], kernels, gate_vec, False)
    output, pull_back = jax.vjp(forward, *floats)
    grads = pull_back(cotangent.astype(jnp.float32))
    return (output.astype(jnp.bfloat16), grads[0], grads[1], grads[2], grads[3], grads[4], grads[5], grads[6], grads[7], grads[8], grads[9])
```

```python
from functools import partial
from types import SimpleNamespace

import jax
import jax.numpy as jnp
from jax import lax
from jax.experimental import pallas as pl
from jax.experimental.pallas import tpu as pltpu
from jax.sharding import PartitionSpec as P

SEG = 8
SIDE = 7


epsilon = 1e-05


def framed(values):
    return values.reshape(-1, SIDE, SIDE, values.shape[-1])


def shifted(frame_grid, row_step, col_step, dilation):
    padded = jnp.pad(frame_grid, ((0, 0), (dilation, dilation), (dilation, dilation), (0, 0)))
    return padded[
        :,
        dilation + row_step : dilation + row_step + SIDE,
        dilation + col_step : dilation + col_step + SIDE,
        :,
    ]


def depthwise(values, kernel, dilation):
    frame_grid = framed(values)
    running = jnp.zeros_like(frame_grid)
    for tap_index in range(9):
        running = (
            running
            + shifted(
                frame_grid,
                (tap_index // 3 - 1) * dilation,
                (tap_index % 3 - 1) * dilation,
                dilation,
            )
            * kernel[tap_index]
        )
    return running.reshape(values.shape)


def patch_rows(values):
    frame_grid = framed(values)
    pieces = [
        shifted(frame_grid, tap_index // 3 - 1, tap_index % 3 - 1, 1) for tap_index in range(9)
    ]
    return jnp.concatenate(pieces, axis=-1).reshape(values.shape[0], 9 * values.shape[1])


def unpatch(grad_rows, chan_width):
    frame_grid = grad_rows.reshape(-1, SIDE, SIDE, 9, chan_width)
    running = jnp.zeros(frame_grid.shape[:3] + (chan_width,), jnp.float32)
    for tap_index in range(9):
        running = running + shifted(
            frame_grid[:, :, :, tap_index, :], 1 - tap_index // 3, 1 - tap_index % 3, 1
        )
    return running.reshape(-1, chan_width)


def neighbours(values, boundary):
    clip_count = boundary.shape[0]
    frame_grid = values.reshape(clip_count, SEG, SIDE * SIDE, values.shape[-1])
    stop_mask = (boundary == 1)[:, :, None, None]
    start_mask = jnp.concatenate([jnp.ones_like(stop_mask[:, :1]), stop_mask[:, :-1]], axis=1)
    after_seg = jnp.concatenate([frame_grid[:, 1:], frame_grid[:, -1:]], axis=1)
    before = jnp.concatenate([frame_grid[:, :1], frame_grid[:, :-1]], axis=1)
    later_seg = jnp.where(stop_mask, frame_grid, after_seg)
    earlier = jnp.where(start_mask, frame_grid, before)
    return (later_seg.reshape(values.shape), earlier.reshape(values.shape))


def temporal(values, kernels, gate_vec, boundary, short_range):
    later_seg, earlier = neighbours(values, boundary)
    if short_range:
        return values + depthwise(later_seg - earlier, kernels[0], 1)
    change = later_seg - values
    logits = depthwise(change, kernels[1], 1) + depthwise(change, kernels[2], 2) + gate_vec
    return values + values * jax.nn.sigmoid(logits)


def columns(values, col_start, col_share):
    return lax.dynamic_slice_in_dim(values, col_start, col_share, values.ndim - 1)


def contract(left, right, left_dim, right_dim):
    return lax.dot_general(
        left, right, (((left_dim,), (right_dim,)), ((), ())), preferred_element_type=jnp.float32
    )


def normalize(values, gain_vec, bias_vec, pixel_total):
    col_sum, sq_sum = lax.psum((jnp.sum(values, axis=0), jnp.sum(values * values, axis=0)), "clip")
    mean_val = col_sum / pixel_total
    inv_std = lax.rsqrt(sq_sum / pixel_total - mean_val * mean_val + epsilon)
    centred = (values - mean_val) * inv_std
    return (centred * gain_vec + bias_vec, centred, inv_std)


def normalize_back(grad_rows, centred, inv_std, gain_vec, pixel_total):
    shift_sum, gain_sum = lax.psum(
        (jnp.sum(grad_rows, axis=0), jnp.sum(grad_rows * centred, axis=0)), "clip"
    )
    grad_in = inv_std * gain_vec * (grad_rows - (shift_sum + centred * gain_sum) / pixel_total)
    return (grad_in, gain_sum, shift_sum)


def block_forward(inputs, boundary, weights, short_range, pixel_total):
    w_red, gain_pair, bias_pair, w_cv, w_ex, gain_out, bias_out, kernels, gate_vec = weights
    reduced = jnp.dot(inputs, w_red, preferred_element_type=jnp.float32)
    norm_one, centred_one, inv_one = normalize(reduced, gain_pair[0], bias_pair[0], pixel_total)
    hidden, gelu_one = jax.vjp(jax.nn.gelu, norm_one)
    mixed_act, mix_back = jax.vjp(
        partial(temporal, boundary=boundary, short_range=short_range), hidden, kernels, gate_vec
    )
    gathered = lax.all_gather(mixed_act.astype(jnp.bfloat16), "chan", axis=1, tiled=True)
    patches = patch_rows(gathered)
    conv_out = jnp.dot(
        patches, w_cv.reshape(-1, w_cv.shape[-1]), preferred_element_type=jnp.float32
    )
    norm_two, centred_two, inv_two = normalize(conv_out, gain_pair[1], bias_pair[1], pixel_total)
    inner_full, gelu_two = jax.vjp(jax.nn.gelu, norm_two)
    inner_act = inner_full.astype(jnp.bfloat16)
    partial_out = jnp.dot(inner_act, w_ex, preferred_element_type=jnp.float32)
    expanded = lax.psum(partial_out.astype(jnp.bfloat16), "chan").astype(jnp.float32)
    norm_three, centred_three, inv_three = normalize(expanded, gain_out, bias_out, pixel_total)
    output_full, gelu_three = jax.vjp(jax.nn.gelu, norm_three + inputs.astype(jnp.float32))
    kept_state = (
        centred_one,
        inv_one,
        gelu_one,
        mix_back,
        patches,
        centred_two,
        inv_two,
        gelu_two,
        inner_act,
        centred_three,
        inv_three,
        gelu_three,
        gain_out,
    )
    return (output_full.astype(jnp.bfloat16), kept_state)


def block_backward(grad_out, inputs, weights, kept_state, pixel_total):
    w_red, gain_pair, bias_pair, w_cv, w_ex, gain_out, bias_out, kernels, gate_vec = weights
    (
        centred_one,
        inv_one,
        gelu_one,
        mix_back,
        patches,
        centred_two,
        inv_two,
        gelu_two,
        inner_act,
        centred_three,
        inv_three,
        gelu_three,
        gain_use,
    ) = kept_state
    grad_pre = gelu_three(grad_out)[0]
    grad_exp, gain_three, bias_three = normalize_back(
        grad_pre, centred_three, inv_three, gain_use, pixel_total
    )
    low_exp = grad_exp.astype(jnp.bfloat16)
    grad_wex = contract(inner_act, low_exp, 0, 0)
    grad_inner = contract(low_exp, w_ex, 1, 1)
    grad_two = gelu_two(grad_inner)[0]
    grad_cv, gain_two, bias_two = normalize_back(
        grad_two, centred_two, inv_two, gain_pair[1], pixel_total
    )
    low_cv = grad_cv.astype(jnp.bfloat16)
    flat_cv = w_cv.reshape(-1, w_cv.shape[-1])
    grad_wcv = contract(patches, low_cv, 0, 0).reshape(w_cv.shape)
    grad_patch = contract(low_cv, flat_cv, 1, 1)
    grad_mixed = lax.psum_scatter(
        unpatch(grad_patch, w_cv.shape[1]).astype(jnp.bfloat16),
        "chan",
        scatter_dimension=1,
        tiled=True,
    ).astype(jnp.float32)
    grad_hidden, grad_kern, grad_gate = mix_back(grad_mixed)
    grad_one = gelu_one(grad_hidden)[0]
    grad_red, gain_one, bias_one = normalize_back(
        grad_one, centred_one, inv_one, gain_pair[0], pixel_total
    )
    low_red = grad_red.astype(jnp.bfloat16)
    grad_wred = contract(inputs, low_red, 0, 0)
    partial_in = contract(low_red, w_red, 1, 1)
    grad_in = grad_pre + lax.psum(partial_in.astype(jnp.bfloat16), "chan").astype(jnp.float32)
    weight_terms = (grad_wred, grad_wcv, grad_wex, grad_kern, grad_gate)
    norm_terms = (gain_one, bias_one, gain_two, bias_two, gain_three, bias_three)
    return (grad_in, weight_terms, norm_terms)


def body(
    frames_in,
    boundary,
    w_reduce,
    gain_inner,
    bias_inner,
    w_conv,
    w_expand,
    gain_outer,
    bias_outer,
    depth_kernels,
    gate_bias,
    cotangent,
):
    row_count = frames_in.shape[0]
    pixel_total = row_count * lax.axis_size("clip")
    col_share = frames_in.shape[1] // lax.axis_size("chan")
    col_start = lax.axis_index("chan") * col_share
    block_weights = [
        (
            w_reduce[block_index],
            gain_inner[block_index],
            bias_inner[block_index],
            w_conv[block_index],
            w_expand[block_index],
            gain_outer[block_index],
            bias_outer[block_index],
            depth_kernels,
            gate_bias,
        )
        for block_index in range(2)
    ]
    first_out, kept_zero = block_forward(frames_in, boundary, block_weights[0], True, pixel_total)
    final_out, kept_one = block_forward(first_out, boundary, block_weights[1], False, pixel_total)
    layer_inputs = [frames_in, first_out]
    kept_states = [kept_zero, kept_one]
    grad_flow = cotangent.astype(jnp.float32)
    weight_sums = [None, None]
    norm_sums = [None, None]
    for block_index in (1, 0):
        grad_flow, weight_terms, norm_terms = block_backward(
            grad_flow,
            layer_inputs[block_index],
            block_weights[block_index],
            kept_states[block_index],
            pixel_total,
        )
        grad_wred, grad_wcv, grad_wex, grad_kern, grad_gate = weight_terms
        weight_terms = (
            lax.psum(grad_wred.astype(jnp.bfloat16), "clip").astype(jnp.float32),
            lax.psum(grad_wcv.astype(jnp.bfloat16), "clip").astype(jnp.float32),
            lax.psum(grad_wex.astype(jnp.bfloat16), "clip").astype(jnp.float32),
            lax.psum(grad_kern.astype(jnp.bfloat16), "clip").astype(jnp.float32),
            lax.psum(grad_gate.astype(jnp.bfloat16), "clip").astype(jnp.float32),
        )
        weight_sums[block_index] = weight_terms
        norm_sums[block_index] = norm_terms
    grad_reduce = jnp.stack([weight_sums[0][0], weight_sums[1][0]])
    grad_conv = jnp.stack([weight_sums[0][1], weight_sums[1][1]])
    grad_expand = jnp.stack([weight_sums[0][2], weight_sums[1][2]])
    grad_kernels = weight_sums[0][3] + weight_sums[1][3]
    grad_gate_bias = weight_sums[0][4] + weight_sums[1][4]
    grad_gain_inner = jnp.stack(
        [
            jnp.stack([norm_sums[0][0], norm_sums[0][2]]),
            jnp.stack([norm_sums[1][0], norm_sums[1][2]]),
        ]
    )
    grad_bias_inner = jnp.stack(
        [
            jnp.stack([norm_sums[0][1], norm_sums[0][3]]),
            jnp.stack([norm_sums[1][1], norm_sums[1][3]]),
        ]
    )
    grad_gain_outer = jnp.stack([norm_sums[0][4], norm_sums[1][4]])
    grad_bias_outer = jnp.stack([norm_sums[0][5], norm_sums[1][5]])
    activations = columns(final_out, col_start, col_share)
    input_grad = columns(grad_flow, col_start, col_share)
    grad_gain_outer = columns(grad_gain_outer, col_start, col_share)
    grad_bias_outer = columns(grad_bias_outer, col_start, col_share)
    return (
        activations,
        input_grad,
        grad_reduce,
        grad_gain_inner,
        grad_bias_inner,
        grad_conv,
        grad_expand,
        grad_gain_outer,
        grad_bias_outer,
        grad_kernels,
        grad_gate_bias,
    )


MESH = pl.DeviceIdType.MESH
LANES = 128
FRAME = SIDE * 8
PAIR = 2 * FRAME
GELU_A = 0.7978845608028654
GELU_B = 0.044715
COPIES = 224
LOADS = 40


def fused_fits(mesh, frame_shape, reduce_shape):
    n_clip, n_chan = mesh.shape["clip"], mesh.shape["chan"]
    share = reduce_shape[2] // n_chan
    frames = frame_shape[0] // (n_clip * SIDE * SIDE)
    return n_chan == 4 and share == LANES and frames == 2 * SEG


def gelu(z):
    return 0.5 * z * (1.0 + jnp.tanh(GELU_A * (z + GELU_B * z * z * z)))


def gelu_both(z):
    square = z * z
    t = jnp.tanh(GELU_A * (z + GELU_B * square * z))
    slope = 0.5 * (1.0 + t) + 0.5 * z * (1.0 - t * t) * (GELU_A * (1.0 + 3.0 * GELU_B * square))
    return 0.5 * z * (1.0 + t), slope


def real_columns(shape):
    return lax.rem(lax.broadcasted_iota(jnp.int32, shape, len(shape) - 2), 8) < SIDE


def real(values):
    return jnp.where(real_columns(values.shape), values, 0.0)


def fold(values):
    return jnp.sum(values.reshape(-1, 8, values.shape[-1]), axis=0)


def tiles(values):
    return values.reshape(SIDE, 8, values.shape[-1])


def flat(values):
    return values.reshape(FRAME, values.shape[-1])


def row_pad(v, reach):
    zeros = jnp.zeros((reach,) + v.shape[1:], v.dtype)
    return jnp.concatenate([zeros, v, zeros], axis=0)


def col_shift(v, step):
    if step == 0:
        return v
    moved = pltpu.roll(v, (-step) % 8, v.ndim - 2)
    if abs(step) == 2:
        place = lax.broadcasted_iota(jnp.int32, v.shape, v.ndim - 2)
        moved = jnp.where(place < 6 if step > 0 else place >= 2, moved, 0.0)
    return moved


def dw_tiles(v, taps, reach, sign):
    padded = row_pad(v, reach)
    total = None
    for b in (-1, 0, 1):
        part = None
        for a in (-1, 0, 1):
            start = reach + sign * reach * a
            term = taps[3 * (a + 1) + b + 1] * padded[start : start + SIDE]
            part = term if part is None else part + term
        part = col_shift(part, sign * reach * b)
        total = part if total is None else total + part
    return total


def dot(left, right, left_dim=1, right_dim=0):
    return lax.dot_general(
        left, right, (((left_dim,), (right_dim,)), ((), ())), preferred_element_type=jnp.float32
    )


NAMES = (
    "x_hbm", "cot_hbm", "wred_hbm", "wconv_hbm", "wexp_hbm", "bnd", "gi", "bi", "go", "bo",
    "dk", "gb", "act_out", "gin_out", "ggi", "gbi", "ggo", "gbo", "gk_out", "ggb_out", "gc_out",
    "ge_out", "gr_out", "x", "cot", "wr0", "wrf", "wef", "wc", "dkb", "red", "hid", "sig",
    "conv", "mixf", "inf", "ex", "out0", "act", "y", "gpre", "gin", "gexp", "gs", "pb", "ysend",
    "rcore", "ryy", "grf", "gm", "gd", "g1", "gk", "kst", "stn", "stw", "gc", "geo", "ge",
    "gro", "gr", "ssem", "rsem", "lsem",
)


def fused_kernel(n_clip, n_chan, pixel_total, *refs):
    r = SimpleNamespace(**dict(zip(NAMES, refs)))
    rows, cs = r.cot.shape
    ib = LANES
    inner = ib * n_chan
    chunk = rows // 2
    frames = rows // FRAME
    bf16, f32 = jnp.bfloat16, jnp.float32
    clip = lax.axis_index("clip")
    chan = lax.axis_index("chan")
    core, high = lax.rem(chan, 2), lax.div(chan, 2)
    j_core = (1 - core) + 2 * high
    j_y = core + 2 * (1 - high)
    j_far = (1 - core) + 2 * (1 - high)
    others = (j_core, j_y, j_far)
    clip_others = [lax.rem(clip + d, n_clip) for d in range(1, n_clip)]

    def cols(j):
        return pl.ds(pl.multiple_of(j * ib, ib), ib)

    def wide(j):
        return pl.ds(pl.multiple_of(j * cs, cs), cs)

    def part(h):
        return pl.ds(h * chunk, chunk)

    counters = {"copy": 0, "load": 0}
    unsent = []

    def remote(src, dst, target):
        index = counters["copy"]
        counters["copy"] += 1
        made = pltpu.make_async_remote_copy(
            src_ref=src,
            dst_ref=dst,
            send_sem=r.ssem.at[index],
            recv_sem=r.rsem.at[index],
            device_id=target,
            device_id_type=MESH,
        )
        made.start()
        unsent.append(made)
        return made

    def sent(made):
        made.wait_send()
        unsent[:] = [other for other in unsent if other is not made]

    def local(src, dst):
        index = counters["load"]
        counters["load"] += 1
        made = pltpu.make_async_copy(src, dst, r.lsem.at[index])
        made.start()
        return made

    load_wr0 = local(r.wred_hbm.at[0], r.wr0)
    load_x = [local(r.x_hbm.at[part(h)], r.x.at[part(h)]) for h in range(2)]
    load_we = [
        local(r.wexp_hbm.at[s, :, wide(chan)], r.wef.at[s, cols(chan)]) for s in range(2)
    ]
    load_wr = [
        local(r.wred_hbm.at[s, wide(chan)], r.wrf.at[s, :, cols(chan)]) for s in range(2)
    ]
    load_wc = [
        [
            local(r.wconv_hbm.at[s, tap], r.wc.at[s, :, tap * ib : (tap + 1) * ib])
            for tap in range(9)
        ]
        for s in range(2)
    ]
    load_cot = local(r.cot_hbm, r.cot)

    barrier = pltpu.get_barrier_semaphore()
    for target in clip_others:
        pl.semaphore_signal(barrier, inc=1, device_id=(target, chan), device_id_type=MESH)
    for target in others:
        pl.semaphore_signal(barrier, inc=1, device_id=(clip, target), device_id_type=MESH)
    pl.semaphore_wait(barrier, n_clip - 1 + n_chan - 1)

    def share_we(s):
        return [
            remote(r.wexp_hbm.at[s, :, wide(j)], r.wef.at[s, cols(chan)], (clip, j))
            for j in others
        ]

    def share_wr(s):
        return [
            remote(r.wred_hbm.at[s, wide(j)], r.wrf.at[s, :, cols(chan)], (clip, j))
            for j in others
        ]

    def arrive(copies):
        for made in copies:
            made.wait_recv()

    def stat_start(buf, slot, values):
        for k, value in enumerate(values):
            buf[slot, clip, k : k + 1, :] = jnp.sum(value, axis=0, keepdims=True)
        return [remote(buf.at[slot, clip], buf.at[slot, clip], (t, chan)) for t in clip_others]

    def stat_end(buf, slot, copies):
        arrive(copies)
        total = buf[slot, 0]
        for k in range(1, n_clip):
            total = total + buf[slot, k]
        return total[0:1], total[1:2]

    def moments(pair):
        mean = pair[0] / pixel_total
        return mean, lax.rsqrt(pair[1] / pixel_total - mean * mean + epsilon)

    def gather_start(full, h):
        mine = full.at[part(h), cols(chan)]
        return [remote(mine, mine, (clip, j_y)), remote(mine, mine, (clip, j_core))]

    def gather_pass(full, h, copies):
        copies[0].wait_recv()
        theirs = full.at[part(h), cols(j_y)]
        copies.append(remote(theirs, theirs, (clip, j_core)))

    def gather_end(copies):
        copies[1].wait_recv()
        copies[2].wait_recv()

    def scatter_start(slot, h):
        return [
            remote(r.pb.at[part(h), cols(j_far)], r.rcore.at[slot, 1, part(h)], (clip, j_core)),
            remote(r.pb.at[part(h), cols(j_core)], r.rcore.at[slot, 0, part(h)], (clip, j_core)),
        ]

    def scatter_pass(slot, h, copies):
        copies[0].wait_recv()
        both = r.pb[part(h), cols(j_y)].astype(f32) + r.rcore[slot, 1, part(h)].astype(f32)
        r.ysend[slot % 2, part(h)] = both.astype(bf16)
        copies.append(
            remote(r.ysend.at[slot % 2, part(h)], r.ryy.at[slot, part(h)], (clip, j_y))
        )

    def scatter_end(slot, h, copies):
        copies[1].wait_recv()
        copies[2].wait_recv()
        sent(copies[0])
        sent(copies[1])
        sent(copies[2])

    def scatter_value(slot, at):
        mine = r.pb[at, cols(chan)].astype(f32)
        return mine + r.rcore[slot, 0, at].astype(f32) + r.ryy[slot, at].astype(f32)

    def keep_flag(f):
        return 1.0 - r.bnd[lax.div(f, SEG), lax.rem(f, SEG)].astype(f32)

    def taps_of(index):
        return [r.dkb[9 * index + tap] for tap in range(9)]

    def pair_rows(h, i):
        return pl.ds(pl.multiple_of(h * chunk + i * PAIR, 16), PAIR)

    def frame_rows(f):
        return pl.ds(pl.multiple_of(f * FRAME, 8), FRAME)

    pairs = frames // 4
    zero_n = jnp.zeros((8, ib), f32)
    zero_w = jnp.zeros((8, cs), f32)
    STEP = 32
    steps = rows // STEP

    def step_rows(i):
        return pl.ds(pl.multiple_of(i * STEP, STEP), STEP)

    moments_in = [[None, None, None], [None, None, None]]

    def row(ref, s, k=None):
        return ref[s, k : k + 1, :] if k is not None else ref[s : s + 1, wide(chan)]

    def norm_inner(s, k, x):
        mean, inv = moments_in[s][k]
        centred = (x - mean) * inv
        return centred, centred * row(r.gi, s, k) + row(r.bi, s, k)

    def norm_outer(s, x):
        mean, inv = moments_in[s][2]
        centred = (x - mean) * inv
        return centred, centred * row(r.go, s) + row(r.bo, s)

    def inner_input(s, at):
        return r.x[at, wide(chan)] if s == 0 else r.out0[at]

    def temporal_forward(s, h):
        def hide(i, _):
            at = pair_rows(h, i)
            r.hid[s, at] = real(gelu(norm_inner(s, 0, r.red[s, at])[1]))
            return _

        lax.fori_loop(0, pairs, hide, 0)

        def mix(i, before):
            base = pl.multiple_of(h * chunk + i * PAIR, 16)
            last = jnp.minimum(base + PAIR, (h + 1) * chunk - FRAME)
            f = h * (frames // 2) + 2 * i
            h0 = tiles(r.hid[s, pl.ds(base, FRAME)])
            h1 = tiles(r.hid[s, pl.ds(base + FRAME, FRAME)])
            h2 = tiles(r.hid[s, pl.ds(pl.multiple_of(last, 8), FRAME)])
            e0 = keep_flag(f) * (h1 - h0)
            e1 = keep_flag(f + 1) * (h2 - h1)
            if s == 0:
                taps = taps_of(0)
                m0 = real(h0 + dw_tiles(e0 + before, taps, 1, 1))
                m1 = real(h1 + dw_tiles(e1 + e0, taps, 1, 1))
            else:
                near, far = taps_of(1), taps_of(2)
                mixed = []
                for k, (hk, ek) in enumerate(((h0, e0), (h1, e1))):
                    logits = dw_tiles(ek, near, 1, 1) + dw_tiles(ek, far, 2, 1) + r.gb[...]
                    gate = 0.5 * (1.0 + jnp.tanh(0.5 * logits))
                    r.sig[pl.ds(base + k * FRAME, FRAME)] = flat(gate)
                    mixed.append(hk + hk * gate)
                m0, m1 = mixed
            both = jnp.concatenate([flat(m0), flat(m1)], axis=0).astype(bf16)
            r.mixf[s, pl.ds(base, PAIR), cols(chan)] = both
            return e1

        lax.fori_loop(0, pairs, mix, jnp.zeros((SIDE, 8, ib), f32))

    def conv_forward(s, h, sums):
        r.y[...] = dot(r.mixf[s, part(h)], r.wc[s])

        def add_taps(i, sums):
            at = pl.ds(pl.multiple_of(i * FRAME, 8), FRAME)
            total = None
            for b in (-1, 0, 1):
                run = None
                for a in (-1, 0, 1):
                    tap = 3 * (a + 1) + b + 1
                    term = row_pad(tiles(r.y[at, tap * ib : (tap + 1) * ib]), 1)
                    term = term[1 + a : 1 + a + SIDE]
                    run = term if run is None else run + term
                run = col_shift(run, b)
                total = run if total is None else total + run
            total = flat(real(total))
            r.conv[s, pl.ds(pl.multiple_of(h * chunk + i * FRAME, 8), FRAME)] = total
            return sums[0] + fold(total), sums[1] + fold(total * total)

        return lax.fori_loop(0, frames // 2, add_taps, sums)

    def forward(s, stat_base, wide_slot):
        copies = []
        for h in range(2):
            temporal_forward(s, h)
            copies.append(gather_start(r.mixf.at[s], h))
        sums = (zero_n, zero_n)
        for made in load_wc[s]:
            made.wait()
        gather_pass(r.mixf.at[s], 0, copies[0])
        for h in range(2):
            gather_end(copies[h])
            sums = conv_forward(s, h, sums)
            if h == 0:
                gather_pass(r.mixf.at[s], 1, copies[1])
        made = stat_start(r.stn, stat_base, sums)
        yield
        moments_in[s][1] = moments(stat_end(r.stn, stat_base, made))
        copies = []
        for h in range(2):

            def inside(i, _):
                at = pair_rows(h, i)
                value = real(gelu(norm_inner(s, 1, r.conv[s, at])[1]))
                r.inf[s, at, cols(chan)] = value.astype(bf16)
                return _

            lax.fori_loop(0, pairs, inside, 0)
            copies.append(gather_start(r.inf.at[s], h))
        yield
        gather_pass(r.inf.at[s], 0, copies[0])
        gather_pass(r.inf.at[s], 1, copies[1])
        sums = (zero_w, zero_w)
        for h in range(2):
            gather_end(copies[h])
            value = dot(r.inf[s, part(h)], r.wef[s])
            r.ex[s, part(h)] = value
            sums = (sums[0] + fold(value), sums[1] + fold(value * value))
        made = stat_start(r.stw, wide_slot, sums)
        yield
        moments_in[s][2] = moments(stat_end(r.stw, wide_slot, made))

    def spread_taps():
        for index in range(3):
            for tap in range(9):
                r.dkb[9 * index + tap] = jnp.broadcast_to(r.dk[index, tap : tap + 1, :], (8, ib))

    def clear(i, _):
        r.gk[i] = zero_n
        return _

    weights_in = {}
    weights_in["we0"] = share_we(0)
    sums = (zero_n, zero_n)
    load_wr0.wait()
    for h in range(2):
        load_x[h].wait()
        value = dot(r.x[part(h)], r.wr0[...])
        r.red[0, part(h)] = value
        sums = (sums[0] + fold(value), sums[1] + fold(value * value))
    made = stat_start(r.stn, 0, sums)
    spread_taps()
    lax.fori_loop(0, r.gk.shape[0], clear, 0)
    moments_in[0][0] = moments(stat_end(r.stn, 0, made))

    stage = forward(0, 1, 0)
    next(stage)
    weights_in["wr1"] = share_wr(1)
    next(stage)
    load_we[0].wait()
    arrive(weights_in["we0"])
    next(stage)
    for _ in stage:
        pass

    def out_zero(i, _):
        at = step_rows(i)
        z = norm_outer(0, r.ex[0, at])[1] + inner_input(0, at).astype(f32)
        r.out0[at] = real(gelu(z)).astype(bf16)
        return _

    lax.fori_loop(0, steps, out_zero, 0)

    def scatter_all(slot, product, use, beside=None):
        copies = []
        for h in range(2):
            r.pb[part(h)] = product(h).astype(bf16)
            copies.append(scatter_start(slot, h))
        scatter_pass(slot, 0, copies[0])
        scatter_pass(slot, 1, copies[1])
        if beside is not None:
            beside()
        for h in range(2):
            scatter_end(slot, h, copies[h])
            use(h)

    held = {"sums": (zero_n, zero_n)}

    def use_reduced(h):
        value = scatter_value(0, part(h))
        r.red[1, part(h)] = value
        held["sums"] = (held["sums"][0] + fold(value), held["sums"][1] + fold(value * value))

    load_wr[1].wait()
    arrive(weights_in["wr1"])
    scatter_all(0, lambda h: dot(r.out0[part(h)], r.wrf[1]), use_reduced)
    made = stat_start(r.stn, 2, held["sums"])
    weights_in["we1"] = share_we(1)
    moments_in[1][0] = moments(stat_end(r.stn, 2, made))
    stage = forward(1, 3, 1)
    next(stage)
    weights_in["wr0"] = share_wr(0)
    next(stage)
    load_we[1].wait()
    arrive(weights_in["we1"])
    next(stage)
    for _ in stage:
        pass

    load_cot.wait()

    def out_one(i, sums):
        at = step_rows(i)
        centred, z = norm_outer(1, r.ex[1, at])
        value, slope = gelu_both(z + r.out0[at].astype(f32))
        r.act[at] = value.astype(bf16)
        grad = r.cot[at].astype(f32) * slope
        r.gpre[at] = grad
        return sums[0] + fold(grad), sums[1] + fold(grad * centred)

    def top_zero(i, sums):
        at = step_rows(i)
        centred, z = norm_outer(0, r.ex[0, at])
        grad = r.gin[at] * gelu_both(z + inner_input(0, at).astype(f32))[1]
        r.gpre[at] = grad
        return sums[0] + fold(grad), sums[1] + fold(grad * centred)

    def backward(s, stat_base, wide_slot, slot):
        made = stat_start(
            r.stw, wide_slot, lax.fori_loop(0, steps, out_one if s else top_zero, (zero_w, zero_w))
        )
        if s == 1:
            local_out.append(local(r.act, r.act_out))
        shift_sum, gain_sum = stat_end(r.stw, wide_slot, made)
        r.gbo[s : s + 1] = shift_sum
        r.ggo[s : s + 1] = gain_sum
        mean, inv = moments_in[s][2]
        scale = inv * row(r.go, s)
        shift_mean, gain_mean = shift_sum / pixel_total, gain_sum / pixel_total

        def expand_back(i, _):
            at = step_rows(i)
            centred = (r.ex[s, at] - mean) * inv
            grad = scale * (r.gpre[at] - (shift_mean + centred * gain_mean))
            r.gexp[at] = real(grad).astype(bf16)
            return _

        lax.fori_loop(0, steps, expand_back, 0)
        held["sums"] = (zero_n, zero_n)

        def weight_expand():
            r.geo[s] = dot(r.inf[s], r.gexp[...], 0, 0).astype(bf16)
            weights_out.append(local(r.geo.at[s, cols(chan)], r.ge.at[s, :, wide(chan)]))
            for j in others:
                arrivals.append(
                    remote(r.geo.at[s, cols(j)], r.ge.at[s, :, wide(chan)], (clip, j))
                )

        def use_inner(h):
            def one(i, sums):
                at = pair_rows(h, i)
                centred, z = norm_inner(s, 1, r.conv[s, at])
                grad = real(scatter_value(slot, at) * gelu_both(z)[1])
                r.g1[at] = grad
                return sums[0] + fold(grad), sums[1] + fold(grad * centred)

            held["sums"] = lax.fori_loop(0, pairs, one, held["sums"])

        scatter_all(
            slot, lambda h: dot(r.gexp[part(h)], r.wef[s], 1, 1), use_inner, weight_expand
        )
        made = stat_start(r.stn, stat_base, held["sums"])
        shift_sum, gain_sum = stat_end(r.stn, stat_base, made)
        r.gbi[s, 1:2] = shift_sum
        r.ggi[s, 1:2] = gain_sum
        mean, inv = moments_in[s][1]
        scale = inv * row(r.gi, s, 1)
        shift_mean, gain_mean = shift_sum / pixel_total, gain_sum / pixel_total

        def conv_back(i, _):
            at = pair_rows(0, i)
            centred = (r.conv[s, at] - mean) * inv
            grad = real(scale * (r.g1[at] - (shift_mean + centred * gain_mean)))
            halves = [tiles(grad[:FRAME]), tiles(grad[FRAME:])]
            for b in (-1, 0, 1):
                moved = [row_pad(col_shift(v, -b), 1) for v in halves]
                for a in (-1, 0, 1):
                    tap = 3 * (a + 1) + b + 1
                    both = jnp.concatenate([flat(v[1 - a : 1 - a + SIDE]) for v in moved], axis=0)
                    r.gs[at, tap * ib : (tap + 1) * ib] = both.astype(bf16)
            return _

        lax.fori_loop(0, 2 * pairs, conv_back, 0)

        def weight_conv():
            for piece in range(n_chan):
                at = pl.ds(piece * ib, ib)
                value = dot(r.mixf[s, :, piece * ib : (piece + 1) * ib], r.gs[...], 0, 0)
                r.gc[s, at] = value.astype(bf16)

        def use_mixed(h):
            def one(i, _):
                at = pair_rows(h, i)
                r.gm[at] = real(scatter_value(slot + 1, at))
                return _

            lax.fori_loop(0, pairs, one, 0)

        scatter_all(
            slot + 1, lambda h: dot(r.gs[part(h)], r.wc[s], 1, 1), use_mixed, weight_conv
        )

        def tap_sums(grad, v, index, reach):
            for b in (-1, 0, 1):
                padded = row_pad(col_shift(v, reach * b), reach)
                for a in (-1, 0, 1):
                    start = reach + reach * a
                    place = 9 * index + 3 * (a + 1) + b + 1
                    r.gk[place] = r.gk[place] + jnp.sum(grad * padded[start : start + SIDE], axis=0)

        def mix_back(f, before):
            at = frame_rows(f)
            following = frame_rows(jnp.minimum(f + 1, frames - 1))
            here = tiles(r.hid[s, at])
            step = keep_flag(f) * (tiles(r.hid[s, following]) - here)
            grad = tiles(r.gm[at])
            if s == 0:
                r.gd[at] = flat(dw_tiles(grad, taps_of(0), 1, -1))
                tap_sums(grad, step + before, 0, 1)
            else:
                gate = tiles(r.sig[at])
                grad = grad * here * gate * (1.0 - gate)
                r.gd[at] = flat(dw_tiles(grad, taps_of(1), 1, -1) + dw_tiles(grad, taps_of(2), 2, -1))
                tap_sums(grad, step, 1, 1)
                tap_sums(grad, step, 2, 2)
                r.gk[27] = r.gk[27] + jnp.sum(grad, axis=0)
            return step

        lax.fori_loop(0, frames, mix_back, jnp.zeros((SIDE, 8, ib), f32))

        def hide_back(f, sums):
            at = frame_rows(f)
            previous = frame_rows(jnp.maximum(f - 1, 0))
            keep = keep_flag(f)
            keep_before = jnp.where(f > 0, keep_flag(jnp.maximum(f - 1, 0)), 0.0)
            now = r.gd[at]
            earlier = r.gd[previous]
            grad = r.gm[at]
            if s == 0:
                following = frame_rows(jnp.minimum(f + 1, frames - 1))
                later = now + r.gd[following]
                earlier = earlier + now
            else:
                later = now
                grad = grad * (1.0 + r.sig[at])
            grad = grad + keep_before * earlier - keep * later
            centred, z = norm_inner(s, 0, r.red[s, at])
            grad = real(grad * gelu_both(z)[1])
            r.g1[at] = grad
            return sums[0] + fold(grad), sums[1] + fold(grad * centred)

        sums = lax.fori_loop(0, frames, hide_back, (zero_n, zero_n))
        made = stat_start(r.stn, stat_base + 1, sums)
        shift_sum, gain_sum = stat_end(r.stn, stat_base + 1, made)
        r.gbi[s, 0:1] = shift_sum
        r.ggi[s, 0:1] = gain_sum
        mean, inv = moments_in[s][0]
        scale = inv * row(r.gi, s, 0)
        shift_mean, gain_mean = shift_sum / pixel_total, gain_sum / pixel_total
        copies = []
        for h in range(2):

            def reduce_back(i, _):
                at = pair_rows(h, i)
                centred = (r.red[s, at] - mean) * inv
                grad = real(scale * (r.g1[at] - (shift_mean + centred * gain_mean)))
                r.grf[s, at, cols(chan)] = grad.astype(bf16)
                return _

            lax.fori_loop(0, pairs, reduce_back, 0)
            copies.append(gather_start(r.grf.at[s], h))
        if s == 0:
            own = r.grf[0, :, cols(chan)]
            for piece in range(n_chan):
                at = slice(piece * cs, (piece + 1) * cs)
                r.gr[0, at] = dot(r.x[:, at], own, 0, 0).astype(bf16)
        gather_pass(r.grf.at[s], 0, copies[0])
        gather_pass(r.grf.at[s], 1, copies[1])
        if s == 0:
            load_wr[0].wait()
            arrive(weights_in["wr0"])
        for h in range(2):
            gather_end(copies[h])
            r.gin[part(h)] = dot(r.grf[s, part(h)], r.wrf[s], 1, 1) + r.gpre[part(h)]
            if s == 0:
                local_out.append(local(r.gin.at[part(h)], r.gin_out.at[part(h)]))
        if s == 1:
            r.gro[...] = dot(r.out0[...], r.grf[1], 0, 0).astype(bf16)
            weights_out.append(local(r.gro.at[:, cols(chan)], r.gr.at[1, wide(chan)]))
            for j in others:
                arrivals.append(remote(r.gro.at[:, cols(j)], r.gr.at[1, wide(chan)], (clip, j)))

    local_out, weights_out, arrivals = [], [], []
    backward(1, 4, 2, 1)
    backward(0, 6, 3, 3)

    for place in range(r.gk.shape[0]):
        r.kst[clip, place : place + 1, :] = jnp.sum(r.gk[place], axis=0, keepdims=True)
    made = [remote(r.kst.at[clip], r.kst.at[clip], (t, chan)) for t in clip_others]
    arrive(arrivals)
    for copy in weights_out:
        copy.wait()
    for s in range(2):
        local_out.append(local(r.gc.at[s], r.gc_out.at[s]))
        local_out.append(local(r.ge.at[s], r.ge_out.at[s]))
        local_out.append(local(r.gr.at[s], r.gr_out.at[s]))
    arrive(made)
    total = r.kst[0]
    for k in range(1, n_clip):
        total = total + r.kst[k]
    for index in range(3):
        r.gk_out[index] = total[9 * index : 9 * index + 9]
    r.ggb_out[...] = total[27:28]
    for copy in local_out:
        copy.wait()
    for copy in list(unsent):
        sent(copy)


def fused_call(n_clip, n_chan, pixel_total, *operands):
    rows, width = operands[0].shape
    cs = width // n_chan
    ib = LANES
    inner = ib * n_chan
    bf16, f32 = jnp.bfloat16, jnp.float32
    whole = pl.BlockSpec(memory_space=pltpu.VMEM)
    anywhere = pl.BlockSpec(memory_space=pl.ANY)
    scalars = pl.BlockSpec(memory_space=pltpu.SMEM)
    shape = jax.ShapeDtypeStruct
    V = pltpu.VMEM
    scratch = dict(
        x=V((rows, width), bf16),
        cot=V((rows, cs), bf16),
        wr0=V((width, ib), bf16),
        wrf=V((2, cs, inner), bf16),
        wef=V((2, inner, cs), bf16),
        wc=V((2, inner, 9 * ib), bf16),
        dkb=V((27, 8, ib), f32),
        red=V((2, rows, ib), f32),
        hid=V((2, rows, ib), f32),
        sig=V((rows, ib), f32),
        conv=V((2, rows, ib), f32),
        mixf=V((2, rows, inner), bf16),
        inf=V((2, rows, inner), bf16),
        ex=V((2, rows, cs), f32),
        out0=V((rows, cs), bf16),
        act=V((rows, cs), bf16),
        y=V((rows // 2, 9 * ib), f32),
        gpre=V((rows, cs), f32),
        gin=V((rows, cs), f32),
        gexp=V((rows, cs), bf16),
        gs=V((rows, 9 * ib), bf16),
        pb=V((rows, inner), bf16),
        ysend=V((2, rows, ib), bf16),
        rcore=V((5, 2, rows, ib), bf16),
        ryy=V((5, rows, ib), bf16),
        grf=V((2, rows, inner), bf16),
        gm=V((rows, ib), f32),
        gd=V((rows, ib), f32),
        g1=V((rows, ib), f32),
        gk=V((32, 8, ib), f32),
        kst=V((n_clip, 32, ib), f32),
        stn=V((8, n_clip, 2, ib), f32),
        stw=V((4, n_clip, 2, cs), f32),
        gc=V((2, inner, 9 * ib), bf16),
        geo=V((2, inner, cs), bf16),
        ge=V((2, ib, width), bf16),
        gro=V((cs, inner), bf16),
        gr=V((2, width, ib), bf16),
        ssem=pltpu.SemaphoreType.DMA((COPIES,)),
        rsem=pltpu.SemaphoreType.DMA((COPIES,)),
        lsem=pltpu.SemaphoreType.DMA((LOADS,)),
    )
    first = NAMES.index("x")
    return pl.pallas_call(
        partial(fused_kernel, n_clip, n_chan, pixel_total),
        out_shape=[
            shape((rows, cs), bf16),
            shape((rows, cs), f32),
            shape((2, 2, ib), f32),
            shape((2, 2, ib), f32),
            shape((2, cs), f32),
            shape((2, cs), f32),
            shape((3, 9, ib), f32),
            shape((1, ib), f32),
            shape((2, inner, 9 * ib), bf16),
            shape((2, ib, width), bf16),
            shape((2, width, ib), bf16),
        ],
        in_specs=[anywhere] * 5 + [scalars] + [whole] * 6,
        out_specs=[anywhere] * 2 + [whole] * 6 + [anywhere] * 3,
        scratch_shapes=[scratch[name] for name in NAMES[first:]],
        compiler_params=pltpu.CompilerParams(
            collective_id=0, has_side_effects=True, vmem_limit_bytes=62 * 1024 * 1024
        ),
    )(*operands)


def padded_rows(values):
    frame_rows = values.reshape(-1, SIDE, values.shape[-1])
    return jnp.pad(frame_rows, ((0, 0), (0, 1), (0, 0))).reshape(-1, values.shape[-1])


def real_rows(values):
    return values.reshape(-1, 8, values.shape[-1])[:, :SIDE].reshape(-1, values.shape[-1])


def fused(
    frames_in,
    boundary,
    w_reduce,
    gain_inner,
    bias_inner,
    w_conv,
    w_expand,
    gain_outer,
    bias_outer,
    depth_kernels,
    gate_bias,
    cotangent,
):
    n_clip, n_chan = lax.axis_size("clip"), lax.axis_size("chan")
    col_share = frames_in.shape[1] // n_chan
    pixel_total = frames_in.shape[0] * n_clip
    col_start = lax.axis_index("chan") * col_share
    act, gin, ggi, gbi, ggo, gbo, gk, ggb, gc, ge, gr = fused_call(
        n_clip,
        n_chan,
        float(pixel_total),
        padded_rows(frames_in),
        padded_rows(columns(cotangent, col_start, col_share)),
        w_reduce,
        w_conv,
        w_expand,
        boundary,
        gain_inner,
        bias_inner,
        gain_outer,
        bias_outer,
        depth_kernels,
        gate_bias.reshape(1, -1),
    )
    gr, gc, ge = lax.psum((gr, gc, ge), "clip")
    gc = gc.reshape(2, gc.shape[1], 9, -1).transpose(0, 2, 1, 3)
    return (
        real_rows(act),
        real_rows(gin),
        gr.astype(jnp.float32),
        ggi,
        gbi,
        gc.astype(jnp.float32),
        ge.astype(jnp.float32),
        ggo,
        gbo,
        gk,
        ggb.reshape(-1),
    )


def solution(mesh):
    in_specs = (
        P("clip", None),
        P("clip", None),
        P(None, None, "chan"),
        P(None, None, "chan"),
        P(None, None, "chan"),
        P(None, None, None, "chan"),
        P(None, "chan", None),
        P(),
        P(),
        P(None, None, "chan"),
        P("chan"),
        P("clip", None),
    )
    out_specs = (
        P("clip", "chan"),
        P("clip", "chan"),
        P(None, None, "chan"),
        P(None, None, "chan"),
        P(None, None, "chan"),
        P(None, None, None, "chan"),
        P(None, "chan", None),
        P(None, "chan"),
        P(None, "chan"),
        P(None, None, "chan"),
        P("chan"),
    )

    def run(*arguments):
        fits = fused_fits(mesh, arguments[0].shape, arguments[2].shape)
        return jax.shard_map(fused if fits else body, mesh=mesh, in_specs=in_specs, out_specs=out_specs, check_vma=False)(*arguments)

    return run
```

```python
from functools import partial
from types import SimpleNamespace

import jax
import jax.numpy as jnp
from jax import lax
from jax.experimental import pallas as pl
from jax.experimental.pallas import tpu as pltpu
from jax.sharding import PartitionSpec as P

SEG = 8
SIDE = 7


epsilon = 1e-05


def framed(values):
    return values.reshape(-1, SIDE, SIDE, values.shape[-1])


def shifted(frame_grid, row_step, col_step, dilation):
    padded = jnp.pad(frame_grid, ((0, 0), (dilation, dilation), (dilation, dilation), (0, 0)))
    return padded[
        :,
        dilation + row_step : dilation + row_step + SIDE,
        dilation + col_step : dilation + col_step + SIDE,
        :,
    ]


def depthwise(values, kernel, dilation):
    frame_grid = framed(values)
    running = jnp.zeros_like(frame_grid)
    for tap_index in range(9):
        running = (
            running
            + shifted(
                frame_grid,
                (tap_index // 3 - 1) * dilation,
                (tap_index % 3 - 1) * dilation,
                dilation,
            )
            * kernel[tap_index]
        )
    return running.reshape(values.shape)


def patch_rows(values):
    frame_grid = framed(values)
    pieces = [
        shifted(frame_grid, tap_index // 3 - 1, tap_index % 3 - 1, 1) for tap_index in range(9)
    ]
    return jnp.concatenate(pieces, axis=-1).reshape(values.shape[0], 9 * values.shape[1])


def unpatch(grad_rows, chan_width):
    frame_grid = grad_rows.reshape(-1, SIDE, SIDE, 9, chan_width)
    running = jnp.zeros(frame_grid.shape[:3] + (chan_width,), jnp.float32)
    for tap_index in range(9):
        running = running + shifted(
            frame_grid[:, :, :, tap_index, :], 1 - tap_index // 3, 1 - tap_index % 3, 1
        )
    return running.reshape(-1, chan_width)


def neighbours(values, boundary):
    clip_count = boundary.shape[0]
    frame_grid = values.reshape(clip_count, SEG, SIDE * SIDE, values.shape[-1])
    stop_mask = (boundary == 1)[:, :, None, None]
    start_mask = jnp.concatenate([jnp.ones_like(stop_mask[:, :1]), stop_mask[:, :-1]], axis=1)
    after_seg = jnp.concatenate([frame_grid[:, 1:], frame_grid[:, -1:]], axis=1)
    before = jnp.concatenate([frame_grid[:, :1], frame_grid[:, :-1]], axis=1)
    later_seg = jnp.where(stop_mask, frame_grid, after_seg)
    earlier = jnp.where(start_mask, frame_grid, before)
    return (later_seg.reshape(values.shape), earlier.reshape(values.shape))


def temporal(values, kernels, gate_vec, boundary, short_range):
    later_seg, earlier = neighbours(values, boundary)
    if short_range:
        return values + depthwise(later_seg - earlier, kernels[0], 1)
    change = later_seg - values
    logits = depthwise(change, kernels[1], 1) + depthwise(change, kernels[2], 2) + gate_vec
    return values + values * jax.nn.sigmoid(logits)


def columns(values, col_start, col_share):
    return lax.dynamic_slice_in_dim(values, col_start, col_share, values.ndim - 1)


def contract(left, right, left_dim, right_dim):
    return lax.dot_general(
        left, right, (((left_dim,), (right_dim,)), ((), ())), preferred_element_type=jnp.float32
    )


def normalize(values, gain_vec, bias_vec, pixel_total):
    col_sum, sq_sum = lax.psum((jnp.sum(values, axis=0), jnp.sum(values * values, axis=0)), "clip")
    mean_val = col_sum / pixel_total
    inv_std = lax.rsqrt(sq_sum / pixel_total - mean_val * mean_val + epsilon)
    centred = (values - mean_val) * inv_std
    return (centred * gain_vec + bias_vec, centred, inv_std)


def normalize_back(grad_rows, centred, inv_std, gain_vec, pixel_total):
    shift_sum, gain_sum = lax.psum(
        (jnp.sum(grad_rows, axis=0), jnp.sum(grad_rows * centred, axis=0)), "clip"
    )
    grad_in = inv_std * gain_vec * (grad_rows - (shift_sum + centred * gain_sum) / pixel_total)
    return (grad_in, gain_sum, shift_sum)


def block_forward(inputs, boundary, weights, short_range, pixel_total):
    w_red, gain_pair, bias_pair, w_cv, w_ex, gain_out, bias_out, kernels, gate_vec = weights
    reduced = jnp.dot(inputs, w_red, preferred_element_type=jnp.float32)
    norm_one, centred_one, inv_one = normalize(reduced, gain_pair[0], bias_pair[0], pixel_total)
    hidden, gelu_one = jax.vjp(jax.nn.gelu, norm_one)
    mixed_act, mix_back = jax.vjp(
        partial(temporal, boundary=boundary, short_range=short_range), hidden, kernels, gate_vec
    )
    gathered = lax.all_gather(mixed_act.astype(jnp.bfloat16), "chan", axis=1, tiled=True)
    patches = patch_rows(gathered)
    conv_out = jnp.dot(
        patches, w_cv.reshape(-1, w_cv.shape[-1]), preferred_element_type=jnp.float32
    )
    norm_two, centred_two, inv_two = normalize(conv_out, gain_pair[1], bias_pair[1], pixel_total)
    inner_full, gelu_two = jax.vjp(jax.nn.gelu, norm_two)
    inner_act = inner_full.astype(jnp.bfloat16)
    partial_out = jnp.dot(inner_act, w_ex, preferred_element_type=jnp.float32)
    expanded = lax.psum(partial_out.astype(jnp.bfloat16), "chan").astype(jnp.float32)
    norm_three, centred_three, inv_three = normalize(expanded, gain_out, bias_out, pixel_total)
    output_full, gelu_three = jax.vjp(jax.nn.gelu, norm_three + inputs.astype(jnp.float32))
    kept_state = (
        centred_one,
        inv_one,
        gelu_one,
        mix_back,
        patches,
        centred_two,
        inv_two,
        gelu_two,
        inner_act,
        centred_three,
        inv_three,
        gelu_three,
        gain_out,
    )
    return (output_full.astype(jnp.bfloat16), kept_state)


def block_backward(grad_out, inputs, weights, kept_state, pixel_total):
    w_red, gain_pair, bias_pair, w_cv, w_ex, gain_out, bias_out, kernels, gate_vec = weights
    (
        centred_one,
        inv_one,
        gelu_one,
        mix_back,
        patches,
        centred_two,
        inv_two,
        gelu_two,
        inner_act,
        centred_three,
        inv_three,
        gelu_three,
        gain_use,
    ) = kept_state
    grad_pre = gelu_three(grad_out)[0]
    grad_exp, gain_three, bias_three = normalize_back(
        grad_pre, centred_three, inv_three, gain_use, pixel_total
    )
    low_exp = grad_exp.astype(jnp.bfloat16)
    grad_wex = contract(inner_act, low_exp, 0, 0)
    grad_inner = contract(low_exp, w_ex, 1, 1)
    grad_two = gelu_two(grad_inner)[0]
    grad_cv, gain_two, bias_two = normalize_back(
        grad_two, centred_two, inv_two, gain_pair[1], pixel_total
    )
    low_cv = grad_cv.astype(jnp.bfloat16)
    flat_cv = w_cv.reshape(-1, w_cv.shape[-1])
    grad_wcv = contract(patches, low_cv, 0, 0).reshape(w_cv.shape)
    grad_patch = contract(low_cv, flat_cv, 1, 1)
    grad_mixed = lax.psum_scatter(
        unpatch(grad_patch, w_cv.shape[1]).astype(jnp.bfloat16),
        "chan",
        scatter_dimension=1,
        tiled=True,
    ).astype(jnp.float32)
    grad_hidden, grad_kern, grad_gate = mix_back(grad_mixed)
    grad_one = gelu_one(grad_hidden)[0]
    grad_red, gain_one, bias_one = normalize_back(
        grad_one, centred_one, inv_one, gain_pair[0], pixel_total
    )
    low_red = grad_red.astype(jnp.bfloat16)
    grad_wred = contract(inputs, low_red, 0, 0)
    partial_in = contract(low_red, w_red, 1, 1)
    grad_in = grad_pre + lax.psum(partial_in.astype(jnp.bfloat16), "chan").astype(jnp.float32)
    weight_terms = (grad_wred, grad_wcv, grad_wex, grad_kern, grad_gate)
    norm_terms = (gain_one, bias_one, gain_two, bias_two, gain_three, bias_three)
    return (grad_in, weight_terms, norm_terms)


def body(
    frames_in,
    boundary,
    w_reduce,
    gain_inner,
    bias_inner,
    w_conv,
    w_expand,
    gain_outer,
    bias_outer,
    depth_kernels,
    gate_bias,
    cotangent,
):
    row_count = frames_in.shape[0]
    pixel_total = row_count * lax.axis_size("clip")
    col_share = frames_in.shape[1] // lax.axis_size("chan")
    col_start = lax.axis_index("chan") * col_share
    block_weights = [
        (
            w_reduce[block_index],
            gain_inner[block_index],
            bias_inner[block_index],
            w_conv[block_index],
            w_expand[block_index],
            gain_outer[block_index],
            bias_outer[block_index],
            depth_kernels,
            gate_bias,
        )
        for block_index in range(2)
    ]
    first_out, kept_zero = block_forward(frames_in, boundary, block_weights[0], True, pixel_total)
    final_out, kept_one = block_forward(first_out, boundary, block_weights[1], False, pixel_total)
    layer_inputs = [frames_in, first_out]
    kept_states = [kept_zero, kept_one]
    grad_flow = cotangent.astype(jnp.float32)
    weight_sums = [None, None]
    norm_sums = [None, None]
    for block_index in (1, 0):
        grad_flow, weight_terms, norm_terms = block_backward(
            grad_flow,
            layer_inputs[block_index],
            block_weights[block_index],
            kept_states[block_index],
            pixel_total,
        )
        grad_wred, grad_wcv, grad_wex, grad_kern, grad_gate = weight_terms
        weight_terms = (
            lax.psum(grad_wred.astype(jnp.bfloat16), "clip").astype(jnp.float32),
            lax.psum(grad_wcv.astype(jnp.bfloat16), "clip").astype(jnp.float32),
            lax.psum(grad_wex.astype(jnp.bfloat16), "clip").astype(jnp.float32),
            lax.psum(grad_kern.astype(jnp.bfloat16), "clip").astype(jnp.float32),
            lax.psum(grad_gate.astype(jnp.bfloat16), "clip").astype(jnp.float32),
        )
        weight_sums[block_index] = weight_terms
        norm_sums[block_index] = norm_terms
    grad_reduce = jnp.stack([weight_sums[0][0], weight_sums[1][0]])
    grad_conv = jnp.stack([weight_sums[0][1], weight_sums[1][1]])
    grad_expand = jnp.stack([weight_sums[0][2], weight_sums[1][2]])
    grad_kernels = weight_sums[0][3] + weight_sums[1][3]
    grad_gate_bias = weight_sums[0][4] + weight_sums[1][4]
    grad_gain_inner = jnp.stack(
        [
            jnp.stack([norm_sums[0][0], norm_sums[0][2]]),
            jnp.stack([norm_sums[1][0], norm_sums[1][2]]),
        ]
    )
    grad_bias_inner = jnp.stack(
        [
            jnp.stack([norm_sums[0][1], norm_sums[0][3]]),
            jnp.stack([norm_sums[1][1], norm_sums[1][3]]),
        ]
    )
    grad_gain_outer = jnp.stack([norm_sums[0][4], norm_sums[1][4]])
    grad_bias_outer = jnp.stack([norm_sums[0][5], norm_sums[1][5]])
    activations = columns(final_out, col_start, col_share)
    input_grad = columns(grad_flow, col_start, col_share)
    grad_gain_outer = columns(grad_gain_outer, col_start, col_share)
    grad_bias_outer = columns(grad_bias_outer, col_start, col_share)
    return (
        activations,
        input_grad,
        grad_reduce,
        grad_gain_inner,
        grad_bias_inner,
        grad_conv,
        grad_expand,
        grad_gain_outer,
        grad_bias_outer,
        grad_kernels,
        grad_gate_bias,
    )


MESH = pl.DeviceIdType.MESH
LANES = 128
FRAME = SIDE * 8
PIXELS = SIDE * SIDE
SPLIT = 5
PAIR = 2 * FRAME
GELU_A = 0.7978845608028654
GELU_B = 0.044715
COPIES = 288
LOADS = 80


def fused_fits(mesh, frame_shape, reduce_shape):
    n_clip, n_chan = mesh.shape["clip"], mesh.shape["chan"]
    share = reduce_shape[2] // n_chan
    frames = frame_shape[0] // (n_clip * SIDE * SIDE)
    return n_chan == 4 and n_clip == 8 and share == LANES and frames == 2 * SEG


def gelu(z):
    return 0.5 * z * (1.0 + jnp.tanh(GELU_A * (z + GELU_B * z * z * z)))


def gelu_both(z):
    square = z * z
    t = jnp.tanh(GELU_A * (z + GELU_B * square * z))
    slope = 0.5 * (1.0 + t) + 0.5 * z * (1.0 - t * t) * (GELU_A * (1.0 + 3.0 * GELU_B * square))
    return 0.5 * z * (1.0 + t), slope


def real_columns(shape):
    return lax.rem(lax.broadcasted_iota(jnp.int32, shape, len(shape) - 2), 8) < SIDE


def real(values):
    return jnp.where(real_columns(values.shape), values, 0.0)


def fold(values):
    return jnp.sum(values.reshape(-1, 8, values.shape[-1]), axis=0)


def tiles(values):
    return values.reshape(SIDE, 8, values.shape[-1])


def flat(values):
    return values.reshape(FRAME, values.shape[-1])


def row_pad(v, reach):
    zeros = jnp.zeros((reach,) + v.shape[1:], v.dtype)
    return jnp.concatenate([zeros, v, zeros], axis=0)


def col_shift(v, step):
    if step == 0:
        return v
    moved = pltpu.roll(v, (-step) % 8, v.ndim - 2)
    if abs(step) == 2:
        place = lax.broadcasted_iota(jnp.int32, v.shape, v.ndim - 2)
        moved = jnp.where(place < 6 if step > 0 else place >= 2, moved, 0.0)
    return moved


def dw_tiles(v, taps, reach, sign):
    padded = row_pad(v, reach)
    total = None
    for b in (-1, 0, 1):
        part = None
        for a in (-1, 0, 1):
            start = reach + sign * reach * a
            term = taps[3 * (a + 1) + b + 1] * padded[start : start + SIDE]
            part = term if part is None else part + term
        part = col_shift(part, sign * reach * b)
        total = part if total is None else total + part
    return total


def dot(left, right, left_dim=1, right_dim=0):
    return lax.dot_general(
        left, right, (((left_dim,), (right_dim,)), ((), ())), preferred_element_type=jnp.float32
    )


NAMES = (
    "x_hbm", "cot_hbm", "wred_hbm", "wconv_hbm", "wexp_hbm", "bnd", "gi", "bi", "go", "bo",
    "dk", "gb", "act_out", "gin_out", "ggi", "gbi", "ggo", "gbo", "gk_out", "ggb_out", "gc_out",
    "ge_out", "gr_out", "x", "cot", "wr0", "wrf", "wef", "wc", "dkb", "red", "hid", "sig",
    "conv", "mixf", "inf", "ex", "out0", "act", "y", "gpre", "gin", "gexp", "gs", "pb", "ysend",
    "rcore", "ryy", "grf", "gm", "gd", "g1", "gk", "kst", "stn", "stw", "gca", "gcb", "geo",
    "ge", "gro", "gr", "rxa", "rxb", "fa", "fb", "fe", "fr", "rxe", "rxr", "rza", "rzb", "rze", "rzr", "ssem", "rsem",
    "lsem",
)


PLAN = {
    (1, 3): (("ge", 1),),
    (1, 4): (("ge", 1), ("gca", 1), ("gcb", 1)),
    (1, 5): (("ge", 1),),
    (1, 6): (("ge", 1), ("gca", 1)),
    (0, 1): (("gca", 1), ("gcb", 1), ("ge", 1)),
    (0, 2): (("gr", 1), ("gcb", 1), ("gca", 1)),
    (0, 3): (("gr", 1), ("gcb", 1), ("gca", 1), ("ge", 0)),
    (0, 4): (("gca", 0), ("gcb", 0), ("gr", 1), ("gcb", 1), ("ge", 0)),
    (0, 5): (("gr", 1), ("ge", 0)),
    (0, 6): (("gr", 0), ("gca", 0), ("gr", 1), ("ge", 0)),
    (0, 7): (
        ("gca", 0),
        ("gcb", 0),
        ("ge", 0),
        ("gr", 0),
        ("gcb", 0),
        ("gca", 0),
        ("gr", 0),
        ("gcb", 0),
        ("gr", 0),
        ("gca", 0),
        ("gcb", 0),
        ("gr", 0),
    ),
}


def fused_kernel(n_clip, n_chan, pixel_total, *refs):
    r = SimpleNamespace(**dict(zip(NAMES, refs)))
    rows, cs = r.cot.shape
    ib = LANES
    frames = rows // PIXELS
    chunk = frames // 2 * FRAME
    n_z = n_clip // 2
    first = -(-rows // 32) * 16
    starts, counts = (0, first), (first, rows - first)
    bf16, f32 = jnp.bfloat16, jnp.float32
    clip = lax.axis_index("clip")
    chan = lax.axis_index("chan")
    core, high = lax.rem(chan, 2), lax.div(chan, 2)
    j_core = (1 - core) + 2 * high
    j_y = core + 2 * (1 - high)
    j_far = (1 - core) + 2 * (1 - high)
    others = (j_core, j_y, j_far)
    z, side = lax.div(clip, 2), lax.rem(clip, 2)
    z_others = [lax.rem(z + d, n_z) for d in range(1, n_z)]
    clip_others = [lax.rem(clip + d, n_clip) for d in range(1, n_clip)]

    def cols(j):
        return pl.ds(pl.multiple_of(j * ib, ib), ib)

    def wide(j):
        return pl.ds(pl.multiple_of(j * cs, cs), cs)

    def part(h):
        return pl.ds(h * chunk, chunk)

    def raw(h):
        return pl.ds(starts[h], counts[h])

    counters = {"copy": 0, "load": 0}
    unsent = []

    def remote(src, dst, target):
        index = counters["copy"]
        counters["copy"] += 1
        made = pltpu.make_async_remote_copy(
            src_ref=src,
            dst_ref=dst,
            send_sem=r.ssem.at[index],
            recv_sem=r.rsem.at[index],
            device_id=target,
            device_id_type=MESH,
        )
        made.start()
        unsent.append(made)
        return made

    def sent(made):
        made.wait_send()
        unsent[:] = [other for other in unsent if other is not made]

    def local(src, dst):
        index = counters["load"]
        counters["load"] += 1
        made = pltpu.make_async_copy(src, dst, r.lsem.at[index])
        made.start()
        return made

    load_wr0 = local(r.wred_hbm.at[0], r.wr0)
    load_x = [local(r.x_hbm.at[raw(h)], r.x.at[raw(h)]) for h in range(2)]
    load_we = [
        local(r.wexp_hbm.at[s, :, wide(chan)], r.wef.at[s, cols(chan)]) for s in range(2)
    ]
    load_wr = [
        local(r.wred_hbm.at[s, wide(chan)], r.wrf.at[s, :, cols(chan)]) for s in range(2)
    ]
    load_wc = [
        [
            local(r.wconv_hbm.at[s, tap], r.wc.at[s, :, tap * ib : (tap + 1) * ib])
            for tap in range(9)
        ]
        for s in range(2)
    ]
    load_cot = local(r.cot_hbm.at[:, wide(chan)], r.cot)

    barrier = pltpu.get_barrier_semaphore()
    for target in clip_others:
        pl.semaphore_signal(barrier, inc=1, device_id=(target, chan), device_id_type=MESH)
    for target in others:
        pl.semaphore_signal(barrier, inc=1, device_id=(clip, target), device_id_type=MESH)
    pl.semaphore_wait(barrier, n_clip - 1 + n_chan - 1)

    def share_we(s):
        return [
            remote(r.wexp_hbm.at[s, :, wide(j)], r.wef.at[s, cols(chan)], (clip, j))
            for j in others
        ]

    def share_wr(s):
        return [
            remote(r.wred_hbm.at[s, wide(j)], r.wrf.at[s, :, cols(chan)], (clip, j))
            for j in others
        ]

    def arrive(copies):
        for made in copies:
            made.wait_recv()

    def stat_start(buf, slot, values):
        for k, value in enumerate(values):
            buf[slot, clip, k : k + 1, :] = jnp.sum(value, axis=0, keepdims=True)
        return [remote(buf.at[slot, clip], buf.at[slot, clip], (t, chan)) for t in clip_others]

    def stat_end(buf, slot, copies):
        arrive(copies)
        total = buf[slot, 0]
        for k in range(1, n_clip):
            total = total + buf[slot, k]
        return total[0:1], total[1:2]

    def moments(pair):
        mean = pair[0] / pixel_total
        return mean, lax.rsqrt(pair[1] / pixel_total - mean * mean + epsilon)

    def gather_start(full, at):
        mine = full.at[at, cols(chan)]
        return [remote(mine, mine, (clip, j_y)), remote(mine, mine, (clip, j_core))]

    def gather_pass(full, at, copies):
        copies[0].wait_recv()
        theirs = full.at[at, cols(j_y)]
        copies.append(remote(theirs, theirs, (clip, j_core)))

    def gather_end(copies):
        copies[1].wait_recv()
        copies[2].wait_recv()

    def scatter_start(slot, at):
        return [
            remote(r.pb.at[at, cols(j_far)], r.rcore.at[slot, 1, at], (clip, j_core)),
            remote(r.pb.at[at, cols(j_core)], r.rcore.at[slot, 0, at], (clip, j_core)),
        ]

    def scatter_pass(slot, at, copies):
        copies[0].wait_recv()
        both = r.pb[at, cols(j_y)].astype(f32) + r.rcore[slot, 1, at].astype(f32)
        r.ysend[slot % 2, at] = both.astype(bf16)
        copies.append(remote(r.ysend.at[slot % 2, at], r.ryy.at[slot, at], (clip, j_y)))

    def scatter_end(copies):
        copies[1].wait_recv()
        copies[2].wait_recv()
        sent(copies[0])
        sent(copies[1])
        sent(copies[2])

    def scatter_value(slot, at):
        mine = r.pb[at, cols(chan)].astype(f32)
        return mine + r.rcore[slot, 0, at].astype(f32) + r.ryy[slot, at].astype(f32)

    def keep_flag(f):
        return 1.0 - r.bnd[lax.div(f, SEG), lax.rem(f, SEG)].astype(f32)

    def taps_of(index):
        return [r.dkb[9 * index + tap] for tap in range(9)]

    def pair_rows(h, i):
        return pl.ds(pl.multiple_of(h * chunk + i * PAIR, 16), PAIR)

    def frame_rows(f):
        return pl.ds(pl.multiple_of(f * FRAME, 8), FRAME)

    def spread(ref, f):
        return jnp.stack(
            [ref[pl.ds(f * PIXELS + SIDE * k, 8), :] for k in range(SIDE)], axis=0
        )

    def squeeze(ref, f, value):
        for k in range(SIDE):
            ref[pl.ds(f * PIXELS + SIDE * k, 8), :] = value[k]

    pairs = frames // 4
    zero_n = jnp.zeros((8, ib), f32)
    zero_w = jnp.zeros((8, cs), f32)

    def each(start, count, step, one, begin):
        def at_step(i, carry):
            return one(pl.ds(pl.multiple_of(start + i * step, 16), step), carry)

        return lax.fori_loop(0, count // step, at_step, begin)

    def narrow(h, one, begin):
        step = next(n for n in (112, 96, 80, 64, 48, 32, 16) if counts[h] % n == 0)
        return each(starts[h], counts[h], step, one, begin)

    def broad(one, begin):
        return each(0, rows, 16, one, begin)

    moments_in = [[None, None, None], [None, None, None]]

    def row(ref, s, k=None):
        return ref[s, k : k + 1, :] if k is not None else ref[s : s + 1, wide(chan)]

    def norm_inner(s, k, x):
        mean, inv = moments_in[s][k]
        centred = (x - mean) * inv
        return centred, centred * row(r.gi, s, k) + row(r.bi, s, k)

    def norm_outer(s, x):
        mean, inv = moments_in[s][2]
        centred = (x - mean) * inv
        return centred, centred * row(r.go, s) + row(r.bo, s)

    def inner_input(s, at):
        return r.x[at, wide(chan)] if s == 0 else r.out0[at]

    def temporal_forward(s, h):
        def hide(i, _):
            f = h * (frames // 2) + i
            value = real(gelu(norm_inner(s, 0, spread(r.red.at[s], f))[1]))
            r.hid[s, frame_rows(f)] = flat(value)
            return _

        lax.fori_loop(0, frames // 2, hide, 0)

        def mix(i, before):
            base = pl.multiple_of(h * chunk + i * PAIR, 16)
            last = jnp.minimum(base + PAIR, (h + 1) * chunk - FRAME)
            f = h * (frames // 2) + 2 * i
            h0 = tiles(r.hid[s, pl.ds(base, FRAME)])
            h1 = tiles(r.hid[s, pl.ds(base + FRAME, FRAME)])
            h2 = tiles(r.hid[s, pl.ds(pl.multiple_of(last, 8), FRAME)])
            e0 = keep_flag(f) * (h1 - h0)
            e1 = keep_flag(f + 1) * (h2 - h1)
            if s == 0:
                taps = taps_of(0)
                m0 = real(h0 + dw_tiles(e0 + before, taps, 1, 1))
                m1 = real(h1 + dw_tiles(e1 + e0, taps, 1, 1))
            else:
                near, far = taps_of(1), taps_of(2)
                mixed = []
                for k, (hk, ek) in enumerate(((h0, e0), (h1, e1))):
                    logits = dw_tiles(ek, near, 1, 1) + dw_tiles(ek, far, 2, 1) + r.gb[...]
                    gate = 0.5 * (1.0 + jnp.tanh(0.5 * logits))
                    r.sig[pl.ds(base + k * FRAME, FRAME)] = flat(gate)
                    mixed.append(hk + hk * gate)
                m0, m1 = mixed
            both = jnp.concatenate([flat(m0), flat(m1)], axis=0).astype(bf16)
            r.mixf[s, pl.ds(base, PAIR), cols(chan)] = both
            return e1

        lax.fori_loop(0, pairs, mix, jnp.zeros((SIDE, 8, ib), f32))

    def conv_forward(s, h, sums):
        r.y[...] = dot(r.mixf[s, part(h)], r.wc[s])

        def add_taps(i, sums):
            at = pl.ds(pl.multiple_of(i * FRAME, 8), FRAME)
            total = None
            for b in (-1, 0, 1):
                run = None
                for a in (-1, 0, 1):
                    tap = 3 * (a + 1) + b + 1
                    term = row_pad(tiles(r.y[at, tap * ib : (tap + 1) * ib]), 1)
                    term = term[1 + a : 1 + a + SIDE]
                    run = term if run is None else run + term
                run = col_shift(run, b)
                total = run if total is None else total + run
            total = real(total)
            squeeze(r.conv.at[s], h * (frames // 2) + i, total)
            return sums[0] + jnp.sum(total, axis=0), sums[1] + jnp.sum(total * total, axis=0)

        return lax.fori_loop(0, frames // 2, add_taps, sums)

    def forward(s, stat_base, wide_slot):
        copies = []
        for h in range(2):
            temporal_forward(s, h)
            copies.append(gather_start(r.mixf.at[s], part(h)))
        sums = (zero_n, zero_n)
        for made in load_wc[s]:
            made.wait()
        gather_pass(r.mixf.at[s], part(0), copies[0])
        for h in range(2):
            gather_end(copies[h])
            sums = conv_forward(s, h, sums)
            if h == 0:
                gather_pass(r.mixf.at[s], part(1), copies[1])
        made = stat_start(r.stn, stat_base, sums)
        yield
        moments_in[s][1] = moments(stat_end(r.stn, stat_base, made))
        copies = []
        for h in range(2):

            def inside(at, _):
                value = gelu(norm_inner(s, 1, r.conv[s, at])[1])
                r.inf[s, at, cols(chan)] = value.astype(bf16)
                return _

            narrow(h, inside, 0)
            copies.append(gather_start(r.inf.at[s], raw(h)))
        yield
        gather_pass(r.inf.at[s], raw(0), copies[0])
        gather_pass(r.inf.at[s], raw(1), copies[1])
        sums = (zero_w, zero_w)
        for h in range(2):
            gather_end(copies[h])
            value = dot(r.inf[s, raw(h)], r.wef[s])
            r.ex[s, raw(h)] = value
            sums = (sums[0] + fold(value), sums[1] + fold(value * value))
        made = stat_start(r.stw, wide_slot, sums)
        yield
        moments_in[s][2] = moments(stat_end(r.stw, wide_slot, made))

    def spread_taps():
        for index in range(3):
            for tap in range(9):
                r.dkb[9 * index + tap] = jnp.broadcast_to(r.dk[index, tap : tap + 1, :], (8, ib))

    def clear(i, _):
        r.gk[i] = zero_n
        return _

    for s in range(2):
        r.red[s, rows : rows + 8] = zero_n

    weights_in = {}
    weights_in["we0"] = share_we(0)
    sums = (zero_n, zero_n)
    load_wr0.wait()
    for h in range(2):
        load_x[h].wait()
        value = dot(r.x[raw(h)], r.wr0[...])
        r.red[0, raw(h)] = value
        sums = (sums[0] + fold(value), sums[1] + fold(value * value))
    made = stat_start(r.stn, 0, sums)
    spread_taps()
    lax.fori_loop(0, r.gk.shape[0], clear, 0)
    moments_in[0][0] = moments(stat_end(r.stn, 0, made))

    stage = forward(0, 1, 0)
    next(stage)
    weights_in["wr1"] = share_wr(1)
    next(stage)
    load_we[0].wait()
    arrive(weights_in["we0"])
    next(stage)
    for _ in stage:
        pass

    def out_zero(at, _):
        z = norm_outer(0, r.ex[0, at])[1] + inner_input(0, at).astype(f32)
        r.out0[at] = gelu(z).astype(bf16)
        return _

    broad(out_zero, 0)

    def scatter_all(slot, chunk_rows, product, use, beside=None):
        copies = []
        for h in range(2):
            r.pb[chunk_rows(h)] = product(h).astype(bf16)
            copies.append(scatter_start(slot, chunk_rows(h)))
        scatter_pass(slot, chunk_rows(0), copies[0])
        scatter_pass(slot, chunk_rows(1), copies[1])
        if beside is not None:
            beside()
        for h in range(2):
            scatter_end(copies[h])
            use(h)

    held = {"sums": (zero_n, zero_n)}

    def use_reduced(h):
        value = scatter_value(0, raw(h))
        r.red[1, raw(h)] = value
        held["sums"] = (held["sums"][0] + fold(value), held["sums"][1] + fold(value * value))

    load_wr[1].wait()
    arrive(weights_in["wr1"])
    scatter_all(0, raw, lambda h: dot(r.out0[raw(h)], r.wrf[1]), use_reduced)
    made = stat_start(r.stn, 2, held["sums"])
    weights_in["we1"] = share_we(1)
    moments_in[1][0] = moments(stat_end(r.stn, 2, made))
    stage = forward(1, 3, 1)
    next(stage)
    weights_in["wr0"] = share_wr(0)
    next(stage)
    load_we[1].wait()
    arrive(weights_in["we1"])
    next(stage)
    for _ in stage:
        pass

    load_cot.wait()

    def out_one(at, sums):
        centred, z = norm_outer(1, r.ex[1, at])
        value, slope = gelu_both(z + r.out0[at].astype(f32))
        r.act[at] = value.astype(bf16)
        grad = r.cot[at].astype(f32) * slope
        r.gpre[at] = grad
        return sums[0] + fold(grad), sums[1] + fold(grad * centred)

    def top_zero(at, sums):
        centred, z = norm_outer(0, r.ex[0, at])
        grad = r.gin[at] * gelu_both(z + inner_input(0, at).astype(f32))[1]
        r.gpre[at] = grad
        return sums[0] + fold(grad), sums[1] + fold(grad * centred)

    def backward(s, stat_base, wide_slot, slot):
        sums = broad(out_one if s else top_zero, (zero_w, zero_w))
        made = stat_start(r.stw, wide_slot, sums)
        if s == 1:
            local_out.append(local(r.act, r.act_out))
        service(s, 1)
        shift_sum, gain_sum = stat_end(r.stw, wide_slot, made)
        r.gbo[s : s + 1] = shift_sum
        r.ggo[s : s + 1] = gain_sum
        mean, inv = moments_in[s][2]
        scale = inv * row(r.go, s)
        shift_mean, gain_mean = shift_sum / pixel_total, gain_sum / pixel_total

        def expand_back(at, _):
            centred = (r.ex[s, at] - mean) * inv
            grad = scale * (r.gpre[at] - (shift_mean + centred * gain_mean))
            r.gexp[at] = grad.astype(bf16)
            return _

        broad(expand_back, 0)
        held["sums"] = (zero_n, zero_n)

        def weight_expand():
            value = dot(r.inf[s], r.gexp[...], 0, 0).astype(bf16)
            r.geo[s] = value.reshape(r.geo.shape[1:])
            place = r.ge.at[s, :, :, :, wide(chan)]
            turned["ge", s] = [local(r.geo.at[s, chan], place)], [
                remote(r.geo.at[s, j], place, (clip, j)) for j in others
            ]
            service(s, 2)

        def use_inner(h):
            def one(at, sums):
                centred, z = norm_inner(s, 1, r.conv[s, at])
                grad = scatter_value(slot, at) * gelu_both(z)[1]
                r.g1[at] = grad
                return sums[0] + fold(grad), sums[1] + fold(grad * centred)

            held["sums"] = narrow(h, one, held["sums"])

        scatter_all(
            slot, raw, lambda h: dot(r.gexp[raw(h)], r.wef[s], 1, 1), use_inner, weight_expand
        )
        made = stat_start(r.stn, stat_base, held["sums"])
        service(s, 3)
        shift_sum, gain_sum = stat_end(r.stn, stat_base, made)
        r.gbi[s, 1:2] = shift_sum
        r.ggi[s, 1:2] = gain_sum
        mean, inv = moments_in[s][1]
        scale = inv * row(r.gi, s, 1)
        shift_mean, gain_mean = shift_sum / pixel_total, gain_sum / pixel_total

        def conv_back(i, _):
            at = pair_rows(0, i)
            halves = []
            for f in (2 * i, 2 * i + 1):
                centred = (spread(r.conv.at[s], f) - mean) * inv
                grad = scale * (spread(r.g1, f) - (shift_mean + centred * gain_mean))
                halves.append(real(grad))
            for b in (-1, 0, 1):
                moved = [row_pad(col_shift(v, -b), 1) for v in halves]
                for a in (-1, 0, 1):
                    tap = 3 * (a + 1) + b + 1
                    both = jnp.concatenate([flat(v[1 - a : 1 - a + SIDE]) for v in moved], axis=0)
                    r.gs[at, tap * ib : (tap + 1) * ib] = both.astype(bf16)
            return _

        lax.fori_loop(0, 2 * pairs, conv_back, 0)

        def weight_conv():
            for ref, taps in ((r.gca, slice(0, SPLIT * ib)), (r.gcb, slice(SPLIT * ib, 9 * ib))):
                value = dot(r.mixf[s], r.gs[:, taps], 0, 0).astype(bf16)
                ref[s] = value.reshape(ref.shape[1:])
            service(s, 4)

        def use_mixed(h):
            def one(i, _):
                at = pair_rows(h, i)
                r.gm[at] = real(scatter_value(slot + 1, at))
                return _

            lax.fori_loop(0, pairs, one, 0)

        scatter_all(
            slot + 1, part, lambda h: dot(r.gs[part(h)], r.wc[s], 1, 1), use_mixed, weight_conv
        )

        def tap_sums(grad, v, index, reach):
            for b in (-1, 0, 1):
                padded = row_pad(col_shift(v, reach * b), reach)
                for a in (-1, 0, 1):
                    start = reach + reach * a
                    place = 9 * index + 3 * (a + 1) + b + 1
                    r.gk[place] = r.gk[place] + jnp.sum(grad * padded[start : start + SIDE], axis=0)

        def mix_back(f, before):
            at = frame_rows(f)
            following = frame_rows(jnp.minimum(f + 1, frames - 1))
            here = tiles(r.hid[s, at])
            step = keep_flag(f) * (tiles(r.hid[s, following]) - here)
            grad = tiles(r.gm[at])
            if s == 0:
                r.gd[at] = flat(dw_tiles(grad, taps_of(0), 1, -1))
                tap_sums(grad, step + before, 0, 1)
            else:
                gate = tiles(r.sig[at])
                grad = grad * here * gate * (1.0 - gate)
                r.gd[at] = flat(dw_tiles(grad, taps_of(1), 1, -1) + dw_tiles(grad, taps_of(2), 2, -1))
                tap_sums(grad, step, 1, 1)
                tap_sums(grad, step, 2, 2)
                r.gk[27] = r.gk[27] + jnp.sum(grad, axis=0)
            return step

        lax.fori_loop(0, frames, mix_back, jnp.zeros((SIDE, 8, ib), f32))

        def hide_back(f, sums):
            at = frame_rows(f)
            previous = frame_rows(jnp.maximum(f - 1, 0))
            keep = keep_flag(f)
            keep_before = jnp.where(f > 0, keep_flag(jnp.maximum(f - 1, 0)), 0.0)
            now = r.gd[at]
            earlier = r.gd[previous]
            grad = r.gm[at]
            if s == 0:
                following = frame_rows(jnp.minimum(f + 1, frames - 1))
                later = now + r.gd[following]
                earlier = earlier + now
            else:
                later = now
                grad = grad * (1.0 + r.sig[at])
            grad = grad + keep_before * earlier - keep * later
            centred, z = norm_inner(s, 0, spread(r.red.at[s], f))
            grad = real(tiles(grad) * gelu_both(z)[1])
            squeeze(r.g1, f, grad)
            return sums[0] + jnp.sum(grad, axis=0), sums[1] + jnp.sum(grad * centred, axis=0)

        sums = lax.fori_loop(0, frames, hide_back, (zero_n, zero_n))
        made = stat_start(r.stn, stat_base + 1, sums)
        service(s, 5)
        shift_sum, gain_sum = stat_end(r.stn, stat_base + 1, made)
        r.gbi[s, 0:1] = shift_sum
        r.ggi[s, 0:1] = gain_sum
        mean, inv = moments_in[s][0]
        scale = inv * row(r.gi, s, 0)
        shift_mean, gain_mean = shift_sum / pixel_total, gain_sum / pixel_total
        copies = []
        for h in range(2):

            def reduce_back(at, _):
                centred = (r.red[s, at] - mean) * inv
                grad = scale * (r.g1[at] - (shift_mean + centred * gain_mean))
                r.grf[s, at, cols(chan)] = grad.astype(bf16)
                return _

            narrow(h, reduce_back, 0)
            copies.append(gather_start(r.grf.at[s], raw(h)))
        if s == 0:
            own = r.grf[0, :, cols(chan)]
            for piece in range(n_chan):
                value = dot(r.x[:, piece * cs : (piece + 1) * cs], own, 0, 0).astype(bf16)
                r.gr[0, piece] = value.reshape(r.gr.shape[2:])
        service(s, 6)
        gather_pass(r.grf.at[s], raw(0), copies[0])
        gather_pass(r.grf.at[s], raw(1), copies[1])
        if s == 0:
            load_wr[0].wait()
            arrive(weights_in["wr0"])
        for h in range(2):
            gather_end(copies[h])
            r.gin[raw(h)] = dot(r.grf[s, raw(h)], r.wrf[s], 1, 1) + r.gpre[raw(h)]
            if s == 0:
                local_out.append(local(r.gin.at[raw(h)], r.gin_out.at[raw(h)]))
        if s == 1:
            value = dot(r.out0[...], r.grf[1], 0, 0).astype(bf16)
            r.gro[...] = value.reshape(r.gro.shape)
            place = r.gr.at[1, chan]
            turned["gr", 1] = [local(r.gro.at[:, :, cols(chan)], place)], [
                remote(r.gro.at[:, :, cols(j)], place, (clip, j)) for j in others
            ]

    turned = {}

    def reduce_task(name, s, ref, from_side, from_z, result, write_out):
        mine, across = ref.at[s], (2 * z + 1 - side, chan)
        if (name, s) in turned:
            for copy in turned[name, s][0]:
                copy.wait()
            arrive(turned[name, s][1])
        made = remote(mine.at[:, 1 - side], from_side.at[s], across)
        yield
        made.wait_recv()
        for k in range(n_z):
            both = ref[s, k, side].astype(f32) + from_side[s, k].astype(f32)
            ref[s, k, side] = both.astype(bf16)
        made = [
            remote(mine.at[there, side], from_z.at[s, k], (2 * there + side, chan))
            for k, there in enumerate(z_others)
        ]
        yield
        arrive(made)
        total = ref[s, z, side].astype(f32)
        for k in range(n_z - 1):
            total = total + from_z[s, k].astype(f32)
        result[s, z, side] = total.astype(bf16)
        done = result.at[s, z, side]
        made = [remote(done, done, (2 * there + side, chan)) for there in z_others]
        yield
        arrive(made)
        done = result.at[s, :, side]
        made = remote(done, done, across)
        yield
        made.wait_recv()
        write_out(s)
        yield

    def write_conv(result, base):
        def write(s):
            for k in range(result.shape[-1] // ib):
                here = result.at[s, :, :, :, k * ib : (k + 1) * ib]
                local_out.append(local(here, r.gc_out.at[s, base + k]))

        return write

    def write_expand(s):
        local_out.append(local(r.fe.at[s], r.ge_out.at[s]))

    def write_reduce(s):
        local_out.append(local(r.fr.at[s], r.gr_out.at[s]))

    kinds = {
        "gca": (r.gca, r.rxa, r.rza, r.fa, write_conv(r.fa, 0)),
        "gcb": (r.gcb, r.rxb, r.rzb, r.fb, write_conv(r.fb, SPLIT)),
        "ge": (r.ge, r.rxe, r.rze, r.fe, write_expand),
        "gr": (r.gr, r.rxr, r.rzr, r.fr, write_reduce),
    }
    tasks = {(name, s): reduce_task(name, s, *kinds[name]) for name in kinds for s in range(2)}

    def advance(*steps):
        for step in steps:
            next(tasks[step])

    def service(s, point):
        advance(*PLAN.get((s, point), ()))

    local_out = []
    backward(1, 4, 2, 1)
    backward(0, 6, 3, 3)

    for place in range(r.gk.shape[0]):
        r.kst[clip, place : place + 1, :] = jnp.sum(r.gk[place], axis=0, keepdims=True)
    made = [remote(r.kst.at[clip], r.kst.at[clip], (t, chan)) for t in clip_others]
    service(0, 7)
    arrive(made)
    total = r.kst[0]
    for k in range(1, n_clip):
        total = total + r.kst[k]
    for index in range(3):
        r.gk_out[index] = total[9 * index : 9 * index + 9]
    r.ggb_out[...] = total[27:28]
    for copy in local_out:
        copy.wait()
    for copy in list(unsent):
        sent(copy)
    assert counters["copy"] <= COPIES and counters["load"] <= LOADS, counters


def fused_call(n_clip, n_chan, pixel_total, *operands):
    rows, width = operands[0].shape
    cs = width // n_chan
    ib = LANES
    inner = ib * n_chan
    n_z = n_clip // 2
    padded = rows // PIXELS * FRAME
    over = rows + 8
    bf16, f32 = jnp.bfloat16, jnp.float32
    whole = pl.BlockSpec(memory_space=pltpu.VMEM)
    anywhere = pl.BlockSpec(memory_space=pl.ANY)
    scalars = pl.BlockSpec(memory_space=pltpu.SMEM)
    shape = jax.ShapeDtypeStruct
    V = pltpu.VMEM
    scratch = dict(
        x=V((rows, width), bf16),
        cot=V((rows, cs), bf16),
        wr0=V((width, ib), bf16),
        wrf=V((2, cs, inner), bf16),
        wef=V((2, inner, cs), bf16),
        wc=V((2, inner, 9 * ib), bf16),
        dkb=V((27, 8, ib), f32),
        red=V((2, over, ib), f32),
        hid=V((2, padded, ib), f32),
        sig=V((padded, ib), f32),
        conv=V((2, over, ib), f32),
        mixf=V((2, padded, inner), bf16),
        inf=V((2, rows, inner), bf16),
        ex=V((2, rows, cs), f32),
        out0=V((rows, cs), bf16),
        act=V((rows, cs), bf16),
        y=V((padded // 2, 9 * ib), f32),
        gpre=V((rows, cs), f32),
        gin=V((rows, cs), f32),
        gexp=V((rows, cs), bf16),
        gs=V((padded, 9 * ib), bf16),
        pb=V((padded, inner), bf16),
        ysend=V((2, padded, ib), bf16),
        rcore=V((5, 2, padded, ib), bf16),
        ryy=V((5, padded, ib), bf16),
        grf=V((2, rows, inner), bf16),
        gm=V((padded, ib), f32),
        gd=V((padded, ib), f32),
        g1=V((over, ib), f32),
        gk=V((32, 8, ib), f32),
        kst=V((n_clip, 32, ib), f32),
        stn=V((8, n_clip, 2, ib), f32),
        stw=V((4, n_clip, 2, cs), f32),
        gca=V((2, n_z, 2, inner // n_clip, SPLIT * ib), bf16),
        gcb=V((2, n_z, 2, inner // n_clip, (9 - SPLIT) * ib), bf16),
        geo=V((2, n_chan, n_z, 2, ib // n_clip, cs), bf16),
        ge=V((2, n_z, 2, ib // n_clip, width), bf16),
        gro=V((2, cs // 2, inner), bf16),
        gr=V((2, n_z, 2, width // n_clip, ib), bf16),
        fa=V((2, n_z, 2, inner // n_clip, SPLIT * ib), bf16),
        fb=V((2, n_z, 2, inner // n_clip, (9 - SPLIT) * ib), bf16),
        fe=V((2, n_z, 2, ib // n_clip, width), bf16),
        fr=V((2, n_z, 2, width // n_clip, ib), bf16),
        rxa=V((2, n_z, inner // n_clip, SPLIT * ib), bf16),
        rxb=V((2, n_z, inner // n_clip, (9 - SPLIT) * ib), bf16),
        rxe=V((2, n_z, ib // n_clip, width), bf16),
        rxr=V((2, n_z, width // n_clip, ib), bf16),
        rza=V((2, n_z - 1, inner // n_clip, SPLIT * ib), bf16),
        rzb=V((2, n_z - 1, inner // n_clip, (9 - SPLIT) * ib), bf16),
        rze=V((2, n_z - 1, ib // n_clip, width), bf16),
        rzr=V((2, n_z - 1, width // n_clip, ib), bf16),
        ssem=pltpu.SemaphoreType.DMA((COPIES,)),
        rsem=pltpu.SemaphoreType.DMA((COPIES,)),
        lsem=pltpu.SemaphoreType.DMA((LOADS,)),
    )
    first = NAMES.index("x")
    return pl.pallas_call(
        partial(fused_kernel, n_clip, n_chan, pixel_total),
        out_shape=[
            shape((rows, cs), bf16),
            shape((rows, cs), f32),
            shape((2, 2, ib), f32),
            shape((2, 2, ib), f32),
            shape((2, cs), f32),
            shape((2, cs), f32),
            shape((3, 9, ib), f32),
            shape((1, ib), f32),
            shape((2, 9, n_z, 2, inner // n_clip, ib), bf16),
            shape((2, n_z, 2, ib // n_clip, width), bf16),
            shape((2, n_z, 2, width // n_clip, ib), bf16),
        ],
        in_specs=[anywhere] * 5 + [scalars] + [whole] * 6,
        out_specs=[anywhere] * 2 + [whole] * 6 + [anywhere] * 3,
        scratch_shapes=[scratch[name] for name in NAMES[first:]],
        compiler_params=pltpu.CompilerParams(
            collective_id=0, has_side_effects=True, vmem_limit_bytes=62 * 1024 * 1024
        ),
    )(*operands)


def fused(
    frames_in,
    boundary,
    w_reduce,
    gain_inner,
    bias_inner,
    w_conv,
    w_expand,
    gain_outer,
    bias_outer,
    depth_kernels,
    gate_bias,
    cotangent,
):
    n_clip, n_chan = lax.axis_size("clip"), lax.axis_size("chan")
    pixel_total = frames_in.shape[0] * n_clip
    act, gin, ggi, gbi, ggo, gbo, gk, ggb, gc, ge, gr = fused_call(
        n_clip,
        n_chan,
        float(pixel_total),
        frames_in,
        cotangent,
        w_reduce,
        w_conv,
        w_expand,
        boundary,
        gain_inner,
        bias_inner,
        gain_outer,
        bias_outer,
        depth_kernels,
        gate_bias.reshape(1, -1),
    )
    return (
        act,
        gin,
        gr.astype(jnp.float32).reshape(w_reduce.shape),
        ggi,
        gbi,
        gc.astype(jnp.float32).reshape(w_conv.shape),
        ge.astype(jnp.float32).reshape(w_expand.shape),
        ggo,
        gbo,
        gk,
        ggb.reshape(-1),
    )


def solution(mesh):
    in_specs = (
        P("clip", None),
        P("clip", None),
        P(None, None, "chan"),
        P(None, None, "chan"),
        P(None, None, "chan"),
        P(None, None, None, "chan"),
        P(None, "chan", None),
        P(),
        P(),
        P(None, None, "chan"),
        P("chan"),
        P("clip", None),
    )
    out_specs = (
        P("clip", "chan"),
        P("clip", "chan"),
        P(None, None, "chan"),
        P(None, None, "chan"),
        P(None, None, "chan"),
        P(None, None, None, "chan"),
        P(None, "chan", None),
        P(None, "chan"),
        P(None, "chan"),
        P(None, None, "chan"),
        P("chan"),
    )

    def run(*arguments):
        fits = fused_fits(mesh, arguments[0].shape, arguments[2].shape)
        return jax.shard_map(fused if fits else body, mesh=mesh, in_specs=in_specs, out_specs=out_specs, check_vma=False)(*arguments)

    return run
```

```python
from functools import partial
from types import SimpleNamespace

import jax
import jax.numpy as jnp
from jax import lax
from jax.experimental import pallas as pl
from jax.experimental.pallas import tpu as pltpu
from jax.sharding import PartitionSpec as P

SEG = 8
SIDE = 7


epsilon = 1e-05


def framed(values):
    return values.reshape(-1, SIDE, SIDE, values.shape[-1])


def shifted(frame_grid, row_step, col_step, dilation):
    padded = jnp.pad(frame_grid, ((0, 0), (dilation, dilation), (dilation, dilation), (0, 0)))
    return padded[
        :,
        dilation + row_step : dilation + row_step + SIDE,
        dilation + col_step : dilation + col_step + SIDE,
        :,
    ]


def depthwise(values, kernel, dilation):
    frame_grid = framed(values)
    running = jnp.zeros_like(frame_grid)
    for tap_index in range(9):
        running = (
            running
            + shifted(
                frame_grid,
                (tap_index // 3 - 1) * dilation,
                (tap_index % 3 - 1) * dilation,
                dilation,
            )
            * kernel[tap_index]
        )
    return running.reshape(values.shape)


def patch_rows(values):
    frame_grid = framed(values)
    pieces = [
        shifted(frame_grid, tap_index // 3 - 1, tap_index % 3 - 1, 1) for tap_index in range(9)
    ]
    return jnp.concatenate(pieces, axis=-1).reshape(values.shape[0], 9 * values.shape[1])


def unpatch(grad_rows, chan_width):
    frame_grid = grad_rows.reshape(-1, SIDE, SIDE, 9, chan_width)
    running = jnp.zeros(frame_grid.shape[:3] + (chan_width,), jnp.float32)
    for tap_index in range(9):
        running = running + shifted(
            frame_grid[:, :, :, tap_index, :], 1 - tap_index // 3, 1 - tap_index % 3, 1
        )
    return running.reshape(-1, chan_width)


def neighbours(values, boundary):
    clip_count = boundary.shape[0]
    frame_grid = values.reshape(clip_count, SEG, SIDE * SIDE, values.shape[-1])
    stop_mask = (boundary == 1)[:, :, None, None]
    start_mask = jnp.concatenate([jnp.ones_like(stop_mask[:, :1]), stop_mask[:, :-1]], axis=1)
    after_seg = jnp.concatenate([frame_grid[:, 1:], frame_grid[:, -1:]], axis=1)
    before = jnp.concatenate([frame_grid[:, :1], frame_grid[:, :-1]], axis=1)
    later_seg = jnp.where(stop_mask, frame_grid, after_seg)
    earlier = jnp.where(start_mask, frame_grid, before)
    return (later_seg.reshape(values.shape), earlier.reshape(values.shape))


def temporal(values, kernels, gate_vec, boundary, short_range):
    later_seg, earlier = neighbours(values, boundary)
    if short_range:
        return values + depthwise(later_seg - earlier, kernels[0], 1)
    change = later_seg - values
    logits = depthwise(change, kernels[1], 1) + depthwise(change, kernels[2], 2) + gate_vec
    return values + values * jax.nn.sigmoid(logits)


def columns(values, col_start, col_share):
    return lax.dynamic_slice_in_dim(values, col_start, col_share, values.ndim - 1)


def contract(left, right, left_dim, right_dim):
    return lax.dot_general(
        left, right, (((left_dim,), (right_dim,)), ((), ())), preferred_element_type=jnp.float32
    )


def normalize(values, gain_vec, bias_vec, pixel_total):
    col_sum, sq_sum = lax.psum((jnp.sum(values, axis=0), jnp.sum(values * values, axis=0)), "clip")
    mean_val = col_sum / pixel_total
    inv_std = lax.rsqrt(sq_sum / pixel_total - mean_val * mean_val + epsilon)
    centred = (values - mean_val) * inv_std
    return (centred * gain_vec + bias_vec, centred, inv_std)


def normalize_back(grad_rows, centred, inv_std, gain_vec, pixel_total):
    shift_sum, gain_sum = lax.psum(
        (jnp.sum(grad_rows, axis=0), jnp.sum(grad_rows * centred, axis=0)), "clip"
    )
    grad_in = inv_std * gain_vec * (grad_rows - (shift_sum + centred * gain_sum) / pixel_total)
    return (grad_in, gain_sum, shift_sum)


def block_forward(inputs, boundary, weights, short_range, pixel_total):
    w_red, gain_pair, bias_pair, w_cv, w_ex, gain_out, bias_out, kernels, gate_vec = weights
    reduced = jnp.dot(inputs, w_red, preferred_element_type=jnp.float32)
    norm_one, centred_one, inv_one = normalize(reduced, gain_pair[0], bias_pair[0], pixel_total)
    hidden, gelu_one = jax.vjp(jax.nn.gelu, norm_one)
    mixed_act, mix_back = jax.vjp(
        partial(temporal, boundary=boundary, short_range=short_range), hidden, kernels, gate_vec
    )
    gathered = lax.all_gather(mixed_act.astype(jnp.bfloat16), "chan", axis=1, tiled=True)
    patches = patch_rows(gathered)
    conv_out = jnp.dot(
        patches, w_cv.reshape(-1, w_cv.shape[-1]), preferred_element_type=jnp.float32
    )
    norm_two, centred_two, inv_two = normalize(conv_out, gain_pair[1], bias_pair[1], pixel_total)
    inner_full, gelu_two = jax.vjp(jax.nn.gelu, norm_two)
    inner_act = inner_full.astype(jnp.bfloat16)
    partial_out = jnp.dot(inner_act, w_ex, preferred_element_type=jnp.float32)
    expanded = lax.psum(partial_out.astype(jnp.bfloat16), "chan").astype(jnp.float32)
    norm_three, centred_three, inv_three = normalize(expanded, gain_out, bias_out, pixel_total)
    output_full, gelu_three = jax.vjp(jax.nn.gelu, norm_three + inputs.astype(jnp.float32))
    kept_state = (
        centred_one,
        inv_one,
        gelu_one,
        mix_back,
        patches,
        centred_two,
        inv_two,
        gelu_two,
        inner_act,
        centred_three,
        inv_three,
        gelu_three,
        gain_out,
    )
    return (output_full.astype(jnp.bfloat16), kept_state)


def block_backward(grad_out, inputs, weights, kept_state, pixel_total):
    w_red, gain_pair, bias_pair, w_cv, w_ex, gain_out, bias_out, kernels, gate_vec = weights
    (
        centred_one,
        inv_one,
        gelu_one,
        mix_back,
        patches,
        centred_two,
        inv_two,
        gelu_two,
        inner_act,
        centred_three,
        inv_three,
        gelu_three,
        gain_use,
    ) = kept_state
    grad_pre = gelu_three(grad_out)[0]
    grad_exp, gain_three, bias_three = normalize_back(
        grad_pre, centred_three, inv_three, gain_use, pixel_total
    )
    low_exp = grad_exp.astype(jnp.bfloat16)
    grad_wex = contract(inner_act, low_exp, 0, 0)
    grad_inner = contract(low_exp, w_ex, 1, 1)
    grad_two = gelu_two(grad_inner)[0]
    grad_cv, gain_two, bias_two = normalize_back(
        grad_two, centred_two, inv_two, gain_pair[1], pixel_total
    )
    low_cv = grad_cv.astype(jnp.bfloat16)
    flat_cv = w_cv.reshape(-1, w_cv.shape[-1])
    grad_wcv = contract(patches, low_cv, 0, 0).reshape(w_cv.shape)
    grad_patch = contract(low_cv, flat_cv, 1, 1)
    grad_mixed = lax.psum_scatter(
        unpatch(grad_patch, w_cv.shape[1]).astype(jnp.bfloat16),
        "chan",
        scatter_dimension=1,
        tiled=True,
    ).astype(jnp.float32)
    grad_hidden, grad_kern, grad_gate = mix_back(grad_mixed)
    grad_one = gelu_one(grad_hidden)[0]
    grad_red, gain_one, bias_one = normalize_back(
        grad_one, centred_one, inv_one, gain_pair[0], pixel_total
    )
    low_red = grad_red.astype(jnp.bfloat16)
    grad_wred = contract(inputs, low_red, 0, 0)
    partial_in = contract(low_red, w_red, 1, 1)
    grad_in = grad_pre + lax.psum(partial_in.astype(jnp.bfloat16), "chan").astype(jnp.float32)
    weight_terms = (grad_wred, grad_wcv, grad_wex, grad_kern, grad_gate)
    norm_terms = (gain_one, bias_one, gain_two, bias_two, gain_three, bias_three)
    return (grad_in, weight_terms, norm_terms)


def body(
    frames_in,
    boundary,
    w_reduce,
    gain_inner,
    bias_inner,
    w_conv,
    w_expand,
    gain_outer,
    bias_outer,
    depth_kernels,
    gate_bias,
    cotangent,
):
    row_count = frames_in.shape[0]
    pixel_total = row_count * lax.axis_size("clip")
    col_share = frames_in.shape[1] // lax.axis_size("chan")
    col_start = lax.axis_index("chan") * col_share
    block_weights = [
        (
            w_reduce[block_index],
            gain_inner[block_index],
            bias_inner[block_index],
            w_conv[block_index],
            w_expand[block_index],
            gain_outer[block_index],
            bias_outer[block_index],
            depth_kernels,
            gate_bias,
        )
        for block_index in range(2)
    ]
    first_out, kept_zero = block_forward(frames_in, boundary, block_weights[0], True, pixel_total)
    final_out, kept_one = block_forward(first_out, boundary, block_weights[1], False, pixel_total)
    layer_inputs = [frames_in, first_out]
    kept_states = [kept_zero, kept_one]
    grad_flow = cotangent.astype(jnp.float32)
    weight_sums = [None, None]
    norm_sums = [None, None]
    for block_index in (1, 0):
        grad_flow, weight_terms, norm_terms = block_backward(
            grad_flow,
            layer_inputs[block_index],
            block_weights[block_index],
            kept_states[block_index],
            pixel_total,
        )
        grad_wred, grad_wcv, grad_wex, grad_kern, grad_gate = weight_terms
        weight_terms = (
            lax.psum(grad_wred.astype(jnp.bfloat16), "clip").astype(jnp.float32),
            lax.psum(grad_wcv.astype(jnp.bfloat16), "clip").astype(jnp.float32),
            lax.psum(grad_wex.astype(jnp.bfloat16), "clip").astype(jnp.float32),
            lax.psum(grad_kern.astype(jnp.bfloat16), "clip").astype(jnp.float32),
            lax.psum(grad_gate.astype(jnp.bfloat16), "clip").astype(jnp.float32),
        )
        weight_sums[block_index] = weight_terms
        norm_sums[block_index] = norm_terms
    grad_reduce = jnp.stack([weight_sums[0][0], weight_sums[1][0]])
    grad_conv = jnp.stack([weight_sums[0][1], weight_sums[1][1]])
    grad_expand = jnp.stack([weight_sums[0][2], weight_sums[1][2]])
    grad_kernels = weight_sums[0][3] + weight_sums[1][3]
    grad_gate_bias = weight_sums[0][4] + weight_sums[1][4]
    grad_gain_inner = jnp.stack(
        [
            jnp.stack([norm_sums[0][0], norm_sums[0][2]]),
            jnp.stack([norm_sums[1][0], norm_sums[1][2]]),
        ]
    )
    grad_bias_inner = jnp.stack(
        [
            jnp.stack([norm_sums[0][1], norm_sums[0][3]]),
            jnp.stack([norm_sums[1][1], norm_sums[1][3]]),
        ]
    )
    grad_gain_outer = jnp.stack([norm_sums[0][4], norm_sums[1][4]])
    grad_bias_outer = jnp.stack([norm_sums[0][5], norm_sums[1][5]])
    activations = columns(final_out, col_start, col_share)
    input_grad = columns(grad_flow, col_start, col_share)
    grad_gain_outer = columns(grad_gain_outer, col_start, col_share)
    grad_bias_outer = columns(grad_bias_outer, col_start, col_share)
    return (
        activations,
        input_grad,
        grad_reduce,
        grad_gain_inner,
        grad_bias_inner,
        grad_conv,
        grad_expand,
        grad_gain_outer,
        grad_bias_outer,
        grad_kernels,
        grad_gate_bias,
    )


MESH = pl.DeviceIdType.MESH
LANES = 128
FRAME = SIDE * 8
PIXELS = SIDE * SIDE
SPLIT = 5
PAIR = 2 * FRAME
GELU_A = 0.7978845608028654
GELU_B = 0.044715
COPIES = 288
LOADS = 80


def fused_fits(mesh, frame_shape, reduce_shape):
    n_clip, n_chan = mesh.shape["clip"], mesh.shape["chan"]
    share = reduce_shape[2] // n_chan
    frames = frame_shape[0] // (n_clip * SIDE * SIDE)
    return n_chan == 4 and n_clip == 8 and share == LANES and frames == 2 * SEG


def gelu(z):
    return 0.5 * z * (1.0 + jnp.tanh(GELU_A * (z + GELU_B * z * z * z)))


def gelu_both(z):
    square = z * z
    t = jnp.tanh(GELU_A * (z + GELU_B * square * z))
    slope = 0.5 * (1.0 + t) + 0.5 * z * (1.0 - t * t) * (GELU_A * (1.0 + 3.0 * GELU_B * square))
    return 0.5 * z * (1.0 + t), slope


def real_columns(shape):
    return lax.rem(lax.broadcasted_iota(jnp.int32, shape, len(shape) - 2), 8) < SIDE


def real(values):
    return jnp.where(real_columns(values.shape), values, 0.0)


def fold(values):
    return jnp.sum(values.reshape(-1, 8, values.shape[-1]), axis=0)


def tiles(values):
    return values.reshape(SIDE, 8, values.shape[-1])


def flat(values):
    return values.reshape(FRAME, values.shape[-1])


def row_pad(v, reach):
    zeros = jnp.zeros((reach,) + v.shape[1:], v.dtype)
    return jnp.concatenate([zeros, v, zeros], axis=0)


def col_shift(v, step):
    if step == 0:
        return v
    moved = pltpu.roll(v, (-step) % 8, v.ndim - 2)
    if abs(step) == 2:
        place = lax.broadcasted_iota(jnp.int32, v.shape, v.ndim - 2)
        moved = jnp.where(place < 6 if step > 0 else place >= 2, moved, 0.0)
    return moved


def dw_tiles(v, taps, reach, sign):
    padded = row_pad(v, reach)
    total = None
    for b in (-1, 0, 1):
        part = None
        for a in (-1, 0, 1):
            start = reach + sign * reach * a
            term = taps[3 * (a + 1) + b + 1] * padded[start : start + SIDE]
            part = term if part is None else part + term
        part = col_shift(part, sign * reach * b)
        total = part if total is None else total + part
    return total


def dot(left, right, left_dim=1, right_dim=0):
    return lax.dot_general(
        left, right, (((left_dim,), (right_dim,)), ((), ())), preferred_element_type=jnp.float32
    )


NAMES = (
    "x_hbm", "cot_hbm", "wred_hbm", "wconv_hbm", "wexp_hbm", "bnd", "gi", "bi", "go", "bo",
    "dk", "gb", "act_out", "gin_out", "ggi", "gbi", "ggo", "gbo", "gk_out", "ggb_out", "gc_out",
    "ge_out", "gr_out", "x", "cot", "wr0", "wrf", "wef", "wc", "dkb", "red", "hid", "sig",
    "conv", "mixf", "inf", "ex", "out0", "act", "y", "gpre", "gin", "gexp", "gs", "pb", "ysend",
    "rcore", "ryy", "grf", "gm", "gd", "g1", "gk", "kst", "stn", "stw", "gca", "gcb", "geo",
    "ge", "gro", "gr", "rxa", "rxb", "fa", "fb", "fe", "fr", "rxe", "rxr", "rza", "rzb", "rze", "rzr", "ssem", "rsem",
    "lsem",
)


PLAN = {
    (1, 3): (("ge", 1),),
    (1, 4): (("ge", 1), ("gca", 1), ("gcb", 1)),
    (1, 5): (("ge", 1),),
    (1, 6): (("ge", 1), ("gca", 1)),
    (0, 1): (("gca", 1), ("gcb", 1), ("ge", 1)),
    (0, 2): (("gr", 1), ("gcb", 1), ("gca", 1)),
    (0, 3): (("gr", 1), ("gcb", 1), ("gca", 1), ("ge", 0)),
    (0, 4): (("gca", 0), ("gcb", 0), ("gr", 1), ("gcb", 1), ("ge", 0)),
    (0, 5): (("gr", 1), ("ge", 0)),
    (0, 6): (("gr", 0), ("gca", 0), ("gr", 1), ("ge", 0)),
    (0, 7): (
        ("gca", 0),
        ("gcb", 0),
        ("ge", 0),
        ("gr", 0),
        ("gcb", 0),
        ("gca", 0),
        ("gr", 0),
        ("gcb", 0),
        ("gr", 0),
        ("gca", 0),
        ("gcb", 0),
        ("gr", 0),
    ),
}


def fused_kernel(n_clip, n_chan, pixel_total, *refs):
    r = SimpleNamespace(**dict(zip(NAMES, refs)))
    rows, cs = r.cot.shape
    ib = LANES
    frames = rows // PIXELS
    chunk = frames // 2 * FRAME
    n_z = n_clip // 2
    first = -(-rows // 32) * 16
    starts, counts = (0, first), (first, rows - first)
    bf16, f32 = jnp.bfloat16, jnp.float32
    clip = lax.axis_index("clip")
    chan = lax.axis_index("chan")
    core, high = lax.rem(chan, 2), lax.div(chan, 2)
    j_core = (1 - core) + 2 * high
    j_y = core + 2 * (1 - high)
    j_far = (1 - core) + 2 * (1 - high)
    others = (j_core, j_y, j_far)
    z, side = lax.div(clip, 2), lax.rem(clip, 2)
    z_others = [lax.rem(z + d, n_z) for d in range(1, n_z)]
    clip_others = [lax.rem(clip + d, n_clip) for d in range(1, n_clip)]

    def cols(j):
        return pl.ds(pl.multiple_of(j * ib, ib), ib)

    def wide(j):
        return pl.ds(pl.multiple_of(j * cs, cs), cs)

    def part(h):
        return pl.ds(h * chunk, chunk)

    def raw(h):
        return pl.ds(starts[h], counts[h])

    counters = {"copy": 0, "load": 0}
    unsent = []

    def remote(src, dst, target):
        index = counters["copy"]
        counters["copy"] += 1
        made = pltpu.make_async_remote_copy(
            src_ref=src,
            dst_ref=dst,
            send_sem=r.ssem.at[index],
            recv_sem=r.rsem.at[index],
            device_id=target,
            device_id_type=MESH,
        )
        made.start()
        unsent.append(made)
        return made

    def sent(made):
        made.wait_send()
        unsent[:] = [other for other in unsent if other is not made]

    def local(src, dst):
        index = counters["load"]
        counters["load"] += 1
        made = pltpu.make_async_copy(src, dst, r.lsem.at[index])
        made.start()
        return made

    load_wr0 = local(r.wred_hbm.at[0], r.wr0)
    load_x = [local(r.x_hbm.at[raw(h)], r.x.at[raw(h)]) for h in range(2)]
    load_we = [
        local(r.wexp_hbm.at[s, :, wide(chan)], r.wef.at[s, cols(chan)]) for s in range(2)
    ]
    load_wr = [
        local(r.wred_hbm.at[s, wide(chan)], r.wrf.at[s, :, cols(chan)]) for s in range(2)
    ]
    load_wc = [
        [
            local(r.wconv_hbm.at[s, tap], r.wc.at[s, :, tap * ib : (tap + 1) * ib])
            for tap in range(9)
        ]
        for s in range(2)
    ]
    load_cot = local(r.cot_hbm.at[:, wide(chan)], r.cot)

    barrier = pltpu.get_barrier_semaphore()
    for target in clip_others:
        pl.semaphore_signal(barrier, inc=1, device_id=(target, chan), device_id_type=MESH)
    for target in others:
        pl.semaphore_signal(barrier, inc=1, device_id=(clip, target), device_id_type=MESH)
    pl.semaphore_wait(barrier, n_clip - 1 + n_chan - 1)

    def share_we(s):
        return [
            remote(r.wexp_hbm.at[s, :, wide(j)], r.wef.at[s, cols(chan)], (clip, j))
            for j in others
        ]

    def share_wr(s):
        return [
            remote(r.wred_hbm.at[s, wide(j)], r.wrf.at[s, :, cols(chan)], (clip, j))
            for j in others
        ]

    def arrive(copies):
        for made in copies:
            made.wait_recv()

    def stat_start(buf, slot, values):
        for k, value in enumerate(values):
            buf[slot, clip, k : k + 1, :] = jnp.sum(value, axis=0, keepdims=True)
        return [remote(buf.at[slot, clip], buf.at[slot, clip], (t, chan)) for t in clip_others]

    def stat_end(buf, slot, copies):
        arrive(copies)
        total = buf[slot, 0]
        for k in range(1, n_clip):
            total = total + buf[slot, k]
        return total[0:1], total[1:2]

    def moments(pair):
        mean = pair[0] / pixel_total
        return mean, lax.rsqrt(pair[1] / pixel_total - mean * mean + epsilon)

    def gather_start(full, at):
        mine = full.at[at, cols(chan)]
        return [remote(mine, mine, (clip, j_y)), remote(mine, mine, (clip, j_core))]

    def gather_pass(full, at, copies):
        copies[0].wait_recv()
        theirs = full.at[at, cols(j_y)]
        copies.append(remote(theirs, theirs, (clip, j_core)))

    def gather_end(copies):
        copies[1].wait_recv()
        copies[2].wait_recv()

    def scatter_start(slot, at):
        return [
            remote(r.pb.at[at, cols(j_far)], r.rcore.at[slot, 1, at], (clip, j_core)),
            remote(r.pb.at[at, cols(j_core)], r.rcore.at[slot, 0, at], (clip, j_core)),
        ]

    def scatter_pass(slot, at, copies):
        copies[0].wait_recv()
        both = r.pb[at, cols(j_y)].astype(f32) + r.rcore[slot, 1, at].astype(f32)
        r.ysend[slot % 2, at] = both.astype(bf16)
        copies.append(remote(r.ysend.at[slot % 2, at], r.ryy.at[slot, at], (clip, j_y)))

    def scatter_end(copies):
        copies[1].wait_recv()
        copies[2].wait_recv()
        sent(copies[0])
        sent(copies[1])
        sent(copies[2])

    def scatter_value(slot, at):
        mine = r.pb[at, cols(chan)].astype(f32)
        return mine + r.rcore[slot, 0, at].astype(f32) + r.ryy[slot, at].astype(f32)

    def keep_flag(f):
        return 1.0 - r.bnd[lax.div(f, SEG), lax.rem(f, SEG)].astype(f32)

    def taps_of(index):
        return [r.dkb[9 * index + tap] for tap in range(9)]

    def pair_rows(h, i):
        return pl.ds(pl.multiple_of(h * chunk + i * PAIR, 16), PAIR)

    def frame_rows(f):
        return pl.ds(pl.multiple_of(f * FRAME, 8), FRAME)

    def spread(ref, f):
        return jnp.stack(
            [ref[pl.ds(f * PIXELS + SIDE * k, 8), :] for k in range(SIDE)], axis=0
        )

    def squeeze(ref, f, value):
        for k in range(SIDE):
            ref[pl.ds(f * PIXELS + SIDE * k, 8), :] = value[k]

    pairs = frames // 4
    zero_n = jnp.zeros((8, ib), f32)
    zero_w = jnp.zeros((8, cs), f32)

    def each(start, count, step, one, begin):
        def at_step(i, carry):
            return one(pl.ds(pl.multiple_of(start + i * step, 16), step), carry)

        return lax.fori_loop(0, count // step, at_step, begin)

    def narrow(h, one, begin):
        step = next(n for n in (112, 96, 80, 64, 48, 32, 16) if counts[h] % n == 0)
        return each(starts[h], counts[h], step, one, begin)

    def broad(one, begin):
        return each(0, rows, 16, one, begin)

    moments_in = [[None, None, None], [None, None, None]]

    def row(ref, s, k=None):
        return ref[s, k : k + 1, :] if k is not None else ref[s : s + 1, wide(chan)]

    def norm_inner(s, k, x):
        mean, inv = moments_in[s][k]
        centred = (x - mean) * inv
        return centred, centred * row(r.gi, s, k) + row(r.bi, s, k)

    def norm_outer(s, x):
        mean, inv = moments_in[s][2]
        centred = (x - mean) * inv
        return centred, centred * row(r.go, s) + row(r.bo, s)

    def inner_input(s, at):
        return r.x[at, wide(chan)] if s == 0 else r.out0[at]

    def temporal_forward(s, h):
        def hide(i, _):
            f = h * (frames // 2) + i
            value = real(gelu(norm_inner(s, 0, spread(r.red.at[s], f))[1]))
            r.hid[s, frame_rows(f)] = flat(value)
            return _

        lax.fori_loop(0, frames // 2, hide, 0)

        def mix(i, before):
            base = pl.multiple_of(h * chunk + i * PAIR, 16)
            last = jnp.minimum(base + PAIR, (h + 1) * chunk - FRAME)
            f = h * (frames // 2) + 2 * i
            h0 = tiles(r.hid[s, pl.ds(base, FRAME)])
            h1 = tiles(r.hid[s, pl.ds(base + FRAME, FRAME)])
            h2 = tiles(r.hid[s, pl.ds(pl.multiple_of(last, 8), FRAME)])
            e0 = keep_flag(f) * (h1 - h0)
            e1 = keep_flag(f + 1) * (h2 - h1)
            if s == 0:
                taps = taps_of(0)
                m0 = real(h0 + dw_tiles(e0 + before, taps, 1, 1))
                m1 = real(h1 + dw_tiles(e1 + e0, taps, 1, 1))
            else:
                near, far = taps_of(1), taps_of(2)
                mixed = []
                for k, (hk, ek) in enumerate(((h0, e0), (h1, e1))):
                    logits = dw_tiles(ek, near, 1, 1) + dw_tiles(ek, far, 2, 1) + r.gb[...]
                    gate = 0.5 * (1.0 + jnp.tanh(0.5 * logits))
                    r.sig[pl.ds(base + k * FRAME, FRAME)] = flat(gate)
                    mixed.append(hk + hk * gate)
                m0, m1 = mixed
            both = jnp.concatenate([flat(m0), flat(m1)], axis=0).astype(bf16)
            r.mixf[s, pl.ds(base, PAIR), cols(chan)] = both
            return e1

        lax.fori_loop(0, pairs, mix, jnp.zeros((SIDE, 8, ib), f32))

    def conv_forward(s, h, sums):
        r.y[...] = dot(r.mixf[s, part(h)], r.wc[s])

        def add_taps(i, sums):
            at = pl.ds(pl.multiple_of(i * FRAME, 8), FRAME)
            total = None
            for b in (-1, 0, 1):
                run = None
                for a in (-1, 0, 1):
                    tap = 3 * (a + 1) + b + 1
                    term = row_pad(tiles(r.y[at, tap * ib : (tap + 1) * ib]), 1)
                    term = term[1 + a : 1 + a + SIDE]
                    run = term if run is None else run + term
                run = col_shift(run, b)
                total = run if total is None else total + run
            total = real(total)
            squeeze(r.conv.at[s], h * (frames // 2) + i, total)
            return sums[0] + jnp.sum(total, axis=0), sums[1] + jnp.sum(total * total, axis=0)

        return lax.fori_loop(0, frames // 2, add_taps, sums)

    def forward(s, stat_base, wide_slot):
        copies = []
        for h in range(2):
            temporal_forward(s, h)
            copies.append(gather_start(r.mixf.at[s], part(h)))
        sums = (zero_n, zero_n)
        for made in load_wc[s]:
            made.wait()
        gather_pass(r.mixf.at[s], part(0), copies[0])
        for h in range(2):
            gather_end(copies[h])
            sums = conv_forward(s, h, sums)
            if h == 0:
                gather_pass(r.mixf.at[s], part(1), copies[1])
        made = stat_start(r.stn, stat_base, sums)
        yield
        moments_in[s][1] = moments(stat_end(r.stn, stat_base, made))
        copies = []
        for h in range(2):

            def inside(at, _):
                value = gelu(norm_inner(s, 1, r.conv[s, at])[1])
                r.inf[s, at, cols(chan)] = value.astype(bf16)
                return _

            narrow(h, inside, 0)
            copies.append(gather_start(r.inf.at[s], raw(h)))
        yield
        gather_pass(r.inf.at[s], raw(0), copies[0])
        gather_pass(r.inf.at[s], raw(1), copies[1])
        sums = (zero_w, zero_w)
        for h in range(2):
            gather_end(copies[h])
            value = dot(r.inf[s, raw(h)], r.wef[s])
            r.ex[s, raw(h)] = value
            sums = (sums[0] + fold(value), sums[1] + fold(value * value))
        made = stat_start(r.stw, wide_slot, sums)
        yield
        moments_in[s][2] = moments(stat_end(r.stw, wide_slot, made))

    def spread_taps():
        for index in range(3):
            for tap in range(9):
                r.dkb[9 * index + tap] = jnp.broadcast_to(r.dk[tap, index : index + 1, :], (8, ib))

    def clear(i, _):
        r.gk[i] = zero_n
        return _

    for s in range(2):
        r.red[s, rows : rows + 8] = zero_n

    weights_in = {}
    weights_in["we0"] = share_we(0)
    weights_in["wr1"] = share_wr(1)
    sums = (zero_n, zero_n)
    load_wr0.wait()
    for h in range(2):
        load_x[h].wait()
        value = dot(r.x[raw(h)], r.wr0[...])
        r.red[0, raw(h)] = value
        sums = (sums[0] + fold(value), sums[1] + fold(value * value))
    made = stat_start(r.stn, 0, sums)
    spread_taps()
    lax.fori_loop(0, r.gk.shape[0], clear, 0)
    moments_in[0][0] = moments(stat_end(r.stn, 0, made))

    stage = forward(0, 1, 0)
    next(stage)
    next(stage)
    load_we[0].wait()
    arrive(weights_in["we0"])
    next(stage)
    weights_in["we1"] = share_we(1)
    for _ in stage:
        pass

    def out_zero(at, _):
        z = norm_outer(0, r.ex[0, at])[1] + inner_input(0, at).astype(f32)
        r.out0[at] = gelu(z).astype(bf16)
        return _

    broad(out_zero, 0)

    def scatter_all(slot, chunk_rows, product, use, beside=None):
        copies = []
        for h in range(2):
            r.pb[chunk_rows(h)] = product(h).astype(bf16)
            copies.append(scatter_start(slot, chunk_rows(h)))
        scatter_pass(slot, chunk_rows(0), copies[0])
        scatter_pass(slot, chunk_rows(1), copies[1])
        if beside is not None:
            beside()
        for h in range(2):
            scatter_end(copies[h])
            use(h)

    held = {"sums": (zero_n, zero_n)}

    def use_reduced(h):
        value = scatter_value(0, raw(h))
        r.red[1, raw(h)] = value
        held["sums"] = (held["sums"][0] + fold(value), held["sums"][1] + fold(value * value))

    load_wr[1].wait()
    arrive(weights_in["wr1"])
    scatter_all(0, raw, lambda h: dot(r.out0[raw(h)], r.wrf[1]), use_reduced)
    made = stat_start(r.stn, 2, held["sums"])
    moments_in[1][0] = moments(stat_end(r.stn, 2, made))
    stage = forward(1, 3, 1)
    next(stage)
    next(stage)
    load_we[1].wait()
    arrive(weights_in["we1"])
    next(stage)
    weights_in["wr0"] = share_wr(0)
    for _ in stage:
        pass

    load_cot.wait()

    def out_one(at, sums):
        centred, z = norm_outer(1, r.ex[1, at])
        value, slope = gelu_both(z + r.out0[at].astype(f32))
        r.act[at] = value.astype(bf16)
        grad = r.cot[at].astype(f32) * slope
        r.gpre[at] = grad
        return sums[0] + fold(grad), sums[1] + fold(grad * centred)

    def top_zero(at, sums):
        centred, z = norm_outer(0, r.ex[0, at])
        grad = r.gin[at] * gelu_both(z + inner_input(0, at).astype(f32))[1]
        r.gpre[at] = grad
        return sums[0] + fold(grad), sums[1] + fold(grad * centred)

    def backward(s, stat_base, wide_slot, slot):
        sums = broad(out_one if s else top_zero, (zero_w, zero_w))
        made = stat_start(r.stw, wide_slot, sums)
        if s == 1:
            local_out.append(local(r.act, r.act_out))
        service(s, 1)
        shift_sum, gain_sum = stat_end(r.stw, wide_slot, made)
        r.gbo[s : s + 1] = shift_sum
        r.ggo[s : s + 1] = gain_sum
        mean, inv = moments_in[s][2]
        scale = inv * row(r.go, s)
        shift_mean, gain_mean = shift_sum / pixel_total, gain_sum / pixel_total

        def expand_back(at, _):
            centred = (r.ex[s, at] - mean) * inv
            grad = scale * (r.gpre[at] - (shift_mean + centred * gain_mean))
            r.gexp[at] = grad.astype(bf16)
            return _

        broad(expand_back, 0)
        held["sums"] = (zero_n, zero_n)

        def weight_expand():
            value = dot(r.inf[s], r.gexp[...], 0, 0).astype(bf16)
            r.geo[s] = value.reshape(r.geo.shape[1:])
            place = r.ge.at[s, :, :, :, wide(chan)]
            turned["ge", s] = [local(r.geo.at[s, chan], place)], [
                remote(r.geo.at[s, j], place, (clip, j)) for j in others
            ]
            service(s, 2)

        def use_inner(h):
            def one(at, sums):
                centred, z = norm_inner(s, 1, r.conv[s, at])
                grad = scatter_value(slot, at) * gelu_both(z)[1]
                r.g1[at] = grad
                return sums[0] + fold(grad), sums[1] + fold(grad * centred)

            held["sums"] = narrow(h, one, held["sums"])

        scatter_all(
            slot, raw, lambda h: dot(r.gexp[raw(h)], r.wef[s], 1, 1), use_inner, weight_expand
        )
        made = stat_start(r.stn, stat_base, held["sums"])
        service(s, 3)
        shift_sum, gain_sum = stat_end(r.stn, stat_base, made)
        r.gbi[s, 1:2] = shift_sum
        r.ggi[s, 1:2] = gain_sum
        mean, inv = moments_in[s][1]
        scale = inv * row(r.gi, s, 1)
        shift_mean, gain_mean = shift_sum / pixel_total, gain_sum / pixel_total

        def conv_back(i, _):
            at = pair_rows(0, i)
            halves = []
            for f in (2 * i, 2 * i + 1):
                centred = (spread(r.conv.at[s], f) - mean) * inv
                grad = scale * (spread(r.g1, f) - (shift_mean + centred * gain_mean))
                halves.append(real(grad))
            for b in (-1, 0, 1):
                moved = [row_pad(col_shift(v, -b), 1) for v in halves]
                for a in (-1, 0, 1):
                    tap = 3 * (a + 1) + b + 1
                    both = jnp.concatenate([flat(v[1 - a : 1 - a + SIDE]) for v in moved], axis=0)
                    r.gs[at, tap * ib : (tap + 1) * ib] = both.astype(bf16)
            return _

        lax.fori_loop(0, 2 * pairs, conv_back, 0)

        def weight_conv():
            for ref, taps in ((r.gca, slice(0, SPLIT * ib)), (r.gcb, slice(SPLIT * ib, 9 * ib))):
                value = dot(r.mixf[s], r.gs[:, taps], 0, 0).astype(bf16)
                ref[s] = value.reshape(ref.shape[1:])
            service(s, 4)

        def use_mixed(h):
            def one(i, _):
                at = pair_rows(h, i)
                r.gm[at] = real(scatter_value(slot + 1, at))
                return _

            lax.fori_loop(0, pairs, one, 0)

        scatter_all(
            slot + 1, part, lambda h: dot(r.gs[part(h)], r.wc[s], 1, 1), use_mixed, weight_conv
        )

        def tap_sums(grad, v, index, reach):
            for b in (-1, 0, 1):
                padded = row_pad(col_shift(v, reach * b), reach)
                for a in (-1, 0, 1):
                    start = reach + reach * a
                    place = 9 * index + 3 * (a + 1) + b + 1
                    r.gk[place] = r.gk[place] + jnp.sum(grad * padded[start : start + SIDE], axis=0)

        def mix_back(f, before):
            at = frame_rows(f)
            following = frame_rows(jnp.minimum(f + 1, frames - 1))
            here = tiles(r.hid[s, at])
            step = keep_flag(f) * (tiles(r.hid[s, following]) - here)
            grad = tiles(r.gm[at])
            if s == 0:
                r.gd[at] = flat(dw_tiles(grad, taps_of(0), 1, -1))
                tap_sums(grad, step + before, 0, 1)
            else:
                gate = tiles(r.sig[at])
                grad = grad * here * gate * (1.0 - gate)
                r.gd[at] = flat(dw_tiles(grad, taps_of(1), 1, -1) + dw_tiles(grad, taps_of(2), 2, -1))
                tap_sums(grad, step, 1, 1)
                tap_sums(grad, step, 2, 2)
                r.gk[27] = r.gk[27] + jnp.sum(grad, axis=0)
            return step

        lax.fori_loop(0, frames, mix_back, jnp.zeros((SIDE, 8, ib), f32))

        def hide_back(f, sums):
            at = frame_rows(f)
            previous = frame_rows(jnp.maximum(f - 1, 0))
            keep = keep_flag(f)
            keep_before = jnp.where(f > 0, keep_flag(jnp.maximum(f - 1, 0)), 0.0)
            now = r.gd[at]
            earlier = r.gd[previous]
            grad = r.gm[at]
            if s == 0:
                following = frame_rows(jnp.minimum(f + 1, frames - 1))
                later = now + r.gd[following]
                earlier = earlier + now
            else:
                later = now
                grad = grad * (1.0 + r.sig[at])
            grad = grad + keep_before * earlier - keep * later
            centred, z = norm_inner(s, 0, spread(r.red.at[s], f))
            grad = real(tiles(grad) * gelu_both(z)[1])
            squeeze(r.g1, f, grad)
            return sums[0] + jnp.sum(grad, axis=0), sums[1] + jnp.sum(grad * centred, axis=0)

        sums = lax.fori_loop(0, frames, hide_back, (zero_n, zero_n))
        made = stat_start(r.stn, stat_base + 1, sums)
        service(s, 5)
        shift_sum, gain_sum = stat_end(r.stn, stat_base + 1, made)
        r.gbi[s, 0:1] = shift_sum
        r.ggi[s, 0:1] = gain_sum
        mean, inv = moments_in[s][0]
        scale = inv * row(r.gi, s, 0)
        shift_mean, gain_mean = shift_sum / pixel_total, gain_sum / pixel_total
        copies = []
        for h in range(2):

            def reduce_back(at, _):
                centred = (r.red[s, at] - mean) * inv
                grad = scale * (r.g1[at] - (shift_mean + centred * gain_mean))
                r.grf[s, at, cols(chan)] = grad.astype(bf16)
                return _

            narrow(h, reduce_back, 0)
            copies.append(gather_start(r.grf.at[s], raw(h)))
        if s == 0:
            own = r.grf[0, :, cols(chan)]
            for piece in range(n_chan):
                value = dot(r.x[:, piece * cs : (piece + 1) * cs], own, 0, 0).astype(bf16)
                r.gr[0, piece] = value.reshape(r.gr.shape[2:])
        service(s, 6)
        gather_pass(r.grf.at[s], raw(0), copies[0])
        gather_pass(r.grf.at[s], raw(1), copies[1])
        if s == 0:
            load_wr[0].wait()
            arrive(weights_in["wr0"])
        for h in range(2):
            gather_end(copies[h])
            r.gin[raw(h)] = dot(r.grf[s, raw(h)], r.wrf[s], 1, 1) + r.gpre[raw(h)]
            if s == 0:
                local_out.append(local(r.gin.at[raw(h)], r.gin_out.at[raw(h)]))
        if s == 1:
            value = dot(r.out0[...], r.grf[1], 0, 0).astype(bf16)
            r.gro[...] = value.reshape(r.gro.shape)
            place = r.gr.at[1, chan]
            turned["gr", 1] = [local(r.gro.at[:, :, cols(chan)], place)], [
                remote(r.gro.at[:, :, cols(j)], place, (clip, j)) for j in others
            ]

    turned = {}

    def reduce_task(name, s, ref, from_side, from_z, result, write_out):
        mine, across = ref.at[s], (2 * z + 1 - side, chan)
        if (name, s) in turned:
            for copy in turned[name, s][0]:
                copy.wait()
            arrive(turned[name, s][1])
        made = remote(mine.at[:, 1 - side], from_side.at[s], across)
        yield
        made.wait_recv()
        for k in range(n_z):
            both = ref[s, k, side].astype(f32) + from_side[s, k].astype(f32)
            ref[s, k, side] = both.astype(bf16)
        made = [
            remote(mine.at[there, side], from_z.at[s, k], (2 * there + side, chan))
            for k, there in enumerate(z_others)
        ]
        yield
        arrive(made)
        total = ref[s, z, side].astype(f32)
        for k in range(n_z - 1):
            total = total + from_z[s, k].astype(f32)
        result[s, z, side] = total.astype(bf16)
        done = result.at[s, z, side]
        made = [remote(done, done, (2 * there + side, chan)) for there in z_others]
        yield
        arrive(made)
        done = result.at[s, :, side]
        made = remote(done, done, across)
        yield
        made.wait_recv()
        write_out(s)
        yield

    def write_conv(result, base):
        def write(s):
            for k in range(result.shape[-1] // ib):
                here = result.at[s, :, :, :, k * ib : (k + 1) * ib]
                local_out.append(local(here, r.gc_out.at[s, base + k]))

        return write

    def write_expand(s):
        local_out.append(local(r.fe.at[s], r.ge_out.at[s]))

    def write_reduce(s):
        local_out.append(local(r.fr.at[s], r.gr_out.at[s]))

    kinds = {
        "gca": (r.gca, r.rxa, r.rza, r.fa, write_conv(r.fa, 0)),
        "gcb": (r.gcb, r.rxb, r.rzb, r.fb, write_conv(r.fb, SPLIT)),
        "ge": (r.ge, r.rxe, r.rze, r.fe, write_expand),
        "gr": (r.gr, r.rxr, r.rzr, r.fr, write_reduce),
    }
    tasks = {(name, s): reduce_task(name, s, *kinds[name]) for name in kinds for s in range(2)}

    def advance(*steps):
        for step in steps:
            next(tasks[step])

    def service(s, point):
        advance(*PLAN.get((s, point), ()))

    local_out = []
    backward(1, 4, 2, 1)
    backward(0, 6, 3, 3)

    for place in range(r.gk.shape[0]):
        r.kst[clip, place : place + 1, :] = jnp.sum(r.gk[place], axis=0, keepdims=True)
    made = [remote(r.kst.at[clip], r.kst.at[clip], (t, chan)) for t in clip_others]
    service(0, 7)
    arrive(made)
    total = r.kst[0]
    for k in range(1, n_clip):
        total = total + r.kst[k]
    for index in range(3):
        for tap in range(9):
            place = 9 * index + tap
            r.gk_out[tap, index : index + 1, :] = total[place : place + 1]
    r.ggb_out[...] = total[27:28]
    for copy in local_out:
        copy.wait()
    for copy in list(unsent):
        sent(copy)
    assert counters["copy"] <= COPIES and counters["load"] <= LOADS, counters


def fused_call(n_clip, n_chan, pixel_total, *operands):
    rows, width = operands[0].shape
    cs = width // n_chan
    ib = LANES
    inner = ib * n_chan
    n_z = n_clip // 2
    padded = rows // PIXELS * FRAME
    over = rows + 8
    bf16, f32 = jnp.bfloat16, jnp.float32
    whole = pl.BlockSpec(memory_space=pltpu.VMEM)
    anywhere = pl.BlockSpec(memory_space=pl.ANY)
    scalars = pl.BlockSpec(memory_space=pltpu.SMEM)
    shape = jax.ShapeDtypeStruct
    V = pltpu.VMEM
    scratch = dict(
        x=V((rows, width), bf16),
        cot=V((rows, cs), bf16),
        wr0=V((width, ib), bf16),
        wrf=V((2, cs, inner), bf16),
        wef=V((2, inner, cs), bf16),
        wc=V((2, inner, 9 * ib), bf16),
        dkb=V((27, 8, ib), f32),
        red=V((2, over, ib), f32),
        hid=V((2, padded, ib), f32),
        sig=V((padded, ib), f32),
        conv=V((2, over, ib), f32),
        mixf=V((2, padded, inner), bf16),
        inf=V((2, rows, inner), bf16),
        ex=V((2, rows, cs), f32),
        out0=V((rows, cs), bf16),
        act=V((rows, cs), bf16),
        y=V((padded // 2, 9 * ib), f32),
        gpre=V((rows, cs), f32),
        gin=V((rows, cs), f32),
        gexp=V((rows, cs), bf16),
        gs=V((padded, 9 * ib), bf16),
        pb=V((padded, inner), bf16),
        ysend=V((2, padded, ib), bf16),
        rcore=V((5, 2, padded, ib), bf16),
        ryy=V((5, padded, ib), bf16),
        grf=V((2, rows, inner), bf16),
        gm=V((padded, ib), f32),
        gd=V((padded, ib), f32),
        g1=V((over, ib), f32),
        gk=V((32, 8, ib), f32),
        kst=V((n_clip, 32, ib), f32),
        stn=V((8, n_clip, 2, ib), f32),
        stw=V((4, n_clip, 2, cs), f32),
        gca=V((2, n_z, 2, inner // n_clip, SPLIT * ib), bf16),
        gcb=V((2, n_z, 2, inner // n_clip, (9 - SPLIT) * ib), bf16),
        geo=V((2, n_chan, n_z, 2, ib // n_clip, cs), bf16),
        ge=V((2, n_z, 2, ib // n_clip, width), bf16),
        gro=V((2, cs // 2, inner), bf16),
        gr=V((2, n_z, 2, width // n_clip, ib), bf16),
        fa=V((2, n_z, 2, inner // n_clip, SPLIT * ib), bf16),
        fb=V((2, n_z, 2, inner // n_clip, (9 - SPLIT) * ib), bf16),
        fe=V((2, n_z, 2, ib // n_clip, width), bf16),
        fr=V((2, n_z, 2, width // n_clip, ib), bf16),
        rxa=V((2, n_z, inner // n_clip, SPLIT * ib), bf16),
        rxb=V((2, n_z, inner // n_clip, (9 - SPLIT) * ib), bf16),
        rxe=V((2, n_z, ib // n_clip, width), bf16),
        rxr=V((2, n_z, width // n_clip, ib), bf16),
        rza=V((2, n_z - 1, inner // n_clip, SPLIT * ib), bf16),
        rzb=V((2, n_z - 1, inner // n_clip, (9 - SPLIT) * ib), bf16),
        rze=V((2, n_z - 1, ib // n_clip, width), bf16),
        rzr=V((2, n_z - 1, width // n_clip, ib), bf16),
        ssem=pltpu.SemaphoreType.DMA((COPIES,)),
        rsem=pltpu.SemaphoreType.DMA((COPIES,)),
        lsem=pltpu.SemaphoreType.DMA((LOADS,)),
    )
    first = NAMES.index("x")
    return pl.pallas_call(
        partial(fused_kernel, n_clip, n_chan, pixel_total),
        out_shape=[
            shape((rows, cs), bf16),
            shape((rows, cs), f32),
            shape((2, 2, ib), f32),
            shape((2, 2, ib), f32),
            shape((2, cs), f32),
            shape((2, cs), f32),
            shape((9, 3, ib), f32),
            shape((1, ib), f32),
            shape((2, 9, n_z, 2, inner // n_clip, ib), bf16),
            shape((2, n_z, 2, ib // n_clip, width), bf16),
            shape((2, n_z, 2, width // n_clip, ib), bf16),
        ],
        in_specs=[anywhere] * 5 + [scalars] + [whole] * 6,
        out_specs=[anywhere] * 2 + [whole] * 6 + [anywhere] * 3,
        scratch_shapes=[scratch[name] for name in NAMES[first:]],
        compiler_params=pltpu.CompilerParams(
            collective_id=0, has_side_effects=True, vmem_limit_bytes=62 * 1024 * 1024
        ),
    )(*operands)


def finish_kernel(*refs):
    count = len(refs) // 2
    sources, results = refs[:count], refs[count:]
    for here, there in zip(sources[:5], results[:5]):
        there[...] = here[...].astype(there.dtype)

    @pl.when(pl.program_id(0) == 0)
    def _():
        for here, there in zip(sources[5:], results[5:]):
            there[...] = here[...]


def finish(steps, gc, ge, gr, act, gin, *small):
    arrays = [a.reshape(-1, a.shape[-1]) for a in (gc, ge, gr)] + [act, gin]
    blocks = [
        pl.BlockSpec((-(-a.shape[0] // (16 * steps)) * 16, a.shape[1]), lambda i: (i, 0))
        for a in arrays
    ]
    whole = [pl.BlockSpec(memory_space=pltpu.VMEM)] * len(small)
    shapes = [jax.ShapeDtypeStruct(a.shape, jnp.float32) for a in arrays[:3]]
    shapes += [jax.ShapeDtypeStruct(a.shape, a.dtype) for a in (act, gin, *small)]
    return pl.pallas_call(
        finish_kernel,
        grid=(steps,),
        out_shape=shapes,
        in_specs=blocks + whole,
        out_specs=blocks + whole,
        compiler_params=pltpu.CompilerParams(vmem_limit_bytes=62 * 1024 * 1024),
    )(*arrays, *small)


def fused(
    frames_in,
    boundary,
    w_reduce,
    gain_inner,
    bias_inner,
    w_conv,
    w_expand,
    gain_outer,
    bias_outer,
    depth_kernels,
    gate_bias,
    cotangent,
):
    n_clip, n_chan = lax.axis_size("clip"), lax.axis_size("chan")
    pixel_total = frames_in.shape[0] * n_clip
    act, gin, ggi, gbi, ggo, gbo, gk, ggb, gc, ge, gr = fused_call(
        n_clip,
        n_chan,
        float(pixel_total),
        frames_in,
        cotangent,
        w_reduce,
        w_conv,
        w_expand,
        boundary,
        gain_inner,
        bias_inner,
        gain_outer,
        bias_outer,
        depth_kernels.transpose(1, 0, 2),
        gate_bias.reshape(1, -1),
    )
    gc, ge, gr, act, gin, ggi, gbi, ggo, gbo, gk, ggb = finish(
        2, gc, ge, gr, act, gin, ggi, gbi, ggo, gbo, gk, ggb
    )
    return (
        act,
        gin,
        gr.reshape(w_reduce.shape),
        ggi,
        gbi,
        gc.reshape(w_conv.shape),
        ge.reshape(w_expand.shape),
        ggo,
        gbo,
        gk.transpose(1, 0, 2),
        ggb.reshape(-1),
    )


def solution(mesh):
    in_specs = (
        P("clip", None),
        P("clip", None),
        P(None, None, "chan"),
        P(None, None, "chan"),
        P(None, None, "chan"),
        P(None, None, None, "chan"),
        P(None, "chan", None),
        P(),
        P(),
        P(None, None, "chan"),
        P("chan"),
        P("clip", None),
    )
    out_specs = (
        P("clip", "chan"),
        P("clip", "chan"),
        P(None, None, "chan"),
        P(None, None, "chan"),
        P(None, None, "chan"),
        P(None, None, None, "chan"),
        P(None, "chan", None),
        P(None, "chan"),
        P(None, "chan"),
        P(None, None, "chan"),
        P("chan"),
    )

    def run(*arguments):
        fits = fused_fits(mesh, arguments[0].shape, arguments[2].shape)
        return jax.shard_map(fused if fits else body, mesh=mesh, in_specs=in_specs, out_specs=out_specs, check_vma=False)(*arguments)

    return run
```

```python
from functools import partial
from types import SimpleNamespace

import jax
import jax.numpy as jnp
from jax import lax
from jax.experimental import pallas as pl
from jax.experimental.pallas import tpu as pltpu
from jax.sharding import PartitionSpec as P

SEG = 8
SIDE = 7


epsilon = 1e-05


def framed(values):
    return values.reshape(-1, SIDE, SIDE, values.shape[-1])


def shifted(frame_grid, row_step, col_step, dilation):
    padded = jnp.pad(frame_grid, ((0, 0), (dilation, dilation), (dilation, dilation), (0, 0)))
    return padded[
        :,
        dilation + row_step : dilation + row_step + SIDE,
        dilation + col_step : dilation + col_step + SIDE,
        :,
    ]


def depthwise(values, kernel, dilation):
    frame_grid = framed(values)
    running = jnp.zeros_like(frame_grid)
    for tap_index in range(9):
        running = (
            running
            + shifted(
                frame_grid,
                (tap_index // 3 - 1) * dilation,
                (tap_index % 3 - 1) * dilation,
                dilation,
            )
            * kernel[tap_index]
        )
    return running.reshape(values.shape)


def patch_rows(values):
    frame_grid = framed(values)
    pieces = [
        shifted(frame_grid, tap_index // 3 - 1, tap_index % 3 - 1, 1) for tap_index in range(9)
    ]
    return jnp.concatenate(pieces, axis=-1).reshape(values.shape[0], 9 * values.shape[1])


def unpatch(grad_rows, chan_width):
    frame_grid = grad_rows.reshape(-1, SIDE, SIDE, 9, chan_width)
    running = jnp.zeros(frame_grid.shape[:3] + (chan_width,), jnp.float32)
    for tap_index in range(9):
        running = running + shifted(
            frame_grid[:, :, :, tap_index, :], 1 - tap_index // 3, 1 - tap_index % 3, 1
        )
    return running.reshape(-1, chan_width)


def neighbours(values, boundary):
    clip_count = boundary.shape[0]
    frame_grid = values.reshape(clip_count, SEG, SIDE * SIDE, values.shape[-1])
    stop_mask = (boundary == 1)[:, :, None, None]
    start_mask = jnp.concatenate([jnp.ones_like(stop_mask[:, :1]), stop_mask[:, :-1]], axis=1)
    after_seg = jnp.concatenate([frame_grid[:, 1:], frame_grid[:, -1:]], axis=1)
    before = jnp.concatenate([frame_grid[:, :1], frame_grid[:, :-1]], axis=1)
    later_seg = jnp.where(stop_mask, frame_grid, after_seg)
    earlier = jnp.where(start_mask, frame_grid, before)
    return (later_seg.reshape(values.shape), earlier.reshape(values.shape))


def temporal(values, kernels, gate_vec, boundary, short_range):
    later_seg, earlier = neighbours(values, boundary)
    if short_range:
        return values + depthwise(later_seg - earlier, kernels[0], 1)
    change = later_seg - values
    logits = depthwise(change, kernels[1], 1) + depthwise(change, kernels[2], 2) + gate_vec
    return values + values * jax.nn.sigmoid(logits)


def columns(values, col_start, col_share):
    return lax.dynamic_slice_in_dim(values, col_start, col_share, values.ndim - 1)


def contract(left, right, left_dim, right_dim):
    return lax.dot_general(
        left, right, (((left_dim,), (right_dim,)), ((), ())), preferred_element_type=jnp.float32
    )


def normalize(values, gain_vec, bias_vec, pixel_total):
    col_sum, sq_sum = lax.psum((jnp.sum(values, axis=0), jnp.sum(values * values, axis=0)), "clip")
    mean_val = col_sum / pixel_total
    inv_std = lax.rsqrt(sq_sum / pixel_total - mean_val * mean_val + epsilon)
    centred = (values - mean_val) * inv_std
    return (centred * gain_vec + bias_vec, centred, inv_std)


def normalize_back(grad_rows, centred, inv_std, gain_vec, pixel_total):
    shift_sum, gain_sum = lax.psum(
        (jnp.sum(grad_rows, axis=0), jnp.sum(grad_rows * centred, axis=0)), "clip"
    )
    grad_in = inv_std * gain_vec * (grad_rows - (shift_sum + centred * gain_sum) / pixel_total)
    return (grad_in, gain_sum, shift_sum)


def block_forward(inputs, boundary, weights, short_range, pixel_total):
    w_red, gain_pair, bias_pair, w_cv, w_ex, gain_out, bias_out, kernels, gate_vec = weights
    reduced = jnp.dot(inputs, w_red, preferred_element_type=jnp.float32)
    norm_one, centred_one, inv_one = normalize(reduced, gain_pair[0], bias_pair[0], pixel_total)
    hidden, gelu_one = jax.vjp(jax.nn.gelu, norm_one)
    mixed_act, mix_back = jax.vjp(
        partial(temporal, boundary=boundary, short_range=short_range), hidden, kernels, gate_vec
    )
    gathered = lax.all_gather(mixed_act.astype(jnp.bfloat16), "chan", axis=1, tiled=True)
    patches = patch_rows(gathered)
    conv_out = jnp.dot(
        patches, w_cv.reshape(-1, w_cv.shape[-1]), preferred_element_type=jnp.float32
    )
    norm_two, centred_two, inv_two = normalize(conv_out, gain_pair[1], bias_pair[1], pixel_total)
    inner_full, gelu_two = jax.vjp(jax.nn.gelu, norm_two)
    inner_act = inner_full.astype(jnp.bfloat16)
    partial_out = jnp.dot(inner_act, w_ex, preferred_element_type=jnp.float32)
    expanded = lax.psum(partial_out.astype(jnp.bfloat16), "chan").astype(jnp.float32)
    norm_three, centred_three, inv_three = normalize(expanded, gain_out, bias_out, pixel_total)
    output_full, gelu_three = jax.vjp(jax.nn.gelu, norm_three + inputs.astype(jnp.float32))
    kept_state = (
        centred_one,
        inv_one,
        gelu_one,
        mix_back,
        patches,
        centred_two,
        inv_two,
        gelu_two,
        inner_act,
        centred_three,
        inv_three,
        gelu_three,
        gain_out,
    )
    return (output_full.astype(jnp.bfloat16), kept_state)


def block_backward(grad_out, inputs, weights, kept_state, pixel_total):
    w_red, gain_pair, bias_pair, w_cv, w_ex, gain_out, bias_out, kernels, gate_vec = weights
    (
        centred_one,
        inv_one,
        gelu_one,
        mix_back,
        patches,
        centred_two,
        inv_two,
        gelu_two,
        inner_act,
        centred_three,
        inv_three,
        gelu_three,
        gain_use,
    ) = kept_state
    grad_pre = gelu_three(grad_out)[0]
    grad_exp, gain_three, bias_three = normalize_back(
        grad_pre, centred_three, inv_three, gain_use, pixel_total
    )
    low_exp = grad_exp.astype(jnp.bfloat16)
    grad_wex = contract(inner_act, low_exp, 0, 0)
    grad_inner = contract(low_exp, w_ex, 1, 1)
    grad_two = gelu_two(grad_inner)[0]
    grad_cv, gain_two, bias_two = normalize_back(
        grad_two, centred_two, inv_two, gain_pair[1], pixel_total
    )
    low_cv = grad_cv.astype(jnp.bfloat16)
    flat_cv = w_cv.reshape(-1, w_cv.shape[-1])
    grad_wcv = contract(patches, low_cv, 0, 0).reshape(w_cv.shape)
    grad_patch = contract(low_cv, flat_cv, 1, 1)
    grad_mixed = lax.psum_scatter(
        unpatch(grad_patch, w_cv.shape[1]).astype(jnp.bfloat16),
        "chan",
        scatter_dimension=1,
        tiled=True,
    ).astype(jnp.float32)
    grad_hidden, grad_kern, grad_gate = mix_back(grad_mixed)
    grad_one = gelu_one(grad_hidden)[0]
    grad_red, gain_one, bias_one = normalize_back(
        grad_one, centred_one, inv_one, gain_pair[0], pixel_total
    )
    low_red = grad_red.astype(jnp.bfloat16)
    grad_wred = contract(inputs, low_red, 0, 0)
    partial_in = contract(low_red, w_red, 1, 1)
    grad_in = grad_pre + lax.psum(partial_in.astype(jnp.bfloat16), "chan").astype(jnp.float32)
    weight_terms = (grad_wred, grad_wcv, grad_wex, grad_kern, grad_gate)
    norm_terms = (gain_one, bias_one, gain_two, bias_two, gain_three, bias_three)
    return (grad_in, weight_terms, norm_terms)


def body(
    frames_in,
    boundary,
    w_reduce,
    gain_inner,
    bias_inner,
    w_conv,
    w_expand,
    gain_outer,
    bias_outer,
    depth_kernels,
    gate_bias,
    cotangent,
):
    row_count = frames_in.shape[0]
    pixel_total = row_count * lax.axis_size("clip")
    col_share = frames_in.shape[1] // lax.axis_size("chan")
    col_start = lax.axis_index("chan") * col_share
    block_weights = [
        (
            w_reduce[block_index],
            gain_inner[block_index],
            bias_inner[block_index],
            w_conv[block_index],
            w_expand[block_index],
            gain_outer[block_index],
            bias_outer[block_index],
            depth_kernels,
            gate_bias,
        )
        for block_index in range(2)
    ]
    first_out, kept_zero = block_forward(frames_in, boundary, block_weights[0], True, pixel_total)
    final_out, kept_one = block_forward(first_out, boundary, block_weights[1], False, pixel_total)
    layer_inputs = [frames_in, first_out]
    kept_states = [kept_zero, kept_one]
    grad_flow = cotangent.astype(jnp.float32)
    weight_sums = [None, None]
    norm_sums = [None, None]
    for block_index in (1, 0):
        grad_flow, weight_terms, norm_terms = block_backward(
            grad_flow,
            layer_inputs[block_index],
            block_weights[block_index],
            kept_states[block_index],
            pixel_total,
        )
        grad_wred, grad_wcv, grad_wex, grad_kern, grad_gate = weight_terms
        weight_terms = (
            lax.psum(grad_wred.astype(jnp.bfloat16), "clip").astype(jnp.float32),
            lax.psum(grad_wcv.astype(jnp.bfloat16), "clip").astype(jnp.float32),
            lax.psum(grad_wex.astype(jnp.bfloat16), "clip").astype(jnp.float32),
            lax.psum(grad_kern.astype(jnp.bfloat16), "clip").astype(jnp.float32),
            lax.psum(grad_gate.astype(jnp.bfloat16), "clip").astype(jnp.float32),
        )
        weight_sums[block_index] = weight_terms
        norm_sums[block_index] = norm_terms
    grad_reduce = jnp.stack([weight_sums[0][0], weight_sums[1][0]])
    grad_conv = jnp.stack([weight_sums[0][1], weight_sums[1][1]])
    grad_expand = jnp.stack([weight_sums[0][2], weight_sums[1][2]])
    grad_kernels = weight_sums[0][3] + weight_sums[1][3]
    grad_gate_bias = weight_sums[0][4] + weight_sums[1][4]
    grad_gain_inner = jnp.stack(
        [
            jnp.stack([norm_sums[0][0], norm_sums[0][2]]),
            jnp.stack([norm_sums[1][0], norm_sums[1][2]]),
        ]
    )
    grad_bias_inner = jnp.stack(
        [
            jnp.stack([norm_sums[0][1], norm_sums[0][3]]),
            jnp.stack([norm_sums[1][1], norm_sums[1][3]]),
        ]
    )
    grad_gain_outer = jnp.stack([norm_sums[0][4], norm_sums[1][4]])
    grad_bias_outer = jnp.stack([norm_sums[0][5], norm_sums[1][5]])
    activations = columns(final_out, col_start, col_share)
    input_grad = columns(grad_flow, col_start, col_share)
    grad_gain_outer = columns(grad_gain_outer, col_start, col_share)
    grad_bias_outer = columns(grad_bias_outer, col_start, col_share)
    return (
        activations,
        input_grad,
        grad_reduce,
        grad_gain_inner,
        grad_bias_inner,
        grad_conv,
        grad_expand,
        grad_gain_outer,
        grad_bias_outer,
        grad_kernels,
        grad_gate_bias,
    )


MESH = pl.DeviceIdType.MESH
LANES = 128
FRAME = SIDE * 8
PIXELS = SIDE * SIDE
PAIR = 2 * FRAME
GELU_A = 0.7978845608028654
GELU_B = 0.044715
SENDS = 64
LOADS = 32


def fused_fits(mesh, frame_shape, reduce_shape):
    n_clip, n_chan = mesh.shape["clip"], mesh.shape["chan"]
    share = reduce_shape[2] // n_chan
    frames = frame_shape[0] // (n_clip * SIDE * SIDE)
    return n_chan == 4 and n_clip == 8 and share == LANES and frames == 2 * SEG


def gelu(z):
    return 0.5 * z * (1.0 + jnp.tanh(GELU_A * (z + GELU_B * z * z * z)))


def gelu_both(z):
    square = z * z
    t = jnp.tanh(GELU_A * (z + GELU_B * square * z))
    slope = 0.5 * (1.0 + t) + 0.5 * z * (1.0 - t * t) * (GELU_A * (1.0 + 3.0 * GELU_B * square))
    return 0.5 * z * (1.0 + t), slope


def real_columns(shape):
    return lax.rem(lax.broadcasted_iota(jnp.int32, shape, len(shape) - 2), 8) < SIDE


def real(values):
    return jnp.where(real_columns(values.shape), values, 0.0)


def fold(values):
    return jnp.sum(values.reshape(-1, 8, values.shape[-1]), axis=0)


def tiles(values):
    return values.reshape(SIDE, 8, values.shape[-1])


def flat(values):
    return values.reshape(FRAME, values.shape[-1])


def row_pad(v, reach):
    zeros = jnp.zeros((reach,) + v.shape[1:], v.dtype)
    return jnp.concatenate([zeros, v, zeros], axis=0)


def col_shift(v, step):
    if step == 0:
        return v
    moved = pltpu.roll(v, (-step) % 8, v.ndim - 2)
    if abs(step) == 2:
        place = lax.broadcasted_iota(jnp.int32, v.shape, v.ndim - 2)
        moved = jnp.where(place < 6 if step > 0 else place >= 2, moved, 0.0)
    return moved


def dw_tiles(v, taps, reach, sign):
    padded = row_pad(v, reach)
    total = None
    for b in (-1, 0, 1):
        part = None
        for a in (-1, 0, 1):
            start = reach + sign * reach * a
            term = taps[3 * (a + 1) + b + 1] * padded[start : start + SIDE]
            part = term if part is None else part + term
        part = col_shift(part, sign * reach * b)
        total = part if total is None else total + part
    return total


def dot(left, right, left_dim=1, right_dim=0):
    return lax.dot_general(
        left, right, (((left_dim,), (right_dim,)), ((), ())), preferred_element_type=jnp.float32
    )


NAMES = (
    "x_hbm", "cot_hbm", "wred_hbm", "wconv_hbm", "wexp_hbm", "bnd", "gi", "bi", "go", "bo",
    "dk", "gb", "act_out", "gin_out", "ggi", "gbi", "ggo", "gbo", "gk_out", "ggb_out", "gc_out",
    "ge_out", "gr_out", "x", "cot", "wr0", "wrf", "wef", "wc", "dkb", "red", "hid", "sig",
    "conv", "mixf", "inf", "ex", "out0", "act", "y", "gpre", "gin", "gexp", "gs", "pb", "ysend",
    "rcore", "ryy", "grf", "gm", "gd", "g1", "gk", "kst", "stn", "stw", "gc", "geo", "ge",
    "gro", "gr", "xc", "xe", "xr", "zc", "ze", "zr", "fc", "fe", "fr", "ssem", "rsem", "lsem",
)


PIECES = {"gc": 9, "ge": 1, "gr": 2}
ARRIVALS = 40 + 8 * sum(PIECES.values())
PLAN = {
    (1, "conv_before"): (
        ("e0", 1),
    ),
    (1, "conv"): (
        ("c0", 1), ("c5", 1), ("c2", 1),
    ),
    (1, "red"): (
        ("c0", 1), ("e0", 1), ("c4", 1), ("c6", 1), ("c8", 1), ("c7", 1), ("c1", 1), ("c3", 1),
    ),
    (1, "gather"): (
        ("c5", 1), ("c2", 1), ("c4", 1),
    ),
    (0, "top"): (
        ("c0", 1), ("c5", 1), ("e0", 1), ("c6", 1), ("c8", 1), ("c7", 1), ("c1", 1),
    ),
    (0, "expand_before"): (
        ("r0", 1), ("r1", 1),
    ),
    (0, "inner"): (
        ("c0", 1), ("c5", 1), ("c2", 1), ("e0", 1), ("c4", 1), ("r0", 1), ("c6", 1), ("c8", 1),
        ("c7", 1), ("c3", 1), ("r1", 1),
    ),
    (0, "conv_before"): (
        ("c0", 1), ("c1", 1), ("e0", 0),
    ),
    (0, "conv"): (
        ("c8", 0), ("c5", 1), ("c0", 0), ("c2", 1), ("e0", 1),
    ),
    (0, "hide_before"): (
        ("c3", 1),
    ),
    (0, "red"): (
        ("c8", 0), ("c1", 0), ("c2", 0), ("c5", 0), ("c6", 0), ("c4", 1), ("r0", 1), ("c6", 1),
        ("c8", 1), ("e0", 0),
    ),
    (0, "gather"): (
        ("c2", 1),
    ),
    (0, "end"): (
        ("c3", 0), ("c4", 0), ("c7", 0), ("r0", 0), ("r1", 0), ("c7", 1), ("r1", 1), ("c0", 0),
        ("c1", 1), ("c3", 1), ("c1", 0), ("c8", 0), ("c2", 0), ("c5", 0), ("r0", 1), ("c6", 0),
        ("c4", 1), ("c6", 1), ("c8", 1), ("e0", 0), ("c3", 0), ("c4", 0), ("c7", 0), ("r1", 1),
        ("c0", 0), ("r0", 0), ("c1", 0), ("c8", 0), ("r1", 0), ("c2", 0), ("c7", 1), ("c5", 0),
        ("c1", 1), ("c6", 0), ("c3", 1), ("r0", 1), ("e0", 0), ("r1", 1), ("c3", 0), ("c8", 0),
        ("c4", 0), ("c7", 0), ("c0", 0), ("e0", 0), ("r0", 0), ("c0", 0), ("c1", 0), ("r1", 0),
        ("c1", 0), ("c2", 0), ("c5", 0), ("c6", 0), ("c2", 0), ("c3", 0), ("c5", 0), ("c4", 0),
        ("c6", 0), ("c7", 0), ("c3", 0), ("c4", 0), ("r0", 0), ("c7", 0), ("r1", 0), ("r0", 0),
        ("r1", 0),
    ),
}


def fused_kernel(n_clip, n_chan, pixel_total, *refs):
    r = SimpleNamespace(**dict(zip(NAMES, refs)))
    rows, cs = r.cot.shape
    ib = LANES
    frames = rows // PIXELS
    chunk = frames // 2 * FRAME
    n_z = n_clip // 2
    first = -(-rows // 32) * 16
    starts, counts = (0, first), (first, rows - first)
    bf16, f32 = jnp.bfloat16, jnp.float32
    clip = lax.axis_index("clip")
    chan = lax.axis_index("chan")
    core, high = lax.rem(chan, 2), lax.div(chan, 2)
    j_core = (1 - core) + 2 * high
    j_y = core + 2 * (1 - high)
    j_far = (1 - core) + 2 * (1 - high)
    others = (j_core, j_y, j_far)
    z, side = lax.div(clip, 2), lax.rem(clip, 2)
    z_others = [lax.rem(z + d, n_z) for d in range(1, n_z)]
    clip_others = [lax.rem(clip + d, n_clip) for d in range(1, n_clip)]

    def cols(j):
        return pl.ds(pl.multiple_of(j * ib, ib), ib)

    def wide(j):
        return pl.ds(pl.multiple_of(j * cs, cs), cs)

    def part(h):
        return pl.ds(h * chunk, chunk)

    def raw(h):
        return pl.ds(starts[h], counts[h])

    def spans(total):
        tiles_left, at, chunks = total // 16, 0, []
        for left in range(4, 0, -1):
            take = -(-tiles_left // left)
            chunks.append((at * 16, take * 16))
            at, tiles_left = at + take, tiles_left - take
        return chunks

    raw_spans, padded_spans = spans(rows), spans(frames * FRAME)

    places, in_flight, counters = {}, {}, {"send": 0, "load": 0, "phase": 0, "sums": 0}

    def arrival(key):
        return r.rsem.at[places.setdefault(key, len(places))]

    def sent(index):
        if index in in_flight:
            in_flight.pop(index).wait_send()

    def remote(src, dst, target, key):
        index = counters["send"] % SENDS
        counters["send"] += 1
        sent(index)
        made = pltpu.make_async_remote_copy(
            src_ref=src,
            dst_ref=dst,
            send_sem=r.ssem.at[index],
            recv_sem=arrival(key),
            device_id=target,
            device_id_type=MESH,
        )
        made.start()
        in_flight[index] = made
        return made, index

    def arrive(place, key):
        pltpu.make_async_remote_copy(
            src_ref=place,
            dst_ref=place,
            send_sem=r.ssem.at[0],
            recv_sem=arrival(key),
            device_id=(clip, j_core),
            device_id_type=MESH,
        ).wait_recv()

    def local(src, dst, index=None):
        if index is None:
            index = counters["load"]
            counters["load"] += 1
        made = pltpu.make_async_copy(src, dst, r.lsem.at[index])
        made.start()
        return made

    outgoing = {}

    def write_out(src, dst):
        turn = counters.setdefault("out", 0) % 8
        counters["out"] += 1
        if turn in outgoing:
            outgoing.pop(turn).wait()
        outgoing[turn] = local(src, dst, LOADS - 8 + turn)

    load_wr0 = local(r.wred_hbm.at[0], r.wr0)
    load_x = [local(r.x_hbm.at[raw(h)], r.x.at[raw(h)]) for h in range(2)]
    load_we = [
        local(r.wexp_hbm.at[s, :, wide(chan)], r.wef.at[s, cols(chan)]) for s in range(2)
    ]
    load_wr = [
        local(r.wred_hbm.at[s, wide(chan)], r.wrf.at[s, :, cols(chan)]) for s in range(2)
    ]
    load_wc = []
    for s in range(2):
        index = counters["load"]
        counters["load"] += 1
        for tap in range(9):
            local(r.wconv_hbm.at[s, tap], r.wc.at[s, :, tap * ib : (tap + 1) * ib], index)
        load_wc.append(pltpu.make_async_copy(r.wc.at[s], r.wc.at[s], r.lsem.at[index]))
    load_cot = local(r.cot_hbm.at[:, wide(chan)], r.cot)

    barrier = pltpu.get_barrier_semaphore()
    for target in clip_others:
        pl.semaphore_signal(barrier, inc=1, device_id=(target, chan), device_id_type=MESH)
    for target in others:
        pl.semaphore_signal(barrier, inc=1, device_id=(clip, target), device_id_type=MESH)
    pl.semaphore_wait(barrier, n_clip - 1 + n_chan - 1)

    def share_we(s):
        for j in others:
            target = r.wef.at[s, cols(chan)]
            remote(r.wexp_hbm.at[s, :, wide(j)], target, (clip, j), ("we", s))

    def share_wr(s):
        for j in others:
            target = r.wrf.at[s, :, cols(chan)]
            remote(r.wred_hbm.at[s, wide(j)], target, (clip, j), ("wr", s))

    def shared_we(s):
        load_we[s].wait()
        arrive(r.wef.at[s, pl.ds(0, (n_chan - 1) * ib)], ("we", s))

    def shared_wr(s):
        load_wr[s].wait()
        arrive(r.wrf.at[s, :, pl.ds(0, (n_chan - 1) * ib)], ("wr", s))

    def stat_start(buf, slot, values):
        for k, value in enumerate(values):
            buf[slot, clip, k : k + 1, :] = jnp.sum(value, axis=0, keepdims=True)
        key = ("sums", counters["sums"] % 2)
        counters["sums"] += 1
        for t in clip_others:
            remote(buf.at[slot, clip], buf.at[slot, clip], (t, chan), key)
        return key

    def stat_end(buf, slot, key):
        arrive(buf.at[slot, pl.ds(0, n_clip - 1)], key)
        total = buf[slot, 0]
        for k in range(1, n_clip):
            total = total + buf[slot, k]
        return total[0:1], total[1:2]

    def moments(pair):
        mean = pair[0] / pixel_total
        return mean, lax.rsqrt(pair[1] / pixel_total - mean * mean + epsilon)

    def phase_keys(count):
        turn = counters["phase"] % 2
        counters["phase"] += 1
        return [[("chan", turn, k, i) for i in range(3)] for k in range(count)]

    def gather_start(full, at, key):
        mine = full.at[at, cols(chan)]
        remote(mine, mine, (clip, j_y), key[0])
        remote(mine, mine, (clip, j_core), key[1])

    def gather_pass(full, at, key):
        theirs = full.at[at, cols(j_y)]
        arrive(theirs, key[0])
        remote(theirs, theirs, (clip, j_core), key[2])

    def gather_end(full, at, key):
        arrive(full.at[at, cols(j_core)], key[1])
        arrive(full.at[at, cols(j_far)], key[2])

    def pair(value):
        return pl.ds(pl.multiple_of(value * 2 * ib, 2 * ib), 2 * ib)

    def scatter_value(slot, at):
        mine = r.pb[at, cols(chan)].astype(f32)
        return mine + r.rcore[slot, 0, at].astype(f32) + r.ryy[slot, at].astype(f32)

    def keep_flag(f):
        return 1.0 - r.bnd[lax.div(f, SEG), lax.rem(f, SEG)].astype(f32)

    def taps_of(index):
        return [r.dkb[9 * index + tap] for tap in range(9)]

    def pair_rows(h, i):
        return pl.ds(pl.multiple_of(h * chunk + i * PAIR, 16), PAIR)

    def frame_rows(f):
        return pl.ds(pl.multiple_of(f * FRAME, 8), FRAME)

    def spread(ref, f):
        return jnp.stack(
            [ref[pl.ds(f * PIXELS + SIDE * k, 8), :] for k in range(SIDE)], axis=0
        )

    def squeeze(ref, f, value):
        for k in range(SIDE):
            ref[pl.ds(f * PIXELS + SIDE * k, 8), :] = value[k]

    pairs = frames // 4
    carried = {}
    zero_n = jnp.zeros((8, ib), f32)
    zero_w = jnp.zeros((8, cs), f32)

    def each(start, count, step, one, begin):
        def at_step(i, carry):
            return one(pl.ds(pl.multiple_of(start + i * step, 16), step), carry)

        return lax.fori_loop(0, count // step, at_step, begin)

    def narrow(start, count, one, begin):
        step = next(n for n in (112, 96, 80, 64, 48, 32, 16) if count % n == 0)
        return each(start, count, step, one, begin)

    def broad(one, begin):
        return each(0, rows, 16, one, begin)

    moments_in = [[None, None, None], [None, None, None]]

    def row(ref, s, k=None):
        return ref[s, k : k + 1, :] if k is not None else ref[s : s + 1, wide(chan)]

    def norm_inner(s, k, x):
        mean, inv = moments_in[s][k]
        centred = (x - mean) * inv
        return centred, centred * row(r.gi, s, k) + row(r.bi, s, k)

    def norm_outer(s, x):
        mean, inv = moments_in[s][2]
        centred = (x - mean) * inv
        return centred, centred * row(r.go, s) + row(r.bo, s)

    def inner_input(s, at):
        return r.x[at, wide(chan)] if s == 0 else r.out0[at]

    def temporal_forward(s, k):
        h, first_pair = k // 2, k % 2 * (pairs // 2)

        def hide(i, _):
            f = h * (frames // 2) + i
            value = real(gelu(norm_inner(s, 0, spread(r.red.at[s], f))[1]))
            r.hid[s, frame_rows(f)] = flat(value)
            return _

        if first_pair == 0:
            lax.fori_loop(0, frames // 2, hide, 0)

        def mix(i, before):
            base = pl.multiple_of(h * chunk + i * PAIR, 16)
            last = jnp.minimum(base + PAIR, (h + 1) * chunk - FRAME)
            f = h * (frames // 2) + 2 * i
            h0 = tiles(r.hid[s, pl.ds(base, FRAME)])
            h1 = tiles(r.hid[s, pl.ds(base + FRAME, FRAME)])
            h2 = tiles(r.hid[s, pl.ds(pl.multiple_of(last, 8), FRAME)])
            e0 = keep_flag(f) * (h1 - h0)
            e1 = keep_flag(f + 1) * (h2 - h1)
            if s == 0:
                taps = taps_of(0)
                m0 = real(h0 + dw_tiles(e0 + before, taps, 1, 1))
                m1 = real(h1 + dw_tiles(e1 + e0, taps, 1, 1))
            else:
                near, far = taps_of(1), taps_of(2)
                mixed = []
                for k, (hk, ek) in enumerate(((h0, e0), (h1, e1))):
                    logits = dw_tiles(ek, near, 1, 1) + dw_tiles(ek, far, 2, 1) + r.gb[...]
                    gate = 0.5 * (1.0 + jnp.tanh(0.5 * logits))
                    r.sig[pl.ds(base + k * FRAME, FRAME)] = flat(gate)
                    mixed.append(hk + hk * gate)
                m0, m1 = mixed
            both = jnp.concatenate([flat(m0), flat(m1)], axis=0).astype(bf16)
            r.mixf[s, pl.ds(base, PAIR), cols(chan)] = both
            return e1

        before = carried.get(s) if first_pair else jnp.zeros((SIDE, 8, ib), f32)
        carried[s] = lax.fori_loop(first_pair, first_pair + pairs // 2, mix, before)

    def conv_forward(s, k, sums):
        r.y[...] = dot(r.mixf[s, pl.ds(*padded_spans[k])], r.wc[s])

        def add_taps(i, sums):
            at = pl.ds(pl.multiple_of(i * FRAME, 8), FRAME)
            total = None
            for b in (-1, 0, 1):
                run = None
                for a in (-1, 0, 1):
                    tap = 3 * (a + 1) + b + 1
                    term = row_pad(tiles(r.y[at, tap * ib : (tap + 1) * ib]), 1)
                    term = term[1 + a : 1 + a + SIDE]
                    run = term if run is None else run + term
                run = col_shift(run, b)
                total = run if total is None else total + run
            total = real(total)
            squeeze(r.conv.at[s], k * (frames // 4) + i, total)
            return sums[0] + jnp.sum(total, axis=0), sums[1] + jnp.sum(total * total, axis=0)

        return lax.fori_loop(0, frames // 4, add_taps, sums)

    def forward(s, stat_base, wide_slot):
        keys = phase_keys(4)
        quarters = [pl.ds(*span) for span in padded_spans]
        for k in range(4):
            temporal_forward(s, k)
            gather_start(r.mixf.at[s], quarters[k], keys[k])
            if k > 0:
                gather_pass(r.mixf.at[s], quarters[k - 1], keys[k - 1])
        sums = (zero_n, zero_n)
        load_wc[s].wait()
        for k in range(4):
            gather_end(r.mixf.at[s], quarters[k], keys[k])
            if k == 0:
                gather_pass(r.mixf.at[s], quarters[3], keys[3])
            sums = conv_forward(s, k, sums)
        made = stat_start(r.stn, stat_base, sums)
        yield
        moments_in[s][1] = moments(stat_end(r.stn, stat_base, made))
        keys = phase_keys(2)
        for h in range(2):

            def inside(at, _):
                value = gelu(norm_inner(s, 1, r.conv[s, at])[1])
                r.inf[s, at, cols(chan)] = value.astype(bf16)
                return _

            narrow(starts[h], counts[h], inside, 0)
            gather_start(r.inf.at[s], raw(h), keys[h])
        yield
        gather_pass(r.inf.at[s], raw(0), keys[0])
        gather_pass(r.inf.at[s], raw(1), keys[1])
        sums = (zero_w, zero_w)
        for h in range(2):
            gather_end(r.inf.at[s], raw(h), keys[h])
            value = dot(r.inf[s, raw(h)], r.wef[s])
            r.ex[s, raw(h)] = value
            sums = (sums[0] + fold(value), sums[1] + fold(value * value))
        made = stat_start(r.stw, wide_slot, sums)
        yield
        moments_in[s][2] = moments(stat_end(r.stw, wide_slot, made))

    def spread_taps():
        for index in range(3):
            for tap in range(9):
                r.dkb[9 * index + tap] = jnp.broadcast_to(r.dk[tap, index : index + 1, :], (8, ib))

    def clear(i, _):
        r.gk[i] = zero_n
        return _

    for s in range(2):
        r.red[s, rows : rows + 8] = zero_n

    share_we(0)
    share_wr(1)
    sums = (zero_n, zero_n)
    load_wr0.wait()
    for h in range(2):
        load_x[h].wait()
        value = dot(r.x[raw(h)], r.wr0[...])
        r.red[0, raw(h)] = value
        sums = (sums[0] + fold(value), sums[1] + fold(value * value))
    made = stat_start(r.stn, 0, sums)
    spread_taps()
    lax.fori_loop(0, r.gk.shape[0], clear, 0)
    moments_in[0][0] = moments(stat_end(r.stn, 0, made))

    stage = forward(0, 1, 0)
    next(stage)
    next(stage)
    shared_we(0)
    next(stage)
    share_we(1)
    for _ in stage:
        pass

    def out_zero(at, _):
        z = norm_outer(0, r.ex[0, at])[1] + inner_input(0, at).astype(f32)
        r.out0[at] = gelu(z).astype(bf16)
        return _

    broad(out_zero, 0)

    def scatter_all(slot, chunks, product, use, beside=None):
        keys = phase_keys(4)
        ats = [pl.ds(*span) for span in chunks]
        borrowed = []

        def start(k, away):
            two = pair(1 - high if away else high)
            r.pb[ats[k], two] = product(ats[k], two).astype(bf16)
            block, index = (j_far, 1) if away else (j_core, 0)
            target = r.rcore.at[slot, index, ats[k]]
            made = remote(r.pb.at[ats[k], cols(block)], target, (clip, j_core), keys[k][index])
            borrowed.append(made[1])

        def hand_on(k):
            at = ats[k]
            arrive(r.rcore.at[slot, 1, at], keys[k][1])
            both = r.pb[at, cols(j_y)].astype(f32) + r.rcore[slot, 1, at].astype(f32)
            r.ysend[slot % 2, at] = both.astype(bf16)
            made = remote(r.ysend.at[slot % 2, at], r.ryy.at[slot, at], (clip, j_y), keys[k][2])
            borrowed.append(made[1])

        start(0, True)
        start(1, True)
        hand_on(0)
        start(2, True)
        hand_on(1)
        start(3, True)
        hand_on(2)
        start(0, False)
        hand_on(3)
        for k in range(1, 4):
            start(k, False)
        if beside is not None:
            beside()
        for k in range(4):
            arrive(r.rcore.at[slot, 0, ats[k]], keys[k][0])
            arrive(r.ryy.at[slot, ats[k]], keys[k][2])
            use(*chunks[k])
        for index in borrowed:
            sent(index)

    held = {"sums": (zero_n, zero_n)}

    def use_reduced(begin, count):
        at = pl.ds(begin, count)
        value = scatter_value(0, at)
        r.red[1, at] = value
        held["sums"] = (held["sums"][0] + fold(value), held["sums"][1] + fold(value * value))

    shared_wr(1)
    scatter_all(0, raw_spans, lambda at, two: dot(r.out0[at], r.wrf[1, :, two]), use_reduced)
    made = stat_start(r.stn, 2, held["sums"])
    moments_in[1][0] = moments(stat_end(r.stn, 2, made))
    stage = forward(1, 3, 1)
    next(stage)
    next(stage)
    shared_we(1)
    next(stage)
    share_wr(0)
    for _ in stage:
        pass

    load_cot.wait()

    def out_one(at, sums):
        centred, z = norm_outer(1, r.ex[1, at])
        value, slope = gelu_both(z + r.out0[at].astype(f32))
        r.act[at] = value.astype(bf16)
        grad = r.cot[at].astype(f32) * slope
        r.gpre[at] = grad
        return sums[0] + fold(grad), sums[1] + fold(grad * centred)

    def top_zero(at, sums):
        centred, z = norm_outer(0, r.ex[0, at])
        grad = r.gin[at] * gelu_both(z + inner_input(0, at).astype(f32))[1]
        r.gpre[at] = grad
        return sums[0] + fold(grad), sums[1] + fold(grad * centred)

    def backward(s, stat_base, wide_slot, slot):
        sums = broad(out_one if s else top_zero, (zero_w, zero_w))
        made = stat_start(r.stw, wide_slot, sums)
        if s == 1:
            write_out(r.act, r.act_out)
        service(s, "top")
        shift_sum, gain_sum = stat_end(r.stw, wide_slot, made)
        r.gbo[s : s + 1] = shift_sum
        r.ggo[s : s + 1] = gain_sum
        mean, inv = moments_in[s][2]
        scale = inv * row(r.go, s)
        shift_mean, gain_mean = shift_sum / pixel_total, gain_sum / pixel_total

        def expand_back(at, _):
            centred = (r.ex[s, at] - mean) * inv
            grad = scale * (r.gpre[at] - (shift_mean + centred * gain_mean))
            r.gexp[at] = grad.astype(bf16)
            return _

        broad(expand_back, 0)
        held["sums"] = (zero_n, zero_n)
        service(s, "expand_before")

        def weight_expand():
            value = dot(r.inf[s], r.gexp[...], 0, 0).astype(bf16)
            r.geo[s] = value.reshape(r.geo.shape[1:])
            place = r.ge.at[s, :, :, :, wide(chan)]
            turned["ge", s] = local(r.geo.at[s, chan], place)
            for j in others:
                remote(r.geo.at[s, j], place, (clip, j), ("ge", s))
            service(s, "expand")

        def use_inner(begin, count):
            def one(at, sums):
                centred, z = norm_inner(s, 1, r.conv[s, at])
                grad = scatter_value(slot, at) * gelu_both(z)[1]
                r.g1[at] = grad
                return sums[0] + fold(grad), sums[1] + fold(grad * centred)

            held["sums"] = narrow(begin, count, one, held["sums"])

        scatter_all(
            slot,
            raw_spans,
            lambda at, two: dot(r.gexp[at], r.wef[s, two], 1, 1),
            use_inner,
            weight_expand,
        )
        made = stat_start(r.stn, stat_base, held["sums"])
        service(s, "inner")
        shift_sum, gain_sum = stat_end(r.stn, stat_base, made)
        r.gbi[s, 1:2] = shift_sum
        r.ggi[s, 1:2] = gain_sum
        mean, inv = moments_in[s][1]
        scale = inv * row(r.gi, s, 1)
        shift_mean, gain_mean = shift_sum / pixel_total, gain_sum / pixel_total

        def conv_back(i, _):
            at = pair_rows(0, i)
            halves = []
            for f in (2 * i, 2 * i + 1):
                centred = (spread(r.conv.at[s], f) - mean) * inv
                grad = scale * (spread(r.g1, f) - (shift_mean + centred * gain_mean))
                halves.append(real(grad))
            for b in (-1, 0, 1):
                moved = [row_pad(col_shift(v, -b), 1) for v in halves]
                for a in (-1, 0, 1):
                    tap = 3 * (a + 1) + b + 1
                    both = jnp.concatenate([flat(v[1 - a : 1 - a + SIDE]) for v in moved], axis=0)
                    r.gs[at, tap * ib : (tap + 1) * ib] = both.astype(bf16)
            return _

        lax.fori_loop(0, 2 * pairs, conv_back, 0)

        service(s, "conv_before")

        def weight_conv():
            for k in range(3):
                taps = slice(3 * k * ib, 3 * (k + 1) * ib)
                value = dot(r.mixf[s], r.gs[:, taps], 0, 0).astype(bf16)
                r.gc[s, :, :, :, taps] = value.reshape(r.gc.shape[1:4] + (3 * ib,))
            service(s, "conv")

        def use_mixed(begin, count):
            def one(at, _):
                r.gm[at] = real(scatter_value(slot + 1, at))
                return _

            narrow(begin, count, one, 0)

        scatter_all(
            slot + 1,
            padded_spans,
            lambda at, two: dot(r.gs[at], r.wc[s, two], 1, 1),
            use_mixed,
            weight_conv,
        )

        def tap_sums(grad, v, index, reach):
            for b in (-1, 0, 1):
                padded = row_pad(col_shift(v, reach * b), reach)
                for a in (-1, 0, 1):
                    start = reach + reach * a
                    place = 9 * index + 3 * (a + 1) + b + 1
                    r.gk[place] = r.gk[place] + jnp.sum(grad * padded[start : start + SIDE], axis=0)

        def mix_back(f, before):
            at = frame_rows(f)
            following = frame_rows(jnp.minimum(f + 1, frames - 1))
            here = tiles(r.hid[s, at])
            step = keep_flag(f) * (tiles(r.hid[s, following]) - here)
            grad = tiles(r.gm[at])
            if s == 0:
                r.gd[at] = flat(dw_tiles(grad, taps_of(0), 1, -1))
                tap_sums(grad, step + before, 0, 1)
            else:
                gate = tiles(r.sig[at])
                grad = grad * here * gate * (1.0 - gate)
                r.gd[at] = flat(dw_tiles(grad, taps_of(1), 1, -1) + dw_tiles(grad, taps_of(2), 2, -1))
                tap_sums(grad, step, 1, 1)
                tap_sums(grad, step, 2, 2)
                r.gk[27] = r.gk[27] + jnp.sum(grad, axis=0)
            return step

        lax.fori_loop(0, frames, mix_back, jnp.zeros((SIDE, 8, ib), f32))

        service(s, "hide_before")

        def hide_back(f, sums):
            at = frame_rows(f)
            previous = frame_rows(jnp.maximum(f - 1, 0))
            keep = keep_flag(f)
            keep_before = jnp.where(f > 0, keep_flag(jnp.maximum(f - 1, 0)), 0.0)
            now = r.gd[at]
            earlier = r.gd[previous]
            grad = r.gm[at]
            if s == 0:
                following = frame_rows(jnp.minimum(f + 1, frames - 1))
                later = now + r.gd[following]
                earlier = earlier + now
            else:
                later = now
                grad = grad * (1.0 + r.sig[at])
            grad = grad + keep_before * earlier - keep * later
            centred, z = norm_inner(s, 0, spread(r.red.at[s], f))
            grad = real(tiles(grad) * gelu_both(z)[1])
            squeeze(r.g1, f, grad)
            return sums[0] + jnp.sum(grad, axis=0), sums[1] + jnp.sum(grad * centred, axis=0)

        sums = lax.fori_loop(0, frames, hide_back, (zero_n, zero_n))
        made = stat_start(r.stn, stat_base + 1, sums)
        service(s, "red")
        shift_sum, gain_sum = stat_end(r.stn, stat_base + 1, made)
        r.gbi[s, 0:1] = shift_sum
        r.ggi[s, 0:1] = gain_sum
        mean, inv = moments_in[s][0]
        scale = inv * row(r.gi, s, 0)
        shift_mean, gain_mean = shift_sum / pixel_total, gain_sum / pixel_total
        keys = phase_keys(2)
        for h in range(2):

            def reduce_back(at, _):
                centred = (r.red[s, at] - mean) * inv
                grad = scale * (r.g1[at] - (shift_mean + centred * gain_mean))
                r.grf[s, at, cols(chan)] = grad.astype(bf16)
                return _

            narrow(starts[h], counts[h], reduce_back, 0)
            gather_start(r.grf.at[s], raw(h), keys[h])
        if s == 0:
            own = r.grf[0, :, cols(chan)]
            for piece in range(n_chan):
                value = dot(r.x[:, piece * cs : (piece + 1) * cs], own, 0, 0).astype(bf16)
                r.gr[0, piece] = value.reshape(r.gr.shape[2:])
        service(s, "gather")
        gather_pass(r.grf.at[s], raw(0), keys[0])
        gather_pass(r.grf.at[s], raw(1), keys[1])
        if s == 0:
            shared_wr(0)
        for h in range(2):
            gather_end(r.grf.at[s], raw(h), keys[h])
            r.gin[raw(h)] = dot(r.grf[s, raw(h)], r.wrf[s], 1, 1) + r.gpre[raw(h)]
            if s == 0:
                write_out(r.gin.at[raw(h)], r.gin_out.at[raw(h)])
        service(s, "last")
        if s == 1:
            value = dot(r.out0[...], r.grf[1], 0, 0).astype(bf16)
            r.gro[...] = value.reshape(r.gro.shape)
            place = r.gr.at[1, chan]
            turned["gr", 1] = local(r.gro.at[:, :, cols(chan)], place)
            for j in others:
                remote(r.gro.at[:, :, cols(j)], place, (clip, j), ("gr", 1))

    turned = {}

    def reduce_task(kind, s, line, place):
        ref, from_side, from_z, result = kinds[kind]
        mine, done = ref.at[s, :, :, line, place], result.at[s, :, :, line, place]
        side_in, z_in = from_side.at[s, :, line, place], from_z.at[s, :, line, place]
        across = (2 * z + 1 - side, chan)
        key = (kind, s, line.start, place.start)
        if (kind, s) in turned:
            turned.pop((kind, s)).wait()
            three = pl.ds(0, (n_chan - 1) * cs)
            arrive(
                r.ge.at[s, :, :, :, three] if kind == "ge" else r.gr.at[s, pl.ds(0, n_chan - 1)],
                (kind, s),
            )
        remote(mine.at[:, 1 - side], side_in, across, key + (0,))
        yield
        arrive(side_in, key + (0,))
        for k in range(n_z):
            both = ref[s, k, side, line, place].astype(f32)
            both = both + from_side[s, k, line, place].astype(f32)
            ref[s, k, side, line, place] = both.astype(bf16)
        for k, there in enumerate(z_others):
            remote(mine.at[there, side], z_in.at[k], (2 * there + side, chan), key + (1,))
        yield
        arrive(z_in, key + (1,))
        total = ref[s, z, side, line, place].astype(f32)
        for k in range(n_z - 1):
            total = total + from_z[s, k, line, place].astype(f32)
        result[s, z, side, line, place] = total.astype(bf16)
        own = done.at[z, side]
        for there in z_others:
            remote(own, own, (2 * there + side, chan), key + (2,))
        yield
        arrive(done.at[pl.ds(0, n_z - 1), side], key + (2,))
        remote(done.at[:, side], done.at[:, side], across, key + (3,))
        yield
        arrive(done.at[:, 1 - side], key + (3,))
        if kind == "gc":
            base = place.start // ib
            for k in range((place.stop - place.start) // ib):
                here = r.fc.at[s, :, :, :, (base + k) * ib : (base + k + 1) * ib]
                write_out(here, r.gc_out.at[s, base + k])
        else:
            out = {"ge": r.ge_out, "gr": r.gr_out}[kind]
            write_out(done, out.at[s, :, :, line, place])
        yield

    kinds = {
        "gc": (r.gc, r.xc, r.zc, r.fc),
        "ge": (r.ge, r.xe, r.ze, r.fe),
        "gr": (r.gr, r.xr, r.zr, r.fr),
    }
    def cut(size, count):
        return [slice(k * (size // count), (k + 1) * (size // count)) for k in range(count)]

    tasks = {}
    for s in range(2):
        for k, place in enumerate(cut(9 * ib, PIECES["gc"])):
            tasks[f"c{k}", s] = reduce_task("gc", s, slice(0, r.gc.shape[3]), place)
        for k, place in enumerate(cut(r.ge.shape[4], PIECES["ge"])):
            tasks[f"e{k}", s] = reduce_task("ge", s, slice(0, r.ge.shape[3]), place)
        for k, line in enumerate(cut(r.gr.shape[3], PIECES["gr"])):
            tasks[f"r{k}", s] = reduce_task("gr", s, line, slice(0, ib))

    def advance(*steps):
        for step in steps:
            next(tasks[step])

    def service(s, point):
        advance(*PLAN.get((s, point), ()))

    backward(1, 4, 2, 1)
    backward(0, 6, 3, 3)

    for place in range(r.gk.shape[0]):
        r.kst[clip, place : place + 1, :] = jnp.sum(r.gk[place], axis=0, keepdims=True)
    for t in clip_others:
        remote(r.kst.at[clip], r.kst.at[clip], (t, chan), "taps")
    service(0, "end")
    arrive(r.kst.at[pl.ds(0, n_clip - 1)], "taps")
    total = r.kst[0]
    for k in range(1, n_clip):
        total = total + r.kst[k]
    for index in range(3):
        for tap in range(9):
            place = 9 * index + tap
            r.gk_out[tap, index : index + 1, :] = total[place : place + 1]
    r.ggb_out[...] = total[27:28]
    for copy in outgoing.values():
        copy.wait()
    for index in list(in_flight):
        sent(index)
    assert len(places) <= ARRIVALS and counters["load"] <= LOADS - 8, (places, counters)


def fused_call(n_clip, n_chan, pixel_total, *operands):
    rows, width = operands[0].shape
    cs = width // n_chan
    ib = LANES
    inner = ib * n_chan
    n_z = n_clip // 2
    padded = rows // PIXELS * FRAME
    over = rows + 8
    bf16, f32 = jnp.bfloat16, jnp.float32
    whole = pl.BlockSpec(memory_space=pltpu.VMEM)
    anywhere = pl.BlockSpec(memory_space=pl.ANY)
    scalars = pl.BlockSpec(memory_space=pltpu.SMEM)
    shape = jax.ShapeDtypeStruct
    V = pltpu.VMEM
    scratch = dict(
        x=V((rows, width), bf16),
        cot=V((rows, cs), bf16),
        wr0=V((width, ib), bf16),
        wrf=V((2, cs, inner), bf16),
        wef=V((2, inner, cs), bf16),
        wc=V((2, inner, 9 * ib), bf16),
        dkb=V((27, 8, ib), f32),
        red=V((2, over, ib), f32),
        hid=V((2, padded, ib), f32),
        sig=V((padded, ib), f32),
        conv=V((2, over, ib), f32),
        mixf=V((2, padded, inner), bf16),
        inf=V((2, rows, inner), bf16),
        ex=V((2, rows, cs), f32),
        out0=V((rows, cs), bf16),
        act=V((rows, cs), bf16),
        y=V((padded // 4, 9 * ib), f32),
        gpre=V((rows, cs), f32),
        gin=V((rows, cs), f32),
        gexp=V((rows, cs), bf16),
        gs=V((padded, 9 * ib), bf16),
        pb=V((padded, inner), bf16),
        ysend=V((2, padded, ib), bf16),
        rcore=V((5, 2, padded, ib), bf16),
        ryy=V((5, padded, ib), bf16),
        grf=V((2, rows, inner), bf16),
        gm=V((padded, ib), f32),
        gd=V((padded, ib), f32),
        g1=V((over, ib), f32),
        gk=V((32, 8, ib), f32),
        kst=V((n_clip, 32, ib), f32),
        stn=V((8, n_clip, 2, ib), f32),
        stw=V((4, n_clip, 2, cs), f32),
        gc=V((2, n_z, 2, inner // n_clip, 9 * ib), bf16),
        geo=V((2, n_chan, n_z, 2, ib // n_clip, cs), bf16),
        ge=V((2, n_z, 2, ib // n_clip, width), bf16),
        gro=V((2, cs // 2, inner), bf16),
        gr=V((2, n_z, 2, width // n_clip, ib), bf16),
        fc=V((2, n_z, 2, inner // n_clip, 9 * ib), bf16),
        fe=V((2, n_z, 2, ib // n_clip, width), bf16),
        fr=V((2, n_z, 2, width // n_clip, ib), bf16),
        xc=V((2, n_z, inner // n_clip, 9 * ib), bf16),
        xe=V((2, n_z, ib // n_clip, width), bf16),
        xr=V((2, n_z, width // n_clip, ib), bf16),
        zc=V((2, n_z - 1, inner // n_clip, 9 * ib), bf16),
        ze=V((2, n_z - 1, ib // n_clip, width), bf16),
        zr=V((2, n_z - 1, width // n_clip, ib), bf16),
        ssem=pltpu.SemaphoreType.DMA((SENDS,)),
        rsem=pltpu.SemaphoreType.DMA((ARRIVALS,)),
        lsem=pltpu.SemaphoreType.DMA((LOADS,)),
    )
    first = NAMES.index("x")
    return pl.pallas_call(
        partial(fused_kernel, n_clip, n_chan, pixel_total),
        out_shape=[
            shape((rows, cs), bf16),
            shape((rows, cs), f32),
            shape((2, 2, ib), f32),
            shape((2, 2, ib), f32),
            shape((2, cs), f32),
            shape((2, cs), f32),
            shape((9, 3, ib), f32),
            shape((1, ib), f32),
            shape((2, 9, n_z, 2, inner // n_clip, ib), bf16),
            shape((2, n_z, 2, ib // n_clip, width), bf16),
            shape((2, n_z, 2, width // n_clip, ib), bf16),
        ],
        in_specs=[anywhere] * 5 + [scalars] + [whole] * 6,
        out_specs=[anywhere] * 2 + [whole] * 6 + [anywhere] * 3,
        scratch_shapes=[scratch[name] for name in NAMES[first:]],
        compiler_params=pltpu.CompilerParams(
            collective_id=0, has_side_effects=True, vmem_limit_bytes=62 * 1024 * 1024
        ),
    )(*operands)


def finish_kernel(*refs):
    count = len(refs) // 2
    sources, results = refs[:count], refs[count:]
    for here, there in zip(sources[:5], results[:5]):
        there[...] = here[...].astype(there.dtype)

    @pl.when(pl.program_id(0) == 0)
    def _():
        for here, there in zip(sources[5:], results[5:]):
            there[...] = here[...]


def finish(steps, gc, ge, gr, act, gin, *small):
    arrays = [a.reshape(-1, a.shape[-1]) for a in (gc, ge, gr)] + [act, gin]
    blocks = [
        pl.BlockSpec((-(-a.shape[0] // (16 * steps)) * 16, a.shape[1]), lambda i: (i, 0))
        for a in arrays
    ]
    whole = [pl.BlockSpec(memory_space=pltpu.VMEM)] * len(small)
    shapes = [jax.ShapeDtypeStruct(a.shape, jnp.float32) for a in arrays[:3]]
    shapes += [jax.ShapeDtypeStruct(a.shape, a.dtype) for a in (act, gin, *small)]
    return pl.pallas_call(
        finish_kernel,
        grid=(steps,),
        out_shape=shapes,
        in_specs=blocks + whole,
        out_specs=blocks + whole,
        compiler_params=pltpu.CompilerParams(vmem_limit_bytes=62 * 1024 * 1024),
    )(*arrays, *small)


def fused(
    frames_in,
    boundary,
    w_reduce,
    gain_inner,
    bias_inner,
    w_conv,
    w_expand,
    gain_outer,
    bias_outer,
    depth_kernels,
    gate_bias,
    cotangent,
):
    n_clip, n_chan = lax.axis_size("clip"), lax.axis_size("chan")
    pixel_total = frames_in.shape[0] * n_clip
    act, gin, ggi, gbi, ggo, gbo, gk, ggb, gc, ge, gr = fused_call(
        n_clip,
        n_chan,
        float(pixel_total),
        frames_in,
        cotangent,
        w_reduce,
        w_conv,
        w_expand,
        boundary,
        gain_inner,
        bias_inner,
        gain_outer,
        bias_outer,
        depth_kernels.transpose(1, 0, 2),
        gate_bias.reshape(1, -1),
    )
    gc, ge, gr, act, gin, ggi, gbi, ggo, gbo, gk, ggb = finish(
        2, gc, ge, gr, act, gin, ggi, gbi, ggo, gbo, gk, ggb
    )
    return (
        act,
        gin,
        gr.reshape(w_reduce.shape),
        ggi,
        gbi,
        gc.reshape(w_conv.shape),
        ge.reshape(w_expand.shape),
        ggo,
        gbo,
        gk.transpose(1, 0, 2),
        ggb.reshape(-1),
    )


def solution(mesh):
    in_specs = (
        P("clip", None),
        P("clip", None),
        P(None, None, "chan"),
        P(None, None, "chan"),
        P(None, None, "chan"),
        P(None, None, None, "chan"),
        P(None, "chan", None),
        P(),
        P(),
        P(None, None, "chan"),
        P("chan"),
        P("clip", None),
    )
    out_specs = (
        P("clip", "chan"),
        P("clip", "chan"),
        P(None, None, "chan"),
        P(None, None, "chan"),
        P(None, None, "chan"),
        P(None, None, None, "chan"),
        P(None, "chan", None),
        P(None, "chan"),
        P(None, "chan"),
        P(None, None, "chan"),
        P("chan"),
    )

    def run(*arguments):
        fits = fused_fits(mesh, arguments[0].shape, arguments[2].shape)
        return jax.shard_map(fused if fits else body, mesh=mesh, in_specs=in_specs, out_specs=out_specs, check_vma=False)(*arguments)

    return run
```

```python
from functools import partial
from types import SimpleNamespace

import jax
import jax.numpy as jnp
from jax import lax
from jax.experimental import pallas as pl
from jax.experimental.pallas import tpu as pltpu
from jax.sharding import PartitionSpec as P

SEG = 8
SIDE = 7


epsilon = 1e-05


def framed(values):
    return values.reshape(-1, SIDE, SIDE, values.shape[-1])


def shifted(frame_grid, row_step, col_step, dilation):
    padded = jnp.pad(frame_grid, ((0, 0), (dilation, dilation), (dilation, dilation), (0, 0)))
    return padded[
        :,
        dilation + row_step : dilation + row_step + SIDE,
        dilation + col_step : dilation + col_step + SIDE,
        :,
    ]


def depthwise(values, kernel, dilation):
    frame_grid = framed(values)
    running = jnp.zeros_like(frame_grid)
    for tap_index in range(9):
        running = (
            running
            + shifted(
                frame_grid,
                (tap_index // 3 - 1) * dilation,
                (tap_index % 3 - 1) * dilation,
                dilation,
            )
            * kernel[tap_index]
        )
    return running.reshape(values.shape)


def patch_rows(values):
    frame_grid = framed(values)
    pieces = [
        shifted(frame_grid, tap_index // 3 - 1, tap_index % 3 - 1, 1) for tap_index in range(9)
    ]
    return jnp.concatenate(pieces, axis=-1).reshape(values.shape[0], 9 * values.shape[1])


def unpatch(grad_rows, chan_width):
    frame_grid = grad_rows.reshape(-1, SIDE, SIDE, 9, chan_width)
    running = jnp.zeros(frame_grid.shape[:3] + (chan_width,), jnp.float32)
    for tap_index in range(9):
        running = running + shifted(
            frame_grid[:, :, :, tap_index, :], 1 - tap_index // 3, 1 - tap_index % 3, 1
        )
    return running.reshape(-1, chan_width)


def neighbours(values, boundary):
    clip_count = boundary.shape[0]
    frame_grid = values.reshape(clip_count, SEG, SIDE * SIDE, values.shape[-1])
    stop_mask = (boundary == 1)[:, :, None, None]
    start_mask = jnp.concatenate([jnp.ones_like(stop_mask[:, :1]), stop_mask[:, :-1]], axis=1)
    after_seg = jnp.concatenate([frame_grid[:, 1:], frame_grid[:, -1:]], axis=1)
    before = jnp.concatenate([frame_grid[:, :1], frame_grid[:, :-1]], axis=1)
    later_seg = jnp.where(stop_mask, frame_grid, after_seg)
    earlier = jnp.where(start_mask, frame_grid, before)
    return (later_seg.reshape(values.shape), earlier.reshape(values.shape))


def temporal(values, kernels, gate_vec, boundary, short_range):
    later_seg, earlier = neighbours(values, boundary)
    if short_range:
        return values + depthwise(later_seg - earlier, kernels[0], 1)
    change = later_seg - values
    logits = depthwise(change, kernels[1], 1) + depthwise(change, kernels[2], 2) + gate_vec
    return values + values * jax.nn.sigmoid(logits)


def columns(values, col_start, col_share):
    return lax.dynamic_slice_in_dim(values, col_start, col_share, values.ndim - 1)


def contract(left, right, left_dim, right_dim):
    return lax.dot_general(
        left, right, (((left_dim,), (right_dim,)), ((), ())), preferred_element_type=jnp.float32
    )


def normalize(values, gain_vec, bias_vec, pixel_total):
    col_sum, sq_sum = lax.psum((jnp.sum(values, axis=0), jnp.sum(values * values, axis=0)), "clip")
    mean_val = col_sum / pixel_total
    inv_std = lax.rsqrt(sq_sum / pixel_total - mean_val * mean_val + epsilon)
    centred = (values - mean_val) * inv_std
    return (centred * gain_vec + bias_vec, centred, inv_std)


def normalize_back(grad_rows, centred, inv_std, gain_vec, pixel_total):
    shift_sum, gain_sum = lax.psum(
        (jnp.sum(grad_rows, axis=0), jnp.sum(grad_rows * centred, axis=0)), "clip"
    )
    grad_in = inv_std * gain_vec * (grad_rows - (shift_sum + centred * gain_sum) / pixel_total)
    return (grad_in, gain_sum, shift_sum)


def block_forward(inputs, boundary, weights, short_range, pixel_total):
    w_red, gain_pair, bias_pair, w_cv, w_ex, gain_out, bias_out, kernels, gate_vec = weights
    reduced = jnp.dot(inputs, w_red, preferred_element_type=jnp.float32)
    norm_one, centred_one, inv_one = normalize(reduced, gain_pair[0], bias_pair[0], pixel_total)
    hidden, gelu_one = jax.vjp(jax.nn.gelu, norm_one)
    mixed_act, mix_back = jax.vjp(
        partial(temporal, boundary=boundary, short_range=short_range), hidden, kernels, gate_vec
    )
    gathered = lax.all_gather(mixed_act.astype(jnp.bfloat16), "chan", axis=1, tiled=True)
    patches = patch_rows(gathered)
    conv_out = jnp.dot(
        patches, w_cv.reshape(-1, w_cv.shape[-1]), preferred_element_type=jnp.float32
    )
    norm_two, centred_two, inv_two = normalize(conv_out, gain_pair[1], bias_pair[1], pixel_total)
    inner_full, gelu_two = jax.vjp(jax.nn.gelu, norm_two)
    inner_act = inner_full.astype(jnp.bfloat16)
    partial_out = jnp.dot(inner_act, w_ex, preferred_element_type=jnp.float32)
    expanded = lax.psum(partial_out.astype(jnp.bfloat16), "chan").astype(jnp.float32)
    norm_three, centred_three, inv_three = normalize(expanded, gain_out, bias_out, pixel_total)
    output_full, gelu_three = jax.vjp(jax.nn.gelu, norm_three + inputs.astype(jnp.float32))
    kept_state = (
        centred_one,
        inv_one,
        gelu_one,
        mix_back,
        patches,
        centred_two,
        inv_two,
        gelu_two,
        inner_act,
        centred_three,
        inv_three,
        gelu_three,
        gain_out,
    )
    return (output_full.astype(jnp.bfloat16), kept_state)


def block_backward(grad_out, inputs, weights, kept_state, pixel_total):
    w_red, gain_pair, bias_pair, w_cv, w_ex, gain_out, bias_out, kernels, gate_vec = weights
    (
        centred_one,
        inv_one,
        gelu_one,
        mix_back,
        patches,
        centred_two,
        inv_two,
        gelu_two,
        inner_act,
        centred_three,
        inv_three,
        gelu_three,
        gain_use,
    ) = kept_state
    grad_pre = gelu_three(grad_out)[0]
    grad_exp, gain_three, bias_three = normalize_back(
        grad_pre, centred_three, inv_three, gain_use, pixel_total
    )
    low_exp = grad_exp.astype(jnp.bfloat16)
    grad_wex = contract(inner_act, low_exp, 0, 0)
    grad_inner = contract(low_exp, w_ex, 1, 1)
    grad_two = gelu_two(grad_inner)[0]
    grad_cv, gain_two, bias_two = normalize_back(
        grad_two, centred_two, inv_two, gain_pair[1], pixel_total
    )
    low_cv = grad_cv.astype(jnp.bfloat16)
    flat_cv = w_cv.reshape(-1, w_cv.shape[-1])
    grad_wcv = contract(patches, low_cv, 0, 0).reshape(w_cv.shape)
    grad_patch = contract(low_cv, flat_cv, 1, 1)
    grad_mixed = lax.psum_scatter(
        unpatch(grad_patch, w_cv.shape[1]).astype(jnp.bfloat16),
        "chan",
        scatter_dimension=1,
        tiled=True,
    ).astype(jnp.float32)
    grad_hidden, grad_kern, grad_gate = mix_back(grad_mixed)
    grad_one = gelu_one(grad_hidden)[0]
    grad_red, gain_one, bias_one = normalize_back(
        grad_one, centred_one, inv_one, gain_pair[0], pixel_total
    )
    low_red = grad_red.astype(jnp.bfloat16)
    grad_wred = contract(inputs, low_red, 0, 0)
    partial_in = contract(low_red, w_red, 1, 1)
    grad_in = grad_pre + lax.psum(partial_in.astype(jnp.bfloat16), "chan").astype(jnp.float32)
    weight_terms = (grad_wred, grad_wcv, grad_wex, grad_kern, grad_gate)
    norm_terms = (gain_one, bias_one, gain_two, bias_two, gain_three, bias_three)
    return (grad_in, weight_terms, norm_terms)


def body(
    frames_in,
    boundary,
    w_reduce,
    gain_inner,
    bias_inner,
    w_conv,
    w_expand,
    gain_outer,
    bias_outer,
    depth_kernels,
    gate_bias,
    cotangent,
):
    row_count = frames_in.shape[0]
    pixel_total = row_count * lax.axis_size("clip")
    col_share = frames_in.shape[1] // lax.axis_size("chan")
    col_start = lax.axis_index("chan") * col_share
    block_weights = [
        (
            w_reduce[block_index],
            gain_inner[block_index],
            bias_inner[block_index],
            w_conv[block_index],
            w_expand[block_index],
            gain_outer[block_index],
            bias_outer[block_index],
            depth_kernels,
            gate_bias,
        )
        for block_index in range(2)
    ]
    first_out, kept_zero = block_forward(frames_in, boundary, block_weights[0], True, pixel_total)
    final_out, kept_one = block_forward(first_out, boundary, block_weights[1], False, pixel_total)
    layer_inputs = [frames_in, first_out]
    kept_states = [kept_zero, kept_one]
    grad_flow = cotangent.astype(jnp.float32)
    weight_sums = [None, None]
    norm_sums = [None, None]
    for block_index in (1, 0):
        grad_flow, weight_terms, norm_terms = block_backward(
            grad_flow,
            layer_inputs[block_index],
            block_weights[block_index],
            kept_states[block_index],
            pixel_total,
        )
        grad_wred, grad_wcv, grad_wex, grad_kern, grad_gate = weight_terms
        weight_terms = (
            lax.psum(grad_wred.astype(jnp.bfloat16), "clip").astype(jnp.float32),
            lax.psum(grad_wcv.astype(jnp.bfloat16), "clip").astype(jnp.float32),
            lax.psum(grad_wex.astype(jnp.bfloat16), "clip").astype(jnp.float32),
            lax.psum(grad_kern.astype(jnp.bfloat16), "clip").astype(jnp.float32),
            lax.psum(grad_gate.astype(jnp.bfloat16), "clip").astype(jnp.float32),
        )
        weight_sums[block_index] = weight_terms
        norm_sums[block_index] = norm_terms
    grad_reduce = jnp.stack([weight_sums[0][0], weight_sums[1][0]])
    grad_conv = jnp.stack([weight_sums[0][1], weight_sums[1][1]])
    grad_expand = jnp.stack([weight_sums[0][2], weight_sums[1][2]])
    grad_kernels = weight_sums[0][3] + weight_sums[1][3]
    grad_gate_bias = weight_sums[0][4] + weight_sums[1][4]
    grad_gain_inner = jnp.stack(
        [
            jnp.stack([norm_sums[0][0], norm_sums[0][2]]),
            jnp.stack([norm_sums[1][0], norm_sums[1][2]]),
        ]
    )
    grad_bias_inner = jnp.stack(
        [
            jnp.stack([norm_sums[0][1], norm_sums[0][3]]),
            jnp.stack([norm_sums[1][1], norm_sums[1][3]]),
        ]
    )
    grad_gain_outer = jnp.stack([norm_sums[0][4], norm_sums[1][4]])
    grad_bias_outer = jnp.stack([norm_sums[0][5], norm_sums[1][5]])
    activations = columns(final_out, col_start, col_share)
    input_grad = columns(grad_flow, col_start, col_share)
    grad_gain_outer = columns(grad_gain_outer, col_start, col_share)
    grad_bias_outer = columns(grad_bias_outer, col_start, col_share)
    return (
        activations,
        input_grad,
        grad_reduce,
        grad_gain_inner,
        grad_bias_inner,
        grad_conv,
        grad_expand,
        grad_gain_outer,
        grad_bias_outer,
        grad_kernels,
        grad_gate_bias,
    )


MESH = pl.DeviceIdType.MESH
LANES = 128
FRAME = SIDE * 8
PIXELS = SIDE * SIDE
PAIR = 2 * FRAME
GELU_A = 0.7978845608028654
GELU_B = 0.044715
SENDS = 64
LOADS = 32


def fused_fits(mesh, frame_shape, reduce_shape):
    n_clip, n_chan = mesh.shape["clip"], mesh.shape["chan"]
    share = reduce_shape[2] // n_chan
    frames = frame_shape[0] // (n_clip * SIDE * SIDE)
    return n_chan == 4 and n_clip == 8 and share == LANES and frames == 2 * SEG


def gelu(z):
    return 0.5 * z * (1.0 + jnp.tanh(GELU_A * (z + GELU_B * z * z * z)))


def gelu_both(z):
    square = z * z
    t = jnp.tanh(GELU_A * (z + GELU_B * square * z))
    slope = 0.5 * (1.0 + t) + 0.5 * z * (1.0 - t * t) * (GELU_A * (1.0 + 3.0 * GELU_B * square))
    return 0.5 * z * (1.0 + t), slope


def real_columns(shape):
    return lax.rem(lax.broadcasted_iota(jnp.int32, shape, len(shape) - 2), 8) < SIDE


def real(values):
    return jnp.where(real_columns(values.shape), values, 0.0)


def fold(values):
    return jnp.sum(values.reshape(-1, 8, values.shape[-1]), axis=0)


def tiles(values):
    return values.reshape(SIDE, 8, values.shape[-1])


def flat(values):
    return values.reshape(FRAME, values.shape[-1])


def row_pad(v, reach):
    zeros = jnp.zeros((reach,) + v.shape[1:], v.dtype)
    return jnp.concatenate([zeros, v, zeros], axis=0)


def col_shift(v, step):
    if step == 0:
        return v
    moved = pltpu.roll(v, (-step) % 8, v.ndim - 2)
    if abs(step) == 2:
        place = lax.broadcasted_iota(jnp.int32, v.shape, v.ndim - 2)
        moved = jnp.where(place < 6 if step > 0 else place >= 2, moved, 0.0)
    return moved


def dw_tiles(v, taps, reach, sign):
    padded = row_pad(v, reach)
    total = None
    for b in (-1, 0, 1):
        part = None
        for a in (-1, 0, 1):
            start = reach + sign * reach * a
            term = taps[3 * (a + 1) + b + 1] * padded[start : start + SIDE]
            part = term if part is None else part + term
        part = col_shift(part, sign * reach * b)
        total = part if total is None else total + part
    return total


def dot(left, right, left_dim=1, right_dim=0):
    return lax.dot_general(
        left, right, (((left_dim,), (right_dim,)), ((), ())), preferred_element_type=jnp.float32
    )


NAMES = (
    "x_hbm", "cot_hbm", "wred_hbm", "wconv_hbm", "wexp_hbm", "bnd", "gi", "bi", "go", "bo",
    "dk", "gb", "act_out", "gin_out", "ggi", "gbi", "ggo", "gbo", "gk_out", "ggb_out", "gc_out",
    "ge_out", "gr_out", "x", "cot", "wr0", "wrf", "wef", "wc", "dkb", "red", "hid", "sig",
    "conv", "mixf", "inf", "ex", "out0", "act", "y", "gpre", "gin", "gexp", "gs", "pb", "ysend",
    "rcore", "ryy", "grf", "gm", "gd", "g1", "gk", "kst", "stn", "stw", "gc", "geo", "ge",
    "gro", "gr", "xc", "xe", "xr", "zc", "ze", "zr", "fc", "fe", "fr", "ssem", "rsem", "lsem",
)


PIECES = {"gc": 3, "ge": 4, "gr": 4}
ARRIVALS = 40 + 8 * sum(PIECES.values())
PLAN = {
    (1, "conv_before"): (
        ("e1", 1), ("e2", 1), ("e3", 1), ("e0", 1),
    ),
    (1, "conv"): (
        ("c0", 1), ("e1", 1), ("e2", 1), ("c2", 1),
    ),
    (1, "conv_use"): (
        ("e3", 1), ("e0", 1),
    ),
    (1, "hide_before"): (
        ("e1", 1), ("e2", 1),
    ),
    (1, "red"): (
        ("c0", 1), ("e3", 1), ("c2", 1), ("e0", 1), ("c1", 1), ("e1", 1),
    ),
    (1, "red_after"): (
        ("e2", 1),
    ),
    (1, "last"): (
        ("e1", 1), ("e3", 1),
    ),
    (0, "top"): (
        ("c0", 1), ("e2", 1), ("e3", 1), ("c2", 1), ("e0", 1), ("c1", 1),
    ),
    (0, "expand_before"): (
        ("r3", 1), ("r1", 1), ("r2", 1), ("r0", 1),
    ),
    (0, "expand"): (
        ("c0", 1), ("r3", 1), ("r1", 1), ("e0", 1),
    ),
    (0, "inner"): (
        ("r2", 1), ("c2", 1), ("r0", 1), ("c1", 1),
    ),
    (0, "conv_before"): (
        ("c0", 1), ("r3", 1), ("e1", 0), ("r1", 1), ("e0", 0), ("e2", 0), ("e3", 0), ("r2", 1),
    ),
    (0, "conv"): (
        ("c2", 0), ("e1", 0), ("c1", 0), ("e0", 0), ("e2", 0), ("c0", 0), ("c2", 1), ("r0", 1),
    ),
    (0, "conv_use"): (
        ("r3", 1), ("e3", 0),
    ),
    (0, "hide_before"): (
        ("c2", 0),
    ),
    (0, "red"): (
        ("e1", 0), ("c1", 0), ("r1", 1), ("e0", 0), ("e2", 0), ("c0", 0), ("e3", 0), ("r2", 1),
        ("r0", 1), ("c1", 1), ("r3", 1),
    ),
    (0, "gather"): (
        ("r1", 0), ("r1", 1), ("r0", 0),
    ),
    (0, "gather_use"): (
        ("c2", 0), ("e1", 0), ("r2", 0), ("r2", 1), ("r0", 1), ("r3", 0),
    ),
    (0, "end"): (
        ("c1", 0), ("e0", 0), ("c1", 1), ("e2", 0), ("r1", 0), ("r0", 0), ("e1", 0), ("c0", 0),
        ("r2", 0), ("e3", 0), ("r3", 0), ("c2", 0), ("e0", 0), ("e2", 0), ("e3", 0), ("c1", 0),
        ("r1", 0), ("r0", 0), ("c2", 0), ("c1", 0), ("c0", 0), ("r2", 0), ("r3", 0), ("r1", 0),
        ("r0", 0), ("c0", 0), ("r2", 0), ("r1", 0), ("r3", 0), ("r0", 0), ("r2", 0), ("r3", 0),
    ),
}


def fused_kernel(n_clip, n_chan, pixel_total, *refs):
    r = SimpleNamespace(**dict(zip(NAMES, refs)))
    rows, cs = r.cot.shape
    ib = LANES
    frames = rows // PIXELS
    chunk = frames // 2 * FRAME
    n_z = n_clip // 2
    first = -(-rows // 32) * 16
    starts, counts = (0, first), (first, rows - first)
    bf16, f32 = jnp.bfloat16, jnp.float32
    clip = lax.axis_index("clip")
    chan = lax.axis_index("chan")
    core, high = lax.rem(chan, 2), lax.div(chan, 2)
    j_core = (1 - core) + 2 * high
    j_y = core + 2 * (1 - high)
    j_far = (1 - core) + 2 * (1 - high)
    others = (j_core, j_y, j_far)
    z, side = lax.div(clip, 2), lax.rem(clip, 2)
    z_others = [lax.rem(z + d, n_z) for d in range(1, n_z)]
    clip_others = [lax.rem(clip + d, n_clip) for d in range(1, n_clip)]

    def cols(j):
        return pl.ds(pl.multiple_of(j * ib, ib), ib)

    def wide(j):
        return pl.ds(pl.multiple_of(j * cs, cs), cs)

    def part(h):
        return pl.ds(h * chunk, chunk)

    def raw(h):
        return pl.ds(starts[h], counts[h])

    def spans(total):
        tiles_left, at, chunks = total // 16, 0, []
        for left in range(4, 0, -1):
            take = -(-tiles_left // left)
            chunks.append((at * 16, take * 16))
            at, tiles_left = at + take, tiles_left - take
        return chunks

    raw_spans, padded_spans = spans(rows), spans(frames * FRAME)

    places, in_flight, counters = {}, {}, {"send": 0, "load": 0, "phase": 0, "sums": 0}

    def arrival(key):
        return r.rsem.at[places.setdefault(key, len(places))]

    def sent(index):
        if index in in_flight:
            in_flight.pop(index).wait_send()

    def remote(src, dst, target, key):
        index = counters["send"] % SENDS
        counters["send"] += 1
        sent(index)
        made = pltpu.make_async_remote_copy(
            src_ref=src,
            dst_ref=dst,
            send_sem=r.ssem.at[index],
            recv_sem=arrival(key),
            device_id=target,
            device_id_type=MESH,
        )
        made.start()
        in_flight[index] = made
        return made, index

    def arrive(place, key):
        pltpu.make_async_remote_copy(
            src_ref=place,
            dst_ref=place,
            send_sem=r.ssem.at[0],
            recv_sem=arrival(key),
            device_id=(clip, j_core),
            device_id_type=MESH,
        ).wait_recv()

    def local(src, dst, index=None):
        if index is None:
            index = counters["load"]
            counters["load"] += 1
        made = pltpu.make_async_copy(src, dst, r.lsem.at[index])
        made.start()
        return made

    outgoing = {}

    def write_out(src, dst):
        turn = counters.setdefault("out", 0) % 8
        counters["out"] += 1
        if turn in outgoing:
            outgoing.pop(turn).wait()
        outgoing[turn] = local(src, dst, LOADS - 8 + turn)

    load_wr0 = local(r.wred_hbm.at[0], r.wr0)
    load_x = [local(r.x_hbm.at[raw(h)], r.x.at[raw(h)]) for h in range(2)]
    load_we = [
        local(r.wexp_hbm.at[s, :, wide(chan)], r.wef.at[s, cols(chan)]) for s in range(2)
    ]
    load_wr = [
        local(r.wred_hbm.at[s, wide(chan)], r.wrf.at[s, :, cols(chan)]) for s in range(2)
    ]
    load_wc = []
    for s in range(2):
        index = counters["load"]
        counters["load"] += 1
        for tap in range(9):
            local(r.wconv_hbm.at[s, tap], r.wc.at[s, :, tap * ib : (tap + 1) * ib], index)
        load_wc.append(pltpu.make_async_copy(r.wc.at[s], r.wc.at[s], r.lsem.at[index]))
    load_cot = local(r.cot_hbm.at[:, wide(chan)], r.cot)

    barrier = pltpu.get_barrier_semaphore()
    for target in clip_others:
        pl.semaphore_signal(barrier, inc=1, device_id=(target, chan), device_id_type=MESH)
    for target in others:
        pl.semaphore_signal(barrier, inc=1, device_id=(clip, target), device_id_type=MESH)

    def share_we(s, half):
        size = ib // 2
        for j in others:
            here = r.wexp_hbm.at[s, pl.ds(half * size, size), wide(j)]
            target = r.wef.at[s, pl.ds(pl.multiple_of(chan * ib + half * size, size), size)]
            remote(here, target, (clip, j), ("we", s))

    def share_wr(s, half):
        size = cs // 2
        for j in others:
            here = r.wred_hbm.at[s, pl.ds(pl.multiple_of(j * cs + half * size, size), size)]
            target = r.wrf.at[s, pl.ds(half * size, size), cols(chan)]
            remote(here, target, (clip, j), ("wr", s))

    def shared_we(s):
        load_we[s].wait()
        arrive(r.wef.at[s, pl.ds(0, (n_chan - 1) * ib)], ("we", s))

    def shared_wr(s):
        load_wr[s].wait()
        arrive(r.wrf.at[s, :, pl.ds(0, (n_chan - 1) * ib)], ("wr", s))

    def stat_start(buf, slot, values):
        for k, value in enumerate(values):
            buf[slot, clip, k : k + 1, :] = jnp.sum(value, axis=0, keepdims=True)
        key = ("sums", counters["sums"] % 2)
        counters["sums"] += 1
        for t in clip_others:
            remote(buf.at[slot, clip], buf.at[slot, clip], (t, chan), key)
        return key

    def stat_end(buf, slot, key):
        arrive(buf.at[slot, pl.ds(0, n_clip - 1)], key)
        total = buf[slot, 0]
        for k in range(1, n_clip):
            total = total + buf[slot, k]
        return total[0:1], total[1:2]

    def moments(pair):
        mean = pair[0] / pixel_total
        return mean, lax.rsqrt(pair[1] / pixel_total - mean * mean + epsilon)

    def phase_keys(count):
        turn = counters["phase"] % 2
        counters["phase"] += 1
        return [[("chan", turn, k, i) for i in range(3)] for k in range(count)]

    def gather_start(full, at, key):
        mine = full.at[at, cols(chan)]
        remote(mine, mine, (clip, j_y), key[0])
        remote(mine, mine, (clip, j_core), key[1])

    def gather_pass(full, at, key):
        theirs = full.at[at, cols(j_y)]
        arrive(theirs, key[0])
        remote(theirs, theirs, (clip, j_core), key[2])

    def gather_end(full, at, key):
        arrive(full.at[at, cols(j_core)], key[1])
        arrive(full.at[at, cols(j_far)], key[2])

    def pair(value):
        return pl.ds(pl.multiple_of(value * 2 * ib, 2 * ib), 2 * ib)

    def scatter_value(slot, at):
        mine = r.pb[at, cols(chan)].astype(f32)
        return mine + r.rcore[slot, 0, at].astype(f32) + r.ryy[slot, at].astype(f32)

    def keep_flag(f):
        return 1.0 - r.bnd[lax.div(f, SEG), lax.rem(f, SEG)].astype(f32)

    def taps_of(index):
        return [r.dkb[9 * index + tap] for tap in range(9)]

    def pair_rows(h, i):
        return pl.ds(pl.multiple_of(h * chunk + i * PAIR, 16), PAIR)

    def frame_rows(f):
        return pl.ds(pl.multiple_of(f * FRAME, 8), FRAME)

    def spread(ref, f):
        return jnp.stack(
            [ref[pl.ds(f * PIXELS + SIDE * k, 8), :] for k in range(SIDE)], axis=0
        )

    def squeeze(ref, f, value):
        for k in range(SIDE):
            ref[pl.ds(f * PIXELS + SIDE * k, 8), :] = value[k]

    pairs = frames // 4
    carried = {}
    zero_n = jnp.zeros((8, ib), f32)
    zero_w = jnp.zeros((8, cs), f32)

    def each(start, count, step, one, begin):
        def at_step(i, carry):
            return one(pl.ds(pl.multiple_of(start + i * step, 16), step), carry)

        return lax.fori_loop(0, count // step, at_step, begin)

    def narrow(start, count, one, begin):
        step = next(n for n in (112, 96, 80, 64, 48, 32, 16) if count % n == 0)
        return each(start, count, step, one, begin)

    def broad(k, one, begin):
        return each(*raw_spans[k], 16, one, begin)

    moments_in = [[None, None, None], [None, None, None]]

    def row(ref, s, k=None):
        return ref[s, k : k + 1, :] if k is not None else ref[s : s + 1, wide(chan)]

    def norm_inner(s, k, x):
        mean, inv = moments_in[s][k]
        centred = (x - mean) * inv
        return centred, centred * row(r.gi, s, k) + row(r.bi, s, k)

    def norm_outer(s, x):
        mean, inv = moments_in[s][2]
        centred = (x - mean) * inv
        return centred, centred * row(r.go, s) + row(r.bo, s)

    def inner_input(s, at):
        return r.x[at, wide(chan)] if s == 0 else r.out0[at]

    def temporal_forward(s, k):
        h, first_pair = k // 2, k % 2 * (pairs // 2)

        def hide(i, _):
            f = h * (frames // 2) + i
            value = real(gelu(norm_inner(s, 0, spread(r.red.at[s], f))[1]))
            r.hid[s, frame_rows(f)] = flat(value)
            return _

        if first_pair == 0:
            lax.fori_loop(0, frames // 2, hide, 0)

        def mix(i, before):
            base = pl.multiple_of(h * chunk + i * PAIR, 16)
            last = jnp.minimum(base + PAIR, (h + 1) * chunk - FRAME)
            f = h * (frames // 2) + 2 * i
            h0 = tiles(r.hid[s, pl.ds(base, FRAME)])
            h1 = tiles(r.hid[s, pl.ds(base + FRAME, FRAME)])
            h2 = tiles(r.hid[s, pl.ds(pl.multiple_of(last, 8), FRAME)])
            e0 = keep_flag(f) * (h1 - h0)
            e1 = keep_flag(f + 1) * (h2 - h1)
            if s == 0:
                taps = taps_of(0)
                m0 = real(h0 + dw_tiles(e0 + before, taps, 1, 1))
                m1 = real(h1 + dw_tiles(e1 + e0, taps, 1, 1))
            else:
                near, far = taps_of(1), taps_of(2)
                mixed = []
                for k, (hk, ek) in enumerate(((h0, e0), (h1, e1))):
                    logits = dw_tiles(ek, near, 1, 1) + dw_tiles(ek, far, 2, 1) + r.gb[...]
                    gate = 0.5 * (1.0 + jnp.tanh(0.5 * logits))
                    r.sig[pl.ds(base + k * FRAME, FRAME)] = flat(gate)
                    mixed.append(hk + hk * gate)
                m0, m1 = mixed
            both = jnp.concatenate([flat(m0), flat(m1)], axis=0).astype(bf16)
            r.mixf[s, pl.ds(base, PAIR), cols(chan)] = both
            return e1

        before = carried.get(s) if first_pair else jnp.zeros((SIDE, 8, ib), f32)
        carried[s] = lax.fori_loop(first_pair, first_pair + pairs // 2, mix, before)

    def conv_forward(s, k, sums):
        r.y[...] = dot(r.mixf[s, pl.ds(*padded_spans[k])], r.wc[s])

        def add_taps(i, sums):
            at = pl.ds(pl.multiple_of(i * FRAME, 8), FRAME)
            total = None
            for b in (-1, 0, 1):
                run = None
                for a in (-1, 0, 1):
                    tap = 3 * (a + 1) + b + 1
                    term = row_pad(tiles(r.y[at, tap * ib : (tap + 1) * ib]), 1)
                    term = term[1 + a : 1 + a + SIDE]
                    run = term if run is None else run + term
                run = col_shift(run, b)
                total = run if total is None else total + run
            total = real(total)
            squeeze(r.conv.at[s], k * (frames // 4) + i, total)
            return sums[0] + jnp.sum(total, axis=0), sums[1] + jnp.sum(total * total, axis=0)

        return lax.fori_loop(0, frames // 4, add_taps, sums)

    def forward(s, stat_base, wide_slot):
        keys = phase_keys(4)
        quarters = [pl.ds(*span) for span in padded_spans]
        for k in range(4):
            temporal_forward(s, k)
            gather_start(r.mixf.at[s], quarters[k], keys[k])
            if k > 0:
                gather_pass(r.mixf.at[s], quarters[k - 1], keys[k - 1])
        sums = (zero_n, zero_n)
        load_wc[s].wait()
        for k in range(4):
            gather_end(r.mixf.at[s], quarters[k], keys[k])
            if k == 0:
                gather_pass(r.mixf.at[s], quarters[3], keys[3])
            sums = conv_forward(s, k, sums)
        made = stat_start(r.stn, stat_base, sums)
        yield
        moments_in[s][1] = moments(stat_end(r.stn, stat_base, made))
        keys = phase_keys(2)
        for h in range(2):

            def inside(at, _):
                value = gelu(norm_inner(s, 1, r.conv[s, at])[1])
                r.inf[s, at, cols(chan)] = value.astype(bf16)
                return _

            narrow(starts[h], counts[h], inside, 0)
            gather_start(r.inf.at[s], raw(h), keys[h])
        yield
        gather_pass(r.inf.at[s], raw(0), keys[0])
        gather_pass(r.inf.at[s], raw(1), keys[1])
        sums = (zero_w, zero_w)
        for h in range(2):
            gather_end(r.inf.at[s], raw(h), keys[h])
            value = dot(r.inf[s, raw(h)], r.wef[s])
            r.ex[s, raw(h)] = value
            sums = (sums[0] + fold(value), sums[1] + fold(value * value))
        made = stat_start(r.stw, wide_slot, sums)
        yield
        moments_in[s][2] = moments(stat_end(r.stw, wide_slot, made))

    def spread_taps():
        for index in range(3):
            for tap in range(9):
                r.dkb[9 * index + tap] = jnp.broadcast_to(r.dk[tap, index : index + 1, :], (8, ib))

    def clear(i, _):
        r.gk[i] = zero_n
        return _

    for s in range(2):
        r.red[s, rows : rows + 8] = zero_n

    sums = (zero_n, zero_n)
    load_wr0.wait()
    for h in range(2):
        load_x[h].wait()
        value = dot(r.x[raw(h)], r.wr0[...])
        r.red[0, raw(h)] = value
        sums = (sums[0] + fold(value), sums[1] + fold(value * value))
    pl.semaphore_wait(barrier, n_clip - 1 + n_chan - 1)
    made = stat_start(r.stn, 0, sums)
    share_we(0, 0)
    share_we(0, 1)
    spread_taps()
    lax.fori_loop(0, r.gk.shape[0], clear, 0)
    moments_in[0][0] = moments(stat_end(r.stn, 0, made))

    stage = forward(0, 1, 0)
    next(stage)
    share_wr(1, 0)
    next(stage)
    shared_we(0)
    next(stage)
    share_wr(1, 1)
    for _ in stage:
        pass

    def out_zero(at, _):
        z = norm_outer(0, r.ex[0, at])[1] + inner_input(0, at).astype(f32)
        r.out0[at] = gelu(z).astype(bf16)
        return _


    def scatter_all(slot, chunks, prepare, product, use, beside=None, midway=None):
        keys = phase_keys(4)
        ats = [pl.ds(*span) for span in chunks]
        borrowed = []

        def start(k, away):
            if away:
                prepare(k)
            two = pair(1 - high if away else high)
            r.pb[ats[k], two] = product(ats[k], two).astype(bf16)
            block, index = (j_far, 1) if away else (j_core, 0)
            target = r.rcore.at[slot, index, ats[k]]
            made = remote(r.pb.at[ats[k], cols(block)], target, (clip, j_core), keys[k][index])
            borrowed.append(made[1])

        def hand_on(k):
            at = ats[k]
            arrive(r.rcore.at[slot, 1, at], keys[k][1])
            both = r.pb[at, cols(j_y)].astype(f32) + r.rcore[slot, 1, at].astype(f32)
            r.ysend[slot % 2, at] = both.astype(bf16)
            made = remote(r.ysend.at[slot % 2, at], r.ryy.at[slot, at], (clip, j_y), keys[k][2])
            borrowed.append(made[1])

        start(0, True)
        start(1, True)
        hand_on(0)
        start(2, True)
        hand_on(1)
        start(3, True)
        hand_on(2)
        start(0, False)
        hand_on(3)
        for k in range(1, 4):
            start(k, False)
        if beside is not None:
            beside()
        for k in range(4):
            arrive(r.rcore.at[slot, 0, ats[k]], keys[k][0])
            arrive(r.ryy.at[slot, ats[k]], keys[k][2])
            use(*chunks[k])
            if midway is not None and k == 1:
                midway()
        for index in borrowed:
            sent(index)

    held = {"sums": (zero_n, zero_n)}

    def use_reduced(begin, count):
        at = pl.ds(begin, count)
        value = scatter_value(0, at)
        r.red[1, at] = value
        held["sums"] = (held["sums"][0] + fold(value), held["sums"][1] + fold(value * value))

    shared_wr(1)
    scatter_all(
        0,
        raw_spans,
        lambda k: broad(k, out_zero, 0),
        lambda at, two: dot(r.out0[at], r.wrf[1, :, two]),
        use_reduced,
    )
    made = stat_start(r.stn, 2, held["sums"])
    share_we(1, 0)
    moments_in[1][0] = moments(stat_end(r.stn, 2, made))
    stage = forward(1, 3, 1)
    next(stage)
    share_we(1, 1)
    next(stage)
    shared_we(1)
    next(stage)
    share_wr(0, 0)
    share_wr(0, 1)
    for _ in stage:
        pass

    load_cot.wait()

    def out_one(at, sums):
        centred, z = norm_outer(1, r.ex[1, at])
        value, slope = gelu_both(z + r.out0[at].astype(f32))
        r.act[at] = value.astype(bf16)
        grad = r.cot[at].astype(f32) * slope
        r.gpre[at] = grad
        return sums[0] + fold(grad), sums[1] + fold(grad * centred)

    def top_zero(at, sums):
        centred, z = norm_outer(0, r.ex[0, at])
        grad = r.gin[at] * gelu_both(z + inner_input(0, at).astype(f32))[1]
        r.gpre[at] = grad
        return sums[0] + fold(grad), sums[1] + fold(grad * centred)

    top_sums = {}

    def backward(s, stat_base, wide_slot, slot):
        if s == 1:
            top_sums["now"] = (zero_w, zero_w)
            for k in range(4):
                top_sums["now"] = broad(k, out_one, top_sums["now"])
        sums = top_sums["now"]
        made = stat_start(r.stw, wide_slot, sums)
        if s == 1:
            write_out(r.act, r.act_out)
        service(s, "top")
        shift_sum, gain_sum = stat_end(r.stw, wide_slot, made)
        r.gbo[s : s + 1] = shift_sum
        r.ggo[s : s + 1] = gain_sum
        mean, inv = moments_in[s][2]
        scale = inv * row(r.go, s)
        shift_mean, gain_mean = shift_sum / pixel_total, gain_sum / pixel_total

        def expand_back(at, _):
            centred = (r.ex[s, at] - mean) * inv
            grad = scale * (r.gpre[at] - (shift_mean + centred * gain_mean))
            r.gexp[at] = grad.astype(bf16)
            return _

        held["sums"] = (zero_n, zero_n)
        service(s, "expand_before")

        def weight_expand():
            value = dot(r.inf[s], r.gexp[...], 0, 0).astype(bf16)
            r.geo[s] = value.reshape(r.geo.shape[1:])
            place = r.ge.at[s, :, :, :, wide(chan)]
            turned["ge", s] = local(r.geo.at[s, chan], place)
            for j in others:
                remote(r.geo.at[s, j], place, (clip, j), ("ge", s))
            service(s, "expand")

        def use_inner(begin, count):
            def one(at, sums):
                centred, z = norm_inner(s, 1, r.conv[s, at])
                grad = scatter_value(slot, at) * gelu_both(z)[1]
                r.g1[at] = grad
                return sums[0] + fold(grad), sums[1] + fold(grad * centred)

            held["sums"] = narrow(begin, count, one, held["sums"])

        scatter_all(
            slot,
            raw_spans,
            lambda k: broad(k, expand_back, 0),
            lambda at, two: dot(r.gexp[at], r.wef[s, two], 1, 1),
            use_inner,
            weight_expand,
            lambda: service(s, "expand_use"),
        )
        made = stat_start(r.stn, stat_base, held["sums"])
        service(s, "inner")
        shift_sum, gain_sum = stat_end(r.stn, stat_base, made)
        r.gbi[s, 1:2] = shift_sum
        r.ggi[s, 1:2] = gain_sum
        mean, inv = moments_in[s][1]
        scale = inv * row(r.gi, s, 1)
        shift_mean, gain_mean = shift_sum / pixel_total, gain_sum / pixel_total

        def conv_back(i, _):
            at = pair_rows(0, i)
            halves = []
            for f in (2 * i, 2 * i + 1):
                centred = (spread(r.conv.at[s], f) - mean) * inv
                grad = scale * (spread(r.g1, f) - (shift_mean + centred * gain_mean))
                halves.append(real(grad))
            for b in (-1, 0, 1):
                moved = [row_pad(col_shift(v, -b), 1) for v in halves]
                for a in (-1, 0, 1):
                    tap = 3 * (a + 1) + b + 1
                    both = jnp.concatenate([flat(v[1 - a : 1 - a + SIDE]) for v in moved], axis=0)
                    r.gs[at, tap * ib : (tap + 1) * ib] = both.astype(bf16)
            return _


        service(s, "conv_before")

        def weight_conv():
            for k in range(3):
                taps = slice(3 * k * ib, 3 * (k + 1) * ib)
                value = dot(r.mixf[s], r.gs[:, taps], 0, 0).astype(bf16)
                r.gc[s, :, :, :, taps] = value.reshape(r.gc.shape[1:4] + (3 * ib,))
            service(s, "conv")

        def use_mixed(begin, count):
            def one(at, _):
                r.gm[at] = real(scatter_value(slot + 1, at))
                return _

            narrow(begin, count, one, 0)

        scatter_all(
            slot + 1,
            padded_spans,
            lambda k: lax.fori_loop(k * pairs // 2, (k + 1) * pairs // 2, conv_back, 0),
            lambda at, two: dot(r.gs[at], r.wc[s, two], 1, 1),
            use_mixed,
            weight_conv,
            lambda: service(s, "conv_use"),
        )

        def tap_sums(grad, v, index, reach):
            for b in (-1, 0, 1):
                padded = row_pad(col_shift(v, reach * b), reach)
                for a in (-1, 0, 1):
                    start = reach + reach * a
                    place = 9 * index + 3 * (a + 1) + b + 1
                    r.gk[place] = r.gk[place] + jnp.sum(grad * padded[start : start + SIDE], axis=0)

        def mix_back(f, before):
            at = frame_rows(f)
            following = frame_rows(jnp.minimum(f + 1, frames - 1))
            here = tiles(r.hid[s, at])
            step = keep_flag(f) * (tiles(r.hid[s, following]) - here)
            grad = tiles(r.gm[at])
            if s == 0:
                r.gd[at] = flat(dw_tiles(grad, taps_of(0), 1, -1))
                tap_sums(grad, step + before, 0, 1)
            else:
                gate = tiles(r.sig[at])
                grad = grad * here * gate * (1.0 - gate)
                r.gd[at] = flat(dw_tiles(grad, taps_of(1), 1, -1) + dw_tiles(grad, taps_of(2), 2, -1))
                tap_sums(grad, step, 1, 1)
                tap_sums(grad, step, 2, 2)
                r.gk[27] = r.gk[27] + jnp.sum(grad, axis=0)
            return step

        lax.fori_loop(0, frames, mix_back, jnp.zeros((SIDE, 8, ib), f32))

        service(s, "hide_before")

        def hide_back(f, sums):
            at = frame_rows(f)
            previous = frame_rows(jnp.maximum(f - 1, 0))
            keep = keep_flag(f)
            keep_before = jnp.where(f > 0, keep_flag(jnp.maximum(f - 1, 0)), 0.0)
            now = r.gd[at]
            earlier = r.gd[previous]
            grad = r.gm[at]
            if s == 0:
                following = frame_rows(jnp.minimum(f + 1, frames - 1))
                later = now + r.gd[following]
                earlier = earlier + now
            else:
                later = now
                grad = grad * (1.0 + r.sig[at])
            grad = grad + keep_before * earlier - keep * later
            centred, z = norm_inner(s, 0, spread(r.red.at[s], f))
            grad = real(tiles(grad) * gelu_both(z)[1])
            squeeze(r.g1, f, grad)
            return sums[0] + jnp.sum(grad, axis=0), sums[1] + jnp.sum(grad * centred, axis=0)

        sums = lax.fori_loop(0, frames, hide_back, (zero_n, zero_n))
        made = stat_start(r.stn, stat_base + 1, sums)
        service(s, "red")
        shift_sum, gain_sum = stat_end(r.stn, stat_base + 1, made)
        r.gbi[s, 0:1] = shift_sum
        r.ggi[s, 0:1] = gain_sum
        mean, inv = moments_in[s][0]
        scale = inv * row(r.gi, s, 0)
        shift_mean, gain_mean = shift_sum / pixel_total, gain_sum / pixel_total
        service(s, "red_after")
        keys = phase_keys(4)
        quarters = [pl.ds(*span) for span in raw_spans]

        def reduce_back(at, _):
            centred = (r.red[s, at] - mean) * inv
            grad = scale * (r.g1[at] - (shift_mean + centred * gain_mean))
            r.grf[s, at, cols(chan)] = grad.astype(bf16)
            return _

        for k in range(4):
            narrow(*raw_spans[k], reduce_back, 0)
            gather_start(r.grf.at[s], quarters[k], keys[k])
        if s == 0:
            own = r.grf[0, :, cols(chan)]
            for piece in range(n_chan):
                value = dot(r.x[:, piece * cs : (piece + 1) * cs], own, 0, 0).astype(bf16)
                r.gr[0, piece] = value.reshape(r.gr.shape[2:])
        service(s, "gather")
        gather_pass(r.grf.at[s], quarters[0], keys[0])
        gather_pass(r.grf.at[s], quarters[1], keys[1])
        if s == 0:
            shared_wr(0)
        else:
            top_sums["now"] = (zero_w, zero_w)
        for k in range(4):
            at = quarters[k]
            gather_end(r.grf.at[s], at, keys[k])
            r.gin[at] = dot(r.grf[s, at], r.wrf[s], 1, 1) + r.gpre[at]
            if k < 2:
                gather_pass(r.grf.at[s], quarters[k + 2], keys[k + 2])
            if s == 0:
                write_out(r.gin.at[at], r.gin_out.at[at])
            else:
                top_sums["now"] = broad(k, top_zero, top_sums["now"])
            if k == 1:
                service(s, "gather_use")
        service(s, "last")
        if s == 1:
            value = dot(r.out0[...], r.grf[1], 0, 0).astype(bf16)
            r.gro[...] = value.reshape(r.gro.shape)
            place = r.gr.at[1, chan]
            turned["gr", 1] = local(r.gro.at[:, :, cols(chan)], place)
            for j in others:
                remote(r.gro.at[:, :, cols(j)], place, (clip, j), ("gr", 1))

    turned = {}

    def reduce_task(kind, s, line, place):
        ref, from_side, from_z, result = kinds[kind]
        mine, done = ref.at[s, :, :, line, place], result.at[s, :, :, line, place]
        side_in, z_in = from_side.at[s, :, line, place], from_z.at[s, :, line, place]
        across = (2 * z + 1 - side, chan)
        key = (kind, s, line.start, place.start)
        if (kind, s) in turned:
            turned.pop((kind, s)).wait()
            three = pl.ds(0, (n_chan - 1) * cs)
            arrive(
                r.ge.at[s, :, :, :, three] if kind == "ge" else r.gr.at[s, pl.ds(0, n_chan - 1)],
                (kind, s),
            )
        remote(mine.at[:, 1 - side], side_in, across, key + (0,))
        yield
        arrive(side_in, key + (0,))
        for k in range(n_z):
            both = ref[s, k, side, line, place].astype(f32)
            both = both + from_side[s, k, line, place].astype(f32)
            ref[s, k, side, line, place] = both.astype(bf16)
        for k, there in enumerate(z_others):
            remote(mine.at[there, side], z_in.at[k], (2 * there + side, chan), key + (1,))
        yield
        arrive(z_in, key + (1,))
        total = ref[s, z, side, line, place].astype(f32)
        for k in range(n_z - 1):
            total = total + from_z[s, k, line, place].astype(f32)
        result[s, z, side, line, place] = total.astype(bf16)
        own = done.at[z, side]
        for there in z_others:
            remote(own, own, (2 * there + side, chan), key + (2,))
        yield
        arrive(done.at[pl.ds(0, n_z - 1), side], key + (2,))
        remote(done.at[:, side], done.at[:, side], across, key + (3,))
        yield
        arrive(done.at[:, 1 - side], key + (3,))
        if kind == "gc":
            base = place.start // ib
            for k in range((place.stop - place.start) // ib):
                here = r.fc.at[s, :, :, :, (base + k) * ib : (base + k + 1) * ib]
                write_out(here, r.gc_out.at[s, base + k])
        else:
            out = {"ge": r.ge_out, "gr": r.gr_out}[kind]
            write_out(done, out.at[s, :, :, line, place])
        yield

    kinds = {
        "gc": (r.gc, r.xc, r.zc, r.fc),
        "ge": (r.ge, r.xe, r.ze, r.fe),
        "gr": (r.gr, r.xr, r.zr, r.fr),
    }
    def cut(size, count):
        return [slice(k * (size // count), (k + 1) * (size // count)) for k in range(count)]

    tasks = {}
    for s in range(2):
        for k, place in enumerate(cut(9 * ib, PIECES["gc"])):
            tasks[f"c{k}", s] = reduce_task("gc", s, slice(0, r.gc.shape[3]), place)
        for k, place in enumerate(cut(r.ge.shape[4], PIECES["ge"])):
            tasks[f"e{k}", s] = reduce_task("ge", s, slice(0, r.ge.shape[3]), place)
        for k, line in enumerate(cut(r.gr.shape[3], PIECES["gr"])):
            tasks[f"r{k}", s] = reduce_task("gr", s, line, slice(0, ib))

    def advance(*steps):
        for step in steps:
            next(tasks[step])

    def service(s, point):
        advance(*PLAN.get((s, point), ()))

    backward(1, 4, 2, 1)
    backward(0, 6, 3, 3)

    for place in range(r.gk.shape[0]):
        r.kst[clip, place : place + 1, :] = jnp.sum(r.gk[place], axis=0, keepdims=True)
    for t in clip_others:
        remote(r.kst.at[clip], r.kst.at[clip], (t, chan), "taps")
    service(0, "end")
    arrive(r.kst.at[pl.ds(0, n_clip - 1)], "taps")
    total = r.kst[0]
    for k in range(1, n_clip):
        total = total + r.kst[k]
    for index in range(3):
        for tap in range(9):
            place = 9 * index + tap
            r.gk_out[tap, index : index + 1, :] = total[place : place + 1]
    r.ggb_out[...] = total[27:28]
    for copy in outgoing.values():
        copy.wait()
    for index in list(in_flight):
        sent(index)
    assert len(places) <= ARRIVALS and counters["load"] <= LOADS - 8, (places, counters)


def fused_call(n_clip, n_chan, pixel_total, *operands):
    rows, width = operands[0].shape
    cs = width // n_chan
    ib = LANES
    inner = ib * n_chan
    n_z = n_clip // 2
    padded = rows // PIXELS * FRAME
    over = rows + 8
    bf16, f32 = jnp.bfloat16, jnp.float32
    whole = pl.BlockSpec(memory_space=pltpu.VMEM)
    anywhere = pl.BlockSpec(memory_space=pl.ANY)
    scalars = pl.BlockSpec(memory_space=pltpu.SMEM)
    shape = jax.ShapeDtypeStruct
    V = pltpu.VMEM
    scratch = dict(
        x=V((rows, width), bf16),
        cot=V((rows, cs), bf16),
        wr0=V((width, ib), bf16),
        wrf=V((2, cs, inner), bf16),
        wef=V((2, inner, cs), bf16),
        wc=V((2, inner, 9 * ib), bf16),
        dkb=V((27, 8, ib), f32),
        red=V((2, over, ib), f32),
        hid=V((2, padded, ib), f32),
        sig=V((padded, ib), f32),
        conv=V((2, over, ib), f32),
        mixf=V((2, padded, inner), bf16),
        inf=V((2, rows, inner), bf16),
        ex=V((2, rows, cs), f32),
        out0=V((rows, cs), bf16),
        act=V((rows, cs), bf16),
        y=V((padded // 4, 9 * ib), f32),
        gpre=V((rows, cs), f32),
        gin=V((rows, cs), f32),
        gexp=V((rows, cs), bf16),
        gs=V((padded, 9 * ib), bf16),
        pb=V((padded, inner), bf16),
        ysend=V((2, padded, ib), bf16),
        rcore=V((5, 2, padded, ib), bf16),
        ryy=V((5, padded, ib), bf16),
        grf=V((2, rows, inner), bf16),
        gm=V((padded, ib), f32),
        gd=V((padded, ib), f32),
        g1=V((over, ib), f32),
        gk=V((32, 8, ib), f32),
        kst=V((n_clip, 32, ib), f32),
        stn=V((8, n_clip, 2, ib), f32),
        stw=V((4, n_clip, 2, cs), f32),
        gc=V((2, n_z, 2, inner // n_clip, 9 * ib), bf16),
        geo=V((2, n_chan, n_z, 2, ib // n_clip, cs), bf16),
        ge=V((2, n_z, 2, ib // n_clip, width), bf16),
        gro=V((2, cs // 2, inner), bf16),
        gr=V((2, n_z, 2, width // n_clip, ib), bf16),
        fc=V((2, n_z, 2, inner // n_clip, 9 * ib), bf16),
        fe=V((2, n_z, 2, ib // n_clip, width), bf16),
        fr=V((2, n_z, 2, width // n_clip, ib), bf16),
        xc=V((2, n_z, inner // n_clip, 9 * ib), bf16),
        xe=V((2, n_z, ib // n_clip, width), bf16),
        xr=V((2, n_z, width // n_clip, ib), bf16),
        zc=V((2, n_z - 1, inner // n_clip, 9 * ib), bf16),
        ze=V((2, n_z - 1, ib // n_clip, width), bf16),
        zr=V((2, n_z - 1, width // n_clip, ib), bf16),
        ssem=pltpu.SemaphoreType.DMA((SENDS,)),
        rsem=pltpu.SemaphoreType.DMA((ARRIVALS,)),
        lsem=pltpu.SemaphoreType.DMA((LOADS,)),
    )
    first = NAMES.index("x")
    return pl.pallas_call(
        partial(fused_kernel, n_clip, n_chan, pixel_total),
        out_shape=[
            shape((rows, cs), bf16),
            shape((rows, cs), f32),
            shape((2, 2, ib), f32),
            shape((2, 2, ib), f32),
            shape((2, cs), f32),
            shape((2, cs), f32),
            shape((9, 3, ib), f32),
            shape((1, ib), f32),
            shape((2, 9, n_z, 2, inner // n_clip, ib), bf16),
            shape((2, n_z, 2, ib // n_clip, width), bf16),
            shape((2, n_z, 2, width // n_clip, ib), bf16),
        ],
        in_specs=[anywhere] * 5 + [scalars] + [whole] * 6,
        out_specs=[anywhere] * 2 + [whole] * 6 + [anywhere] * 3,
        scratch_shapes=[scratch[name] for name in NAMES[first:]],
        compiler_params=pltpu.CompilerParams(
            collective_id=0, has_side_effects=True, vmem_limit_bytes=62 * 1024 * 1024
        ),
    )(*operands)


def finish_kernel(*refs):
    count = len(refs) // 2
    sources, results = refs[:count], refs[count:]
    for here, there in zip(sources[:5], results[:5]):
        there[...] = here[...].astype(there.dtype)

    @pl.when(pl.program_id(0) == 0)
    def _():
        for here, there in zip(sources[5:], results[5:]):
            there[...] = here[...]


def finish(steps, gc, ge, gr, act, gin, *small):
    arrays = [a.reshape(-1, a.shape[-1]) for a in (gc, ge, gr)] + [act, gin]
    blocks = [
        pl.BlockSpec((-(-a.shape[0] // (16 * steps)) * 16, a.shape[1]), lambda i: (i, 0))
        for a in arrays
    ]
    whole = [pl.BlockSpec(memory_space=pltpu.VMEM)] * len(small)
    shapes = [jax.ShapeDtypeStruct(a.shape, jnp.float32) for a in arrays[:3]]
    shapes += [jax.ShapeDtypeStruct(a.shape, a.dtype) for a in (act, gin, *small)]
    return pl.pallas_call(
        finish_kernel,
        grid=(steps,),
        out_shape=shapes,
        in_specs=blocks + whole,
        out_specs=blocks + whole,
        compiler_params=pltpu.CompilerParams(vmem_limit_bytes=62 * 1024 * 1024),
    )(*arrays, *small)


def fused(
    frames_in,
    boundary,
    w_reduce,
    gain_inner,
    bias_inner,
    w_conv,
    w_expand,
    gain_outer,
    bias_outer,
    depth_kernels,
    gate_bias,
    cotangent,
):
    n_clip, n_chan = lax.axis_size("clip"), lax.axis_size("chan")
    pixel_total = frames_in.shape[0] * n_clip
    act, gin, ggi, gbi, ggo, gbo, gk, ggb, gc, ge, gr = fused_call(
        n_clip,
        n_chan,
        float(pixel_total),
        frames_in,
        cotangent,
        w_reduce,
        w_conv,
        w_expand,
        boundary,
        gain_inner,
        bias_inner,
        gain_outer,
        bias_outer,
        depth_kernels.transpose(1, 0, 2),
        gate_bias.reshape(1, -1),
    )
    gc, ge, gr, act, gin, ggi, gbi, ggo, gbo, gk, ggb = finish(
        2, gc, ge, gr, act, gin, ggi, gbi, ggo, gbo, gk, ggb
    )
    return (
        act,
        gin,
        gr.reshape(w_reduce.shape),
        ggi,
        gbi,
        gc.reshape(w_conv.shape),
        ge.reshape(w_expand.shape),
        ggo,
        gbo,
        gk.transpose(1, 0, 2),
        ggb.reshape(-1),
    )


def solution(mesh):
    in_specs = (
        P("clip", None),
        P("clip", None),
        P(None, None, "chan"),
        P(None, None, "chan"),
        P(None, None, "chan"),
        P(None, None, None, "chan"),
        P(None, "chan", None),
        P(),
        P(),
        P(None, None, "chan"),
        P("chan"),
        P("clip", None),
    )
    out_specs = (
        P("clip", "chan"),
        P("clip", "chan"),
        P(None, None, "chan"),
        P(None, None, "chan"),
        P(None, None, "chan"),
        P(None, None, None, "chan"),
        P(None, "chan", None),
        P(None, "chan"),
        P(None, "chan"),
        P(None, None, "chan"),
        P("chan"),
    )

    def run(*arguments):
        fits = fused_fits(mesh, arguments[0].shape, arguments[2].shape)
        return jax.shard_map(fused if fits else body, mesh=mesh, in_specs=in_specs, out_specs=out_specs, check_vma=False)(*arguments)

    return run
```

```python
from functools import partial
from types import SimpleNamespace
from typing import Any, NamedTuple

import jax
import jax.numpy as jnp
from jax import lax
from jax.experimental import pallas as pl
from jax.experimental.pallas import tpu as pltpu
from jax.sharding import PartitionSpec as P

SEG = 8
SIDE = 7


epsilon = 1e-05


def framed(values):
    return values.reshape(-1, SIDE, SIDE, values.shape[-1])


def shifted(frame_grid, row_step, col_step, dilation):
    padded = jnp.pad(frame_grid, ((0, 0), (dilation, dilation), (dilation, dilation), (0, 0)))
    return padded[
        :,
        dilation + row_step : dilation + row_step + SIDE,
        dilation + col_step : dilation + col_step + SIDE,
        :,
    ]


def depthwise(values, kernel, dilation):
    frame_grid = framed(values)
    running = jnp.zeros_like(frame_grid)
    for tap_index in range(9):
        running = (
            running
            + shifted(
                frame_grid,
                (tap_index // 3 - 1) * dilation,
                (tap_index % 3 - 1) * dilation,
                dilation,
            )
            * kernel[tap_index]
        )
    return running.reshape(values.shape)


def patch_rows(values):
    frame_grid = framed(values)
    pieces = [
        shifted(frame_grid, tap_index // 3 - 1, tap_index % 3 - 1, 1) for tap_index in range(9)
    ]
    return jnp.concatenate(pieces, axis=-1).reshape(values.shape[0], 9 * values.shape[1])


def unpatch(grad_rows, chan_width):
    frame_grid = grad_rows.reshape(-1, SIDE, SIDE, 9, chan_width)
    running = jnp.zeros(frame_grid.shape[:3] + (chan_width,), jnp.float32)
    for tap_index in range(9):
        running = running + shifted(
            frame_grid[:, :, :, tap_index, :], 1 - tap_index // 3, 1 - tap_index % 3, 1
        )
    return running.reshape(-1, chan_width)


def neighbours(values, boundary):
    clip_count = boundary.shape[0]
    frame_grid = values.reshape(clip_count, SEG, SIDE * SIDE, values.shape[-1])
    stop_mask = (boundary == 1)[:, :, None, None]
    start_mask = jnp.concatenate([jnp.ones_like(stop_mask[:, :1]), stop_mask[:, :-1]], axis=1)
    after_seg = jnp.concatenate([frame_grid[:, 1:], frame_grid[:, -1:]], axis=1)
    before = jnp.concatenate([frame_grid[:, :1], frame_grid[:, :-1]], axis=1)
    later_seg = jnp.where(stop_mask, frame_grid, after_seg)
    earlier = jnp.where(start_mask, frame_grid, before)
    return (later_seg.reshape(values.shape), earlier.reshape(values.shape))


def temporal(values, kernels, gate_vec, boundary, short_range):
    later_seg, earlier = neighbours(values, boundary)
    if short_range:
        return values + depthwise(later_seg - earlier, kernels[0], 1)
    change = later_seg - values
    logits = depthwise(change, kernels[1], 1) + depthwise(change, kernels[2], 2) + gate_vec
    return values + values * jax.nn.sigmoid(logits)


def columns(values, col_start, col_share):
    return lax.dynamic_slice_in_dim(values, col_start, col_share, values.ndim - 1)


def contract(left, right, left_dim, right_dim):
    return lax.dot_general(
        left, right, (((left_dim,), (right_dim,)), ((), ())), preferred_element_type=jnp.float32
    )


def normalize(values, gain_vec, bias_vec, pixel_total):
    col_sum, sq_sum = lax.psum((jnp.sum(values, axis=0), jnp.sum(values * values, axis=0)), "clip")
    mean_val = col_sum / pixel_total
    inv_std = lax.rsqrt(sq_sum / pixel_total - mean_val * mean_val + epsilon)
    centred = (values - mean_val) * inv_std
    return (centred * gain_vec + bias_vec, centred, inv_std)


def normalize_back(grad_rows, centred, inv_std, gain_vec, pixel_total):
    shift_sum, gain_sum = lax.psum(
        (jnp.sum(grad_rows, axis=0), jnp.sum(grad_rows * centred, axis=0)), "clip"
    )
    grad_in = inv_std * gain_vec * (grad_rows - (shift_sum + centred * gain_sum) / pixel_total)
    return (grad_in, gain_sum, shift_sum)


def block_forward(inputs, boundary, weights, short_range, pixel_total):
    w_red, gain_pair, bias_pair, w_cv, w_ex, gain_out, bias_out, kernels, gate_vec = weights
    reduced = jnp.dot(inputs, w_red, preferred_element_type=jnp.float32)
    norm_one, centred_one, inv_one = normalize(reduced, gain_pair[0], bias_pair[0], pixel_total)
    hidden, gelu_one = jax.vjp(jax.nn.gelu, norm_one)
    mixed_act, mix_back = jax.vjp(
        partial(temporal, boundary=boundary, short_range=short_range), hidden, kernels, gate_vec
    )
    gathered = lax.all_gather(mixed_act.astype(jnp.bfloat16), "chan", axis=1, tiled=True)
    patches = patch_rows(gathered)
    conv_out = jnp.dot(
        patches, w_cv.reshape(-1, w_cv.shape[-1]), preferred_element_type=jnp.float32
    )
    norm_two, centred_two, inv_two = normalize(conv_out, gain_pair[1], bias_pair[1], pixel_total)
    inner_full, gelu_two = jax.vjp(jax.nn.gelu, norm_two)
    inner_act = inner_full.astype(jnp.bfloat16)
    partial_out = jnp.dot(inner_act, w_ex, preferred_element_type=jnp.float32)
    expanded = lax.psum(partial_out.astype(jnp.bfloat16), "chan").astype(jnp.float32)
    norm_three, centred_three, inv_three = normalize(expanded, gain_out, bias_out, pixel_total)
    output_full, gelu_three = jax.vjp(jax.nn.gelu, norm_three + inputs.astype(jnp.float32))
    kept_state = (
        centred_one,
        inv_one,
        gelu_one,
        mix_back,
        patches,
        centred_two,
        inv_two,
        gelu_two,
        inner_act,
        centred_three,
        inv_three,
        gelu_three,
        gain_out,
    )
    return (output_full.astype(jnp.bfloat16), kept_state)


def block_backward(grad_out, inputs, weights, kept_state, pixel_total):
    w_red, gain_pair, bias_pair, w_cv, w_ex, gain_out, bias_out, kernels, gate_vec = weights
    (
        centred_one,
        inv_one,
        gelu_one,
        mix_back,
        patches,
        centred_two,
        inv_two,
        gelu_two,
        inner_act,
        centred_three,
        inv_three,
        gelu_three,
        gain_use,
    ) = kept_state
    grad_pre = gelu_three(grad_out)[0]
    grad_exp, gain_three, bias_three = normalize_back(
        grad_pre, centred_three, inv_three, gain_use, pixel_total
    )
    low_exp = grad_exp.astype(jnp.bfloat16)
    grad_wex = contract(inner_act, low_exp, 0, 0)
    grad_inner = contract(low_exp, w_ex, 1, 1)
    grad_two = gelu_two(grad_inner)[0]
    grad_cv, gain_two, bias_two = normalize_back(
        grad_two, centred_two, inv_two, gain_pair[1], pixel_total
    )
    low_cv = grad_cv.astype(jnp.bfloat16)
    flat_cv = w_cv.reshape(-1, w_cv.shape[-1])
    grad_wcv = contract(patches, low_cv, 0, 0).reshape(w_cv.shape)
    grad_patch = contract(low_cv, flat_cv, 1, 1)
    grad_mixed = lax.psum_scatter(
        unpatch(grad_patch, w_cv.shape[1]).astype(jnp.bfloat16),
        "chan",
        scatter_dimension=1,
        tiled=True,
    ).astype(jnp.float32)
    grad_hidden, grad_kern, grad_gate = mix_back(grad_mixed)
    grad_one = gelu_one(grad_hidden)[0]
    grad_red, gain_one, bias_one = normalize_back(
        grad_one, centred_one, inv_one, gain_pair[0], pixel_total
    )
    low_red = grad_red.astype(jnp.bfloat16)
    grad_wred = contract(inputs, low_red, 0, 0)
    partial_in = contract(low_red, w_red, 1, 1)
    grad_in = grad_pre + lax.psum(partial_in.astype(jnp.bfloat16), "chan").astype(jnp.float32)
    weight_terms = (grad_wred, grad_wcv, grad_wex, grad_kern, grad_gate)
    norm_terms = (gain_one, bias_one, gain_two, bias_two, gain_three, bias_three)
    return (grad_in, weight_terms, norm_terms)


def body(
    frames_in,
    boundary,
    w_reduce,
    gain_inner,
    bias_inner,
    w_conv,
    w_expand,
    gain_outer,
    bias_outer,
    depth_kernels,
    gate_bias,
    cotangent,
):
    row_count = frames_in.shape[0]
    pixel_total = row_count * lax.axis_size("clip")
    col_share = frames_in.shape[1] // lax.axis_size("chan")
    col_start = lax.axis_index("chan") * col_share
    block_weights = [
        (
            w_reduce[block_index],
            gain_inner[block_index],
            bias_inner[block_index],
            w_conv[block_index],
            w_expand[block_index],
            gain_outer[block_index],
            bias_outer[block_index],
            depth_kernels,
            gate_bias,
        )
        for block_index in range(2)
    ]
    first_out, kept_zero = block_forward(frames_in, boundary, block_weights[0], True, pixel_total)
    final_out, kept_one = block_forward(first_out, boundary, block_weights[1], False, pixel_total)
    layer_inputs = [frames_in, first_out]
    kept_states = [kept_zero, kept_one]
    grad_flow = cotangent.astype(jnp.float32)
    weight_sums = [None, None]
    norm_sums = [None, None]
    for block_index in (1, 0):
        grad_flow, weight_terms, norm_terms = block_backward(
            grad_flow,
            layer_inputs[block_index],
            block_weights[block_index],
            kept_states[block_index],
            pixel_total,
        )
        grad_wred, grad_wcv, grad_wex, grad_kern, grad_gate = weight_terms
        weight_terms = (
            lax.psum(grad_wred.astype(jnp.bfloat16), "clip").astype(jnp.float32),
            lax.psum(grad_wcv.astype(jnp.bfloat16), "clip").astype(jnp.float32),
            lax.psum(grad_wex.astype(jnp.bfloat16), "clip").astype(jnp.float32),
            lax.psum(grad_kern.astype(jnp.bfloat16), "clip").astype(jnp.float32),
            lax.psum(grad_gate.astype(jnp.bfloat16), "clip").astype(jnp.float32),
        )
        weight_sums[block_index] = weight_terms
        norm_sums[block_index] = norm_terms
    grad_reduce = jnp.stack([weight_sums[0][0], weight_sums[1][0]])
    grad_conv = jnp.stack([weight_sums[0][1], weight_sums[1][1]])
    grad_expand = jnp.stack([weight_sums[0][2], weight_sums[1][2]])
    grad_kernels = weight_sums[0][3] + weight_sums[1][3]
    grad_gate_bias = weight_sums[0][4] + weight_sums[1][4]
    grad_gain_inner = jnp.stack(
        [
            jnp.stack([norm_sums[0][0], norm_sums[0][2]]),
            jnp.stack([norm_sums[1][0], norm_sums[1][2]]),
        ]
    )
    grad_bias_inner = jnp.stack(
        [
            jnp.stack([norm_sums[0][1], norm_sums[0][3]]),
            jnp.stack([norm_sums[1][1], norm_sums[1][3]]),
        ]
    )
    grad_gain_outer = jnp.stack([norm_sums[0][4], norm_sums[1][4]])
    grad_bias_outer = jnp.stack([norm_sums[0][5], norm_sums[1][5]])
    activations = columns(final_out, col_start, col_share)
    input_grad = columns(grad_flow, col_start, col_share)
    grad_gain_outer = columns(grad_gain_outer, col_start, col_share)
    grad_bias_outer = columns(grad_bias_outer, col_start, col_share)
    return (
        activations,
        input_grad,
        grad_reduce,
        grad_gain_inner,
        grad_bias_inner,
        grad_conv,
        grad_expand,
        grad_gain_outer,
        grad_bias_outer,
        grad_kernels,
        grad_gate_bias,
    )


MESH = pl.DeviceIdType.MESH
LANES = 128
FRAME = SIDE * 8
PIXELS = SIDE * SIDE
PAIR = 2 * FRAME
GELU_A = 0.7978845608028654
GELU_B = 0.044715
SENDS = 64
LOADS = 32


def fused_fits(mesh, frame_shape, reduce_shape):
    n_clip, n_chan = mesh.shape["clip"], mesh.shape["chan"]
    share = reduce_shape[2] // n_chan
    frames = frame_shape[0] // (n_clip * SIDE * SIDE)
    return n_chan == 4 and n_clip == 8 and share == LANES and frames == 2 * SEG


def gelu(z):
    return 0.5 * z * (1.0 + jnp.tanh(GELU_A * (z + GELU_B * z * z * z)))


def gelu_both(z):
    square = z * z
    t = jnp.tanh(GELU_A * (z + GELU_B * square * z))
    slope = 0.5 * (1.0 + t) + 0.5 * z * (1.0 - t * t) * (GELU_A * (1.0 + 3.0 * GELU_B * square))
    return 0.5 * z * (1.0 + t), slope


def real_columns(shape):
    return lax.rem(lax.broadcasted_iota(jnp.int32, shape, len(shape) - 2), 8) < SIDE


def real(values):
    return jnp.where(real_columns(values.shape), values, 0.0)


def fold(values):
    return jnp.sum(values.reshape(-1, 8, values.shape[-1]), axis=0)


def tiles(values):
    return values.reshape(SIDE, 8, values.shape[-1])


def flat(values):
    return values.reshape(FRAME, values.shape[-1])


def row_pad(v, reach):
    zeros = jnp.zeros((reach,) + v.shape[1:], v.dtype)
    return jnp.concatenate([zeros, v, zeros], axis=0)


def col_shift(v, step):
    if step == 0:
        return v
    moved = pltpu.roll(v, (-step) % 8, v.ndim - 2)
    if abs(step) == 2:
        place = lax.broadcasted_iota(jnp.int32, v.shape, v.ndim - 2)
        moved = jnp.where(place < 6 if step > 0 else place >= 2, moved, 0.0)
    return moved


def dw_tiles(v, taps, reach, sign):
    padded = row_pad(v, reach)
    total = None
    for b in (-1, 0, 1):
        part = None
        for a in (-1, 0, 1):
            start = reach + sign * reach * a
            term = taps[3 * (a + 1) + b + 1] * padded[start : start + SIDE]
            part = term if part is None else part + term
        part = col_shift(part, sign * reach * b)
        total = part if total is None else total + part
    return total


def dot(left, right, left_dim=1, right_dim=0):
    return lax.dot_general(
        left, right, (((left_dim,), (right_dim,)), ((), ())), preferred_element_type=jnp.float32
    )


class Refs(NamedTuple):
    x_hbm: Any
    cot_hbm: Any
    wred_hbm: Any
    wconv_hbm: Any
    wexp_hbm: Any
    bnd: Any
    gi: Any
    bi: Any
    go: Any
    bo: Any
    dk: Any
    gb: Any
    act_out: Any
    gin_out: Any
    ggi: Any
    gbi: Any
    ggo: Any
    gbo: Any
    gk_out: Any
    ggb_out: Any
    gc_out: Any
    ge_out: Any
    gr_out: Any
    x: Any
    cot: Any
    wr0: Any
    wrf: Any
    wef: Any
    wc: Any
    dkb: Any
    red: Any
    hid: Any
    sig: Any
    conv: Any
    mixf: Any
    inf: Any
    ex: Any
    out0: Any
    act: Any
    y: Any
    gpre: Any
    gin: Any
    gexp: Any
    gs: Any
    pb: Any
    ysend: Any
    rcore: Any
    ryy: Any
    grf: Any
    gm: Any
    gd: Any
    g1: Any
    gk: Any
    kst: Any
    stn: Any
    stw: Any
    gc: Any
    geo: Any
    ge: Any
    gro: Any
    gr: Any
    xc: Any
    xe: Any
    xr: Any
    zc: Any
    ze: Any
    zr: Any
    fc: Any
    fe: Any
    fr: Any
    ssem: Any
    rsem: Any
    lsem: Any


PIECES = (3, 2, 2)
ARRIVALS = 40 + 12 * sum(PIECES)
TURN, EXPAND, REDUCE, SUMS, CHAN, TAPS = range(-6, 0)
PLAN = {
    (1, 5): (
        110, 111,
    ),
    (1, 6): (
        101, 102,
    ),
    (1, 7): (
        110,
    ),
    (1, 8): (
        110, 111,
    ),
    (1, 9): (
        101, 100,
    ),
    (1, 10): (
        110, 111, 102,
    ),
    (1, 11): (
        101,
    ),
    (1, 12): (
        110, 100,
    ),
    (1, 13): (
        111,
    ),
    (0, 0): (
        101, 110, 102, 100, 111,
    ),
    (0, 1): (
        120, 121,
    ),
    (0, 2): (
        101, 110, 111, 102,
    ),
    (0, 3): (
        120,
    ),
    (0, 4): (
        101, 120, 111, 102, 100, 121,
    ),
    (0, 5): (
        11, 10,
    ),
    (0, 6): (
        101, 120, 0, 2, 11, 1, 100, 121,
    ),
    (0, 8): (
        120, 0, 11, 10,
    ),
    (0, 9): (
        120, 0, 2, 102, 121,
    ),
    (0, 10): (
        11, 1, 100, 10,
    ),
    (0, 11): (
        120, 0, 2, 21, 20,
    ),
    (0, 12): (
        121,
    ),
    (0, 13): (
        11, 1, 102, 10, 0, 100,
    ),
    (0, 14): (
        121, 11, 2, 21, 1, 0, 20, 10, 21, 2, 121, 20, 11, 1, 10, 21, 2, 0, 20, 1, 10, 21, 20, 2,
        21, 20, 1, 21, 20,
    ),
}


def fused_kernel(n_clip, n_chan, pixel_total, *refs):
    r = Refs(*refs)
    rows, cs = r.cot.shape
    ib = LANES
    frames = rows // PIXELS
    chunk = frames // 2 * FRAME
    n_z = n_clip // 2
    first = -(-rows // 32) * 16
    starts, counts = (0, first), (first, rows - first)
    bf16, f32 = jnp.bfloat16, jnp.float32
    clip = lax.axis_index("clip")
    chan = lax.axis_index("chan")
    core, high = lax.rem(chan, 2), lax.div(chan, 2)
    j_core = (1 - core) + 2 * high
    j_y = core + 2 * (1 - high)
    j_far = (1 - core) + 2 * (1 - high)
    others = (j_core, j_y, j_far)
    z, side = lax.div(clip, 2), lax.rem(clip, 2)
    low, z_near, z_far = lax.rem(z, 2), z + 1 - 2 * lax.rem(z, 2), lax.rem(z + 2, 4)
    clip_others = [lax.rem(clip + d, n_clip) for d in range(1, n_clip)]

    def cols(j):
        return pl.ds(pl.multiple_of(j * ib, ib), ib)

    def wide(j):
        return pl.ds(pl.multiple_of(j * cs, cs), cs)

    def part(h):
        return pl.ds(h * chunk, chunk)

    def raw(h):
        return pl.ds(starts[h], counts[h])

    def spans(total):
        tiles_left, at, chunks = total // 16, 0, []
        for left in range(4, 0, -1):
            take = -(-tiles_left // left)
            chunks.append((at * 16, take * 16))
            at, tiles_left = at + take, tiles_left - take
        return chunks

    raw_spans, padded_spans = spans(rows), spans(frames * FRAME)

    places, in_flight = {}, {}
    counters = SimpleNamespace(send=0, load=0, phase=0, sums=0, out=0)

    def arrival(key):
        return r.rsem.at[places.setdefault(key, len(places))]

    def sent(index):
        if index in in_flight:
            in_flight.pop(index).wait_send()

    def remote(src, dst, target, key):
        index = counters.send % SENDS
        counters.send += 1
        sent(index)
        made = pltpu.make_async_remote_copy(
            src_ref=src,
            dst_ref=dst,
            send_sem=r.ssem.at[index],
            recv_sem=arrival(key),
            device_id=target,
            device_id_type=MESH,
        )
        made.start()
        in_flight[index] = made
        return made, index

    def arrive(place, key):
        pltpu.make_async_remote_copy(
            src_ref=place,
            dst_ref=place,
            send_sem=r.ssem.at[0],
            recv_sem=arrival(key),
            device_id=(clip, j_core),
            device_id_type=MESH,
        ).wait_recv()

    def local(src, dst, index=None):
        if index is None:
            index = counters.load
            counters.load += 1
        made = pltpu.make_async_copy(src, dst, r.lsem.at[index])
        made.start()
        return made

    outgoing = {}

    def write_out(src, dst):
        turn = counters.out % 8
        counters.out += 1
        if turn in outgoing:
            outgoing.pop(turn).wait()
        outgoing[turn] = local(src, dst, LOADS - 8 + turn)

    load_wr0 = local(r.wred_hbm.at[0], r.wr0)
    load_x = [local(r.x_hbm.at[raw(h)], r.x.at[raw(h)]) for h in range(2)]
    load_we = [
        local(r.wexp_hbm.at[s, :, wide(chan)], r.wef.at[s, cols(chan)]) for s in range(2)
    ]
    load_wr = [
        local(r.wred_hbm.at[s, wide(chan)], r.wrf.at[s, :, cols(chan)]) for s in range(2)
    ]
    load_wc = []
    for s in range(2):
        index = counters.load
        counters.load += 1
        for tap in range(9):
            local(r.wconv_hbm.at[s, tap], r.wc.at[s, :, tap * ib : (tap + 1) * ib], index)
        load_wc.append(pltpu.make_async_copy(r.wc.at[s], r.wc.at[s], r.lsem.at[index]))
    load_cot = local(r.cot_hbm.at[:, wide(chan)], r.cot)

    barrier = pltpu.get_barrier_semaphore()
    for target in clip_others:
        pl.semaphore_signal(barrier, inc=1, device_id=(target, chan), device_id_type=MESH)
    for target in others:
        pl.semaphore_signal(barrier, inc=1, device_id=(clip, target), device_id_type=MESH)

    def share_we(s, half):
        size = ib // 2
        for j in others:
            here = r.wexp_hbm.at[s, pl.ds(half * size, size), wide(j)]
            target = r.wef.at[s, pl.ds(pl.multiple_of(chan * ib + half * size, size), size)]
            remote(here, target, (clip, j), (EXPAND, s))

    def share_wr(s, half):
        size = cs // 2
        for j in others:
            here = r.wred_hbm.at[s, pl.ds(pl.multiple_of(j * cs + half * size, size), size)]
            target = r.wrf.at[s, pl.ds(half * size, size), cols(chan)]
            remote(here, target, (clip, j), (REDUCE, s))

    def shared_we(s):
        load_we[s].wait()
        arrive(r.wef.at[s, pl.ds(0, (n_chan - 1) * ib)], (EXPAND, s))

    def shared_wr(s):
        load_wr[s].wait()
        arrive(r.wrf.at[s, :, pl.ds(0, (n_chan - 1) * ib)], (REDUCE, s))

    def stat_start(buf, slot, values):
        for k, value in enumerate(values):
            buf[slot, clip, k : k + 1, :] = jnp.sum(value, axis=0, keepdims=True)
        key = (SUMS, counters.sums % 2)
        counters.sums += 1
        for t in clip_others:
            remote(buf.at[slot, clip], buf.at[slot, clip], (t, chan), key)
        return key

    def stat_end(buf, slot, key):
        arrive(buf.at[slot, pl.ds(0, n_clip - 1)], key)
        total = buf[slot, 0]
        for k in range(1, n_clip):
            total = total + buf[slot, k]
        return total[0:1], total[1:2]

    def moments(pair):
        mean = pair[0] / pixel_total
        return mean, lax.rsqrt(pair[1] / pixel_total - mean * mean + epsilon)

    def phase_keys(count):
        turn = counters.phase % 2
        counters.phase += 1
        return [[(CHAN, turn, k, i) for i in range(3)] for k in range(count)]

    def gather_start(full, at, key):
        mine = full.at[at, cols(chan)]
        remote(mine, mine, (clip, j_y), key[0])
        remote(mine, mine, (clip, j_core), key[1])

    def gather_pass(full, at, key):
        theirs = full.at[at, cols(j_y)]
        arrive(theirs, key[0])
        remote(theirs, theirs, (clip, j_core), key[2])

    def gather_end(full, at, key):
        arrive(full.at[at, cols(j_core)], key[1])
        arrive(full.at[at, cols(j_far)], key[2])

    def pair(value):
        return pl.ds(pl.multiple_of(value * 2 * ib, 2 * ib), 2 * ib)

    def scatter_value(slot, at):
        mine = r.pb[at, cols(chan)].astype(f32)
        return mine + r.rcore[slot, 0, at].astype(f32) + r.ryy[slot, at].astype(f32)

    def keep_flag(f):
        return 1.0 - r.bnd[lax.div(f, SEG), lax.rem(f, SEG)].astype(f32)

    def taps_of(index):
        return [r.dkb[9 * index + tap] for tap in range(9)]

    def pair_rows(h, i):
        return pl.ds(pl.multiple_of(h * chunk + i * PAIR, 16), PAIR)

    def frame_rows(f):
        return pl.ds(pl.multiple_of(f * FRAME, 8), FRAME)

    def spread(ref, f):
        return jnp.stack(
            [ref[pl.ds(f * PIXELS + SIDE * k, 8), :] for k in range(SIDE)], axis=0
        )

    def squeeze(ref, f, value):
        for k in range(SIDE):
            ref[pl.ds(f * PIXELS + SIDE * k, 8), :] = value[k]

    pairs = frames // 4
    carried = {}
    zero_n = jnp.zeros((8, ib), f32)
    zero_w = jnp.zeros((8, cs), f32)

    def each(start, count, step, one, begin):
        def at_step(i, carry):
            return one(pl.ds(pl.multiple_of(start + i * step, 16), step), carry)

        return lax.fori_loop(0, count // step, at_step, begin)

    def narrow(start, count, one, begin):
        step = next(n for n in (112, 96, 80, 64, 48, 32, 16) if count % n == 0)
        return each(start, count, step, one, begin)

    def broad(k, one, begin):
        return each(*raw_spans[k], 16, one, begin)

    moments_in = [[None, None, None], [None, None, None]]

    def row(ref, s, k=None):
        return ref[s, k : k + 1, :] if k is not None else ref[s : s + 1, wide(chan)]

    def norm_inner(s, k, x):
        mean, inv = moments_in[s][k]
        centred = (x - mean) * inv
        return centred, centred * row(r.gi, s, k) + row(r.bi, s, k)

    def norm_outer(s, x):
        mean, inv = moments_in[s][2]
        centred = (x - mean) * inv
        return centred, centred * row(r.go, s) + row(r.bo, s)

    def inner_input(s, at):
        return r.x[at, wide(chan)] if s == 0 else r.out0[at]

    def temporal_forward(s, k):
        h, first_pair = k // 2, k % 2 * (pairs // 2)

        def hide(i, _):
            f = h * (frames // 2) + i
            value = real(gelu(norm_inner(s, 0, spread(r.red.at[s], f))[1]))
            r.hid[s, frame_rows(f)] = flat(value)
            return _

        if first_pair == 0:
            lax.fori_loop(0, frames // 2, hide, 0)

        def mix(i, before):
            base = pl.multiple_of(h * chunk + i * PAIR, 16)
            last = jnp.minimum(base + PAIR, (h + 1) * chunk - FRAME)
            f = h * (frames // 2) + 2 * i
            h0 = tiles(r.hid[s, pl.ds(base, FRAME)])
            h1 = tiles(r.hid[s, pl.ds(base + FRAME, FRAME)])
            h2 = tiles(r.hid[s, pl.ds(pl.multiple_of(last, 8), FRAME)])
            e0 = keep_flag(f) * (h1 - h0)
            e1 = keep_flag(f + 1) * (h2 - h1)
            if s == 0:
                taps = taps_of(0)
                m0 = real(h0 + dw_tiles(e0 + before, taps, 1, 1))
                m1 = real(h1 + dw_tiles(e1 + e0, taps, 1, 1))
            else:
                near, far = taps_of(1), taps_of(2)
                mixed = []
                for k, (hk, ek) in enumerate(((h0, e0), (h1, e1))):
                    logits = dw_tiles(ek, near, 1, 1) + dw_tiles(ek, far, 2, 1) + r.gb[...]
                    gate = 0.5 * (1.0 + jnp.tanh(0.5 * logits))
                    r.sig[pl.ds(base + k * FRAME, FRAME)] = flat(gate)
                    mixed.append(hk + hk * gate)
                m0, m1 = mixed
            both = jnp.concatenate([flat(m0), flat(m1)], axis=0).astype(bf16)
            r.mixf[s, pl.ds(base, PAIR), cols(chan)] = both
            return e1

        before = carried.get(s) if first_pair else jnp.zeros((SIDE, 8, ib), f32)
        carried[s] = lax.fori_loop(first_pair, first_pair + pairs // 2, mix, before)

    def conv_forward(s, k, sums):
        r.y[...] = dot(r.mixf[s, pl.ds(*padded_spans[k])], r.wc[s])

        def add_taps(i, sums):
            at = pl.ds(pl.multiple_of(i * FRAME, 8), FRAME)
            total = None
            for b in (-1, 0, 1):
                run = None
                for a in (-1, 0, 1):
                    tap = 3 * (a + 1) + b + 1
                    term = row_pad(tiles(r.y[at, tap * ib : (tap + 1) * ib]), 1)
                    term = term[1 + a : 1 + a + SIDE]
                    run = term if run is None else run + term
                run = col_shift(run, b)
                total = run if total is None else total + run
            total = real(total)
            squeeze(r.conv.at[s], k * (frames // 4) + i, total)
            return sums[0] + jnp.sum(total, axis=0), sums[1] + jnp.sum(total * total, axis=0)

        return lax.fori_loop(0, frames // 4, add_taps, sums)

    def forward(s, stat_base, wide_slot):
        keys = phase_keys(4)
        quarters = [pl.ds(*span) for span in padded_spans]
        for k in range(4):
            temporal_forward(s, k)
            gather_start(r.mixf.at[s], quarters[k], keys[k])
            if k > 0:
                gather_pass(r.mixf.at[s], quarters[k - 1], keys[k - 1])
        sums = (zero_n, zero_n)
        load_wc[s].wait()
        for k in range(4):
            gather_end(r.mixf.at[s], quarters[k], keys[k])
            if k == 0:
                gather_pass(r.mixf.at[s], quarters[3], keys[3])
            sums = conv_forward(s, k, sums)
        made = stat_start(r.stn, stat_base, sums)
        yield
        moments_in[s][1] = moments(stat_end(r.stn, stat_base, made))
        keys = phase_keys(2)
        for h in range(2):

            def inside(at, _):
                value = gelu(norm_inner(s, 1, r.conv[s, at])[1])
                r.inf[s, at, cols(chan)] = value.astype(bf16)
                return _

            narrow(starts[h], counts[h], inside, 0)
            gather_start(r.inf.at[s], raw(h), keys[h])
        yield
        gather_pass(r.inf.at[s], raw(0), keys[0])
        gather_pass(r.inf.at[s], raw(1), keys[1])
        sums = (zero_w, zero_w)
        for h in range(2):
            gather_end(r.inf.at[s], raw(h), keys[h])
            value = dot(r.inf[s, raw(h)], r.wef[s])
            r.ex[s, raw(h)] = value
            sums = (sums[0] + fold(value), sums[1] + fold(value * value))
        made = stat_start(r.stw, wide_slot, sums)
        yield
        moments_in[s][2] = moments(stat_end(r.stw, wide_slot, made))

    def spread_taps():
        for index in range(3):
            for tap in range(9):
                r.dkb[9 * index + tap] = jnp.broadcast_to(r.dk[tap, index : index + 1, :], (8, ib))

    def clear(i, _):
        r.gk[i] = zero_n
        return _

    for s in range(2):
        r.red[s, rows : rows + 8] = zero_n

    sums = (zero_n, zero_n)
    load_wr0.wait()
    for h in range(2):
        load_x[h].wait()
        value = dot(r.x[raw(h)], r.wr0[...])
        r.red[0, raw(h)] = value
        sums = (sums[0] + fold(value), sums[1] + fold(value * value))
    pl.semaphore_wait(barrier, n_clip - 1 + n_chan - 1)
    made = stat_start(r.stn, 0, sums)
    share_we(0, 0)
    share_we(0, 1)
    spread_taps()
    lax.fori_loop(0, r.gk.shape[0], clear, 0)
    moments_in[0][0] = moments(stat_end(r.stn, 0, made))

    stage = forward(0, 1, 0)
    next(stage)
    share_wr(1, 0)
    next(stage)
    shared_we(0)
    next(stage)
    share_wr(1, 1)
    for _ in stage:
        pass

    def out_zero(at, _):
        z = norm_outer(0, r.ex[0, at])[1] + inner_input(0, at).astype(f32)
        r.out0[at] = gelu(z).astype(bf16)
        return _


    def scatter_all(slot, chunks, prepare, product, use, beside=None, midway=None):
        keys = phase_keys(4)
        ats = [pl.ds(*span) for span in chunks]
        borrowed = []

        def start(k, away):
            if away:
                prepare(k)
            two = pair(1 - high if away else high)
            r.pb[ats[k], two] = product(ats[k], two).astype(bf16)
            block, index = (j_far, 1) if away else (j_core, 0)
            target = r.rcore.at[slot, index, ats[k]]
            made = remote(r.pb.at[ats[k], cols(block)], target, (clip, j_core), keys[k][index])
            borrowed.append(made[1])

        def hand_on(k):
            at = ats[k]
            arrive(r.rcore.at[slot, 1, at], keys[k][1])
            both = r.pb[at, cols(j_y)].astype(f32) + r.rcore[slot, 1, at].astype(f32)
            r.ysend[slot % 2, at] = both.astype(bf16)
            made = remote(r.ysend.at[slot % 2, at], r.ryy.at[slot, at], (clip, j_y), keys[k][2])
            borrowed.append(made[1])

        start(0, True)
        start(1, True)
        hand_on(0)
        start(2, True)
        hand_on(1)
        start(3, True)
        hand_on(2)
        start(0, False)
        hand_on(3)
        for k in range(1, 4):
            start(k, False)
        if beside is not None:
            beside()
        for k in range(4):
            arrive(r.rcore.at[slot, 0, ats[k]], keys[k][0])
            arrive(r.ryy.at[slot, ats[k]], keys[k][2])
            use(*chunks[k])
            if midway is not None and k == 1:
                midway()
        for index in borrowed:
            sent(index)

    held = SimpleNamespace(sums=(zero_n, zero_n))

    def use_reduced(begin, count):
        at = pl.ds(begin, count)
        value = scatter_value(0, at)
        r.red[1, at] = value
        held.sums = (held.sums[0] + fold(value), held.sums[1] + fold(value * value))

    shared_wr(1)
    scatter_all(
        0,
        raw_spans,
        lambda k: broad(k, out_zero, 0),
        lambda at, two: dot(r.out0[at], r.wrf[1, :, two]),
        use_reduced,
    )
    made = stat_start(r.stn, 2, held.sums)
    share_we(1, 0)
    moments_in[1][0] = moments(stat_end(r.stn, 2, made))
    stage = forward(1, 3, 1)
    next(stage)
    share_we(1, 1)
    next(stage)
    shared_we(1)
    next(stage)
    share_wr(0, 0)
    share_wr(0, 1)
    for _ in stage:
        pass

    load_cot.wait()

    def out_one(at, sums):
        centred, z = norm_outer(1, r.ex[1, at])
        value, slope = gelu_both(z + r.out0[at].astype(f32))
        r.act[at] = value.astype(bf16)
        grad = r.cot[at].astype(f32) * slope
        r.gpre[at] = grad
        return sums[0] + fold(grad), sums[1] + fold(grad * centred)

    def top_zero(at, sums):
        centred, z = norm_outer(0, r.ex[0, at])
        grad = r.gin[at] * gelu_both(z + inner_input(0, at).astype(f32))[1]
        r.gpre[at] = grad
        return sums[0] + fold(grad), sums[1] + fold(grad * centred)

    top_sums = SimpleNamespace()

    def backward(s, stat_base, wide_slot, slot):
        if s == 1:
            top_sums.now = (zero_w, zero_w)
            for k in range(4):
                top_sums.now = broad(k, out_one, top_sums.now)
        sums = top_sums.now
        made = stat_start(r.stw, wide_slot, sums)
        if s == 1:
            write_out(r.act, r.act_out)
        service(s, 0)
        shift_sum, gain_sum = stat_end(r.stw, wide_slot, made)
        r.gbo[s : s + 1] = shift_sum
        r.ggo[s : s + 1] = gain_sum
        mean, inv = moments_in[s][2]
        scale = inv * row(r.go, s)
        shift_mean, gain_mean = shift_sum / pixel_total, gain_sum / pixel_total

        def expand_back(at, _):
            centred = (r.ex[s, at] - mean) * inv
            grad = scale * (r.gpre[at] - (shift_mean + centred * gain_mean))
            r.gexp[at] = grad.astype(bf16)
            return _

        held.sums = (zero_n, zero_n)
        service(s, 1)

        def weight_expand():
            value = dot(r.inf[s], r.gexp[...], 0, 0).astype(bf16)
            r.geo[s] = value.reshape(r.geo.shape[1:])
            place = r.ge.at[s, :, :, :, wide(chan)]
            turned[1, s] = local(r.geo.at[s, chan], place)
            for j in others:
                remote(r.geo.at[s, j], place, (clip, j), (TURN, 1, s))
            service(s, 2)

        def use_inner(begin, count):
            def one(at, sums):
                centred, z = norm_inner(s, 1, r.conv[s, at])
                grad = scatter_value(slot, at) * gelu_both(z)[1]
                r.g1[at] = grad
                return sums[0] + fold(grad), sums[1] + fold(grad * centred)

            held.sums = narrow(begin, count, one, held.sums)

        scatter_all(
            slot,
            raw_spans,
            lambda k: broad(k, expand_back, 0),
            lambda at, two: dot(r.gexp[at], r.wef[s, two], 1, 1),
            use_inner,
            weight_expand,
            lambda: service(s, 3),
        )
        made = stat_start(r.stn, stat_base, held.sums)
        service(s, 4)
        shift_sum, gain_sum = stat_end(r.stn, stat_base, made)
        r.gbi[s, 1:2] = shift_sum
        r.ggi[s, 1:2] = gain_sum
        mean, inv = moments_in[s][1]
        scale = inv * row(r.gi, s, 1)
        shift_mean, gain_mean = shift_sum / pixel_total, gain_sum / pixel_total

        def conv_back(i, _):
            at = pair_rows(0, i)
            halves = []
            for f in (2 * i, 2 * i + 1):
                centred = (spread(r.conv.at[s], f) - mean) * inv
                grad = scale * (spread(r.g1, f) - (shift_mean + centred * gain_mean))
                halves.append(real(grad))
            for b in (-1, 0, 1):
                moved = [row_pad(col_shift(v, -b), 1) for v in halves]
                for a in (-1, 0, 1):
                    tap = 3 * (a + 1) + b + 1
                    both = jnp.concatenate([flat(v[1 - a : 1 - a + SIDE]) for v in moved], axis=0)
                    r.gs[at, tap * ib : (tap + 1) * ib] = both.astype(bf16)
            return _


        service(s, 5)

        def weight_conv():
            for k in range(3):
                taps = slice(3 * k * ib, 3 * (k + 1) * ib)
                value = dot(r.mixf[s], r.gs[:, taps], 0, 0).astype(bf16)
                r.gc[s, :, :, :, taps] = value.reshape(r.gc.shape[1:4] + (3 * ib,))
            service(s, 6)

        def use_mixed(begin, count):
            def one(at, _):
                r.gm[at] = real(scatter_value(slot + 1, at))
                return _

            narrow(begin, count, one, 0)

        scatter_all(
            slot + 1,
            padded_spans,
            lambda k: lax.fori_loop(k * pairs // 2, (k + 1) * pairs // 2, conv_back, 0),
            lambda at, two: dot(r.gs[at], r.wc[s, two], 1, 1),
            use_mixed,
            weight_conv,
            lambda: service(s, 7),
        )

        def tap_sums(grad, v, index, reach):
            for b in (-1, 0, 1):
                padded = row_pad(col_shift(v, reach * b), reach)
                for a in (-1, 0, 1):
                    start = reach + reach * a
                    place = 9 * index + 3 * (a + 1) + b + 1
                    r.gk[place] = r.gk[place] + jnp.sum(grad * padded[start : start + SIDE], axis=0)

        def mix_back(f, before):
            at = frame_rows(f)
            following = frame_rows(jnp.minimum(f + 1, frames - 1))
            here = tiles(r.hid[s, at])
            step = keep_flag(f) * (tiles(r.hid[s, following]) - here)
            grad = tiles(r.gm[at])
            if s == 0:
                r.gd[at] = flat(dw_tiles(grad, taps_of(0), 1, -1))
                tap_sums(grad, step + before, 0, 1)
            else:
                gate = tiles(r.sig[at])
                grad = grad * here * gate * (1.0 - gate)
                r.gd[at] = flat(dw_tiles(grad, taps_of(1), 1, -1) + dw_tiles(grad, taps_of(2), 2, -1))
                tap_sums(grad, step, 1, 1)
                tap_sums(grad, step, 2, 2)
                r.gk[27] = r.gk[27] + jnp.sum(grad, axis=0)
            return step

        lax.fori_loop(0, frames, mix_back, jnp.zeros((SIDE, 8, ib), f32))

        service(s, 8)

        def hide_back(f, sums):
            at = frame_rows(f)
            previous = frame_rows(jnp.maximum(f - 1, 0))
            keep = keep_flag(f)
            keep_before = jnp.where(f > 0, keep_flag(jnp.maximum(f - 1, 0)), 0.0)
            now = r.gd[at]
            earlier = r.gd[previous]
            grad = r.gm[at]
            if s == 0:
                following = frame_rows(jnp.minimum(f + 1, frames - 1))
                later = now + r.gd[following]
                earlier = earlier + now
            else:
                later = now
                grad = grad * (1.0 + r.sig[at])
            grad = grad + keep_before * earlier - keep * later
            centred, z = norm_inner(s, 0, spread(r.red.at[s], f))
            grad = real(tiles(grad) * gelu_both(z)[1])
            squeeze(r.g1, f, grad)
            return sums[0] + jnp.sum(grad, axis=0), sums[1] + jnp.sum(grad * centred, axis=0)

        sums = lax.fori_loop(0, frames, hide_back, (zero_n, zero_n))
        made = stat_start(r.stn, stat_base + 1, sums)
        service(s, 9)
        shift_sum, gain_sum = stat_end(r.stn, stat_base + 1, made)
        r.gbi[s, 0:1] = shift_sum
        r.ggi[s, 0:1] = gain_sum
        mean, inv = moments_in[s][0]
        scale = inv * row(r.gi, s, 0)
        shift_mean, gain_mean = shift_sum / pixel_total, gain_sum / pixel_total
        service(s, 10)
        keys = phase_keys(4)
        quarters = [pl.ds(*span) for span in raw_spans]

        def reduce_back(at, _):
            centred = (r.red[s, at] - mean) * inv
            grad = scale * (r.g1[at] - (shift_mean + centred * gain_mean))
            r.grf[s, at, cols(chan)] = grad.astype(bf16)
            return _

        for k in range(4):
            narrow(*raw_spans[k], reduce_back, 0)
            gather_start(r.grf.at[s], quarters[k], keys[k])
        if s == 0:
            own = r.grf[0, :, cols(chan)]
            for piece in range(n_chan):
                value = dot(r.x[:, piece * cs : (piece + 1) * cs], own, 0, 0).astype(bf16)
                r.gr[0, piece] = value.reshape(r.gr.shape[2:])
        service(s, 11)
        gather_pass(r.grf.at[s], quarters[0], keys[0])
        gather_pass(r.grf.at[s], quarters[1], keys[1])
        if s == 0:
            shared_wr(0)
        else:
            top_sums.now = (zero_w, zero_w)
        for k in range(4):
            at = quarters[k]
            gather_end(r.grf.at[s], at, keys[k])
            r.gin[at] = dot(r.grf[s, at], r.wrf[s], 1, 1) + r.gpre[at]
            if k < 2:
                gather_pass(r.grf.at[s], quarters[k + 2], keys[k + 2])
            if s == 0:
                write_out(r.gin.at[at], r.gin_out.at[at])
            else:
                top_sums.now = broad(k, top_zero, top_sums.now)
            if k == 1:
                service(s, 12)
        service(s, 13)
        if s == 1:
            value = dot(r.out0[...], r.grf[1], 0, 0).astype(bf16)
            r.gro[...] = value.reshape(r.gro.shape)
            place = r.gr.at[1, chan]
            turned[2, 1] = local(r.gro.at[:, :, cols(chan)], place)
            for j in others:
                remote(r.gro.at[:, :, cols(j)], place, (clip, j), (TURN, 2, 1))

    turned = {}

    def reduce_task(kind, s, line, place):
        ref, from_side, from_z, result = kinds[kind]
        mine, done = ref.at[s, :, :, line, place], result.at[s, :, :, line, place]
        side_in, z_in = from_side.at[s, :, line, place], from_z.at[s, :, line, place]
        across = (2 * z + 1 - side, chan)
        key = (kind, s, line.start, place.start)
        if (kind, s) in turned:
            turned.pop((kind, s)).wait()
            three = pl.ds(0, (n_chan - 1) * cs)
            arrive(
                r.ge.at[s, :, :, :, three] if kind == 1 else r.gr.at[s, pl.ds(0, n_chan - 1)],
                (TURN, kind, s),
            )
        near, far = (2 * z_near + side, chan), (2 * z_far + side, chan)

        def add(k, term):
            both = ref[s, k, side, line, place].astype(f32) + term.astype(f32)
            return both.astype(bf16)

        remote(mine.at[:, 1 - side], side_in, across, key + (0,))
        yield
        arrive(side_in, key + (0,))
        for k in range(n_z):
            ref[s, k, side, line, place] = add(k, from_side[s, k, line, place])
        for k in range(2):
            remote(mine.at[1 - low + 2 * k, side], z_in.at[k], near, key + (1,))
        yield
        arrive(z_in.at[pl.ds(0, 2)], key + (1,))
        for k in range(2):
            ref[s, low + 2 * k, side, line, place] = add(low + 2 * k, from_z[s, k, line, place])
        remote(mine.at[z_far, side], z_in.at[2], far, key + (2,))
        yield
        arrive(z_in.at[2], key + (2,))
        result[s, z, side, line, place] = add(z, from_z[s, 2, line, place])
        remote(done.at[z, side], done.at[z, side], far, key + (3,))
        yield
        arrive(done.at[z_far, side], key + (3,))
        for k in (z, z_far):
            remote(done.at[k, side], done.at[k, side], near, key + (4,))
        yield
        arrive(done.at[pl.ds(0, 2), side], key + (4,))
        remote(done.at[:, side], done.at[:, side], across, key + (5,))
        yield
        arrive(done.at[:, 1 - side], key + (5,))
        if kind == 0:
            base = place.start // ib
            for k in range((place.stop - place.start) // ib):
                here = r.fc.at[s, :, :, :, (base + k) * ib : (base + k + 1) * ib]
                write_out(here, r.gc_out.at[s, base + k])
        else:
            out = (None, r.ge_out, r.gr_out)[kind]
            write_out(done, out.at[s, :, :, line, place])
        yield

    kinds = (
        (r.gc, r.xc, r.zc, r.fc),
        (r.ge, r.xe, r.ze, r.fe),
        (r.gr, r.xr, r.zr, r.fr),
    )
    def cut(size, count):
        return [slice(k * (size // count), (k + 1) * (size // count)) for k in range(count)]

    tasks = {}
    for s in range(2):
        for k, place in enumerate(cut(9 * ib, PIECES[0])):
            tasks[100 * s + k] = reduce_task(0, s, slice(0, r.gc.shape[3]), place)
        for k, place in enumerate(cut(r.ge.shape[4], PIECES[1])):
            tasks[100 * s + 10 + k] = reduce_task(1, s, slice(0, r.ge.shape[3]), place)
        for k, line in enumerate(cut(r.gr.shape[3], PIECES[2])):
            tasks[100 * s + 20 + k] = reduce_task(2, s, line, slice(0, ib))

    def advance(*steps):
        for step in steps:
            next(tasks[step])

    def service(s, point):
        advance(*PLAN.get((s, point), ()))

    backward(1, 4, 2, 1)
    backward(0, 6, 3, 3)

    for place in range(r.gk.shape[0]):
        r.kst[clip, place : place + 1, :] = jnp.sum(r.gk[place], axis=0, keepdims=True)
    for t in clip_others:
        remote(r.kst.at[clip], r.kst.at[clip], (t, chan), TAPS)
    service(0, 14)
    arrive(r.kst.at[pl.ds(0, n_clip - 1)], TAPS)
    total = r.kst[0]
    for k in range(1, n_clip):
        total = total + r.kst[k]
    for index in range(3):
        for tap in range(9):
            place = 9 * index + tap
            r.gk_out[tap, index : index + 1, :] = total[place : place + 1]
    r.ggb_out[...] = total[27:28]
    for copy in outgoing.values():
        copy.wait()
    for index in list(in_flight):
        sent(index)
    assert len(places) <= ARRIVALS and counters.load <= LOADS - 8


def fused_call(n_clip, n_chan, pixel_total, *operands):
    rows, width = operands[0].shape
    cs = width // n_chan
    ib = LANES
    inner = ib * n_chan
    n_z = n_clip // 2
    padded = rows // PIXELS * FRAME
    over = rows + 8
    bf16, f32 = jnp.bfloat16, jnp.float32
    whole = pl.BlockSpec(memory_space=pltpu.VMEM)
    anywhere = pl.BlockSpec(memory_space=pl.ANY)
    scalars = pl.BlockSpec(memory_space=pltpu.SMEM)
    shape = jax.ShapeDtypeStruct
    V = pltpu.VMEM
    scratch = dict(
        x=V((rows, width), bf16),
        cot=V((rows, cs), bf16),
        wr0=V((width, ib), bf16),
        wrf=V((2, cs, inner), bf16),
        wef=V((2, inner, cs), bf16),
        wc=V((2, inner, 9 * ib), bf16),
        dkb=V((27, 8, ib), f32),
        red=V((2, over, ib), f32),
        hid=V((2, padded, ib), f32),
        sig=V((padded, ib), f32),
        conv=V((2, over, ib), f32),
        mixf=V((2, padded, inner), bf16),
        inf=V((2, rows, inner), bf16),
        ex=V((2, rows, cs), f32),
        out0=V((rows, cs), bf16),
        act=V((rows, cs), bf16),
        y=V((padded // 4, 9 * ib), f32),
        gpre=V((rows, cs), f32),
        gin=V((rows, cs), f32),
        gexp=V((rows, cs), bf16),
        gs=V((padded, 9 * ib), bf16),
        pb=V((padded, inner), bf16),
        ysend=V((2, padded, ib), bf16),
        rcore=V((5, 2, padded, ib), bf16),
        ryy=V((5, padded, ib), bf16),
        grf=V((2, rows, inner), bf16),
        gm=V((padded, ib), f32),
        gd=V((padded, ib), f32),
        g1=V((over, ib), f32),
        gk=V((32, 8, ib), f32),
        kst=V((n_clip, 32, ib), f32),
        stn=V((8, n_clip, 2, ib), f32),
        stw=V((4, n_clip, 2, cs), f32),
        gc=V((2, n_z, 2, inner // n_clip, 9 * ib), bf16),
        geo=V((2, n_chan, n_z, 2, ib // n_clip, cs), bf16),
        ge=V((2, n_z, 2, ib // n_clip, width), bf16),
        gro=V((2, cs // 2, inner), bf16),
        gr=V((2, n_z, 2, width // n_clip, ib), bf16),
        fc=V((2, n_z, 2, inner // n_clip, 9 * ib), bf16),
        fe=V((2, n_z, 2, ib // n_clip, width), bf16),
        fr=V((2, n_z, 2, width // n_clip, ib), bf16),
        xc=V((2, n_z, inner // n_clip, 9 * ib), bf16),
        xe=V((2, n_z, ib // n_clip, width), bf16),
        xr=V((2, n_z, width // n_clip, ib), bf16),
        zc=V((2, n_z - 1, inner // n_clip, 9 * ib), bf16),
        ze=V((2, n_z - 1, ib // n_clip, width), bf16),
        zr=V((2, n_z - 1, width // n_clip, ib), bf16),
        ssem=pltpu.SemaphoreType.DMA((SENDS,)),
        rsem=pltpu.SemaphoreType.DMA((ARRIVALS,)),
        lsem=pltpu.SemaphoreType.DMA((LOADS,)),
    )
    return pl.pallas_call(
        partial(fused_kernel, n_clip, n_chan, pixel_total),
        out_shape=[
            shape((rows, cs), bf16),
            shape((rows, cs), f32),
            shape((2, 2, ib), f32),
            shape((2, 2, ib), f32),
            shape((2, cs), f32),
            shape((2, cs), f32),
            shape((9, 3, ib), f32),
            shape((1, ib), f32),
            shape((2, 9, n_z, 2, inner // n_clip, ib), bf16),
            shape((2, n_z, 2, ib // n_clip, width), bf16),
            shape((2, n_z, 2, width // n_clip, ib), bf16),
        ],
        in_specs=[anywhere] * 5 + [scalars] + [whole] * 6,
        out_specs=[anywhere] * 2 + [whole] * 6 + [anywhere] * 3,
        scratch_shapes=[scratch[name] for name in Refs._fields if name in scratch],
        compiler_params=pltpu.CompilerParams(
            collective_id=0, has_side_effects=True, vmem_limit_bytes=62 * 1024 * 1024
        ),
    )(*operands)


def finish_kernel(*refs):
    count = len(refs) // 2
    sources, results = refs[:count], refs[count:]
    for here, there in zip(sources[:5], results[:5]):
        there[...] = here[...].astype(there.dtype)

    @pl.when(pl.program_id(0) == 0)
    def _():
        for here, there in zip(sources[5:], results[5:]):
            there[...] = here[...]


def finish(steps, gc, ge, gr, act, gin, *small):
    arrays = [a.reshape(-1, a.shape[-1]) for a in (gc, ge, gr)] + [act, gin]
    blocks = [
        pl.BlockSpec((-(-a.shape[0] // (16 * steps)) * 16, a.shape[1]), lambda i: (i, 0))
        for a in arrays
    ]
    whole = [pl.BlockSpec(memory_space=pltpu.VMEM)] * len(small)
    shapes = [jax.ShapeDtypeStruct(a.shape, jnp.float32) for a in arrays[:3]]
    shapes += [jax.ShapeDtypeStruct(a.shape, a.dtype) for a in (act, gin, *small)]
    return pl.pallas_call(
        finish_kernel,
        grid=(steps,),
        out_shape=shapes,
        in_specs=blocks + whole,
        out_specs=blocks + whole,
        compiler_params=pltpu.CompilerParams(vmem_limit_bytes=62 * 1024 * 1024),
    )(*arrays, *small)


def fused(
    frames_in,
    boundary,
    w_reduce,
    gain_inner,
    bias_inner,
    w_conv,
    w_expand,
    gain_outer,
    bias_outer,
    depth_kernels,
    gate_bias,
    cotangent,
):
    n_clip, n_chan = lax.axis_size("clip"), lax.axis_size("chan")
    pixel_total = frames_in.shape[0] * n_clip
    act, gin, ggi, gbi, ggo, gbo, gk, ggb, gc, ge, gr = fused_call(
        n_clip,
        n_chan,
        float(pixel_total),
        frames_in,
        cotangent,
        w_reduce,
        w_conv,
        w_expand,
        boundary,
        gain_inner,
        bias_inner,
        gain_outer,
        bias_outer,
        depth_kernels.transpose(1, 0, 2),
        gate_bias.reshape(1, -1),
    )
    gc, ge, gr, act, gin, ggi, gbi, ggo, gbo, gk, ggb = finish(
        2, gc, ge, gr, act, gin, ggi, gbi, ggo, gbo, gk, ggb
    )
    return (
        act,
        gin,
        gr.reshape(w_reduce.shape),
        ggi,
        gbi,
        gc.reshape(w_conv.shape),
        ge.reshape(w_expand.shape),
        ggo,
        gbo,
        gk.transpose(1, 0, 2),
        ggb.reshape(-1),
    )


def solution(mesh):
    in_specs = (
        P("clip", None),
        P("clip", None),
        P(None, None, "chan"),
        P(None, None, "chan"),
        P(None, None, "chan"),
        P(None, None, None, "chan"),
        P(None, "chan", None),
        P(),
        P(),
        P(None, None, "chan"),
        P("chan"),
        P("clip", None),
    )
    out_specs = (
        P("clip", "chan"),
        P("clip", "chan"),
        P(None, None, "chan"),
        P(None, None, "chan"),
        P(None, None, "chan"),
        P(None, None, None, "chan"),
        P(None, "chan", None),
        P(None, "chan"),
        P(None, "chan"),
        P(None, None, "chan"),
        P("chan"),
    )

    def run(*arguments):
        fits = fused_fits(mesh, arguments[0].shape, arguments[2].shape)
        return jax.shard_map(fused if fits else body, mesh=mesh, in_specs=in_specs, out_specs=out_specs, check_vma=False)(*arguments)

    return run
```

```python
from functools import partial
from types import SimpleNamespace
from typing import Any, NamedTuple

import jax
import jax.numpy as jnp
from jax import lax
from jax.experimental import pallas as pl
from jax.experimental.pallas import tpu as pltpu
from jax.sharding import PartitionSpec as P

SEG = 8
SIDE = 7


epsilon = 1e-05


def framed(values):
    return values.reshape(-1, SIDE, SIDE, values.shape[-1])


def shifted(frame_grid, row_step, col_step, dilation):
    padded = jnp.pad(frame_grid, ((0, 0), (dilation, dilation), (dilation, dilation), (0, 0)))
    return padded[
        :,
        dilation + row_step : dilation + row_step + SIDE,
        dilation + col_step : dilation + col_step + SIDE,
        :,
    ]


def depthwise(values, kernel, dilation):
    frame_grid = framed(values)
    running = jnp.zeros_like(frame_grid)
    for tap_index in range(9):
        running = (
            running
            + shifted(
                frame_grid,
                (tap_index // 3 - 1) * dilation,
                (tap_index % 3 - 1) * dilation,
                dilation,
            )
            * kernel[tap_index]
        )
    return running.reshape(values.shape)


def patch_rows(values):
    frame_grid = framed(values)
    pieces = [
        shifted(frame_grid, tap_index // 3 - 1, tap_index % 3 - 1, 1) for tap_index in range(9)
    ]
    return jnp.concatenate(pieces, axis=-1).reshape(values.shape[0], 9 * values.shape[1])


def unpatch(grad_rows, chan_width):
    frame_grid = grad_rows.reshape(-1, SIDE, SIDE, 9, chan_width)
    running = jnp.zeros(frame_grid.shape[:3] + (chan_width,), jnp.float32)
    for tap_index in range(9):
        running = running + shifted(
            frame_grid[:, :, :, tap_index, :], 1 - tap_index // 3, 1 - tap_index % 3, 1
        )
    return running.reshape(-1, chan_width)


def neighbours(values, boundary):
    clip_count = boundary.shape[0]
    frame_grid = values.reshape(clip_count, SEG, SIDE * SIDE, values.shape[-1])
    stop_mask = (boundary == 1)[:, :, None, None]
    start_mask = jnp.concatenate([jnp.ones_like(stop_mask[:, :1]), stop_mask[:, :-1]], axis=1)
    after_seg = jnp.concatenate([frame_grid[:, 1:], frame_grid[:, -1:]], axis=1)
    before = jnp.concatenate([frame_grid[:, :1], frame_grid[:, :-1]], axis=1)
    later_seg = jnp.where(stop_mask, frame_grid, after_seg)
    earlier = jnp.where(start_mask, frame_grid, before)
    return (later_seg.reshape(values.shape), earlier.reshape(values.shape))


def temporal(values, kernels, gate_vec, boundary, short_range):
    later_seg, earlier = neighbours(values, boundary)
    if short_range:
        return values + depthwise(later_seg - earlier, kernels[0], 1)
    change = later_seg - values
    logits = depthwise(change, kernels[1], 1) + depthwise(change, kernels[2], 2) + gate_vec
    return values + values * jax.nn.sigmoid(logits)


def columns(values, col_start, col_share):
    return lax.dynamic_slice_in_dim(values, col_start, col_share, values.ndim - 1)


def contract(left, right, left_dim, right_dim):
    return lax.dot_general(
        left, right, (((left_dim,), (right_dim,)), ((), ())), preferred_element_type=jnp.float32
    )


def normalize(values, gain_vec, bias_vec, pixel_total):
    col_sum, sq_sum = lax.psum((jnp.sum(values, axis=0), jnp.sum(values * values, axis=0)), "clip")
    mean_val = col_sum / pixel_total
    inv_std = lax.rsqrt(sq_sum / pixel_total - mean_val * mean_val + epsilon)
    centred = (values - mean_val) * inv_std
    return (centred * gain_vec + bias_vec, centred, inv_std)


def normalize_back(grad_rows, centred, inv_std, gain_vec, pixel_total):
    shift_sum, gain_sum = lax.psum(
        (jnp.sum(grad_rows, axis=0), jnp.sum(grad_rows * centred, axis=0)), "clip"
    )
    grad_in = inv_std * gain_vec * (grad_rows - (shift_sum + centred * gain_sum) / pixel_total)
    return (grad_in, gain_sum, shift_sum)


def block_forward(inputs, boundary, weights, short_range, pixel_total):
    w_red, gain_pair, bias_pair, w_cv, w_ex, gain_out, bias_out, kernels, gate_vec = weights
    reduced = jnp.dot(inputs, w_red, preferred_element_type=jnp.float32)
    norm_one, centred_one, inv_one = normalize(reduced, gain_pair[0], bias_pair[0], pixel_total)
    hidden, gelu_one = jax.vjp(jax.nn.gelu, norm_one)
    mixed_act, mix_back = jax.vjp(
        partial(temporal, boundary=boundary, short_range=short_range), hidden, kernels, gate_vec
    )
    gathered = lax.all_gather(mixed_act.astype(jnp.bfloat16), "chan", axis=1, tiled=True)
    patches = patch_rows(gathered)
    conv_out = jnp.dot(
        patches, w_cv.reshape(-1, w_cv.shape[-1]), preferred_element_type=jnp.float32
    )
    norm_two, centred_two, inv_two = normalize(conv_out, gain_pair[1], bias_pair[1], pixel_total)
    inner_full, gelu_two = jax.vjp(jax.nn.gelu, norm_two)
    inner_act = inner_full.astype(jnp.bfloat16)
    partial_out = jnp.dot(inner_act, w_ex, preferred_element_type=jnp.float32)
    expanded = lax.psum(partial_out.astype(jnp.bfloat16), "chan").astype(jnp.float32)
    norm_three, centred_three, inv_three = normalize(expanded, gain_out, bias_out, pixel_total)
    output_full, gelu_three = jax.vjp(jax.nn.gelu, norm_three + inputs.astype(jnp.float32))
    kept_state = (
        centred_one,
        inv_one,
        gelu_one,
        mix_back,
        patches,
        centred_two,
        inv_two,
        gelu_two,
        inner_act,
        centred_three,
        inv_three,
        gelu_three,
        gain_out,
    )
    return (output_full.astype(jnp.bfloat16), kept_state)


def block_backward(grad_out, inputs, weights, kept_state, pixel_total):
    w_red, gain_pair, bias_pair, w_cv, w_ex, gain_out, bias_out, kernels, gate_vec = weights
    (
        centred_one,
        inv_one,
        gelu_one,
        mix_back,
        patches,
        centred_two,
        inv_two,
        gelu_two,
        inner_act,
        centred_three,
        inv_three,
        gelu_three,
        gain_use,
    ) = kept_state
    grad_pre = gelu_three(grad_out)[0]
    grad_exp, gain_three, bias_three = normalize_back(
        grad_pre, centred_three, inv_three, gain_use, pixel_total
    )
    low_exp = grad_exp.astype(jnp.bfloat16)
    grad_wex = contract(inner_act, low_exp, 0, 0)
    grad_inner = contract(low_exp, w_ex, 1, 1)
    grad_two = gelu_two(grad_inner)[0]
    grad_cv, gain_two, bias_two = normalize_back(
        grad_two, centred_two, inv_two, gain_pair[1], pixel_total
    )
    low_cv = grad_cv.astype(jnp.bfloat16)
    flat_cv = w_cv.reshape(-1, w_cv.shape[-1])
    grad_wcv = contract(patches, low_cv, 0, 0).reshape(w_cv.shape)
    grad_patch = contract(low_cv, flat_cv, 1, 1)
    grad_mixed = lax.psum_scatter(
        unpatch(grad_patch, w_cv.shape[1]).astype(jnp.bfloat16),
        "chan",
        scatter_dimension=1,
        tiled=True,
    ).astype(jnp.float32)
    grad_hidden, grad_kern, grad_gate = mix_back(grad_mixed)
    grad_one = gelu_one(grad_hidden)[0]
    grad_red, gain_one, bias_one = normalize_back(
        grad_one, centred_one, inv_one, gain_pair[0], pixel_total
    )
    low_red = grad_red.astype(jnp.bfloat16)
    grad_wred = contract(inputs, low_red, 0, 0)
    partial_in = contract(low_red, w_red, 1, 1)
    grad_in = grad_pre + lax.psum(partial_in.astype(jnp.bfloat16), "chan").astype(jnp.float32)
    weight_terms = (grad_wred, grad_wcv, grad_wex, grad_kern, grad_gate)
    norm_terms = (gain_one, bias_one, gain_two, bias_two, gain_three, bias_three)
    return (grad_in, weight_terms, norm_terms)


def body(
    frames_in,
    boundary,
    w_reduce,
    gain_inner,
    bias_inner,
    w_conv,
    w_expand,
    gain_outer,
    bias_outer,
    depth_kernels,
    gate_bias,
    cotangent,
):
    row_count = frames_in.shape[0]
    pixel_total = row_count * lax.axis_size("clip")
    col_share = frames_in.shape[1] // lax.axis_size("chan")
    col_start = lax.axis_index("chan") * col_share
    block_weights = [
        (
            w_reduce[block_index],
            gain_inner[block_index],
            bias_inner[block_index],
            w_conv[block_index],
            w_expand[block_index],
            gain_outer[block_index],
            bias_outer[block_index],
            depth_kernels,
            gate_bias,
        )
        for block_index in range(2)
    ]
    first_out, kept_zero = block_forward(frames_in, boundary, block_weights[0], True, pixel_total)
    final_out, kept_one = block_forward(first_out, boundary, block_weights[1], False, pixel_total)
    layer_inputs = [frames_in, first_out]
    kept_states = [kept_zero, kept_one]
    grad_flow = cotangent.astype(jnp.float32)
    weight_sums = [None, None]
    norm_sums = [None, None]
    for block_index in (1, 0):
        grad_flow, weight_terms, norm_terms = block_backward(
            grad_flow,
            layer_inputs[block_index],
            block_weights[block_index],
            kept_states[block_index],
            pixel_total,
        )
        grad_wred, grad_wcv, grad_wex, grad_kern, grad_gate = weight_terms
        weight_terms = (
            lax.psum(grad_wred.astype(jnp.bfloat16), "clip").astype(jnp.float32),
            lax.psum(grad_wcv.astype(jnp.bfloat16), "clip").astype(jnp.float32),
            lax.psum(grad_wex.astype(jnp.bfloat16), "clip").astype(jnp.float32),
            lax.psum(grad_kern.astype(jnp.bfloat16), "clip").astype(jnp.float32),
            lax.psum(grad_gate.astype(jnp.bfloat16), "clip").astype(jnp.float32),
        )
        weight_sums[block_index] = weight_terms
        norm_sums[block_index] = norm_terms
    grad_reduce = jnp.stack([weight_sums[0][0], weight_sums[1][0]])
    grad_conv = jnp.stack([weight_sums[0][1], weight_sums[1][1]])
    grad_expand = jnp.stack([weight_sums[0][2], weight_sums[1][2]])
    grad_kernels = weight_sums[0][3] + weight_sums[1][3]
    grad_gate_bias = weight_sums[0][4] + weight_sums[1][4]
    grad_gain_inner = jnp.stack(
        [
            jnp.stack([norm_sums[0][0], norm_sums[0][2]]),
            jnp.stack([norm_sums[1][0], norm_sums[1][2]]),
        ]
    )
    grad_bias_inner = jnp.stack(
        [
            jnp.stack([norm_sums[0][1], norm_sums[0][3]]),
            jnp.stack([norm_sums[1][1], norm_sums[1][3]]),
        ]
    )
    grad_gain_outer = jnp.stack([norm_sums[0][4], norm_sums[1][4]])
    grad_bias_outer = jnp.stack([norm_sums[0][5], norm_sums[1][5]])
    activations = columns(final_out, col_start, col_share)
    input_grad = columns(grad_flow, col_start, col_share)
    grad_gain_outer = columns(grad_gain_outer, col_start, col_share)
    grad_bias_outer = columns(grad_bias_outer, col_start, col_share)
    return (
        activations,
        input_grad,
        grad_reduce,
        grad_gain_inner,
        grad_bias_inner,
        grad_conv,
        grad_expand,
        grad_gain_outer,
        grad_bias_outer,
        grad_kernels,
        grad_gate_bias,
    )


MESH = pl.DeviceIdType.MESH
LANES = 128
FRAME = SIDE * 8
PIXELS = SIDE * SIDE
PAIR = 2 * FRAME
GELU_A = 0.7978845608028654
GELU_B = 0.044715
SENDS = 64
LOADS = 32


def fused_fits(mesh, frame_shape, reduce_shape):
    n_clip, n_chan = mesh.shape["clip"], mesh.shape["chan"]
    share = reduce_shape[2] // n_chan
    frames = frame_shape[0] // (n_clip * SIDE * SIDE)
    return n_chan == 4 and n_clip == 8 and share == LANES and frames == 2 * SEG


def gelu(z):
    return 0.5 * z * (1.0 + jnp.tanh(GELU_A * (z + GELU_B * z * z * z)))


def gelu_both(z):
    square = z * z
    t = jnp.tanh(GELU_A * (z + GELU_B * square * z))
    slope = 0.5 * (1.0 + t) + 0.5 * z * (1.0 - t * t) * (GELU_A * (1.0 + 3.0 * GELU_B * square))
    return 0.5 * z * (1.0 + t), slope


def real_columns(shape):
    return lax.rem(lax.broadcasted_iota(jnp.int32, shape, len(shape) - 2), 8) < SIDE


def real(values):
    return jnp.where(real_columns(values.shape), values, 0.0)


def fold(values):
    return jnp.sum(values.reshape(-1, 8, values.shape[-1]), axis=0)


def tiles(values):
    return values.reshape(SIDE, 8, values.shape[-1])


def flat(values):
    return values.reshape(FRAME, values.shape[-1])


def row_pad(v, reach):
    zeros = jnp.zeros((reach,) + v.shape[1:], v.dtype)
    return jnp.concatenate([zeros, v, zeros], axis=0)


def col_shift(v, step):
    if step == 0:
        return v
    moved = pltpu.roll(v, (-step) % 8, v.ndim - 2)
    if abs(step) == 2:
        place = lax.broadcasted_iota(jnp.int32, v.shape, v.ndim - 2)
        moved = jnp.where(place < 6 if step > 0 else place >= 2, moved, 0.0)
    return moved


def dw_tiles(v, taps, reach, sign):
    padded = row_pad(v, reach)
    total = None
    for b in (-1, 0, 1):
        part = None
        for a in (-1, 0, 1):
            start = reach + sign * reach * a
            term = taps[3 * (a + 1) + b + 1] * padded[start : start + SIDE]
            part = term if part is None else part + term
        part = col_shift(part, sign * reach * b)
        total = part if total is None else total + part
    return total


def dot(left, right, left_dim=1, right_dim=0):
    return lax.dot_general(
        left, right, (((left_dim,), (right_dim,)), ((), ())), preferred_element_type=jnp.float32
    )


class Refs(NamedTuple):
    x_hbm: Any
    cot_hbm: Any
    wred_hbm: Any
    wconv_hbm: Any
    wexp_hbm: Any
    bnd: Any
    gi: Any
    bi: Any
    go: Any
    bo: Any
    dk: Any
    gb: Any
    act_out: Any
    gin_out: Any
    ggi: Any
    gbi: Any
    ggo: Any
    gbo: Any
    gk_out: Any
    ggb_out: Any
    gc_out: Any
    ge_out: Any
    gr_out: Any
    x: Any
    cot: Any
    wr0: Any
    wrf: Any
    wef: Any
    wc: Any
    dkb: Any
    red: Any
    hid: Any
    sig: Any
    conv: Any
    mixf: Any
    inf: Any
    ex: Any
    out0: Any
    act: Any
    y: Any
    gpre: Any
    gin: Any
    gexp: Any
    gs: Any
    pb: Any
    ysend: Any
    rcore: Any
    ryy: Any
    grf: Any
    gm: Any
    gd: Any
    g1: Any
    gk: Any
    kst: Any
    stn: Any
    stw: Any
    gc: Any
    geo: Any
    ge: Any
    gro: Any
    gr: Any
    xc: Any
    xe: Any
    xr: Any
    zc: Any
    ze: Any
    zr: Any
    fc: Any
    fe: Any
    fr: Any
    ssem: Any
    rsem: Any
    lsem: Any


PIECES = (3, 2, 2)
ARRIVALS = 40 + 12 * sum(PIECES)
TURN, EXPAND, REDUCE, SUMS, CHAN, TAPS = range(-6, 0)
PLAN = {
    (1, 5): (
        111, 110,
    ),
    (1, 6): (
        101,
    ),
    (1, 7): (
        111, 110,
    ),
    (1, 8): (
        111,
    ),
    (1, 9): (
        101, 100, 102, 110,
    ),
    (1, 10): (
        111,
    ),
    (1, 11): (
        101,
    ),
    (1, 12): (
        100, 110,
    ),
    (1, 13): (
        111,
    ),
    (0, 0): (
        111, 101, 100, 102, 110,
    ),
    (0, 1): (
        120, 121,
    ),
    (0, 2): (
        111, 101, 102,
    ),
    (0, 3): (
        120, 110,
    ),
    (0, 4): (
        101, 100, 120, 102, 121, 110,
    ),
    (0, 5): (
        10, 11,
    ),
    (0, 6): (
        101, 100, 1, 120, 10, 102, 121, 0, 2,
    ),
    (0, 7): (
        11,
    ),
    (0, 8): (
        1, 120,
    ),
    (0, 9): (
        100, 1, 10, 102, 121, 0, 11,
    ),
    (0, 10): (
        2,
    ),
    (0, 11): (
        1, 120, 21, 20, 100, 10, 0,
    ),
    (0, 12): (
        121,
    ),
    (0, 13): (
        102, 2, 11, 1, 120, 10, 21, 121,
    ),
    (0, 14): (
        0, 1, 2, 20, 10, 11, 21, 121, 0, 20, 1, 11, 2, 21, 10, 0, 20, 11, 2, 21, 0, 20, 21, 20, 2,
        21, 20,
    ),
}


def fused_kernel(n_clip, n_chan, pixel_total, *refs):
    r = Refs(*refs)
    rows, cs = r.cot.shape
    ib = LANES
    frames = rows // PIXELS
    chunk = frames // 2 * FRAME
    n_z = n_clip // 2
    first = -(-rows // 32) * 16
    starts, counts = (0, first), (first, rows - first)
    bf16, f32 = jnp.bfloat16, jnp.float32
    clip = lax.axis_index("clip")
    chan = lax.axis_index("chan")
    core, high = lax.rem(chan, 2), lax.div(chan, 2)
    j_core = (1 - core) + 2 * high
    j_y = core + 2 * (1 - high)
    j_far = (1 - core) + 2 * (1 - high)
    others = (j_core, j_y, j_far)
    z, side = lax.div(clip, 2), lax.rem(clip, 2)
    low, z_near, z_far = lax.rem(z, 2), z + 1 - 2 * lax.rem(z, 2), lax.rem(z + 2, 4)
    clip_others = [lax.rem(clip + d, n_clip) for d in range(1, n_clip)]

    def cols(j):
        return pl.ds(pl.multiple_of(j * ib, ib), ib)

    def wide(j):
        return pl.ds(pl.multiple_of(j * cs, cs), cs)

    def part(h):
        return pl.ds(h * chunk, chunk)

    def raw(h):
        return pl.ds(starts[h], counts[h])

    def spans(total):
        tiles_left, at, chunks = total // 16, 0, []
        for left in range(4, 0, -1):
            take = -(-tiles_left // left)
            chunks.append((at * 16, take * 16))
            at, tiles_left = at + take, tiles_left - take
        return chunks

    raw_spans, padded_spans = spans(rows), spans(frames * FRAME)

    places, in_flight = {}, {}
    counters = SimpleNamespace(send=0, load=0, phase=0, sums=0, out=0)

    def arrival(key):
        return r.rsem.at[places.setdefault(key, len(places))]

    def sent(index):
        if index in in_flight:
            in_flight.pop(index).wait_send()

    def remote(src, dst, target, key):
        index = counters.send % SENDS
        counters.send += 1
        sent(index)
        made = pltpu.make_async_remote_copy(
            src_ref=src,
            dst_ref=dst,
            send_sem=r.ssem.at[index],
            recv_sem=arrival(key),
            device_id=target,
            device_id_type=MESH,
        )
        made.start()
        in_flight[index] = made
        return made, index

    def arrive(place, key):
        pltpu.make_async_remote_copy(
            src_ref=place,
            dst_ref=place,
            send_sem=r.ssem.at[0],
            recv_sem=arrival(key),
            device_id=(clip, j_core),
            device_id_type=MESH,
        ).wait_recv()

    def local(src, dst, index=None):
        if index is None:
            index = counters.load
            counters.load += 1
        made = pltpu.make_async_copy(src, dst, r.lsem.at[index])
        made.start()
        return made

    outgoing = {}

    def write_out(src, dst):
        turn = counters.out % 8
        counters.out += 1
        if turn in outgoing:
            outgoing.pop(turn).wait()
        outgoing[turn] = local(src, dst, LOADS - 8 + turn)

    load_wr0 = local(r.wred_hbm.at[0], r.wr0)
    load_x = [local(r.x_hbm.at[raw(h)], r.x.at[raw(h)]) for h in range(2)]
    load_we = [
        local(r.wexp_hbm.at[s, :, wide(chan)], r.wef.at[s, cols(chan)]) for s in range(2)
    ]
    load_wr = [
        local(r.wred_hbm.at[s, wide(chan)], r.wrf.at[s, :, cols(chan)]) for s in range(2)
    ]
    load_wc = []
    for s in range(2):
        index = counters.load
        counters.load += 1
        for tap in range(9):
            local(r.wconv_hbm.at[s, tap], r.wc.at[s, :, tap * ib : (tap + 1) * ib], index)
        load_wc.append(pltpu.make_async_copy(r.wc.at[s], r.wc.at[s], r.lsem.at[index]))
    load_cot = local(r.cot_hbm.at[:, wide(chan)], r.cot)

    barrier = pltpu.get_barrier_semaphore()
    for target in clip_others:
        pl.semaphore_signal(barrier, inc=1, device_id=(target, chan), device_id_type=MESH)
    for target in others:
        pl.semaphore_signal(barrier, inc=1, device_id=(clip, target), device_id_type=MESH)

    def share_we(s, half):
        size = ib // 2
        for j in others:
            here = r.wexp_hbm.at[s, pl.ds(half * size, size), wide(j)]
            target = r.wef.at[s, pl.ds(pl.multiple_of(chan * ib + half * size, size), size)]
            remote(here, target, (clip, j), (EXPAND, s))

    def share_wr(s, half):
        size = cs // 2
        for j in others:
            here = r.wred_hbm.at[s, pl.ds(pl.multiple_of(j * cs + half * size, size), size)]
            target = r.wrf.at[s, pl.ds(half * size, size), cols(chan)]
            remote(here, target, (clip, j), (REDUCE, s))

    def shared_we(s):
        load_we[s].wait()
        arrive(r.wef.at[s, pl.ds(0, (n_chan - 1) * ib)], (EXPAND, s))

    def shared_wr(s):
        load_wr[s].wait()
        arrive(r.wrf.at[s, :, pl.ds(0, (n_chan - 1) * ib)], (REDUCE, s))

    def stat_start(buf, slot, values):
        for k, value in enumerate(values):
            buf[slot, clip, k : k + 1, :] = jnp.sum(value, axis=0, keepdims=True)
        key = (SUMS, counters.sums % 2)
        counters.sums += 1
        for t in clip_others:
            remote(buf.at[slot, clip], buf.at[slot, clip], (t, chan), key)
        return key

    def stat_end(buf, slot, key):
        arrive(buf.at[slot, pl.ds(0, n_clip - 1)], key)
        total = buf[slot, 0]
        for k in range(1, n_clip):
            total = total + buf[slot, k]
        return total[0:1], total[1:2]

    def moments(pair):
        mean = pair[0] / pixel_total
        return mean, lax.rsqrt(pair[1] / pixel_total - mean * mean + epsilon)

    def phase_keys(count):
        turn = counters.phase % 2
        counters.phase += 1
        return [[(CHAN, turn, k, i) for i in range(3)] for k in range(count)]

    def gather_start(full, at, key):
        mine = full.at[at, cols(chan)]
        remote(mine, mine, (clip, j_y), key[0])
        remote(mine, mine, (clip, j_core), key[1])

    def gather_pass(full, at, key):
        theirs = full.at[at, cols(j_y)]
        arrive(theirs, key[0])
        remote(theirs, theirs, (clip, j_core), key[2])

    def gather_end(full, at, key):
        arrive(full.at[at, cols(j_core)], key[1])
        arrive(full.at[at, cols(j_far)], key[2])

    def pair(value):
        return pl.ds(pl.multiple_of(value * 2 * ib, 2 * ib), 2 * ib)

    def scatter_value(slot, at):
        mine = r.pb[at, cols(chan)].astype(f32)
        return mine + r.rcore[slot, 0, at].astype(f32) + r.ryy[slot, at].astype(f32)

    def keep_flag(f):
        return 1.0 - r.bnd[lax.div(f, SEG), lax.rem(f, SEG)].astype(f32)

    def taps_of(index):
        return [r.dkb[9 * index + tap] for tap in range(9)]

    def pair_rows(h, i):
        return pl.ds(pl.multiple_of(h * chunk + i * PAIR, 16), PAIR)

    def frame_rows(f):
        return pl.ds(pl.multiple_of(f * FRAME, 8), FRAME)

    def spread(ref, f):
        return jnp.stack(
            [ref[pl.ds(f * PIXELS + SIDE * k, 8), :] for k in range(SIDE)], axis=0
        )

    def squeeze(ref, f, value):
        for k in range(SIDE):
            ref[pl.ds(f * PIXELS + SIDE * k, 8), :] = value[k]

    pairs = frames // 4
    carried = {}
    zero_n = jnp.zeros((8, ib), f32)
    zero_w = jnp.zeros((8, cs), f32)

    def each(start, count, step, one, begin):
        def at_step(i, carry):
            return one(pl.ds(pl.multiple_of(start + i * step, 16), step), carry)

        return lax.fori_loop(0, count // step, at_step, begin)

    def narrow(start, count, one, begin):
        step = next(n for n in (112, 96, 80, 64, 48, 32, 16) if count % n == 0)
        return each(start, count, step, one, begin)

    def broad(k, one, begin):
        return each(*raw_spans[k], 16, one, begin)

    moments_in = [[None, None, None], [None, None, None]]

    def row(ref, s, k=None):
        return ref[s, k : k + 1, :] if k is not None else ref[s : s + 1, wide(chan)]

    def norm_inner(s, k, x):
        mean, inv = moments_in[s][k]
        centred = (x - mean) * inv
        return centred, centred * row(r.gi, s, k) + row(r.bi, s, k)

    def norm_outer(s, x):
        mean, inv = moments_in[s][2]
        centred = (x - mean) * inv
        return centred, centred * row(r.go, s) + row(r.bo, s)

    def inner_input(s, at):
        return r.x[at, wide(chan)] if s == 0 else r.out0[at]

    def temporal_forward(s, k):
        h, first_pair = k // 2, k % 2 * (pairs // 2)

        def hide(i, _):
            f = h * (frames // 2) + i
            value = real(gelu(norm_inner(s, 0, spread(r.red.at[s], f))[1]))
            r.hid[s, frame_rows(f)] = flat(value)
            return _

        if first_pair == 0:
            lax.fori_loop(0, frames // 2, hide, 0)

        def mix(i, before):
            base = pl.multiple_of(h * chunk + i * PAIR, 16)
            last = jnp.minimum(base + PAIR, (h + 1) * chunk - FRAME)
            f = h * (frames // 2) + 2 * i
            h0 = tiles(r.hid[s, pl.ds(base, FRAME)])
            h1 = tiles(r.hid[s, pl.ds(base + FRAME, FRAME)])
            h2 = tiles(r.hid[s, pl.ds(pl.multiple_of(last, 8), FRAME)])
            e0 = keep_flag(f) * (h1 - h0)
            e1 = keep_flag(f + 1) * (h2 - h1)
            if s == 0:
                taps = taps_of(0)
                m0 = real(h0 + dw_tiles(e0 + before, taps, 1, 1))
                m1 = real(h1 + dw_tiles(e1 + e0, taps, 1, 1))
            else:
                near, far = taps_of(1), taps_of(2)
                mixed = []
                for k, (hk, ek) in enumerate(((h0, e0), (h1, e1))):
                    logits = dw_tiles(ek, near, 1, 1) + dw_tiles(ek, far, 2, 1) + r.gb[...]
                    gate = 0.5 * (1.0 + jnp.tanh(0.5 * logits))
                    r.sig[pl.ds(base + k * FRAME, FRAME)] = flat(gate)
                    mixed.append(hk + hk * gate)
                m0, m1 = mixed
            both = jnp.concatenate([flat(m0), flat(m1)], axis=0).astype(bf16)
            r.mixf[s, pl.ds(base, PAIR), cols(chan)] = both
            return e1

        before = carried.get(s) if first_pair else jnp.zeros((SIDE, 8, ib), f32)
        carried[s] = lax.fori_loop(first_pair, first_pair + pairs // 2, mix, before, unroll=True)

    def conv_forward(s, k, sums):
        r.y[...] = dot(r.mixf[s, pl.ds(*padded_spans[k])], r.wc[s])

        def add_taps(i, sums):
            at = pl.ds(pl.multiple_of(i * FRAME, 8), FRAME)
            total = None
            for b in (-1, 0, 1):
                run = None
                for a in (-1, 0, 1):
                    tap = 3 * (a + 1) + b + 1
                    term = row_pad(tiles(r.y[at, tap * ib : (tap + 1) * ib]), 1)
                    term = term[1 + a : 1 + a + SIDE]
                    run = term if run is None else run + term
                run = col_shift(run, b)
                total = run if total is None else total + run
            total = real(total)
            squeeze(r.conv.at[s], k * (frames // 4) + i, total)
            return sums[0] + jnp.sum(total, axis=0), sums[1] + jnp.sum(total * total, axis=0)

        return lax.fori_loop(0, frames // 4, add_taps, sums, unroll=True)

    def forward(s, stat_base, wide_slot):
        keys = phase_keys(4)
        quarters = [pl.ds(*span) for span in padded_spans]
        for k in range(4):
            temporal_forward(s, k)
            gather_start(r.mixf.at[s], quarters[k], keys[k])
            if k > 0:
                gather_pass(r.mixf.at[s], quarters[k - 1], keys[k - 1])
        sums = (zero_n, zero_n)
        load_wc[s].wait()
        for k in range(4):
            gather_end(r.mixf.at[s], quarters[k], keys[k])
            if k == 0:
                gather_pass(r.mixf.at[s], quarters[3], keys[3])
            sums = conv_forward(s, k, sums)
        made = stat_start(r.stn, stat_base, sums)
        yield
        moments_in[s][1] = moments(stat_end(r.stn, stat_base, made))
        keys = phase_keys(2)
        for h in range(2):

            def inside(at, _):
                value = gelu(norm_inner(s, 1, r.conv[s, at])[1])
                r.inf[s, at, cols(chan)] = value.astype(bf16)
                return _

            narrow(starts[h], counts[h], inside, 0)
            gather_start(r.inf.at[s], raw(h), keys[h])
        yield
        gather_pass(r.inf.at[s], raw(0), keys[0])
        gather_pass(r.inf.at[s], raw(1), keys[1])
        sums = (zero_w, zero_w)
        for h in range(2):
            gather_end(r.inf.at[s], raw(h), keys[h])
            value = dot(r.inf[s, raw(h)], r.wef[s])
            r.ex[s, raw(h)] = value
            sums = (sums[0] + fold(value), sums[1] + fold(value * value))
        made = stat_start(r.stw, wide_slot, sums)
        yield
        moments_in[s][2] = moments(stat_end(r.stw, wide_slot, made))

    def spread_taps():
        for index in range(3):
            for tap in range(9):
                r.dkb[9 * index + tap] = jnp.broadcast_to(r.dk[tap, index : index + 1, :], (8, ib))

    def clear(i, _):
        r.gk[i] = zero_n
        return _

    for s in range(2):
        r.red[s, rows : rows + 8] = zero_n

    sums = (zero_n, zero_n)
    load_wr0.wait()
    for h in range(2):
        load_x[h].wait()
        value = dot(r.x[raw(h)], r.wr0[...])
        r.red[0, raw(h)] = value
        sums = (sums[0] + fold(value), sums[1] + fold(value * value))
    pl.semaphore_wait(barrier, n_clip - 1 + n_chan - 1)
    made = stat_start(r.stn, 0, sums)
    share_we(0, 0)
    share_we(0, 1)
    spread_taps()
    lax.fori_loop(0, r.gk.shape[0], clear, 0)
    moments_in[0][0] = moments(stat_end(r.stn, 0, made))

    stage = forward(0, 1, 0)
    next(stage)
    share_wr(1, 0)
    next(stage)
    shared_we(0)
    next(stage)
    share_wr(1, 1)
    for _ in stage:
        pass

    def out_zero(at, _):
        z = norm_outer(0, r.ex[0, at])[1] + inner_input(0, at).astype(f32)
        r.out0[at] = gelu(z).astype(bf16)
        return _


    def scatter_all(slot, chunks, prepare, product, use, beside=None, midway=None):
        keys = phase_keys(4)
        ats = [pl.ds(*span) for span in chunks]
        borrowed = []

        def start(k, away):
            if away:
                prepare(k)
            two = pair(1 - high if away else high)
            r.pb[ats[k], two] = product(ats[k], two).astype(bf16)
            block, index = (j_far, 1) if away else (j_core, 0)
            target = r.rcore.at[slot, index, ats[k]]
            made = remote(r.pb.at[ats[k], cols(block)], target, (clip, j_core), keys[k][index])
            borrowed.append(made[1])

        def hand_on(k):
            at = ats[k]
            arrive(r.rcore.at[slot, 1, at], keys[k][1])
            both = r.pb[at, cols(j_y)].astype(f32) + r.rcore[slot, 1, at].astype(f32)
            r.ysend[slot % 2, at] = both.astype(bf16)
            made = remote(r.ysend.at[slot % 2, at], r.ryy.at[slot, at], (clip, j_y), keys[k][2])
            borrowed.append(made[1])

        start(0, True)
        start(1, True)
        hand_on(0)
        start(2, True)
        hand_on(1)
        start(3, True)
        hand_on(2)
        start(0, False)
        hand_on(3)
        for k in range(1, 4):
            start(k, False)
        if beside is not None:
            beside()
        for k in range(4):
            arrive(r.rcore.at[slot, 0, ats[k]], keys[k][0])
            arrive(r.ryy.at[slot, ats[k]], keys[k][2])
            use(*chunks[k])
            if midway is not None and k == 1:
                midway()
        for index in borrowed:
            sent(index)

    held = SimpleNamespace(sums=(zero_n, zero_n))

    def use_reduced(begin, count):
        at = pl.ds(begin, count)
        value = scatter_value(0, at)
        r.red[1, at] = value
        held.sums = (held.sums[0] + fold(value), held.sums[1] + fold(value * value))

    shared_wr(1)
    scatter_all(
        0,
        raw_spans,
        lambda k: broad(k, out_zero, 0),
        lambda at, two: dot(r.out0[at], r.wrf[1, :, two]),
        use_reduced,
    )
    made = stat_start(r.stn, 2, held.sums)
    share_we(1, 0)
    moments_in[1][0] = moments(stat_end(r.stn, 2, made))
    stage = forward(1, 3, 1)
    next(stage)
    share_we(1, 1)
    next(stage)
    shared_we(1)
    next(stage)
    share_wr(0, 0)
    share_wr(0, 1)
    for _ in stage:
        pass

    load_cot.wait()

    def out_one(at, sums):
        centred, z = norm_outer(1, r.ex[1, at])
        value, slope = gelu_both(z + r.out0[at].astype(f32))
        r.act[at] = value.astype(bf16)
        grad = r.cot[at].astype(f32) * slope
        r.gpre[at] = grad
        return sums[0] + fold(grad), sums[1] + fold(grad * centred)

    def top_zero(at, sums):
        centred, z = norm_outer(0, r.ex[0, at])
        grad = r.gin[at] * gelu_both(z + inner_input(0, at).astype(f32))[1]
        r.gpre[at] = grad
        return sums[0] + fold(grad), sums[1] + fold(grad * centred)

    top_sums = SimpleNamespace()

    def backward(s, stat_base, wide_slot, slot):
        if s == 1:
            top_sums.now = (zero_w, zero_w)
            for k in range(4):
                top_sums.now = broad(k, out_one, top_sums.now)
        sums = top_sums.now
        made = stat_start(r.stw, wide_slot, sums)
        if s == 1:
            write_out(r.act, r.act_out)
        service(s, 0)
        shift_sum, gain_sum = stat_end(r.stw, wide_slot, made)
        r.gbo[s : s + 1] = shift_sum
        r.ggo[s : s + 1] = gain_sum
        mean, inv = moments_in[s][2]
        scale = inv * row(r.go, s)
        shift_mean, gain_mean = shift_sum / pixel_total, gain_sum / pixel_total

        def expand_back(at, _):
            centred = (r.ex[s, at] - mean) * inv
            grad = scale * (r.gpre[at] - (shift_mean + centred * gain_mean))
            r.gexp[at] = grad.astype(bf16)
            return _

        held.sums = (zero_n, zero_n)
        service(s, 1)

        def weight_expand():
            value = dot(r.inf[s], r.gexp[...], 0, 0).astype(bf16)
            r.geo[s] = value.reshape(r.geo.shape[1:])
            place = r.ge.at[s, :, :, :, wide(chan)]
            turned[1, s] = local(r.geo.at[s, chan], place)
            for j in others:
                remote(r.geo.at[s, j], place, (clip, j), (TURN, 1, s))
            service(s, 2)

        def use_inner(begin, count):
            def one(at, sums):
                centred, z = norm_inner(s, 1, r.conv[s, at])
                grad = scatter_value(slot, at) * gelu_both(z)[1]
                r.g1[at] = grad
                return sums[0] + fold(grad), sums[1] + fold(grad * centred)

            held.sums = narrow(begin, count, one, held.sums)

        scatter_all(
            slot,
            raw_spans,
            lambda k: broad(k, expand_back, 0),
            lambda at, two: dot(r.gexp[at], r.wef[s, two], 1, 1),
            use_inner,
            weight_expand,
            lambda: service(s, 3),
        )
        made = stat_start(r.stn, stat_base, held.sums)
        service(s, 4)
        shift_sum, gain_sum = stat_end(r.stn, stat_base, made)
        r.gbi[s, 1:2] = shift_sum
        r.ggi[s, 1:2] = gain_sum
        mean, inv = moments_in[s][1]
        scale = inv * row(r.gi, s, 1)
        shift_mean, gain_mean = shift_sum / pixel_total, gain_sum / pixel_total

        def conv_back(i, _):
            at = pair_rows(0, i)
            halves = []
            for f in (2 * i, 2 * i + 1):
                centred = (spread(r.conv.at[s], f) - mean) * inv
                grad = scale * (spread(r.g1, f) - (shift_mean + centred * gain_mean))
                halves.append(real(grad))
            for b in (-1, 0, 1):
                moved = [row_pad(col_shift(v, -b), 1) for v in halves]
                for a in (-1, 0, 1):
                    tap = 3 * (a + 1) + b + 1
                    both = jnp.concatenate([flat(v[1 - a : 1 - a + SIDE]) for v in moved], axis=0)
                    r.gs[at, tap * ib : (tap + 1) * ib] = both.astype(bf16)
            return _


        service(s, 5)

        def weight_conv():
            for k in range(3):
                taps = slice(3 * k * ib, 3 * (k + 1) * ib)
                value = dot(r.mixf[s], r.gs[:, taps], 0, 0).astype(bf16)
                r.gc[s, :, :, :, taps] = value.reshape(r.gc.shape[1:4] + (3 * ib,))
            service(s, 6)

        def use_mixed(begin, count):
            def one(at, _):
                r.gm[at] = real(scatter_value(slot + 1, at))
                return _

            narrow(begin, count, one, 0)

        scatter_all(
            slot + 1,
            padded_spans,
            lambda k: lax.fori_loop(k * pairs // 2, (k + 1) * pairs // 2, conv_back, 0, unroll=True),
            lambda at, two: dot(r.gs[at], r.wc[s, two], 1, 1),
            use_mixed,
            weight_conv,
            lambda: service(s, 7),
        )

        def tap_sums(grad, v, index, reach):
            for b in (-1, 0, 1):
                padded = row_pad(col_shift(v, reach * b), reach)
                for a in (-1, 0, 1):
                    start = reach + reach * a
                    place = 9 * index + 3 * (a + 1) + b + 1
                    r.gk[place] = r.gk[place] + jnp.sum(grad * padded[start : start + SIDE], axis=0)

        def mix_back(f, before):
            at = frame_rows(f)
            following = frame_rows(jnp.minimum(f + 1, frames - 1))
            here = tiles(r.hid[s, at])
            step = keep_flag(f) * (tiles(r.hid[s, following]) - here)
            grad = tiles(r.gm[at])
            if s == 0:
                r.gd[at] = flat(dw_tiles(grad, taps_of(0), 1, -1))
                tap_sums(grad, step + before, 0, 1)
            else:
                gate = tiles(r.sig[at])
                grad = grad * here * gate * (1.0 - gate)
                r.gd[at] = flat(dw_tiles(grad, taps_of(1), 1, -1) + dw_tiles(grad, taps_of(2), 2, -1))
                tap_sums(grad, step, 1, 1)
                tap_sums(grad, step, 2, 2)
                r.gk[27] = r.gk[27] + jnp.sum(grad, axis=0)
            return step

        lax.fori_loop(0, frames, mix_back, jnp.zeros((SIDE, 8, ib), f32))

        service(s, 8)

        def hide_back(f, sums):
            at = frame_rows(f)
            previous = frame_rows(jnp.maximum(f - 1, 0))
            keep = keep_flag(f)
            keep_before = jnp.where(f > 0, keep_flag(jnp.maximum(f - 1, 0)), 0.0)
            now = r.gd[at]
            earlier = r.gd[previous]
            grad = r.gm[at]
            if s == 0:
                following = frame_rows(jnp.minimum(f + 1, frames - 1))
                later = now + r.gd[following]
                earlier = earlier + now
            else:
                later = now
                grad = grad * (1.0 + r.sig[at])
            grad = grad + keep_before * earlier - keep * later
            centred, z = norm_inner(s, 0, spread(r.red.at[s], f))
            grad = real(tiles(grad) * gelu_both(z)[1])
            squeeze(r.g1, f, grad)
            return sums[0] + jnp.sum(grad, axis=0), sums[1] + jnp.sum(grad * centred, axis=0)

        sums = lax.fori_loop(0, frames, hide_back, (zero_n, zero_n))
        made = stat_start(r.stn, stat_base + 1, sums)
        service(s, 9)
        shift_sum, gain_sum = stat_end(r.stn, stat_base + 1, made)
        r.gbi[s, 0:1] = shift_sum
        r.ggi[s, 0:1] = gain_sum
        mean, inv = moments_in[s][0]
        scale = inv * row(r.gi, s, 0)
        shift_mean, gain_mean = shift_sum / pixel_total, gain_sum / pixel_total
        service(s, 10)
        keys = phase_keys(4)
        quarters = [pl.ds(*span) for span in raw_spans]

        def reduce_back(at, _):
            centred = (r.red[s, at] - mean) * inv
            grad = scale * (r.g1[at] - (shift_mean + centred * gain_mean))
            r.grf[s, at, cols(chan)] = grad.astype(bf16)
            return _

        for k in range(4):
            narrow(*raw_spans[k], reduce_back, 0)
            gather_start(r.grf.at[s], quarters[k], keys[k])
        if s == 0:
            own = r.grf[0, :, cols(chan)]
            for piece in range(n_chan):
                value = dot(r.x[:, piece * cs : (piece + 1) * cs], own, 0, 0).astype(bf16)
                r.gr[0, piece] = value.reshape(r.gr.shape[2:])
        service(s, 11)
        gather_pass(r.grf.at[s], quarters[0], keys[0])
        gather_pass(r.grf.at[s], quarters[1], keys[1])
        if s == 0:
            shared_wr(0)
        else:
            top_sums.now = (zero_w, zero_w)
        for k in range(4):
            at = quarters[k]
            gather_end(r.grf.at[s], at, keys[k])
            r.gin[at] = dot(r.grf[s, at], r.wrf[s], 1, 1) + r.gpre[at]
            if k < 2:
                gather_pass(r.grf.at[s], quarters[k + 2], keys[k + 2])
            if s == 0:
                write_out(r.gin.at[at], r.gin_out.at[at])
            else:
                top_sums.now = broad(k, top_zero, top_sums.now)
            if k == 1:
                service(s, 12)
        service(s, 13)
        if s == 1:
            value = dot(r.out0[...], r.grf[1], 0, 0).astype(bf16)
            r.gro[...] = value.reshape(r.gro.shape)
            place = r.gr.at[1, chan]
            turned[2, 1] = local(r.gro.at[:, :, cols(chan)], place)
            for j in others:
                remote(r.gro.at[:, :, cols(j)], place, (clip, j), (TURN, 2, 1))

    turned = {}

    def reduce_task(kind, s, line, place):
        ref, from_side, from_z, result = kinds[kind]
        mine, done = ref.at[s, :, :, line, place], result.at[s, :, :, line, place]
        side_in, z_in = from_side.at[s, :, line, place], from_z.at[s, :, line, place]
        across = (2 * z + 1 - side, chan)
        key = (kind, s, line.start, place.start)
        if (kind, s) in turned:
            turned.pop((kind, s)).wait()
            three = pl.ds(0, (n_chan - 1) * cs)
            arrive(
                r.ge.at[s, :, :, :, three] if kind == 1 else r.gr.at[s, pl.ds(0, n_chan - 1)],
                (TURN, kind, s),
            )
        near, far = (2 * z_near + side, chan), (2 * z_far + side, chan)

        def add(k, term):
            both = ref[s, k, side, line, place].astype(f32) + term.astype(f32)
            return both.astype(bf16)

        remote(mine.at[:, 1 - side], side_in, across, key + (0,))
        yield
        arrive(side_in, key + (0,))
        for k in range(n_z):
            ref[s, k, side, line, place] = add(k, from_side[s, k, line, place])
        for k in range(2):
            remote(mine.at[1 - low + 2 * k, side], z_in.at[k], near, key + (1,))
        yield
        arrive(z_in.at[pl.ds(0, 2)], key + (1,))
        for k in range(2):
            ref[s, low + 2 * k, side, line, place] = add(low + 2 * k, from_z[s, k, line, place])
        remote(mine.at[z_far, side], z_in.at[2], far, key + (2,))
        yield
        arrive(z_in.at[2], key + (2,))
        result[s, z, side, line, place] = add(z, from_z[s, 2, line, place])
        remote(done.at[z, side], done.at[z, side], far, key + (3,))
        yield
        arrive(done.at[z_far, side], key + (3,))
        for k in (z, z_far):
            remote(done.at[k, side], done.at[k, side], near, key + (4,))
        yield
        arrive(done.at[pl.ds(0, 2), side], key + (4,))
        remote(done.at[:, side], done.at[:, side], across, key + (5,))
        yield
        arrive(done.at[:, 1 - side], key + (5,))
        if kind == 0:
            base = place.start // ib
            for k in range((place.stop - place.start) // ib):
                here = r.fc.at[s, :, :, :, (base + k) * ib : (base + k + 1) * ib]
                write_out(here, r.gc_out.at[s, base + k])
        else:
            out = (None, r.ge_out, r.gr_out)[kind]
            write_out(done, out.at[s, :, :, line, place])
        yield

    kinds = (
        (r.gc, r.xc, r.zc, r.fc),
        (r.ge, r.xe, r.ze, r.fe),
        (r.gr, r.xr, r.zr, r.fr),
    )
    def cut(size, count):
        return [slice(k * (size // count), (k + 1) * (size // count)) for k in range(count)]

    tasks = {}
    for s in range(2):
        for k, place in enumerate(cut(9 * ib, PIECES[0])):
            tasks[100 * s + k] = reduce_task(0, s, slice(0, r.gc.shape[3]), place)
        for k, place in enumerate(cut(r.ge.shape[4], PIECES[1])):
            tasks[100 * s + 10 + k] = reduce_task(1, s, slice(0, r.ge.shape[3]), place)
        for k, line in enumerate(cut(r.gr.shape[3], PIECES[2])):
            tasks[100 * s + 20 + k] = reduce_task(2, s, line, slice(0, ib))

    def advance(*steps):
        for step in steps:
            next(tasks[step])

    def service(s, point):
        advance(*PLAN.get((s, point), ()))

    backward(1, 4, 2, 1)
    backward(0, 6, 3, 3)

    for place in range(r.gk.shape[0]):
        r.kst[clip, place : place + 1, :] = jnp.sum(r.gk[place], axis=0, keepdims=True)
    for t in clip_others:
        remote(r.kst.at[clip], r.kst.at[clip], (t, chan), TAPS)
    service(0, 14)
    arrive(r.kst.at[pl.ds(0, n_clip - 1)], TAPS)
    total = r.kst[0]
    for k in range(1, n_clip):
        total = total + r.kst[k]
    for index in range(3):
        for tap in range(9):
            place = 9 * index + tap
            r.gk_out[tap, index : index + 1, :] = total[place : place + 1]
    r.ggb_out[...] = total[27:28]
    for copy in outgoing.values():
        copy.wait()
    for index in list(in_flight):
        sent(index)
    assert len(places) <= ARRIVALS and counters.load <= LOADS - 8


def fused_call(n_clip, n_chan, pixel_total, *operands):
    rows, width = operands[0].shape
    cs = width // n_chan
    ib = LANES
    inner = ib * n_chan
    n_z = n_clip // 2
    padded = rows // PIXELS * FRAME
    over = rows + 8
    bf16, f32 = jnp.bfloat16, jnp.float32
    whole = pl.BlockSpec(memory_space=pltpu.VMEM)
    anywhere = pl.BlockSpec(memory_space=pl.ANY)
    scalars = pl.BlockSpec(memory_space=pltpu.SMEM)
    shape = jax.ShapeDtypeStruct
    V = pltpu.VMEM
    scratch = dict(
        x=V((rows, width), bf16),
        cot=V((rows, cs), bf16),
        wr0=V((width, ib), bf16),
        wrf=V((2, cs, inner), bf16),
        wef=V((2, inner, cs), bf16),
        wc=V((2, inner, 9 * ib), bf16),
        dkb=V((27, 8, ib), f32),
        red=V((2, over, ib), f32),
        hid=V((2, padded, ib), f32),
        sig=V((padded, ib), f32),
        conv=V((2, over, ib), f32),
        mixf=V((2, padded, inner), bf16),
        inf=V((2, rows, inner), bf16),
        ex=V((2, rows, cs), f32),
        out0=V((rows, cs), bf16),
        act=V((rows, cs), bf16),
        y=V((padded // 4, 9 * ib), f32),
        gpre=V((rows, cs), f32),
        gin=V((rows, cs), f32),
        gexp=V((rows, cs), bf16),
        gs=V((padded, 9 * ib), bf16),
        pb=V((padded, inner), bf16),
        ysend=V((2, padded, ib), bf16),
        rcore=V((5, 2, padded, ib), bf16),
        ryy=V((5, padded, ib), bf16),
        grf=V((2, rows, inner), bf16),
        gm=V((padded, ib), f32),
        gd=V((padded, ib), f32),
        g1=V((over, ib), f32),
        gk=V((32, 8, ib), f32),
        kst=V((n_clip, 32, ib), f32),
        stn=V((8, n_clip, 2, ib), f32),
        stw=V((4, n_clip, 2, cs), f32),
        gc=V((2, n_z, 2, inner // n_clip, 9 * ib), bf16),
        geo=V((2, n_chan, n_z, 2, ib // n_clip, cs), bf16),
        ge=V((2, n_z, 2, ib // n_clip, width), bf16),
        gro=V((2, cs // 2, inner), bf16),
        gr=V((2, n_z, 2, width // n_clip, ib), bf16),
        fc=V((2, n_z, 2, inner // n_clip, 9 * ib), bf16),
        fe=V((2, n_z, 2, ib // n_clip, width), bf16),
        fr=V((2, n_z, 2, width // n_clip, ib), bf16),
        xc=V((2, n_z, inner // n_clip, 9 * ib), bf16),
        xe=V((2, n_z, ib // n_clip, width), bf16),
        xr=V((2, n_z, width // n_clip, ib), bf16),
        zc=V((2, n_z - 1, inner // n_clip, 9 * ib), bf16),
        ze=V((2, n_z - 1, ib // n_clip, width), bf16),
        zr=V((2, n_z - 1, width // n_clip, ib), bf16),
        ssem=pltpu.SemaphoreType.DMA((SENDS,)),
        rsem=pltpu.SemaphoreType.DMA((ARRIVALS,)),
        lsem=pltpu.SemaphoreType.DMA((LOADS,)),
    )
    return pl.pallas_call(
        partial(fused_kernel, n_clip, n_chan, pixel_total),
        out_shape=[
            shape((rows, cs), bf16),
            shape((rows, cs), f32),
            shape((2, 2, ib), f32),
            shape((2, 2, ib), f32),
            shape((2, cs), f32),
            shape((2, cs), f32),
            shape((9, 3, ib), f32),
            shape((1, ib), f32),
            shape((2, 9, n_z, 2, inner // n_clip, ib), bf16),
            shape((2, n_z, 2, ib // n_clip, width), bf16),
            shape((2, n_z, 2, width // n_clip, ib), bf16),
        ],
        in_specs=[anywhere] * 5 + [scalars] + [whole] * 6,
        out_specs=[anywhere] * 2 + [whole] * 6 + [anywhere] * 3,
        scratch_shapes=[scratch[name] for name in Refs._fields if name in scratch],
        compiler_params=pltpu.CompilerParams(
            collective_id=0, has_side_effects=True, vmem_limit_bytes=62 * 1024 * 1024
        ),
    )(*operands)


def finish_kernel(*refs):
    count = len(refs) // 2
    sources, results = refs[:count], refs[count:]
    for here, there in zip(sources[:5], results[:5]):
        there[...] = here[...].astype(there.dtype)

    @pl.when(pl.program_id(0) == 0)
    def _():
        for here, there in zip(sources[5:], results[5:]):
            there[...] = here[...]


def finish(steps, gc, ge, gr, act, gin, *small):
    arrays = [a.reshape(-1, a.shape[-1]) for a in (gc, ge, gr)] + [act, gin]
    blocks = [
        pl.BlockSpec((-(-a.shape[0] // (16 * steps)) * 16, a.shape[1]), lambda i: (i, 0))
        for a in arrays
    ]
    whole = [pl.BlockSpec(memory_space=pltpu.VMEM)] * len(small)
    shapes = [jax.ShapeDtypeStruct(a.shape, jnp.float32) for a in arrays[:3]]
    shapes += [jax.ShapeDtypeStruct(a.shape, a.dtype) for a in (act, gin, *small)]
    return pl.pallas_call(
        finish_kernel,
        grid=(steps,),
        out_shape=shapes,
        in_specs=blocks + whole,
        out_specs=blocks + whole,
        compiler_params=pltpu.CompilerParams(vmem_limit_bytes=62 * 1024 * 1024),
    )(*arrays, *small)


def fused(
    frames_in,
    boundary,
    w_reduce,
    gain_inner,
    bias_inner,
    w_conv,
    w_expand,
    gain_outer,
    bias_outer,
    depth_kernels,
    gate_bias,
    cotangent,
):
    n_clip, n_chan = lax.axis_size("clip"), lax.axis_size("chan")
    pixel_total = frames_in.shape[0] * n_clip
    act, gin, ggi, gbi, ggo, gbo, gk, ggb, gc, ge, gr = fused_call(
        n_clip,
        n_chan,
        float(pixel_total),
        frames_in,
        cotangent,
        w_reduce,
        w_conv,
        w_expand,
        boundary,
        gain_inner,
        bias_inner,
        gain_outer,
        bias_outer,
        depth_kernels.transpose(1, 0, 2),
        gate_bias.reshape(1, -1),
    )
    gc, ge, gr, act, gin, ggi, gbi, ggo, gbo, gk, ggb = finish(
        2, gc, ge, gr, act, gin, ggi, gbi, ggo, gbo, gk, ggb
    )
    return (
        act,
        gin,
        gr.reshape(w_reduce.shape),
        ggi,
        gbi,
        gc.reshape(w_conv.shape),
        ge.reshape(w_expand.shape),
        ggo,
        gbo,
        gk.transpose(1, 0, 2),
        ggb.reshape(-1),
    )


def solution(mesh):
    in_specs = (
        P("clip", None),
        P("clip", None),
        P(None, None, "chan"),
        P(None, None, "chan"),
        P(None, None, "chan"),
        P(None, None, None, "chan"),
        P(None, "chan", None),
        P(),
        P(),
        P(None, None, "chan"),
        P("chan"),
        P("clip", None),
    )
    out_specs = (
        P("clip", "chan"),
        P("clip", "chan"),
        P(None, None, "chan"),
        P(None, None, "chan"),
        P(None, None, "chan"),
        P(None, None, None, "chan"),
        P(None, "chan", None),
        P(None, "chan"),
        P(None, "chan"),
        P(None, None, "chan"),
        P("chan"),
    )

    def run(*arguments):
        fits = fused_fits(mesh, arguments[0].shape, arguments[2].shape)
        return jax.shard_map(fused if fits else body, mesh=mesh, in_specs=in_specs, out_specs=out_specs, check_vma=False)(*arguments)

    return run
```

```python
from functools import partial
from types import SimpleNamespace
from typing import Any, NamedTuple

import jax
import jax.numpy as jnp
from jax import lax
from jax.experimental import pallas as pl
from jax.experimental.pallas import tpu as pltpu
from jax.sharding import PartitionSpec as P

SEG = 8
SIDE = 7


epsilon = 1e-05


def framed(values):
    return values.reshape(-1, SIDE, SIDE, values.shape[-1])


def shifted(frame_grid, row_step, col_step, dilation):
    padded = jnp.pad(frame_grid, ((0, 0), (dilation, dilation), (dilation, dilation), (0, 0)))
    return padded[
        :,
        dilation + row_step : dilation + row_step + SIDE,
        dilation + col_step : dilation + col_step + SIDE,
        :,
    ]


def depthwise(values, kernel, dilation):
    frame_grid = framed(values)
    running = jnp.zeros_like(frame_grid)
    for tap_index in range(9):
        running = (
            running
            + shifted(
                frame_grid,
                (tap_index // 3 - 1) * dilation,
                (tap_index % 3 - 1) * dilation,
                dilation,
            )
            * kernel[tap_index]
        )
    return running.reshape(values.shape)


def patch_rows(values):
    frame_grid = framed(values)
    pieces = [
        shifted(frame_grid, tap_index // 3 - 1, tap_index % 3 - 1, 1) for tap_index in range(9)
    ]
    return jnp.concatenate(pieces, axis=-1).reshape(values.shape[0], 9 * values.shape[1])


def unpatch(grad_rows, chan_width):
    frame_grid = grad_rows.reshape(-1, SIDE, SIDE, 9, chan_width)
    running = jnp.zeros(frame_grid.shape[:3] + (chan_width,), jnp.float32)
    for tap_index in range(9):
        running = running + shifted(
            frame_grid[:, :, :, tap_index, :], 1 - tap_index // 3, 1 - tap_index % 3, 1
        )
    return running.reshape(-1, chan_width)


def neighbours(values, boundary):
    clip_count = boundary.shape[0]
    frame_grid = values.reshape(clip_count, SEG, SIDE * SIDE, values.shape[-1])
    stop_mask = (boundary == 1)[:, :, None, None]
    start_mask = jnp.concatenate([jnp.ones_like(stop_mask[:, :1]), stop_mask[:, :-1]], axis=1)
    after_seg = jnp.concatenate([frame_grid[:, 1:], frame_grid[:, -1:]], axis=1)
    before = jnp.concatenate([frame_grid[:, :1], frame_grid[:, :-1]], axis=1)
    later_seg = jnp.where(stop_mask, frame_grid, after_seg)
    earlier = jnp.where(start_mask, frame_grid, before)
    return (later_seg.reshape(values.shape), earlier.reshape(values.shape))


def temporal(values, kernels, gate_vec, boundary, short_range):
    later_seg, earlier = neighbours(values, boundary)
    if short_range:
        return values + depthwise(later_seg - earlier, kernels[0], 1)
    change = later_seg - values
    logits = depthwise(change, kernels[1], 1) + depthwise(change, kernels[2], 2) + gate_vec
    return values + values * jax.nn.sigmoid(logits)


def columns(values, col_start, col_share):
    return lax.dynamic_slice_in_dim(values, col_start, col_share, values.ndim - 1)


def contract(left, right, left_dim, right_dim):
    return lax.dot_general(
        left, right, (((left_dim,), (right_dim,)), ((), ())), preferred_element_type=jnp.float32
    )


def normalize(values, gain_vec, bias_vec, pixel_total):
    col_sum, sq_sum = lax.psum((jnp.sum(values, axis=0), jnp.sum(values * values, axis=0)), "clip")
    mean_val = col_sum / pixel_total
    inv_std = lax.rsqrt(sq_sum / pixel_total - mean_val * mean_val + epsilon)
    centred = (values - mean_val) * inv_std
    return (centred * gain_vec + bias_vec, centred, inv_std)


def normalize_back(grad_rows, centred, inv_std, gain_vec, pixel_total):
    shift_sum, gain_sum = lax.psum(
        (jnp.sum(grad_rows, axis=0), jnp.sum(grad_rows * centred, axis=0)), "clip"
    )
    grad_in = inv_std * gain_vec * (grad_rows - (shift_sum + centred * gain_sum) / pixel_total)
    return (grad_in, gain_sum, shift_sum)


def block_forward(inputs, boundary, weights, short_range, pixel_total):
    w_red, gain_pair, bias_pair, w_cv, w_ex, gain_out, bias_out, kernels, gate_vec = weights
    reduced = jnp.dot(inputs, w_red, preferred_element_type=jnp.float32)
    norm_one, centred_one, inv_one = normalize(reduced, gain_pair[0], bias_pair[0], pixel_total)
    hidden, gelu_one = jax.vjp(jax.nn.gelu, norm_one)
    mixed_act, mix_back = jax.vjp(
        partial(temporal, boundary=boundary, short_range=short_range), hidden, kernels, gate_vec
    )
    gathered = lax.all_gather(mixed_act.astype(jnp.bfloat16), "chan", axis=1, tiled=True)
    patches = patch_rows(gathered)
    conv_out = jnp.dot(
        patches, w_cv.reshape(-1, w_cv.shape[-1]), preferred_element_type=jnp.float32
    )
    norm_two, centred_two, inv_two = normalize(conv_out, gain_pair[1], bias_pair[1], pixel_total)
    inner_full, gelu_two = jax.vjp(jax.nn.gelu, norm_two)
    inner_act = inner_full.astype(jnp.bfloat16)
    partial_out = jnp.dot(inner_act, w_ex, preferred_element_type=jnp.float32)
    expanded = lax.psum(partial_out.astype(jnp.bfloat16), "chan").astype(jnp.float32)
    norm_three, centred_three, inv_three = normalize(expanded, gain_out, bias_out, pixel_total)
    output_full, gelu_three = jax.vjp(jax.nn.gelu, norm_three + inputs.astype(jnp.float32))
    kept_state = (
        centred_one,
        inv_one,
        gelu_one,
        mix_back,
        patches,
        centred_two,
        inv_two,
        gelu_two,
        inner_act,
        centred_three,
        inv_three,
        gelu_three,
        gain_out,
    )
    return (output_full.astype(jnp.bfloat16), kept_state)


def block_backward(grad_out, inputs, weights, kept_state, pixel_total):
    w_red, gain_pair, bias_pair, w_cv, w_ex, gain_out, bias_out, kernels, gate_vec = weights
    (
        centred_one,
        inv_one,
        gelu_one,
        mix_back,
        patches,
        centred_two,
        inv_two,
        gelu_two,
        inner_act,
        centred_three,
        inv_three,
        gelu_three,
        gain_use,
    ) = kept_state
    grad_pre = gelu_three(grad_out)[0]
    grad_exp, gain_three, bias_three = normalize_back(
        grad_pre, centred_three, inv_three, gain_use, pixel_total
    )
    low_exp = grad_exp.astype(jnp.bfloat16)
    grad_wex = contract(inner_act, low_exp, 0, 0)
    grad_inner = contract(low_exp, w_ex, 1, 1)
    grad_two = gelu_two(grad_inner)[0]
    grad_cv, gain_two, bias_two = normalize_back(
        grad_two, centred_two, inv_two, gain_pair[1], pixel_total
    )
    low_cv = grad_cv.astype(jnp.bfloat16)
    flat_cv = w_cv.reshape(-1, w_cv.shape[-1])
    grad_wcv = contract(patches, low_cv, 0, 0).reshape(w_cv.shape)
    grad_patch = contract(low_cv, flat_cv, 1, 1)
    grad_mixed = lax.psum_scatter(
        unpatch(grad_patch, w_cv.shape[1]).astype(jnp.bfloat16),
        "chan",
        scatter_dimension=1,
        tiled=True,
    ).astype(jnp.float32)
    grad_hidden, grad_kern, grad_gate = mix_back(grad_mixed)
    grad_one = gelu_one(grad_hidden)[0]
    grad_red, gain_one, bias_one = normalize_back(
        grad_one, centred_one, inv_one, gain_pair[0], pixel_total
    )
    low_red = grad_red.astype(jnp.bfloat16)
    grad_wred = contract(inputs, low_red, 0, 0)
    partial_in = contract(low_red, w_red, 1, 1)
    grad_in = grad_pre + lax.psum(partial_in.astype(jnp.bfloat16), "chan").astype(jnp.float32)
    weight_terms = (grad_wred, grad_wcv, grad_wex, grad_kern, grad_gate)
    norm_terms = (gain_one, bias_one, gain_two, bias_two, gain_three, bias_three)
    return (grad_in, weight_terms, norm_terms)


def body(
    frames_in,
    boundary,
    w_reduce,
    gain_inner,
    bias_inner,
    w_conv,
    w_expand,
    gain_outer,
    bias_outer,
    depth_kernels,
    gate_bias,
    cotangent,
):
    row_count = frames_in.shape[0]
    pixel_total = row_count * lax.axis_size("clip")
    col_share = frames_in.shape[1] // lax.axis_size("chan")
    col_start = lax.axis_index("chan") * col_share
    block_weights = [
        (
            w_reduce[block_index],
            gain_inner[block_index],
            bias_inner[block_index],
            w_conv[block_index],
            w_expand[block_index],
            gain_outer[block_index],
            bias_outer[block_index],
            depth_kernels,
            gate_bias,
        )
        for block_index in range(2)
    ]
    first_out, kept_zero = block_forward(frames_in, boundary, block_weights[0], True, pixel_total)
    final_out, kept_one = block_forward(first_out, boundary, block_weights[1], False, pixel_total)
    layer_inputs = [frames_in, first_out]
    kept_states = [kept_zero, kept_one]
    grad_flow = cotangent.astype(jnp.float32)
    weight_sums = [None, None]
    norm_sums = [None, None]
    for block_index in (1, 0):
        grad_flow, weight_terms, norm_terms = block_backward(
            grad_flow,
            layer_inputs[block_index],
            block_weights[block_index],
            kept_states[block_index],
            pixel_total,
        )
        grad_wred, grad_wcv, grad_wex, grad_kern, grad_gate = weight_terms
        weight_terms = (
            lax.psum(grad_wred.astype(jnp.bfloat16), "clip").astype(jnp.float32),
            lax.psum(grad_wcv.astype(jnp.bfloat16), "clip").astype(jnp.float32),
            lax.psum(grad_wex.astype(jnp.bfloat16), "clip").astype(jnp.float32),
            lax.psum(grad_kern.astype(jnp.bfloat16), "clip").astype(jnp.float32),
            lax.psum(grad_gate.astype(jnp.bfloat16), "clip").astype(jnp.float32),
        )
        weight_sums[block_index] = weight_terms
        norm_sums[block_index] = norm_terms
    grad_reduce = jnp.stack([weight_sums[0][0], weight_sums[1][0]])
    grad_conv = jnp.stack([weight_sums[0][1], weight_sums[1][1]])
    grad_expand = jnp.stack([weight_sums[0][2], weight_sums[1][2]])
    grad_kernels = weight_sums[0][3] + weight_sums[1][3]
    grad_gate_bias = weight_sums[0][4] + weight_sums[1][4]
    grad_gain_inner = jnp.stack(
        [
            jnp.stack([norm_sums[0][0], norm_sums[0][2]]),
            jnp.stack([norm_sums[1][0], norm_sums[1][2]]),
        ]
    )
    grad_bias_inner = jnp.stack(
        [
            jnp.stack([norm_sums[0][1], norm_sums[0][3]]),
            jnp.stack([norm_sums[1][1], norm_sums[1][3]]),
        ]
    )
    grad_gain_outer = jnp.stack([norm_sums[0][4], norm_sums[1][4]])
    grad_bias_outer = jnp.stack([norm_sums[0][5], norm_sums[1][5]])
    activations = columns(final_out, col_start, col_share)
    input_grad = columns(grad_flow, col_start, col_share)
    grad_gain_outer = columns(grad_gain_outer, col_start, col_share)
    grad_bias_outer = columns(grad_bias_outer, col_start, col_share)
    return (
        activations,
        input_grad,
        grad_reduce,
        grad_gain_inner,
        grad_bias_inner,
        grad_conv,
        grad_expand,
        grad_gain_outer,
        grad_bias_outer,
        grad_kernels,
        grad_gate_bias,
    )


MESH = pl.DeviceIdType.MESH
LANES = 128
FRAME = SIDE * 8
PIXELS = SIDE * SIDE
PAIR = 2 * FRAME
GELU_A = 0.7978845608028654
GELU_B = 0.044715
SENDS = 48
LOADS = 32


def fused_fits(mesh, frame_shape, reduce_shape):
    n_clip, n_chan = mesh.shape["clip"], mesh.shape["chan"]
    share = reduce_shape[2] // n_chan
    frames = frame_shape[0] // (n_clip * SIDE * SIDE)
    return n_chan == 4 and n_clip == 8 and share == LANES and frames == 2 * SEG


def gelu(z):
    return 0.5 * z * (1.0 + jnp.tanh(GELU_A * (z + GELU_B * z * z * z)))


def gelu_both(z):
    square = z * z
    t = jnp.tanh(GELU_A * (z + GELU_B * square * z))
    slope = 0.5 * (1.0 + t) + 0.5 * z * (1.0 - t * t) * (GELU_A * (1.0 + 3.0 * GELU_B * square))
    return 0.5 * z * (1.0 + t), slope


def real_columns(shape):
    return lax.rem(lax.broadcasted_iota(jnp.int32, shape, len(shape) - 2), 8) < SIDE


def real(values):
    return jnp.where(real_columns(values.shape), values, 0.0)


def fold(values):
    return jnp.sum(values.reshape(-1, 8, values.shape[-1]), axis=0)


def tiles(values):
    return values.reshape(SIDE, 8, values.shape[-1])


def flat(values):
    return values.reshape(FRAME, values.shape[-1])


def row_pad(v, reach):
    zeros = jnp.zeros((reach,) + v.shape[1:], v.dtype)
    return jnp.concatenate([zeros, v, zeros], axis=0)


def col_shift(v, step):
    if step == 0:
        return v
    moved = pltpu.roll(v, (-step) % 8, v.ndim - 2)
    if abs(step) == 2:
        place = lax.broadcasted_iota(jnp.int32, v.shape, v.ndim - 2)
        moved = jnp.where(place < 6 if step > 0 else place >= 2, moved, 0.0)
    return moved


def dw_tiles(v, taps, reach, sign):
    padded = row_pad(v, reach)
    total = None
    for b in (-1, 0, 1):
        part = None
        for a in (-1, 0, 1):
            start = reach + sign * reach * a
            term = taps[3 * (a + 1) + b + 1] * padded[start : start + SIDE]
            part = term if part is None else part + term
        part = col_shift(part, sign * reach * b)
        total = part if total is None else total + part
    return total


def dot(left, right, left_dim=1, right_dim=0):
    return lax.dot_general(
        left, right, (((left_dim,), (right_dim,)), ((), ())), preferred_element_type=jnp.float32
    )


class Refs(NamedTuple):
    x_hbm: Any
    cot_hbm: Any
    wred_hbm: Any
    wconv_hbm: Any
    wexp_hbm: Any
    bnd: Any
    gi: Any
    bi: Any
    go: Any
    bo: Any
    dk: Any
    gb: Any
    act_out: Any
    gin_out: Any
    ggi: Any
    gbi: Any
    ggo: Any
    gbo: Any
    gk_out: Any
    ggb_out: Any
    gc_out: Any
    ge_out: Any
    gr_out: Any
    x: Any
    cot: Any
    wr0: Any
    wrf: Any
    wef: Any
    wc: Any
    dkb: Any
    red: Any
    hid: Any
    sig: Any
    conv: Any
    mixf: Any
    inf: Any
    ex: Any
    out0: Any
    act: Any
    y: Any
    gpre: Any
    gin: Any
    gexp: Any
    gs: Any
    pb: Any
    ysend: Any
    rcore: Any
    ryy: Any
    grf: Any
    gm: Any
    gd: Any
    g1: Any
    gk: Any
    kst: Any
    stn: Any
    stw: Any
    gc: Any
    geo: Any
    ge: Any
    gro: Any
    gr: Any
    xc: Any
    xe: Any
    xr: Any
    zc: Any
    ze: Any
    zr: Any
    fc: Any
    fe: Any
    fr: Any
    ssem: Any
    rsem: Any
    lsem: Any


PIECES = (3, 2, 2)
ARRIVALS = 40 + 12 * sum(PIECES)
TURN, EXPAND, REDUCE, SUMS, CHAN, TAPS = range(-6, 0)
PLAN = {
    (1, 5): (
        111, 110,
    ),
    (1, 6): (
        102,
    ),
    (1, 7): (
        111,
    ),
    (1, 9): (
        111, 110, 102, 100, 101,
    ),
    (1, 11): (
        111, 110,
    ),
    (1, 12): (
        102, 100,
    ),
    (1, 13): (
        111,
    ),
    (0, 0): (
        110, 102, 100, 101,
    ),
    (0, 1): (
        121, 111, 110, 120,
    ),
    (0, 2): (
        110, 102, 100, 101,
    ),
    (0, 3): (
        121,
    ),
    (0, 4): (
        111, 102, 100, 120, 121,
    ),
    (0, 5): (
        11, 110, 10, 101,
    ),
    (0, 6): (
        121, 11, 102, 1, 120,
    ),
    (0, 7): (
        100, 2, 101,
    ),
    (0, 8): (
        121, 11, 1, 10, 120,
    ),
    (0, 9): (
        121, 11, 1, 10, 100, 2, 0, 101,
    ),
    (0, 10): (
        120,
    ),
    (0, 11): (
        121, 11,
    ),
    (0, 12): (
        1, 10, 0,
    ),
    (0, 13): (
        11, 2,
    ),
    (0, 14): (
        20, 21, 120, 1, 101, 0, 10, 11, 2, 1, 20, 10, 0, 21, 20, 2, 120, 21, 0, 20, 1, 2, 21, 10,
        0, 20, 21, 2, 20, 21, 0, 20, 21,
    ),
}


def fused_kernel(n_clip, n_chan, pixel_total, *refs):
    r = Refs(*refs)
    rows, cs = r.cot.shape
    ib = LANES
    frames = rows // PIXELS
    chunk = frames // 2 * FRAME
    n_z = n_clip // 2
    first = -(-rows // 32) * 16
    starts, counts = (0, first), (first, rows - first)
    bf16, f32 = jnp.bfloat16, jnp.float32
    clip = lax.axis_index("clip")
    chan = lax.axis_index("chan")
    core, high = lax.rem(chan, 2), lax.div(chan, 2)
    j_core = (1 - core) + 2 * high
    j_y = core + 2 * (1 - high)
    j_far = (1 - core) + 2 * (1 - high)
    others = (j_core, j_y, j_far)
    z, side = lax.div(clip, 2), lax.rem(clip, 2)
    low, z_near, z_far = lax.rem(z, 2), z + 1 - 2 * lax.rem(z, 2), lax.rem(z + 2, 4)
    clip_others = [lax.rem(clip + d, n_clip) for d in range(1, n_clip)]

    def cols(j):
        return pl.ds(pl.multiple_of(j * ib, ib), ib)

    def wide(j):
        return pl.ds(pl.multiple_of(j * cs, cs), cs)

    def part(h):
        return pl.ds(h * chunk, chunk)

    def raw(h):
        return pl.ds(starts[h], counts[h])

    def spans(total):
        tiles_left, at, chunks = total // 16, 0, []
        for left in range(4, 0, -1):
            take = -(-tiles_left // left)
            chunks.append((at * 16, take * 16))
            at, tiles_left = at + take, tiles_left - take
        return chunks

    raw_spans, padded_spans = spans(rows), spans(frames * FRAME)

    places, in_flight = {}, {}
    counters = SimpleNamespace(send=0, load=0, phase=0, sums=0, out=0)

    def arrival(key):
        return r.rsem.at[places.setdefault(key, len(places))]

    def sent(index):
        if index in in_flight:
            in_flight.pop(index).wait_send()

    def remote(src, dst, target, key):
        index = counters.send % SENDS
        counters.send += 1
        sent(index)
        made = pltpu.make_async_remote_copy(
            src_ref=src,
            dst_ref=dst,
            send_sem=r.ssem.at[index],
            recv_sem=arrival(key),
            device_id=target,
            device_id_type=MESH,
        )
        made.start()
        in_flight[index] = made
        return made, index

    def arrive(place, key):
        pltpu.make_async_remote_copy(
            src_ref=place,
            dst_ref=place,
            send_sem=r.ssem.at[0],
            recv_sem=arrival(key),
            device_id=(clip, j_core),
            device_id_type=MESH,
        ).wait_recv()

    def local(src, dst, index=None):
        if index is None:
            index = counters.load
            counters.load += 1
        made = pltpu.make_async_copy(src, dst, r.lsem.at[index])
        made.start()
        return made

    outgoing = {}

    def write_out(src, dst):
        turn = counters.out % 8
        counters.out += 1
        if turn in outgoing:
            outgoing.pop(turn).wait()
        outgoing[turn] = local(src, dst, LOADS - 8 + turn)

    load_wr0 = local(r.wred_hbm.at[0], r.wr0)
    load_x = [local(r.x_hbm.at[raw(h)], r.x.at[raw(h)]) for h in range(2)]
    load_we = [
        local(r.wexp_hbm.at[s, :, wide(chan)], r.wef.at[s, cols(chan)]) for s in range(2)
    ]
    load_wr = [
        local(r.wred_hbm.at[s, wide(chan)], r.wrf.at[s, :, cols(chan)]) for s in range(2)
    ]
    load_wc = []
    for s in range(2):
        index = counters.load
        counters.load += 1
        for tap in range(9):
            local(r.wconv_hbm.at[s, tap], r.wc.at[s, :, tap * ib : (tap + 1) * ib], index)
        load_wc.append(pltpu.make_async_copy(r.wc.at[s], r.wc.at[s], r.lsem.at[index]))
    load_cot = local(r.cot_hbm.at[:, wide(chan)], r.cot)

    barrier = pltpu.get_barrier_semaphore()
    for target in clip_others:
        pl.semaphore_signal(barrier, inc=1, device_id=(target, chan), device_id_type=MESH)
    for target in others:
        pl.semaphore_signal(barrier, inc=1, device_id=(clip, target), device_id_type=MESH)

    def share_we(s, half):
        size = ib // 2
        for j in others:
            here = r.wexp_hbm.at[s, pl.ds(half * size, size), wide(j)]
            target = r.wef.at[s, pl.ds(pl.multiple_of(chan * ib + half * size, size), size)]
            remote(here, target, (clip, j), (EXPAND, s))

    def share_wr(s, half):
        size = cs // 2
        for j in others:
            here = r.wred_hbm.at[s, pl.ds(pl.multiple_of(j * cs + half * size, size), size)]
            target = r.wrf.at[s, pl.ds(half * size, size), cols(chan)]
            remote(here, target, (clip, j), (REDUCE, s))

    def shared_we(s):
        load_we[s].wait()
        arrive(r.wef.at[s, pl.ds(0, (n_chan - 1) * ib)], (EXPAND, s))

    def shared_wr(s):
        load_wr[s].wait()
        arrive(r.wrf.at[s, :, pl.ds(0, (n_chan - 1) * ib)], (REDUCE, s))

    def stat_start(buf, slot, values):
        for k, value in enumerate(values):
            buf[slot, clip, k : k + 1, :] = jnp.sum(value, axis=0, keepdims=True)
        key = (SUMS, counters.sums % 2)
        counters.sums += 1
        for t in clip_others:
            remote(buf.at[slot, clip], buf.at[slot, clip], (t, chan), key)
        return key

    def stat_end(buf, slot, key):
        arrive(buf.at[slot, pl.ds(0, n_clip - 1)], key)
        total = buf[slot, 0]
        for k in range(1, n_clip):
            total = total + buf[slot, k]
        return total[0:1], total[1:2]

    def moments(pair):
        mean = pair[0] / pixel_total
        return mean, lax.rsqrt(pair[1] / pixel_total - mean * mean + epsilon)

    def phase_keys(count):
        turn = counters.phase % 2
        counters.phase += 1
        return [[(CHAN, turn, k, i) for i in range(3)] for k in range(count)]

    def gather_start(full, at, key):
        mine = full.at[at, cols(chan)]
        remote(mine, mine, (clip, j_y), key[0])
        remote(mine, mine, (clip, j_core), key[1])

    def gather_pass(full, at, key):
        theirs = full.at[at, cols(j_y)]
        arrive(theirs, key[0])
        remote(theirs, theirs, (clip, j_core), key[2])

    def gather_end(full, at, key):
        arrive(full.at[at, cols(j_core)], key[1])
        arrive(full.at[at, cols(j_far)], key[2])

    def pair(value):
        return pl.ds(pl.multiple_of(value * 2 * ib, 2 * ib), 2 * ib)

    def scatter_value(slot, at):
        mine = r.pb[at, cols(chan)].astype(f32)
        return mine + r.rcore[slot, 0, at].astype(f32) + r.ryy[slot, at].astype(f32)

    def keep_flag(f):
        return 1.0 - r.bnd[lax.div(f, SEG), lax.rem(f, SEG)].astype(f32)

    def taps_of(index):
        return [r.dkb[9 * index + tap] for tap in range(9)]

    def pair_rows(h, i):
        return pl.ds(pl.multiple_of(h * chunk + i * PAIR, 16), PAIR)

    def frame_rows(f):
        return pl.ds(pl.multiple_of(f * FRAME, 8), FRAME)

    def spread(ref, f):
        return jnp.stack(
            [ref[pl.ds(f * PIXELS + SIDE * k, 8), :] for k in range(SIDE)], axis=0
        )

    def squeeze(ref, f, value):
        for k in range(SIDE):
            ref[pl.ds(f * PIXELS + SIDE * k, 8), :] = value[k]

    pairs = frames // 4
    carried = {}
    zero_n = jnp.zeros((8, ib), f32)
    zero_w = jnp.zeros((8, cs), f32)

    def each(start, count, step, one, begin):
        def at_step(i, carry):
            return one(pl.ds(pl.multiple_of(start + i * step, 16), step), carry)

        return lax.fori_loop(0, count // step, at_step, begin)

    def narrow(start, count, one, begin):
        step = next(n for n in (112, 96, 80, 64, 48, 32, 16) if count % n == 0)
        return each(start, count, step, one, begin)

    def broad(k, one, begin):
        return each(*raw_spans[k], 16, one, begin)

    moments_in = [[None, None, None], [None, None, None]]

    def row(ref, s, k=None):
        return ref[s, k : k + 1, :] if k is not None else ref[s : s + 1, wide(chan)]

    def norm_inner(s, k, x):
        mean, inv = moments_in[s][k]
        centred = (x - mean) * inv
        return centred, centred * row(r.gi, s, k) + row(r.bi, s, k)

    def norm_outer(s, x):
        mean, inv = moments_in[s][2]
        centred = (x - mean) * inv
        return centred, centred * row(r.go, s) + row(r.bo, s)

    def inner_input(s, at):
        return r.x[at, wide(chan)] if s == 0 else r.out0[at]

    def temporal_forward(s, k):
        h, first_pair = k // 2, k % 2 * (pairs // 2)

        def hide(i, _):
            f = h * (frames // 2) + i
            value = real(gelu(norm_inner(s, 0, spread(r.red.at[s], f))[1]))
            r.hid[s, frame_rows(f)] = flat(value)
            return _

        if first_pair == 0:
            lax.fori_loop(0, frames // 2, hide, 0)

        def mix(i, before):
            base = pl.multiple_of(h * chunk + i * PAIR, 16)
            last = jnp.minimum(base + PAIR, (h + 1) * chunk - FRAME)
            f = h * (frames // 2) + 2 * i
            h0 = tiles(r.hid[s, pl.ds(base, FRAME)])
            h1 = tiles(r.hid[s, pl.ds(base + FRAME, FRAME)])
            h2 = tiles(r.hid[s, pl.ds(pl.multiple_of(last, 8), FRAME)])
            e0 = keep_flag(f) * (h1 - h0)
            e1 = keep_flag(f + 1) * (h2 - h1)
            if s == 0:
                taps = taps_of(0)
                m0 = real(h0 + dw_tiles(e0 + before, taps, 1, 1))
                m1 = real(h1 + dw_tiles(e1 + e0, taps, 1, 1))
            else:
                near, far = taps_of(1), taps_of(2)
                mixed = []
                for k, (hk, ek) in enumerate(((h0, e0), (h1, e1))):
                    logits = dw_tiles(ek, near, 1, 1) + dw_tiles(ek, far, 2, 1) + r.gb[...]
                    gate = 0.5 * (1.0 + jnp.tanh(0.5 * logits))
                    r.sig[pl.ds(base + k * FRAME, FRAME)] = flat(gate)
                    mixed.append(hk + hk * gate)
                m0, m1 = mixed
            both = jnp.concatenate([flat(m0), flat(m1)], axis=0).astype(bf16)
            r.mixf[s, pl.ds(base, PAIR), cols(chan)] = both
            return e1

        before = carried.get(s) if first_pair else jnp.zeros((SIDE, 8, ib), f32)
        carried[s] = lax.fori_loop(first_pair, first_pair + pairs // 2, mix, before, unroll=True)

    def conv_forward(s, k, sums):
        r.y[...] = dot(r.mixf[s, pl.ds(*padded_spans[k])], r.wc[s])

        def add_taps(i, sums):
            at = pl.ds(pl.multiple_of(i * FRAME, 8), FRAME)
            total = None
            for b in (-1, 0, 1):
                run = None
                for a in (-1, 0, 1):
                    tap = 3 * (a + 1) + b + 1
                    term = row_pad(tiles(r.y[at, tap * ib : (tap + 1) * ib]), 1)
                    term = term[1 + a : 1 + a + SIDE]
                    run = term if run is None else run + term
                run = col_shift(run, b)
                total = run if total is None else total + run
            total = real(total)
            squeeze(r.conv.at[s], k * (frames // 4) + i, total)
            return sums[0] + jnp.sum(total, axis=0), sums[1] + jnp.sum(total * total, axis=0)

        return lax.fori_loop(0, frames // 4, add_taps, sums, unroll=True)

    def forward(s, stat_base, wide_slot):
        keys = phase_keys(4)
        quarters = [pl.ds(*span) for span in padded_spans]
        for k in range(4):
            temporal_forward(s, k)
            gather_start(r.mixf.at[s], quarters[k], keys[k])
            if k > 0:
                gather_pass(r.mixf.at[s], quarters[k - 1], keys[k - 1])
        sums = (zero_n, zero_n)
        load_wc[s].wait()
        for k in range(4):
            gather_end(r.mixf.at[s], quarters[k], keys[k])
            if k == 0:
                gather_pass(r.mixf.at[s], quarters[3], keys[3])
            sums = conv_forward(s, k, sums)
        made = stat_start(r.stn, stat_base, sums)
        yield
        moments_in[s][1] = moments(stat_end(r.stn, stat_base, made))
        keys = phase_keys(2)
        for h in range(2):

            def inside(at, _):
                value = gelu(norm_inner(s, 1, r.conv[s, at])[1])
                r.inf[s, at, cols(chan)] = value.astype(bf16)
                return _

            narrow(starts[h], counts[h], inside, 0)
            gather_start(r.inf.at[s], raw(h), keys[h])
        yield
        gather_pass(r.inf.at[s], raw(0), keys[0])
        gather_pass(r.inf.at[s], raw(1), keys[1])
        sums = (zero_w, zero_w)
        for h in range(2):
            gather_end(r.inf.at[s], raw(h), keys[h])
            value = dot(r.inf[s, raw(h)], r.wef[s])
            r.ex[s, raw(h)] = value
            sums = (sums[0] + fold(value), sums[1] + fold(value * value))
        made = stat_start(r.stw, wide_slot, sums)
        yield
        moments_in[s][2] = moments(stat_end(r.stw, wide_slot, made))

    def spread_taps():
        for index in range(3):
            for tap in range(9):
                r.dkb[9 * index + tap] = jnp.broadcast_to(r.dk[tap, index : index + 1, :], (8, ib))

    def clear(i, _):
        r.gk[i] = zero_n
        return _

    for s in range(2):
        r.red[s, rows : rows + 8] = zero_n

    sums = (zero_n, zero_n)
    load_wr0.wait()
    for h in range(2):
        load_x[h].wait()
        value = dot(r.x[raw(h)], r.wr0[...])
        r.red[0, raw(h)] = value
        sums = (sums[0] + fold(value), sums[1] + fold(value * value))
    pl.semaphore_wait(barrier, n_clip - 1 + n_chan - 1)
    made = stat_start(r.stn, 0, sums)
    share_we(0, 0)
    share_we(0, 1)
    spread_taps()
    lax.fori_loop(0, r.gk.shape[0], clear, 0)
    moments_in[0][0] = moments(stat_end(r.stn, 0, made))

    stage = forward(0, 1, 0)
    next(stage)
    share_wr(1, 0)
    next(stage)
    shared_we(0)
    next(stage)
    share_wr(1, 1)
    for _ in stage:
        pass

    def out_zero(at, _):
        z = norm_outer(0, r.ex[0, at])[1] + inner_input(0, at).astype(f32)
        r.out0[at] = gelu(z).astype(bf16)
        return _


    def scatter_all(slot, chunks, prepare, product, use, beside=None, midway=None):
        keys = phase_keys(4)
        ats = [pl.ds(*span) for span in chunks]
        borrowed = []

        def start(k, away):
            if away:
                prepare(k)
            two = pair(1 - high if away else high)
            r.pb[ats[k], two] = product(ats[k], two).astype(bf16)
            block, index = (j_far, 1) if away else (j_core, 0)
            target = r.rcore.at[slot, index, ats[k]]
            made = remote(r.pb.at[ats[k], cols(block)], target, (clip, j_core), keys[k][index])
            borrowed.append(made[1])

        def hand_on(k):
            at = ats[k]
            arrive(r.rcore.at[slot, 1, at], keys[k][1])
            both = r.pb[at, cols(j_y)].astype(f32) + r.rcore[slot, 1, at].astype(f32)
            r.ysend[slot % 2, at] = both.astype(bf16)
            made = remote(r.ysend.at[slot % 2, at], r.ryy.at[slot, at], (clip, j_y), keys[k][2])
            borrowed.append(made[1])

        start(0, True)
        start(1, True)
        hand_on(0)
        start(2, True)
        hand_on(1)
        start(3, True)
        hand_on(2)
        start(0, False)
        hand_on(3)
        for k in range(1, 4):
            start(k, False)
        if beside is not None:
            beside()
        for k in range(4):
            arrive(r.rcore.at[slot, 0, ats[k]], keys[k][0])
            arrive(r.ryy.at[slot, ats[k]], keys[k][2])
            use(*chunks[k])
            if midway is not None and k == 1:
                midway()
        for index in borrowed:
            sent(index)

    held = SimpleNamespace(sums=(zero_n, zero_n))

    def use_reduced(begin, count):
        at = pl.ds(begin, count)
        value = scatter_value(0, at)
        r.red[1, at] = value
        held.sums = (held.sums[0] + fold(value), held.sums[1] + fold(value * value))

    shared_wr(1)
    scatter_all(
        0,
        raw_spans,
        lambda k: broad(k, out_zero, 0),
        lambda at, two: dot(r.out0[at], r.wrf[1, :, two]),
        use_reduced,
    )
    made = stat_start(r.stn, 2, held.sums)
    share_we(1, 0)
    moments_in[1][0] = moments(stat_end(r.stn, 2, made))
    stage = forward(1, 3, 1)
    next(stage)
    share_we(1, 1)
    next(stage)
    shared_we(1)
    next(stage)
    share_wr(0, 0)
    share_wr(0, 1)
    for _ in stage:
        pass

    load_cot.wait()

    def out_one(at, sums):
        centred, z = norm_outer(1, r.ex[1, at])
        value, slope = gelu_both(z + r.out0[at].astype(f32))
        r.act[at] = value.astype(bf16)
        grad = r.cot[at].astype(f32) * slope
        r.gpre[at] = grad
        return sums[0] + fold(grad), sums[1] + fold(grad * centred)

    def top_zero(at, sums):
        centred, z = norm_outer(0, r.ex[0, at])
        grad = r.gin[at] * gelu_both(z + inner_input(0, at).astype(f32))[1]
        r.gpre[at] = grad
        return sums[0] + fold(grad), sums[1] + fold(grad * centred)

    top_sums = SimpleNamespace()

    def backward(s, stat_base, wide_slot, slot):
        if s == 1:
            top_sums.now = (zero_w, zero_w)
            for k in range(4):
                top_sums.now = broad(k, out_one, top_sums.now)
        sums = top_sums.now
        made = stat_start(r.stw, wide_slot, sums)
        if s == 1:
            write_out(r.act, r.act_out)
        service(s, 0)
        shift_sum, gain_sum = stat_end(r.stw, wide_slot, made)
        r.gbo[s : s + 1] = shift_sum
        r.ggo[s : s + 1] = gain_sum
        mean, inv = moments_in[s][2]
        scale = inv * row(r.go, s)
        shift_mean, gain_mean = shift_sum / pixel_total, gain_sum / pixel_total

        def expand_back(at, _):
            centred = (r.ex[s, at] - mean) * inv
            grad = scale * (r.gpre[at] - (shift_mean + centred * gain_mean))
            r.gexp[at] = grad.astype(bf16)
            return _

        held.sums = (zero_n, zero_n)
        service(s, 1)

        def weight_expand():
            value = dot(r.inf[s], r.gexp[...], 0, 0).astype(bf16)
            r.geo[s] = value.reshape(r.geo.shape[1:])
            place = r.ge.at[s, :, :, :, wide(chan)]
            turned[1, s] = local(r.geo.at[s, chan], place)
            for j in others:
                remote(r.geo.at[s, j], place, (clip, j), (TURN, 1, s))
            service(s, 2)

        def use_inner(begin, count):
            def one(at, sums):
                centred, z = norm_inner(s, 1, r.conv[s, at])
                grad = scatter_value(slot, at) * gelu_both(z)[1]
                r.g1[at] = grad
                return sums[0] + fold(grad), sums[1] + fold(grad * centred)

            held.sums = narrow(begin, count, one, held.sums)

        scatter_all(
            slot,
            raw_spans,
            lambda k: broad(k, expand_back, 0),
            lambda at, two: dot(r.gexp[at], r.wef[s, two], 1, 1),
            use_inner,
            weight_expand,
            lambda: service(s, 3),
        )
        made = stat_start(r.stn, stat_base, held.sums)
        service(s, 4)
        shift_sum, gain_sum = stat_end(r.stn, stat_base, made)
        r.gbi[s, 1:2] = shift_sum
        r.ggi[s, 1:2] = gain_sum
        mean, inv = moments_in[s][1]
        scale = inv * row(r.gi, s, 1)
        shift_mean, gain_mean = shift_sum / pixel_total, gain_sum / pixel_total

        def conv_back(i, _):
            at = pair_rows(0, i)
            halves = []
            for f in (2 * i, 2 * i + 1):
                centred = (spread(r.conv.at[s], f) - mean) * inv
                grad = scale * (spread(r.g1, f) - (shift_mean + centred * gain_mean))
                halves.append(real(grad))
            for b in (-1, 0, 1):
                moved = [row_pad(col_shift(v, -b), 1) for v in halves]
                for a in (-1, 0, 1):
                    tap = 3 * (a + 1) + b + 1
                    both = jnp.concatenate([flat(v[1 - a : 1 - a + SIDE]) for v in moved], axis=0)
                    r.gs[at, tap * ib : (tap + 1) * ib] = both.astype(bf16)
            return _


        service(s, 5)

        def weight_conv():
            for k in range(3):
                taps = slice(3 * k * ib, 3 * (k + 1) * ib)
                value = dot(r.mixf[s], r.gs[:, taps], 0, 0).astype(bf16)
                r.gc[s, :, :, :, taps] = value.reshape(r.gc.shape[1:4] + (3 * ib,))
            service(s, 6)

        def use_mixed(begin, count):
            def one(at, _):
                r.gm[at] = real(scatter_value(slot + 1, at))
                return _

            narrow(begin, count, one, 0)

        scatter_all(
            slot + 1,
            padded_spans,
            lambda k: lax.fori_loop(k * pairs // 2, (k + 1) * pairs // 2, conv_back, 0, unroll=True),
            lambda at, two: dot(r.gs[at], r.wc[s, two], 1, 1),
            use_mixed,
            weight_conv,
            lambda: service(s, 7),
        )

        def tap_sums(grad, v, index, reach):
            for b in (-1, 0, 1):
                padded = row_pad(col_shift(v, reach * b), reach)
                for a in (-1, 0, 1):
                    start = reach + reach * a
                    place = 9 * index + 3 * (a + 1) + b + 1
                    r.gk[place] = r.gk[place] + jnp.sum(grad * padded[start : start + SIDE], axis=0)

        def mix_back(f, before):
            at = frame_rows(f)
            following = frame_rows(jnp.minimum(f + 1, frames - 1))
            here = tiles(r.hid[s, at])
            step = keep_flag(f) * (tiles(r.hid[s, following]) - here)
            grad = tiles(r.gm[at])
            if s == 0:
                r.gd[at] = flat(dw_tiles(grad, taps_of(0), 1, -1))
                tap_sums(grad, step + before, 0, 1)
            else:
                gate = tiles(r.sig[at])
                grad = grad * here * gate * (1.0 - gate)
                r.gd[at] = flat(dw_tiles(grad, taps_of(1), 1, -1) + dw_tiles(grad, taps_of(2), 2, -1))
                tap_sums(grad, step, 1, 1)
                tap_sums(grad, step, 2, 2)
                r.gk[27] = r.gk[27] + jnp.sum(grad, axis=0)
            return step

        lax.fori_loop(0, frames, mix_back, jnp.zeros((SIDE, 8, ib), f32))

        service(s, 8)

        def hide_back(f, sums):
            at = frame_rows(f)
            previous = frame_rows(jnp.maximum(f - 1, 0))
            keep = keep_flag(f)
            keep_before = jnp.where(f > 0, keep_flag(jnp.maximum(f - 1, 0)), 0.0)
            now = r.gd[at]
            earlier = r.gd[previous]
            grad = r.gm[at]
            if s == 0:
                following = frame_rows(jnp.minimum(f + 1, frames - 1))
                later = now + r.gd[following]
                earlier = earlier + now
            else:
                later = now
                grad = grad * (1.0 + r.sig[at])
            grad = grad + keep_before * earlier - keep * later
            centred, z = norm_inner(s, 0, spread(r.red.at[s], f))
            grad = real(tiles(grad) * gelu_both(z)[1])
            squeeze(r.g1, f, grad)
            return sums[0] + jnp.sum(grad, axis=0), sums[1] + jnp.sum(grad * centred, axis=0)

        sums = lax.fori_loop(0, frames, hide_back, (zero_n, zero_n))
        made = stat_start(r.stn, stat_base + 1, sums)
        service(s, 9)
        shift_sum, gain_sum = stat_end(r.stn, stat_base + 1, made)
        r.gbi[s, 0:1] = shift_sum
        r.ggi[s, 0:1] = gain_sum
        mean, inv = moments_in[s][0]
        scale = inv * row(r.gi, s, 0)
        shift_mean, gain_mean = shift_sum / pixel_total, gain_sum / pixel_total
        service(s, 10)
        keys = phase_keys(4)
        quarters = [pl.ds(*span) for span in raw_spans]

        def reduce_back(at, _):
            centred = (r.red[s, at] - mean) * inv
            grad = scale * (r.g1[at] - (shift_mean + centred * gain_mean))
            r.grf[s, at, cols(chan)] = grad.astype(bf16)
            return _

        for k in range(4):
            narrow(*raw_spans[k], reduce_back, 0)
            gather_start(r.grf.at[s], quarters[k], keys[k])
        if s == 0:
            own = r.grf[0, :, cols(chan)]
            for piece in range(n_chan):
                value = dot(r.x[:, piece * cs : (piece + 1) * cs], own, 0, 0).astype(bf16)
                r.gr[0, piece] = value.reshape(r.gr.shape[2:])
        service(s, 11)
        gather_pass(r.grf.at[s], quarters[0], keys[0])
        gather_pass(r.grf.at[s], quarters[1], keys[1])
        if s == 0:
            shared_wr(0)
        else:
            top_sums.now = (zero_w, zero_w)
        for k in range(4):
            at = quarters[k]
            gather_end(r.grf.at[s], at, keys[k])
            r.gin[at] = dot(r.grf[s, at], r.wrf[s], 1, 1) + r.gpre[at]
            if k < 2:
                gather_pass(r.grf.at[s], quarters[k + 2], keys[k + 2])
            if s == 0:
                write_out(r.gin.at[at], r.gin_out.at[at])
            else:
                top_sums.now = broad(k, top_zero, top_sums.now)
            if k == 1:
                service(s, 12)
        service(s, 13)
        if s == 1:
            value = dot(r.out0[...], r.grf[1], 0, 0).astype(bf16)
            r.gro[...] = value.reshape(r.gro.shape)
            place = r.gr.at[1, chan]
            turned[2, 1] = local(r.gro.at[:, :, cols(chan)], place)
            for j in others:
                remote(r.gro.at[:, :, cols(j)], place, (clip, j), (TURN, 2, 1))

    turned = {}

    def reduce_task(kind, s, line, place):
        ref, from_side, from_z, result = kinds[kind]
        mine, done = ref.at[s, :, :, line, place], result.at[s, :, :, line, place]
        side_in, z_in = from_side.at[s, :, line, place], from_z.at[s, :, line, place]
        across = (2 * z + 1 - side, chan)
        key = (kind, s, line.start, place.start)
        if (kind, s) in turned:
            turned.pop((kind, s)).wait()
            three = pl.ds(0, (n_chan - 1) * cs)
            arrive(
                r.ge.at[s, :, :, :, three] if kind == 1 else r.gr.at[s, pl.ds(0, n_chan - 1)],
                (TURN, kind, s),
            )
        near, far = (2 * z_near + side, chan), (2 * z_far + side, chan)

        def add(k, term):
            both = ref[s, k, side, line, place].astype(f32) + term.astype(f32)
            return both.astype(bf16)

        remote(mine.at[:, 1 - side], side_in, across, key + (0,))
        yield
        arrive(side_in, key + (0,))
        for k in range(n_z):
            ref[s, k, side, line, place] = add(k, from_side[s, k, line, place])
        for k in range(2):
            remote(mine.at[1 - low + 2 * k, side], z_in.at[k], near, key + (1,))
        yield
        arrive(z_in.at[pl.ds(0, 2)], key + (1,))
        for k in range(2):
            ref[s, low + 2 * k, side, line, place] = add(low + 2 * k, from_z[s, k, line, place])
        remote(mine.at[z_far, side], z_in.at[2], far, key + (2,))
        yield
        arrive(z_in.at[2], key + (2,))
        result[s, z, side, line, place] = add(z, from_z[s, 2, line, place])
        remote(done.at[z, side], done.at[z, side], far, key + (3,))
        yield
        arrive(done.at[z_far, side], key + (3,))
        for k in (z, z_far):
            remote(done.at[k, side], done.at[k, side], near, key + (4,))
        yield
        arrive(done.at[pl.ds(0, 2), side], key + (4,))
        remote(done.at[:, side], done.at[:, side], across, key + (5,))
        yield
        arrive(done.at[:, 1 - side], key + (5,))
        if kind == 0:
            base = place.start // ib
            for k in range((place.stop - place.start) // ib):
                here = r.fc.at[s, :, :, :, (base + k) * ib : (base + k + 1) * ib]
                write_out(here, r.gc_out.at[s, base + k])
        else:
            out = (None, r.ge_out, r.gr_out)[kind]
            write_out(done, out.at[s, :, :, line, place])
        yield

    kinds = (
        (r.gc, r.xc, r.zc, r.fc),
        (r.ge, r.xe, r.ze, r.fe),
        (r.gr, r.xr, r.zr, r.fr),
    )
    def cut(size, count):
        return [slice(k * (size // count), (k + 1) * (size // count)) for k in range(count)]

    tasks = {}
    for s in range(2):
        for k, place in enumerate(cut(9 * ib, PIECES[0])):
            tasks[100 * s + k] = reduce_task(0, s, slice(0, r.gc.shape[3]), place)
        for k, place in enumerate(cut(r.ge.shape[4], PIECES[1])):
            tasks[100 * s + 10 + k] = reduce_task(1, s, slice(0, r.ge.shape[3]), place)
        for k, line in enumerate(cut(r.gr.shape[3], PIECES[2])):
            tasks[100 * s + 20 + k] = reduce_task(2, s, line, slice(0, ib))

    def advance(*steps):
        for step in steps:
            next(tasks[step])

    def service(s, point):
        advance(*PLAN.get((s, point), ()))

    backward(1, 4, 2, 1)
    backward(0, 6, 3, 3)

    for place in range(r.gk.shape[0]):
        r.kst[clip, place : place + 1, :] = jnp.sum(r.gk[place], axis=0, keepdims=True)
    for t in clip_others:
        remote(r.kst.at[clip], r.kst.at[clip], (t, chan), TAPS)
    service(0, 14)
    arrive(r.kst.at[pl.ds(0, n_clip - 1)], TAPS)
    total = r.kst[0]
    for k in range(1, n_clip):
        total = total + r.kst[k]
    for index in range(3):
        for tap in range(9):
            place = 9 * index + tap
            r.gk_out[tap, index : index + 1, :] = total[place : place + 1]
    r.ggb_out[...] = total[27:28]
    for copy in outgoing.values():
        copy.wait()
    for index in list(in_flight):
        sent(index)
    assert len(places) <= ARRIVALS and counters.load <= LOADS - 8


def fused_call(n_clip, n_chan, pixel_total, *operands):
    rows, width = operands[0].shape
    cs = width // n_chan
    ib = LANES
    inner = ib * n_chan
    n_z = n_clip // 2
    padded = rows // PIXELS * FRAME
    over = rows + 8
    bf16, f32 = jnp.bfloat16, jnp.float32
    whole = pl.BlockSpec(memory_space=pltpu.VMEM)
    anywhere = pl.BlockSpec(memory_space=pl.ANY)
    scalars = pl.BlockSpec(memory_space=pltpu.SMEM)
    shape = jax.ShapeDtypeStruct
    V = pltpu.VMEM
    scratch = dict(
        x=V((rows, width), bf16),
        cot=V((rows, cs), bf16),
        wr0=V((width, ib), bf16),
        wrf=V((2, cs, inner), bf16),
        wef=V((2, inner, cs), bf16),
        wc=V((2, inner, 9 * ib), bf16),
        dkb=V((27, 8, ib), f32),
        red=V((2, over, ib), f32),
        hid=V((2, padded, ib), f32),
        sig=V((padded, ib), f32),
        conv=V((2, over, ib), f32),
        mixf=V((2, padded, inner), bf16),
        inf=V((2, rows, inner), bf16),
        ex=V((2, rows, cs), f32),
        out0=V((rows, cs), bf16),
        act=V((rows, cs), bf16),
        y=V((padded // 4, 9 * ib), f32),
        gpre=V((rows, cs), f32),
        gin=V((rows, cs), f32),
        gexp=V((rows, cs), bf16),
        gs=V((padded, 9 * ib), bf16),
        pb=V((padded, inner), bf16),
        ysend=V((2, padded, ib), bf16),
        rcore=V((5, 2, padded, ib), bf16),
        ryy=V((5, padded, ib), bf16),
        grf=V((2, rows, inner), bf16),
        gm=V((padded, ib), f32),
        gd=V((padded, ib), f32),
        g1=V((over, ib), f32),
        gk=V((32, 8, ib), f32),
        kst=V((n_clip, 32, ib), f32),
        stn=V((8, n_clip, 2, ib), f32),
        stw=V((4, n_clip, 2, cs), f32),
        gc=V((2, n_z, 2, inner // n_clip, 9 * ib), bf16),
        geo=V((2, n_chan, n_z, 2, ib // n_clip, cs), bf16),
        ge=V((2, n_z, 2, ib // n_clip, width), bf16),
        gro=V((2, cs // 2, inner), bf16),
        gr=V((2, n_z, 2, width // n_clip, ib), bf16),
        fc=V((2, n_z, 2, inner // n_clip, 9 * ib), bf16),
        fe=V((2, n_z, 2, ib // n_clip, width), bf16),
        fr=V((2, n_z, 2, width // n_clip, ib), bf16),
        xc=V((2, n_z, inner // n_clip, 9 * ib), bf16),
        xe=V((2, n_z, ib // n_clip, width), bf16),
        xr=V((2, n_z, width // n_clip, ib), bf16),
        zc=V((2, n_z - 1, inner // n_clip, 9 * ib), bf16),
        ze=V((2, n_z - 1, ib // n_clip, width), bf16),
        zr=V((2, n_z - 1, width // n_clip, ib), bf16),
        ssem=pltpu.SemaphoreType.DMA((SENDS,)),
        rsem=pltpu.SemaphoreType.DMA((ARRIVALS,)),
        lsem=pltpu.SemaphoreType.DMA((LOADS,)),
    )
    return pl.pallas_call(
        partial(fused_kernel, n_clip, n_chan, pixel_total),
        out_shape=[
            shape((rows, cs), bf16),
            shape((rows, cs), f32),
            shape((2, 2, ib), f32),
            shape((2, 2, ib), f32),
            shape((2, cs), f32),
            shape((2, cs), f32),
            shape((9, 3, ib), f32),
            shape((1, ib), f32),
            shape((2, 9, n_z, 2, inner // n_clip, ib), bf16),
            shape((2, n_z, 2, ib // n_clip, width), bf16),
            shape((2, n_z, 2, width // n_clip, ib), bf16),
        ],
        in_specs=[anywhere] * 5 + [scalars] + [whole] * 6,
        out_specs=[anywhere] * 2 + [whole] * 6 + [anywhere] * 3,
        scratch_shapes=[scratch[name] for name in Refs._fields if name in scratch],
        compiler_params=pltpu.CompilerParams(
            collective_id=0, has_side_effects=True, vmem_limit_bytes=62 * 1024 * 1024
        ),
    )(*operands)


def finish_kernel(*refs):
    count = len(refs) // 2
    sources, results = refs[:count], refs[count:]
    for here, there in zip(sources[:5], results[:5]):
        there[...] = here[...].astype(there.dtype)

    @pl.when(pl.program_id(0) == 0)
    def _():
        for here, there in zip(sources[5:], results[5:]):
            there[...] = here[...]


def finish(steps, gc, ge, gr, act, gin, *small):
    arrays = [a.reshape(-1, a.shape[-1]) for a in (gc, ge, gr)] + [act, gin]
    blocks = [
        pl.BlockSpec((-(-a.shape[0] // (16 * steps)) * 16, a.shape[1]), lambda i: (i, 0))
        for a in arrays
    ]
    whole = [pl.BlockSpec(memory_space=pltpu.VMEM)] * len(small)
    shapes = [jax.ShapeDtypeStruct(a.shape, jnp.float32) for a in arrays[:3]]
    shapes += [jax.ShapeDtypeStruct(a.shape, a.dtype) for a in (act, gin, *small)]
    return pl.pallas_call(
        finish_kernel,
        grid=(steps,),
        out_shape=shapes,
        in_specs=blocks + whole,
        out_specs=blocks + whole,
        compiler_params=pltpu.CompilerParams(vmem_limit_bytes=62 * 1024 * 1024),
    )(*arrays, *small)


def fused(
    frames_in,
    boundary,
    w_reduce,
    gain_inner,
    bias_inner,
    w_conv,
    w_expand,
    gain_outer,
    bias_outer,
    depth_kernels,
    gate_bias,
    cotangent,
):
    n_clip, n_chan = lax.axis_size("clip"), lax.axis_size("chan")
    pixel_total = frames_in.shape[0] * n_clip
    act, gin, ggi, gbi, ggo, gbo, gk, ggb, gc, ge, gr = fused_call(
        n_clip,
        n_chan,
        float(pixel_total),
        frames_in,
        cotangent,
        w_reduce,
        w_conv,
        w_expand,
        boundary,
        gain_inner,
        bias_inner,
        gain_outer,
        bias_outer,
        depth_kernels.transpose(1, 0, 2),
        gate_bias.reshape(1, -1),
    )
    gc, ge, gr, act, gin, ggi, gbi, ggo, gbo, gk, ggb = finish(
        2, gc, ge, gr, act, gin, ggi, gbi, ggo, gbo, gk, ggb
    )
    return (
        act,
        gin,
        gr.reshape(w_reduce.shape),
        ggi,
        gbi,
        gc.reshape(w_conv.shape),
        ge.reshape(w_expand.shape),
        ggo,
        gbo,
        gk.transpose(1, 0, 2),
        ggb.reshape(-1),
    )


def solution(mesh):
    in_specs = (
        P("clip", None),
        P("clip", None),
        P(None, None, "chan"),
        P(None, None, "chan"),
        P(None, None, "chan"),
        P(None, None, None, "chan"),
        P(None, "chan", None),
        P(),
        P(),
        P(None, None, "chan"),
        P("chan"),
        P("clip", None),
    )
    out_specs = (
        P("clip", "chan"),
        P("clip", "chan"),
        P(None, None, "chan"),
        P(None, None, "chan"),
        P(None, None, "chan"),
        P(None, None, None, "chan"),
        P(None, "chan", None),
        P(None, "chan"),
        P(None, "chan"),
        P(None, None, "chan"),
        P("chan"),
    )

    def run(*arguments):
        fits = fused_fits(mesh, arguments[0].shape, arguments[2].shape)
        return jax.shard_map(fused if fits else body, mesh=mesh, in_specs=in_specs, out_specs=out_specs, check_vma=False)(*arguments)

    return run
```

```python
from functools import partial
from types import SimpleNamespace
from typing import Any, NamedTuple

import jax
import jax.numpy as jnp
from jax import lax
from jax.experimental import pallas as pl
from jax.experimental.pallas import tpu as pltpu
from jax.sharding import PartitionSpec as P

SEG = 8
SIDE = 7


epsilon = 1e-05


def framed(values):
    return values.reshape(-1, SIDE, SIDE, values.shape[-1])


def shifted(frame_grid, row_step, col_step, dilation):
    padded = jnp.pad(frame_grid, ((0, 0), (dilation, dilation), (dilation, dilation), (0, 0)))
    return padded[
        :,
        dilation + row_step : dilation + row_step + SIDE,
        dilation + col_step : dilation + col_step + SIDE,
        :,
    ]


def depthwise(values, kernel, dilation):
    frame_grid = framed(values)
    running = jnp.zeros_like(frame_grid)
    for tap_index in range(9):
        running = (
            running
            + shifted(
                frame_grid,
                (tap_index // 3 - 1) * dilation,
                (tap_index % 3 - 1) * dilation,
                dilation,
            )
            * kernel[tap_index]
        )
    return running.reshape(values.shape)


def patch_rows(values):
    frame_grid = framed(values)
    pieces = [
        shifted(frame_grid, tap_index // 3 - 1, tap_index % 3 - 1, 1) for tap_index in range(9)
    ]
    return jnp.concatenate(pieces, axis=-1).reshape(values.shape[0], 9 * values.shape[1])


def unpatch(grad_rows, chan_width):
    frame_grid = grad_rows.reshape(-1, SIDE, SIDE, 9, chan_width)
    running = jnp.zeros(frame_grid.shape[:3] + (chan_width,), jnp.float32)
    for tap_index in range(9):
        running = running + shifted(
            frame_grid[:, :, :, tap_index, :], 1 - tap_index // 3, 1 - tap_index % 3, 1
        )
    return running.reshape(-1, chan_width)


def neighbours(values, boundary):
    clip_count = boundary.shape[0]
    frame_grid = values.reshape(clip_count, SEG, SIDE * SIDE, values.shape[-1])
    stop_mask = (boundary == 1)[:, :, None, None]
    start_mask = jnp.concatenate([jnp.ones_like(stop_mask[:, :1]), stop_mask[:, :-1]], axis=1)
    after_seg = jnp.concatenate([frame_grid[:, 1:], frame_grid[:, -1:]], axis=1)
    before = jnp.concatenate([frame_grid[:, :1], frame_grid[:, :-1]], axis=1)
    later_seg = jnp.where(stop_mask, frame_grid, after_seg)
    earlier = jnp.where(start_mask, frame_grid, before)
    return (later_seg.reshape(values.shape), earlier.reshape(values.shape))


def temporal(values, kernels, gate_vec, boundary, short_range):
    later_seg, earlier = neighbours(values, boundary)
    if short_range:
        return values + depthwise(later_seg - earlier, kernels[0], 1)
    change = later_seg - values
    logits = depthwise(change, kernels[1], 1) + depthwise(change, kernels[2], 2) + gate_vec
    return values + values * jax.nn.sigmoid(logits)


def columns(values, col_start, col_share):
    return lax.dynamic_slice_in_dim(values, col_start, col_share, values.ndim - 1)


def contract(left, right, left_dim, right_dim):
    return lax.dot_general(
        left, right, (((left_dim,), (right_dim,)), ((), ())), preferred_element_type=jnp.float32
    )


def normalize(values, gain_vec, bias_vec, pixel_total):
    col_sum, sq_sum = lax.psum((jnp.sum(values, axis=0), jnp.sum(values * values, axis=0)), "clip")
    mean_val = col_sum / pixel_total
    inv_std = lax.rsqrt(sq_sum / pixel_total - mean_val * mean_val + epsilon)
    centred = (values - mean_val) * inv_std
    return (centred * gain_vec + bias_vec, centred, inv_std)


def normalize_back(grad_rows, centred, inv_std, gain_vec, pixel_total):
    shift_sum, gain_sum = lax.psum(
        (jnp.sum(grad_rows, axis=0), jnp.sum(grad_rows * centred, axis=0)), "clip"
    )
    grad_in = inv_std * gain_vec * (grad_rows - (shift_sum + centred * gain_sum) / pixel_total)
    return (grad_in, gain_sum, shift_sum)


def block_forward(inputs, boundary, weights, short_range, pixel_total):
    w_red, gain_pair, bias_pair, w_cv, w_ex, gain_out, bias_out, kernels, gate_vec = weights
    reduced = jnp.dot(inputs, w_red, preferred_element_type=jnp.float32)
    norm_one, centred_one, inv_one = normalize(reduced, gain_pair[0], bias_pair[0], pixel_total)
    hidden, gelu_one = jax.vjp(jax.nn.gelu, norm_one)
    mixed_act, mix_back = jax.vjp(
        partial(temporal, boundary=boundary, short_range=short_range), hidden, kernels, gate_vec
    )
    gathered = lax.all_gather(mixed_act.astype(jnp.bfloat16), "chan", axis=1, tiled=True)
    patches = patch_rows(gathered)
    conv_out = jnp.dot(
        patches, w_cv.reshape(-1, w_cv.shape[-1]), preferred_element_type=jnp.float32
    )
    norm_two, centred_two, inv_two = normalize(conv_out, gain_pair[1], bias_pair[1], pixel_total)
    inner_full, gelu_two = jax.vjp(jax.nn.gelu, norm_two)
    inner_act = inner_full.astype(jnp.bfloat16)
    partial_out = jnp.dot(inner_act, w_ex, preferred_element_type=jnp.float32)
    expanded = lax.psum(partial_out.astype(jnp.bfloat16), "chan").astype(jnp.float32)
    norm_three, centred_three, inv_three = normalize(expanded, gain_out, bias_out, pixel_total)
    output_full, gelu_three = jax.vjp(jax.nn.gelu, norm_three + inputs.astype(jnp.float32))
    kept_state = (
        centred_one,
        inv_one,
        gelu_one,
        mix_back,
        patches,
        centred_two,
        inv_two,
        gelu_two,
        inner_act,
        centred_three,
        inv_three,
        gelu_three,
        gain_out,
    )
    return (output_full.astype(jnp.bfloat16), kept_state)


def block_backward(grad_out, inputs, weights, kept_state, pixel_total):
    w_red, gain_pair, bias_pair, w_cv, w_ex, gain_out, bias_out, kernels, gate_vec = weights
    (
        centred_one,
        inv_one,
        gelu_one,
        mix_back,
        patches,
        centred_two,
        inv_two,
        gelu_two,
        inner_act,
        centred_three,
        inv_three,
        gelu_three,
        gain_use,
    ) = kept_state
    grad_pre = gelu_three(grad_out)[0]
    grad_exp, gain_three, bias_three = normalize_back(
        grad_pre, centred_three, inv_three, gain_use, pixel_total
    )
    low_exp = grad_exp.astype(jnp.bfloat16)
    grad_wex = contract(inner_act, low_exp, 0, 0)
    grad_inner = contract(low_exp, w_ex, 1, 1)
    grad_two = gelu_two(grad_inner)[0]
    grad_cv, gain_two, bias_two = normalize_back(
        grad_two, centred_two, inv_two, gain_pair[1], pixel_total
    )
    low_cv = grad_cv.astype(jnp.bfloat16)
    flat_cv = w_cv.reshape(-1, w_cv.shape[-1])
    grad_wcv = contract(patches, low_cv, 0, 0).reshape(w_cv.shape)
    grad_patch = contract(low_cv, flat_cv, 1, 1)
    grad_mixed = lax.psum_scatter(
        unpatch(grad_patch, w_cv.shape[1]).astype(jnp.bfloat16),
        "chan",
        scatter_dimension=1,
        tiled=True,
    ).astype(jnp.float32)
    grad_hidden, grad_kern, grad_gate = mix_back(grad_mixed)
    grad_one = gelu_one(grad_hidden)[0]
    grad_red, gain_one, bias_one = normalize_back(
        grad_one, centred_one, inv_one, gain_pair[0], pixel_total
    )
    low_red = grad_red.astype(jnp.bfloat16)
    grad_wred = contract(inputs, low_red, 0, 0)
    partial_in = contract(low_red, w_red, 1, 1)
    grad_in = grad_pre + lax.psum(partial_in.astype(jnp.bfloat16), "chan").astype(jnp.float32)
    weight_terms = (grad_wred, grad_wcv, grad_wex, grad_kern, grad_gate)
    norm_terms = (gain_one, bias_one, gain_two, bias_two, gain_three, bias_three)
    return (grad_in, weight_terms, norm_terms)


def body(
    frames_in,
    boundary,
    w_reduce,
    gain_inner,
    bias_inner,
    w_conv,
    w_expand,
    gain_outer,
    bias_outer,
    depth_kernels,
    gate_bias,
    cotangent,
):
    row_count = frames_in.shape[0]
    pixel_total = row_count * lax.axis_size("clip")
    col_share = frames_in.shape[1] // lax.axis_size("chan")
    col_start = lax.axis_index("chan") * col_share
    block_weights = [
        (
            w_reduce[block_index],
            gain_inner[block_index],
            bias_inner[block_index],
            w_conv[block_index],
            w_expand[block_index],
            gain_outer[block_index],
            bias_outer[block_index],
            depth_kernels,
            gate_bias,
        )
        for block_index in range(2)
    ]
    first_out, kept_zero = block_forward(frames_in, boundary, block_weights[0], True, pixel_total)
    final_out, kept_one = block_forward(first_out, boundary, block_weights[1], False, pixel_total)
    layer_inputs = [frames_in, first_out]
    kept_states = [kept_zero, kept_one]
    grad_flow = cotangent.astype(jnp.float32)
    weight_sums = [None, None]
    norm_sums = [None, None]
    for block_index in (1, 0):
        grad_flow, weight_terms, norm_terms = block_backward(
            grad_flow,
            layer_inputs[block_index],
            block_weights[block_index],
            kept_states[block_index],
            pixel_total,
        )
        grad_wred, grad_wcv, grad_wex, grad_kern, grad_gate = weight_terms
        weight_terms = (
            lax.psum(grad_wred.astype(jnp.bfloat16), "clip").astype(jnp.float32),
            lax.psum(grad_wcv.astype(jnp.bfloat16), "clip").astype(jnp.float32),
            lax.psum(grad_wex.astype(jnp.bfloat16), "clip").astype(jnp.float32),
            lax.psum(grad_kern.astype(jnp.bfloat16), "clip").astype(jnp.float32),
            lax.psum(grad_gate.astype(jnp.bfloat16), "clip").astype(jnp.float32),
        )
        weight_sums[block_index] = weight_terms
        norm_sums[block_index] = norm_terms
    grad_reduce = jnp.stack([weight_sums[0][0], weight_sums[1][0]])
    grad_conv = jnp.stack([weight_sums[0][1], weight_sums[1][1]])
    grad_expand = jnp.stack([weight_sums[0][2], weight_sums[1][2]])
    grad_kernels = weight_sums[0][3] + weight_sums[1][3]
    grad_gate_bias = weight_sums[0][4] + weight_sums[1][4]
    grad_gain_inner = jnp.stack(
        [
            jnp.stack([norm_sums[0][0], norm_sums[0][2]]),
            jnp.stack([norm_sums[1][0], norm_sums[1][2]]),
        ]
    )
    grad_bias_inner = jnp.stack(
        [
            jnp.stack([norm_sums[0][1], norm_sums[0][3]]),
            jnp.stack([norm_sums[1][1], norm_sums[1][3]]),
        ]
    )
    grad_gain_outer = jnp.stack([norm_sums[0][4], norm_sums[1][4]])
    grad_bias_outer = jnp.stack([norm_sums[0][5], norm_sums[1][5]])
    activations = columns(final_out, col_start, col_share)
    input_grad = columns(grad_flow, col_start, col_share)
    grad_gain_outer = columns(grad_gain_outer, col_start, col_share)
    grad_bias_outer = columns(grad_bias_outer, col_start, col_share)
    return (
        activations,
        input_grad,
        grad_reduce,
        grad_gain_inner,
        grad_bias_inner,
        grad_conv,
        grad_expand,
        grad_gain_outer,
        grad_bias_outer,
        grad_kernels,
        grad_gate_bias,
    )


MESH = pl.DeviceIdType.MESH
LANES = 128
FRAME = SIDE * 8
PIXELS = SIDE * SIDE
PAIR = 2 * FRAME
GELU_A = 0.7978845608028654
GELU_B = 0.044715
SENDS = 48
LOADS = 32


def fused_fits(mesh, frame_shape, reduce_shape):
    n_clip, n_chan = mesh.shape["clip"], mesh.shape["chan"]
    share = reduce_shape[2] // n_chan
    frames = frame_shape[0] // (n_clip * SIDE * SIDE)
    return n_chan == 4 and n_clip == 8 and share == LANES and frames == 2 * SEG


def gelu(z):
    return 0.5 * z * (1.0 + jnp.tanh(GELU_A * (z + GELU_B * z * z * z)))


def gelu_both(z):
    square = z * z
    t = jnp.tanh(GELU_A * (z + GELU_B * square * z))
    slope = 0.5 * (1.0 + t) + 0.5 * z * (1.0 - t * t) * (GELU_A * (1.0 + 3.0 * GELU_B * square))
    return 0.5 * z * (1.0 + t), slope


def real_columns(shape):
    return lax.rem(lax.broadcasted_iota(jnp.int32, shape, len(shape) - 2), 8) < SIDE


def real(values):
    return jnp.where(real_columns(values.shape), values, 0.0)


def fold(values):
    return jnp.sum(values.reshape(-1, 8, values.shape[-1]), axis=0)


def tiles(values):
    return values.reshape(SIDE, 8, values.shape[-1])


def flat(values):
    return values.reshape(FRAME, values.shape[-1])


def row_pad(v, reach):
    zeros = jnp.zeros((reach,) + v.shape[1:], v.dtype)
    return jnp.concatenate([zeros, v, zeros], axis=0)


def col_shift(v, step):
    if step == 0:
        return v
    moved = pltpu.roll(v, (-step) % 8, v.ndim - 2)
    if abs(step) == 2:
        place = lax.broadcasted_iota(jnp.int32, v.shape, v.ndim - 2)
        moved = jnp.where(place < 6 if step > 0 else place >= 2, moved, 0.0)
    return moved


def dw_tiles(v, taps, reach, sign):
    padded = row_pad(v, reach)
    total = None
    for b in (-1, 0, 1):
        part = None
        for a in (-1, 0, 1):
            start = reach + sign * reach * a
            term = taps[3 * (a + 1) + b + 1] * padded[start : start + SIDE]
            part = term if part is None else part + term
        part = col_shift(part, sign * reach * b)
        total = part if total is None else total + part
    return total


def dot(left, right, left_dim=1, right_dim=0):
    return lax.dot_general(
        left, right, (((left_dim,), (right_dim,)), ((), ())), preferred_element_type=jnp.float32
    )


class Refs(NamedTuple):
    x_hbm: Any
    cot_hbm: Any
    wred_hbm: Any
    wconv_hbm: Any
    wexp_hbm: Any
    bnd: Any
    gi: Any
    bi: Any
    go: Any
    bo: Any
    dk: Any
    gb: Any
    act_out: Any
    gin_out: Any
    ggi: Any
    gbi: Any
    ggo: Any
    gbo: Any
    gk_out: Any
    ggb_out: Any
    gc_out: Any
    ge_out: Any
    gr_out: Any
    x: Any
    cot: Any
    wr0: Any
    wrf: Any
    wef: Any
    wc: Any
    dkb: Any
    red: Any
    hid: Any
    sig: Any
    conv: Any
    mixf: Any
    inf: Any
    ex: Any
    out0: Any
    act: Any
    y: Any
    gpre: Any
    gin: Any
    gexp: Any
    gs: Any
    pb: Any
    ysend: Any
    rcore: Any
    ryy: Any
    grf: Any
    gm: Any
    gd: Any
    g1: Any
    gk: Any
    kst: Any
    stn: Any
    stw: Any
    gc: Any
    geo: Any
    ge: Any
    gro: Any
    gr: Any
    xc: Any
    xe: Any
    xr: Any
    zc: Any
    ze: Any
    zr: Any
    fc: Any
    fe: Any
    fr: Any
    ssem: Any
    rsem: Any
    lsem: Any


PIECES = (3, 2, 2)
ARRIVALS = 40 + 12 * sum(PIECES)
TURN, EXPAND, REDUCE, SUMS, CHAN, TAPS = range(-6, 0)
PLAN = {
    (1, 5): (
        111, 110,
    ),
    (1, 6): (
        102,
    ),
    (1, 7): (
        111,
    ),
    (1, 9): (
        111, 110, 102, 100, 101,
    ),
    (1, 11): (
        111, 110,
    ),
    (1, 12): (
        102, 100,
    ),
    (1, 13): (
        111,
    ),
    (0, 0): (
        110, 102, 100, 101,
    ),
    (0, 1): (
        121, 111, 110, 120,
    ),
    (0, 2): (
        110, 102, 100, 101,
    ),
    (0, 3): (
        121,
    ),
    (0, 4): (
        111, 102, 100, 120, 121,
    ),
    (0, 5): (
        11, 110, 10, 101,
    ),
    (0, 6): (
        121, 11, 102, 1, 120,
    ),
    (0, 7): (
        100, 2, 101,
    ),
    (0, 8): (
        121, 11, 1, 10, 120,
    ),
    (0, 9): (
        121, 11, 1, 10, 100, 2, 0, 101,
    ),
    (0, 10): (
        120,
    ),
    (0, 11): (
        121, 11,
    ),
    (0, 12): (
        1, 10, 0,
    ),
    (0, 13): (
        11, 2,
    ),
    (0, 14): (
        20, 21, 120, 1, 101, 0, 10, 11, 2, 1, 20, 10, 0, 21, 20, 2, 120, 21, 0, 20, 1, 2, 21, 10,
        0, 20, 21, 2, 20, 21, 0, 20, 21,
    ),
}


def fused_kernel(n_clip, n_chan, pixel_total, *refs):
    r = Refs(*refs)
    rows, cs = r.cot.shape
    ib = LANES
    frames = rows // PIXELS
    chunk = frames // 2 * FRAME
    n_z = n_clip // 2
    first = -(-rows // 32) * 16
    starts, counts = (0, first), (first, rows - first)
    bf16, f32 = jnp.bfloat16, jnp.float32
    clip = lax.axis_index("clip")
    chan = lax.axis_index("chan")
    core, high = lax.rem(chan, 2), lax.div(chan, 2)
    j_core = (1 - core) + 2 * high
    j_y = core + 2 * (1 - high)
    j_far = (1 - core) + 2 * (1 - high)
    others = (j_core, j_y, j_far)
    z, side = lax.div(clip, 2), lax.rem(clip, 2)
    low, z_near, z_far = lax.rem(z, 2), z + 1 - 2 * lax.rem(z, 2), lax.rem(z + 2, 4)
    clip_others = [lax.rem(clip + d, n_clip) for d in range(1, n_clip)]

    def cols(j):
        return pl.ds(pl.multiple_of(j * ib, ib), ib)

    def wide(j):
        return pl.ds(pl.multiple_of(j * cs, cs), cs)

    def part(h):
        return pl.ds(h * chunk, chunk)

    def raw(h):
        return pl.ds(starts[h], counts[h])

    def spans(total):
        tiles_left, at, chunks = total // 16, 0, []
        for left in range(4, 0, -1):
            take = -(-tiles_left // left)
            chunks.append((at * 16, take * 16))
            at, tiles_left = at + take, tiles_left - take
        return chunks

    raw_spans, padded_spans = spans(rows), spans(frames * FRAME)

    places, in_flight = {}, {}
    counters = SimpleNamespace(send=0, load=0, phase=0, sums=0, out=0)

    def arrival(key):
        return r.rsem.at[places.setdefault(key, len(places))]

    def sent(index):
        if index in in_flight:
            in_flight.pop(index).wait_send()

    def remote(src, dst, target, key):
        index = counters.send % SENDS
        counters.send += 1
        sent(index)
        made = pltpu.make_async_remote_copy(
            src_ref=src,
            dst_ref=dst,
            send_sem=r.ssem.at[index],
            recv_sem=arrival(key),
            device_id=target,
            device_id_type=MESH,
        )
        made.start()
        in_flight[index] = made
        return made, index

    def arrive(place, key):
        pltpu.make_async_remote_copy(
            src_ref=place,
            dst_ref=place,
            send_sem=r.ssem.at[0],
            recv_sem=arrival(key),
            device_id=(clip, j_core),
            device_id_type=MESH,
        ).wait_recv()

    def local(src, dst, index=None):
        if index is None:
            index = counters.load
            counters.load += 1
        made = pltpu.make_async_copy(src, dst, r.lsem.at[index])
        made.start()
        return made

    outgoing = {}

    def write_out(src, dst):
        turn = counters.out % 8
        counters.out += 1
        if turn in outgoing:
            outgoing.pop(turn).wait()
        outgoing[turn] = local(src, dst, LOADS - 8 + turn)

    load_wr0 = local(r.wred_hbm.at[0], r.wr0)
    load_x = [local(r.x_hbm.at[raw(h)], r.x.at[raw(h)]) for h in range(2)]
    load_we = [
        local(r.wexp_hbm.at[s, :, wide(chan)], r.wef.at[s, cols(chan)]) for s in range(2)
    ]
    load_wr = [
        local(r.wred_hbm.at[s, wide(chan)], r.wrf.at[s, :, cols(chan)]) for s in range(2)
    ]
    load_wc = []
    for s in range(2):
        index = counters.load
        counters.load += 1
        for tap in range(9):
            local(r.wconv_hbm.at[s, tap], r.wc.at[s, :, tap * ib : (tap + 1) * ib], index)
        load_wc.append(pltpu.make_async_copy(r.wc.at[s], r.wc.at[s], r.lsem.at[index]))
    load_cot = local(r.cot_hbm.at[:, wide(chan)], r.cot)

    barrier = pltpu.get_barrier_semaphore()
    for target in clip_others:
        pl.semaphore_signal(barrier, inc=1, device_id=(target, chan), device_id_type=MESH)
    for target in others:
        pl.semaphore_signal(barrier, inc=1, device_id=(clip, target), device_id_type=MESH)

    def share_we(s, half):
        size = ib // 2
        for j in others:
            here = r.wexp_hbm.at[s, pl.ds(half * size, size), wide(j)]
            target = r.wef.at[s, pl.ds(pl.multiple_of(chan * ib + half * size, size), size)]
            remote(here, target, (clip, j), (EXPAND, s))

    def share_wr(s, half):
        size = cs // 2
        for j in others:
            here = r.wred_hbm.at[s, pl.ds(pl.multiple_of(j * cs + half * size, size), size)]
            target = r.wrf.at[s, pl.ds(half * size, size), cols(chan)]
            remote(here, target, (clip, j), (REDUCE, s))

    def shared_we(s):
        load_we[s].wait()
        arrive(r.wef.at[s, pl.ds(0, (n_chan - 1) * ib)], (EXPAND, s))

    def shared_wr(s):
        load_wr[s].wait()
        arrive(r.wrf.at[s, :, pl.ds(0, (n_chan - 1) * ib)], (REDUCE, s))

    def stat_start(buf, slot, values):
        for k, value in enumerate(values):
            buf[slot, clip, k : k + 1, :] = jnp.sum(value, axis=0, keepdims=True)
        key = (SUMS, counters.sums % 2)
        counters.sums += 1
        for t in clip_others:
            remote(buf.at[slot, clip], buf.at[slot, clip], (t, chan), key)
        return key

    def stat_end(buf, slot, key):
        arrive(buf.at[slot, pl.ds(0, n_clip - 1)], key)
        total = buf[slot, 0]
        for k in range(1, n_clip):
            total = total + buf[slot, k]
        return total[0:1], total[1:2]

    def moments(pair):
        mean = pair[0] / pixel_total
        return mean, lax.rsqrt(pair[1] / pixel_total - mean * mean + epsilon)

    def phase_keys(count):
        turn = counters.phase % 2
        counters.phase += 1
        return [[(CHAN, turn, k, i) for i in range(3)] for k in range(count)]

    def gather_start(full, at, key):
        mine = full.at[at, cols(chan)]
        remote(mine, mine, (clip, j_y), key[0])
        remote(mine, mine, (clip, j_core), key[1])

    def gather_pass(full, at, key):
        theirs = full.at[at, cols(j_y)]
        arrive(theirs, key[0])
        remote(theirs, theirs, (clip, j_core), key[2])

    def gather_end(full, at, key):
        arrive(full.at[at, cols(j_core)], key[1])
        arrive(full.at[at, cols(j_far)], key[2])

    def pair(value):
        return pl.ds(pl.multiple_of(value * 2 * ib, 2 * ib), 2 * ib)

    def scatter_value(slot, at):
        mine = r.pb[at, cols(chan)].astype(f32)
        return mine + r.rcore[slot, 0, at].astype(f32) + r.ryy[slot, at].astype(f32)

    def keep_flag(f):
        return 1.0 - r.bnd[lax.div(f, SEG), lax.rem(f, SEG)].astype(f32)

    def taps_of(index):
        return [r.dkb[9 * index + tap] for tap in range(9)]

    def pair_rows(h, i):
        return pl.ds(pl.multiple_of(h * chunk + i * PAIR, 16), PAIR)

    def frame_rows(f):
        return pl.ds(pl.multiple_of(f * FRAME, 8), FRAME)

    def spread(ref, f):
        return jnp.stack(
            [ref[pl.ds(f * PIXELS + SIDE * k, 8), :] for k in range(SIDE)], axis=0
        )

    def squeeze(ref, f, value):
        for k in range(SIDE):
            ref[pl.ds(f * PIXELS + SIDE * k, 8), :] = value[k]

    pairs = frames // 4
    carried = {}
    zero_n = jnp.zeros((8, ib), f32)
    zero_w = jnp.zeros((8, cs), f32)

    def each(start, count, step, one, begin):
        def at_step(i, carry):
            return one(pl.ds(pl.multiple_of(start + i * step, 16), step), carry)

        return lax.fori_loop(0, count // step, at_step, begin)

    def narrow(start, count, one, begin):
        step = next(n for n in (112, 96, 80, 64, 48, 32, 16) if count % n == 0)
        return each(start, count, step, one, begin)

    def broad(k, one, begin):
        return each(*raw_spans[k], 16, one, begin)

    moments_in = [[None, None, None], [None, None, None]]

    def row(ref, s, k=None):
        return ref[s, k : k + 1, :] if k is not None else ref[s : s + 1, wide(chan)]

    def norm_inner(s, k, x):
        mean, inv = moments_in[s][k]
        centred = (x - mean) * inv
        return centred, centred * row(r.gi, s, k) + row(r.bi, s, k)

    def norm_outer(s, x):
        mean, inv = moments_in[s][2]
        centred = (x - mean) * inv
        return centred, centred * row(r.go, s) + row(r.bo, s)

    def inner_input(s, at):
        return r.x[at, wide(chan)] if s == 0 else r.out0[at]

    def temporal_forward(s, k):
        h, first_pair = k // 2, k % 2 * (pairs // 2)

        def hide(i, _):
            f = h * (frames // 2) + i
            value = real(gelu(norm_inner(s, 0, spread(r.red.at[s], f))[1]))
            r.hid[s, frame_rows(f)] = flat(value)
            return _

        if first_pair == 0:
            lax.fori_loop(0, frames // 2, hide, 0)

        def mix(i, before):
            base = pl.multiple_of(h * chunk + i * PAIR, 16)
            last = jnp.minimum(base + PAIR, (h + 1) * chunk - FRAME)
            f = h * (frames // 2) + 2 * i
            h0 = tiles(r.hid[s, pl.ds(base, FRAME)])
            h1 = tiles(r.hid[s, pl.ds(base + FRAME, FRAME)])
            h2 = tiles(r.hid[s, pl.ds(pl.multiple_of(last, 8), FRAME)])
            e0 = keep_flag(f) * (h1 - h0)
            e1 = keep_flag(f + 1) * (h2 - h1)
            if s == 0:
                taps = taps_of(0)
                m0 = real(h0 + dw_tiles(e0 + before, taps, 1, 1))
                m1 = real(h1 + dw_tiles(e1 + e0, taps, 1, 1))
            else:
                near, far = taps_of(1), taps_of(2)
                mixed = []
                for k, (hk, ek) in enumerate(((h0, e0), (h1, e1))):
                    logits = dw_tiles(ek, near, 1, 1) + dw_tiles(ek, far, 2, 1) + r.gb[...]
                    gate = 0.5 * (1.0 + jnp.tanh(0.5 * logits))
                    r.sig[pl.ds(base + k * FRAME, FRAME)] = flat(gate)
                    mixed.append(hk + hk * gate)
                m0, m1 = mixed
            both = jnp.concatenate([flat(m0), flat(m1)], axis=0).astype(bf16)
            r.mixf[s, pl.ds(base, PAIR), cols(chan)] = both
            return e1

        before = carried.get(s) if first_pair else jnp.zeros((SIDE, 8, ib), f32)
        carried[s] = lax.fori_loop(first_pair, first_pair + pairs // 2, mix, before, unroll=True)

    def conv_forward(s, k, sums):
        r.y[...] = dot(r.mixf[s, pl.ds(*padded_spans[k])], r.wc[s])

        def add_taps(i, sums):
            at = pl.ds(pl.multiple_of(i * FRAME, 8), FRAME)
            total = None
            for b in (-1, 0, 1):
                run = None
                for a in (-1, 0, 1):
                    tap = 3 * (a + 1) + b + 1
                    term = row_pad(tiles(r.y[at, tap * ib : (tap + 1) * ib]), 1)
                    term = term[1 + a : 1 + a + SIDE]
                    run = term if run is None else run + term
                run = col_shift(run, b)
                total = run if total is None else total + run
            total = real(total)
            squeeze(r.conv.at[s], k * (frames // 4) + i, total)
            return sums[0] + jnp.sum(total, axis=0), sums[1] + jnp.sum(total * total, axis=0)

        return lax.fori_loop(0, frames // 4, add_taps, sums, unroll=True)

    def forward(s, stat_base, wide_slot):
        keys = phase_keys(4)
        quarters = [pl.ds(*span) for span in padded_spans]
        for k in range(4):
            temporal_forward(s, k)
            gather_start(r.mixf.at[s], quarters[k], keys[k])
            if k > 0:
                gather_pass(r.mixf.at[s], quarters[k - 1], keys[k - 1])
        sums = (zero_n, zero_n)
        load_wc[s].wait()
        for k in range(4):
            gather_end(r.mixf.at[s], quarters[k], keys[k])
            if k == 0:
                gather_pass(r.mixf.at[s], quarters[3], keys[3])
            sums = conv_forward(s, k, sums)
        made = stat_start(r.stn, stat_base, sums)
        yield
        moments_in[s][1] = moments(stat_end(r.stn, stat_base, made))
        keys = phase_keys(2)
        for h in range(2):

            def inside(at, _):
                value = gelu(norm_inner(s, 1, r.conv[s, at])[1])
                r.inf[s, at, cols(chan)] = value.astype(bf16)
                return _

            narrow(starts[h], counts[h], inside, 0)
            gather_start(r.inf.at[s], raw(h), keys[h])
        yield
        gather_pass(r.inf.at[s], raw(0), keys[0])
        gather_pass(r.inf.at[s], raw(1), keys[1])
        sums = (zero_w, zero_w)
        for h in range(2):
            gather_end(r.inf.at[s], raw(h), keys[h])
            value = dot(r.inf[s, raw(h)], r.wef[s])
            r.ex[s, raw(h)] = value
            sums = (sums[0] + fold(value), sums[1] + fold(value * value))
        made = stat_start(r.stw, wide_slot, sums)
        yield
        moments_in[s][2] = moments(stat_end(r.stw, wide_slot, made))

    def spread_taps():
        for index in range(3):
            for tap in range(9):
                r.dkb[9 * index + tap] = jnp.broadcast_to(r.dk[tap, index : index + 1, :], (8, ib))

    def clear(i, _):
        r.gk[i] = zero_n
        return _

    for s in range(2):
        r.red[s, rows : rows + 8] = zero_n

    sums = (zero_n, zero_n)
    load_wr0.wait()
    for h in range(2):
        load_x[h].wait()
        value = dot(r.x[raw(h)], r.wr0[...])
        r.red[0, raw(h)] = value
        sums = (sums[0] + fold(value), sums[1] + fold(value * value))
    pl.semaphore_wait(barrier, n_clip - 1 + n_chan - 1)
    made = stat_start(r.stn, 0, sums)
    share_we(0, 0)
    share_we(0, 1)
    spread_taps()
    lax.fori_loop(0, r.gk.shape[0], clear, 0)
    moments_in[0][0] = moments(stat_end(r.stn, 0, made))

    stage = forward(0, 1, 0)
    next(stage)
    share_wr(1, 0)
    next(stage)
    shared_we(0)
    next(stage)
    share_wr(1, 1)
    for _ in stage:
        pass

    def out_zero(at, _):
        z = norm_outer(0, r.ex[0, at])[1] + inner_input(0, at).astype(f32)
        r.out0[at] = gelu(z).astype(bf16)
        return _


    def scatter_all(slot, chunks, prepare, product, use, beside=None, midway=None):
        keys = phase_keys(4)
        ats = [pl.ds(*span) for span in chunks]
        borrowed = []

        def start(k, away):
            if away:
                prepare(k)
            two = pair(1 - high if away else high)
            r.pb[ats[k], two] = product(ats[k], two).astype(bf16)
            block, index = (j_far, 1) if away else (j_core, 0)
            target = r.rcore.at[slot, index, ats[k]]
            made = remote(r.pb.at[ats[k], cols(block)], target, (clip, j_core), keys[k][index])
            borrowed.append(made[1])

        def hand_on(k):
            at = ats[k]
            arrive(r.rcore.at[slot, 1, at], keys[k][1])
            both = r.pb[at, cols(j_y)].astype(f32) + r.rcore[slot, 1, at].astype(f32)
            r.ysend[slot % 2, at] = both.astype(bf16)
            made = remote(r.ysend.at[slot % 2, at], r.ryy.at[slot, at], (clip, j_y), keys[k][2])
            borrowed.append(made[1])

        start(0, True)
        start(1, True)
        hand_on(0)
        start(2, True)
        hand_on(1)
        start(3, True)
        hand_on(2)
        start(0, False)
        hand_on(3)
        for k in range(1, 4):
            start(k, False)
        if beside is not None:
            beside()
        for k in range(4):
            arrive(r.rcore.at[slot, 0, ats[k]], keys[k][0])
            arrive(r.ryy.at[slot, ats[k]], keys[k][2])
            use(*chunks[k])
            if midway is not None and k == 1:
                midway()
        for index in borrowed:
            sent(index)

    held = SimpleNamespace(sums=(zero_n, zero_n))

    def use_reduced(begin, count):
        at = pl.ds(begin, count)
        value = scatter_value(0, at)
        r.red[1, at] = value
        held.sums = (held.sums[0] + fold(value), held.sums[1] + fold(value * value))

    shared_wr(1)
    scatter_all(
        0,
        raw_spans,
        lambda k: broad(k, out_zero, 0),
        lambda at, two: dot(r.out0[at], r.wrf[1, :, two]),
        use_reduced,
    )
    made = stat_start(r.stn, 2, held.sums)
    share_we(1, 0)
    moments_in[1][0] = moments(stat_end(r.stn, 2, made))
    stage = forward(1, 3, 1)
    next(stage)
    share_we(1, 1)
    next(stage)
    shared_we(1)
    next(stage)
    share_wr(0, 0)
    share_wr(0, 1)
    for _ in stage:
        pass

    load_cot.wait()

    def out_one(at, sums):
        centred, z = norm_outer(1, r.ex[1, at])
        value, slope = gelu_both(z + r.out0[at].astype(f32))
        r.act[at] = value.astype(bf16)
        grad = r.cot[at].astype(f32) * slope
        r.gpre[at] = grad
        return sums[0] + fold(grad), sums[1] + fold(grad * centred)

    def top_zero(at, sums):
        centred, z = norm_outer(0, r.ex[0, at])
        grad = r.gin[at] * gelu_both(z + inner_input(0, at).astype(f32))[1]
        r.gpre[at] = grad
        return sums[0] + fold(grad), sums[1] + fold(grad * centred)

    top_sums = SimpleNamespace()

    def backward(s, stat_base, wide_slot, slot):
        if s == 1:
            top_sums.now = (zero_w, zero_w)
            for k in range(4):
                top_sums.now = broad(k, out_one, top_sums.now)
        sums = top_sums.now
        made = stat_start(r.stw, wide_slot, sums)
        if s == 1:
            write_out(r.act, r.act_out)
        service(s, 0)
        shift_sum, gain_sum = stat_end(r.stw, wide_slot, made)
        r.gbo[s : s + 1] = shift_sum
        r.ggo[s : s + 1] = gain_sum
        mean, inv = moments_in[s][2]
        scale = inv * row(r.go, s)
        shift_mean, gain_mean = shift_sum / pixel_total, gain_sum / pixel_total

        def expand_back(at, _):
            centred = (r.ex[s, at] - mean) * inv
            grad = scale * (r.gpre[at] - (shift_mean + centred * gain_mean))
            r.gexp[at] = grad.astype(bf16)
            return _

        held.sums = (zero_n, zero_n)
        service(s, 1)

        def weight_expand():
            value = dot(r.inf[s], r.gexp[...], 0, 0).astype(bf16)
            r.geo[s] = value.reshape(r.geo.shape[1:])
            place = r.ge.at[s, :, :, :, wide(chan)]
            turned[1, s] = local(r.geo.at[s, chan], place)
            for j in others:
                remote(r.geo.at[s, j], place, (clip, j), (TURN, 1, s))
            service(s, 2)

        def use_inner(begin, count):
            def one(at, sums):
                centred, z = norm_inner(s, 1, r.conv[s, at])
                grad = scatter_value(slot, at) * gelu_both(z)[1]
                r.g1[at] = grad
                return sums[0] + fold(grad), sums[1] + fold(grad * centred)

            held.sums = narrow(begin, count, one, held.sums)

        scatter_all(
            slot,
            raw_spans,
            lambda k: broad(k, expand_back, 0),
            lambda at, two: dot(r.gexp[at], r.wef[s, two], 1, 1),
            use_inner,
            weight_expand,
            lambda: service(s, 3),
        )
        made = stat_start(r.stn, stat_base, held.sums)
        service(s, 4)
        shift_sum, gain_sum = stat_end(r.stn, stat_base, made)
        r.gbi[s, 1:2] = shift_sum
        r.ggi[s, 1:2] = gain_sum
        mean, inv = moments_in[s][1]
        scale = inv * row(r.gi, s, 1)
        shift_mean, gain_mean = shift_sum / pixel_total, gain_sum / pixel_total

        def conv_back(i, _):
            at = pair_rows(0, i)
            halves = []
            for f in (2 * i, 2 * i + 1):
                centred = (spread(r.conv.at[s], f) - mean) * inv
                grad = scale * (spread(r.g1, f) - (shift_mean + centred * gain_mean))
                halves.append(real(grad))
            for b in (-1, 0, 1):
                moved = [row_pad(col_shift(v, -b), 1) for v in halves]
                for a in (-1, 0, 1):
                    tap = 3 * (a + 1) + b + 1
                    both = jnp.concatenate([flat(v[1 - a : 1 - a + SIDE]) for v in moved], axis=0)
                    r.gs[at, tap * ib : (tap + 1) * ib] = both.astype(bf16)
            return _


        service(s, 5)

        def weight_conv():
            for k in range(3):
                taps = slice(3 * k * ib, 3 * (k + 1) * ib)
                value = dot(r.mixf[s], r.gs[:, taps], 0, 0).astype(bf16)
                r.gc[s, :, :, :, taps] = value.reshape(r.gc.shape[1:4] + (3 * ib,))
            service(s, 6)

        def use_mixed(begin, count):
            def one(at, _):
                r.gm[at] = real(scatter_value(slot + 1, at))
                return _

            narrow(begin, count, one, 0)

        scatter_all(
            slot + 1,
            padded_spans,
            lambda k: lax.fori_loop(k * pairs // 2, (k + 1) * pairs // 2, conv_back, 0, unroll=True),
            lambda at, two: dot(r.gs[at], r.wc[s, two], 1, 1),
            use_mixed,
            weight_conv,
            lambda: service(s, 7),
        )

        def tap_sums(grad, v, index, reach):
            for b in (-1, 0, 1):
                padded = row_pad(col_shift(v, reach * b), reach)
                for a in (-1, 0, 1):
                    start = reach + reach * a
                    place = 9 * index + 3 * (a + 1) + b + 1
                    r.gk[place] = r.gk[place] + jnp.sum(grad * padded[start : start + SIDE], axis=0)

        def mix_back(f, before):
            at = frame_rows(f)
            following = frame_rows(jnp.minimum(f + 1, frames - 1))
            here = tiles(r.hid[s, at])
            step = keep_flag(f) * (tiles(r.hid[s, following]) - here)
            grad = tiles(r.gm[at])
            if s == 0:
                r.gd[at] = flat(dw_tiles(grad, taps_of(0), 1, -1))
                tap_sums(grad, step + before, 0, 1)
            else:
                gate = tiles(r.sig[at])
                grad = grad * here * gate * (1.0 - gate)
                r.gd[at] = flat(dw_tiles(grad, taps_of(1), 1, -1) + dw_tiles(grad, taps_of(2), 2, -1))
                tap_sums(grad, step, 1, 1)
                tap_sums(grad, step, 2, 2)
                r.gk[27] = r.gk[27] + jnp.sum(grad, axis=0)
            return step

        lax.fori_loop(0, frames, mix_back, jnp.zeros((SIDE, 8, ib), f32))

        service(s, 8)

        def hide_back(f, sums):
            at = frame_rows(f)
            previous = frame_rows(jnp.maximum(f - 1, 0))
            keep = keep_flag(f)
            keep_before = jnp.where(f > 0, keep_flag(jnp.maximum(f - 1, 0)), 0.0)
            now = r.gd[at]
            earlier = r.gd[previous]
            grad = r.gm[at]
            if s == 0:
                following = frame_rows(jnp.minimum(f + 1, frames - 1))
                later = now + r.gd[following]
                earlier = earlier + now
            else:
                later = now
                grad = grad * (1.0 + r.sig[at])
            grad = grad + keep_before * earlier - keep * later
            centred, z = norm_inner(s, 0, spread(r.red.at[s], f))
            grad = real(tiles(grad) * gelu_both(z)[1])
            squeeze(r.g1, f, grad)
            return sums[0] + jnp.sum(grad, axis=0), sums[1] + jnp.sum(grad * centred, axis=0)

        sums = lax.fori_loop(0, frames, hide_back, (zero_n, zero_n))
        made = stat_start(r.stn, stat_base + 1, sums)
        service(s, 9)
        shift_sum, gain_sum = stat_end(r.stn, stat_base + 1, made)
        r.gbi[s, 0:1] = shift_sum
        r.ggi[s, 0:1] = gain_sum
        mean, inv = moments_in[s][0]
        scale = inv * row(r.gi, s, 0)
        shift_mean, gain_mean = shift_sum / pixel_total, gain_sum / pixel_total
        service(s, 10)
        keys = phase_keys(4)
        quarters = [pl.ds(*span) for span in raw_spans]

        def reduce_back(at, _):
            centred = (r.red[s, at] - mean) * inv
            grad = scale * (r.g1[at] - (shift_mean + centred * gain_mean))
            r.grf[s, at, cols(chan)] = grad.astype(bf16)
            return _

        for k in range(4):
            narrow(*raw_spans[k], reduce_back, 0)
            gather_start(r.grf.at[s], quarters[k], keys[k])
        if s == 0:
            own = r.grf[0, :, cols(chan)]
            for piece in range(n_chan):
                value = dot(r.x[:, piece * cs : (piece + 1) * cs], own, 0, 0).astype(bf16)
                r.gr[0, piece] = value.reshape(r.gr.shape[2:])
        service(s, 11)
        gather_pass(r.grf.at[s], quarters[0], keys[0])
        gather_pass(r.grf.at[s], quarters[1], keys[1])
        if s == 0:
            shared_wr(0)
        else:
            top_sums.now = (zero_w, zero_w)
        for k in range(4):
            at = quarters[k]
            gather_end(r.grf.at[s], at, keys[k])
            r.gin[at] = dot(r.grf[s, at], r.wrf[s], 1, 1) + r.gpre[at]
            if k < 2:
                gather_pass(r.grf.at[s], quarters[k + 2], keys[k + 2])
            if s == 0:
                write_out(r.gin.at[at], r.gin_out.at[at])
            else:
                top_sums.now = broad(k, top_zero, top_sums.now)
            if k == 1:
                service(s, 12)
        service(s, 13)
        if s == 1:
            value = dot(r.out0[...], r.grf[1], 0, 0).astype(bf16)
            r.gro[...] = value.reshape(r.gro.shape)
            place = r.gr.at[1, chan]
            turned[2, 1] = local(r.gro.at[:, :, cols(chan)], place)
            for j in others:
                remote(r.gro.at[:, :, cols(j)], place, (clip, j), (TURN, 2, 1))

    turned = {}

    def reduce_task(kind, s, line, place):
        ref, from_side, from_z, result = kinds[kind]
        mine, done = ref.at[s, :, :, line, place], result.at[s, :, :, line, place]
        side_in, z_in = from_side.at[s, :, line, place], from_z.at[s, :, line, place]
        across = (2 * z + 1 - side, chan)
        key = (kind, s, line.start, place.start)
        if (kind, s) in turned:
            turned.pop((kind, s)).wait()
            three = pl.ds(0, (n_chan - 1) * cs)
            arrive(
                r.ge.at[s, :, :, :, three] if kind == 1 else r.gr.at[s, pl.ds(0, n_chan - 1)],
                (TURN, kind, s),
            )
        near, far = (2 * z_near + side, chan), (2 * z_far + side, chan)

        def add(k, term):
            both = ref[s, k, side, line, place].astype(f32) + term.astype(f32)
            return both.astype(bf16)

        remote(mine.at[:, 1 - side], side_in, across, key + (0,))
        yield
        arrive(side_in, key + (0,))
        for k in range(n_z):
            ref[s, k, side, line, place] = add(k, from_side[s, k, line, place])
        for k in range(2):
            remote(mine.at[1 - low + 2 * k, side], z_in.at[k], near, key + (1,))
        yield
        arrive(z_in.at[pl.ds(0, 2)], key + (1,))
        for k in range(2):
            ref[s, low + 2 * k, side, line, place] = add(low + 2 * k, from_z[s, k, line, place])
        remote(mine.at[z_far, side], z_in.at[2], far, key + (2,))
        yield
        arrive(z_in.at[2], key + (2,))
        result[s, z, side, line, place] = add(z, from_z[s, 2, line, place])
        remote(done.at[z, side], done.at[z, side], far, key + (3,))
        yield
        arrive(done.at[z_far, side], key + (3,))
        for k in (z, z_far):
            remote(done.at[k, side], done.at[k, side], near, key + (4,))
        yield
        arrive(done.at[pl.ds(0, 2), side], key + (4,))
        remote(done.at[:, side], done.at[:, side], across, key + (5,))
        yield
        arrive(done.at[:, 1 - side], key + (5,))
        if kind == 0:
            base = place.start // ib
            for k in range((place.stop - place.start) // ib):
                here = r.fc.at[s, :, :, :, (base + k) * ib : (base + k + 1) * ib]
                write_out(here, r.gc_out.at[s, base + k])
        else:
            out = (None, r.ge_out, r.gr_out)[kind]
            write_out(done, out.at[s, :, :, line, place])
        yield

    kinds = (
        (r.gc, r.xc, r.zc, r.fc),
        (r.ge, r.xe, r.ze, r.fe),
        (r.gr, r.xr, r.zr, r.fr),
    )
    def cut(size, count):
        return [slice(k * (size // count), (k + 1) * (size // count)) for k in range(count)]

    tasks = {}
    for s in range(2):
        for k, place in enumerate(cut(9 * ib, PIECES[0])):
            tasks[100 * s + k] = reduce_task(0, s, slice(0, r.gc.shape[3]), place)
        for k, place in enumerate(cut(r.ge.shape[4], PIECES[1])):
            tasks[100 * s + 10 + k] = reduce_task(1, s, slice(0, r.ge.shape[3]), place)
        for k, line in enumerate(cut(r.gr.shape[3], PIECES[2])):
            tasks[100 * s + 20 + k] = reduce_task(2, s, line, slice(0, ib))

    def advance(*steps):
        for step in steps:
            next(tasks[step])

    def service(s, point):
        advance(*PLAN.get((s, point), ()))

    backward(1, 4, 2, 1)
    backward(0, 6, 3, 3)

    for place in range(r.gk.shape[0]):
        r.kst[clip, place : place + 1, :] = jnp.sum(r.gk[place], axis=0, keepdims=True)
    for t in clip_others:
        remote(r.kst.at[clip], r.kst.at[clip], (t, chan), TAPS)
    service(0, 14)
    arrive(r.kst.at[pl.ds(0, n_clip - 1)], TAPS)
    total = r.kst[0]
    for k in range(1, n_clip):
        total = total + r.kst[k]
    for index in range(3):
        for tap in range(9):
            place = 9 * index + tap
            r.gk_out[tap, index : index + 1, :] = total[place : place + 1]
    r.ggb_out[...] = total[27:28]
    for copy in outgoing.values():
        copy.wait()
    for index in list(in_flight):
        sent(index)
    assert len(places) <= ARRIVALS and counters.load <= LOADS - 8


def fused_call(n_clip, n_chan, pixel_total, *operands):
    rows, width = operands[0].shape
    cs = width // n_chan
    ib = LANES
    inner = ib * n_chan
    n_z = n_clip // 2
    padded = rows // PIXELS * FRAME
    over = rows + 8
    bf16, f32 = jnp.bfloat16, jnp.float32
    whole = pl.BlockSpec(memory_space=pltpu.VMEM)
    anywhere = pl.BlockSpec(memory_space=pl.ANY)
    scalars = pl.BlockSpec(memory_space=pltpu.SMEM)
    shape = jax.ShapeDtypeStruct
    V = pltpu.VMEM
    scratch = dict(
        x=V((rows, width), bf16),
        cot=V((rows, cs), bf16),
        wr0=V((width, ib), bf16),
        wrf=V((2, cs, inner), bf16),
        wef=V((2, inner, cs), bf16),
        wc=V((2, inner, 9 * ib), bf16),
        dkb=V((27, 8, ib), f32),
        red=V((2, over, ib), f32),
        hid=V((2, padded, ib), f32),
        sig=V((padded, ib), f32),
        conv=V((2, over, ib), f32),
        mixf=V((2, padded, inner), bf16),
        inf=V((2, rows, inner), bf16),
        ex=V((2, rows, cs), f32),
        out0=V((rows, cs), bf16),
        act=V((rows, cs), bf16),
        y=V((padded // 4, 9 * ib), f32),
        gpre=V((rows, cs), f32),
        gin=V((rows, cs), f32),
        gexp=V((rows, cs), bf16),
        gs=V((padded, 9 * ib), bf16),
        pb=V((padded, inner), bf16),
        ysend=V((2, padded, ib), bf16),
        rcore=V((5, 2, padded, ib), bf16),
        ryy=V((5, padded, ib), bf16),
        grf=V((2, rows, inner), bf16),
        gm=V((padded, ib), f32),
        gd=V((padded, ib), f32),
        g1=V((over, ib), f32),
        gk=V((32, 8, ib), f32),
        kst=V((n_clip, 32, ib), f32),
        stn=V((8, n_clip, 2, ib), f32),
        stw=V((4, n_clip, 2, cs), f32),
        gc=V((2, n_z, 2, inner // n_clip, 9 * ib), bf16),
        geo=V((2, n_chan, n_z, 2, ib // n_clip, cs), bf16),
        ge=V((2, n_z, 2, ib // n_clip, width), bf16),
        gro=V((2, cs // 2, inner), bf16),
        gr=V((2, n_z, 2, width // n_clip, ib), bf16),
        fc=V((2, n_z, 2, inner // n_clip, 9 * ib), bf16),
        fe=V((2, n_z, 2, ib // n_clip, width), bf16),
        fr=V((2, n_z, 2, width // n_clip, ib), bf16),
        xc=V((2, n_z, inner // n_clip, 9 * ib), bf16),
        xe=V((2, n_z, ib // n_clip, width), bf16),
        xr=V((2, n_z, width // n_clip, ib), bf16),
        zc=V((2, n_z - 1, inner // n_clip, 9 * ib), bf16),
        ze=V((2, n_z - 1, ib // n_clip, width), bf16),
        zr=V((2, n_z - 1, width // n_clip, ib), bf16),
        ssem=pltpu.SemaphoreType.DMA((SENDS,)),
        rsem=pltpu.SemaphoreType.DMA((ARRIVALS,)),
        lsem=pltpu.SemaphoreType.DMA((LOADS,)),
    )
    return pl.pallas_call(
        partial(fused_kernel, n_clip, n_chan, pixel_total),
        out_shape=[
            shape((rows, cs), bf16),
            shape((rows, cs), f32),
            shape((2, 2, ib), f32),
            shape((2, 2, ib), f32),
            shape((2, cs), f32),
            shape((2, cs), f32),
            shape((9, 3, ib), f32),
            shape((1, ib), f32),
            shape((2, 9, n_z, 2, inner // n_clip, ib), bf16),
            shape((2, n_z, 2, ib // n_clip, width), bf16),
            shape((2, n_z, 2, width // n_clip, ib), bf16),
        ],
        in_specs=[anywhere] * 5 + [scalars] + [whole] * 6,
        out_specs=[anywhere] * 2 + [whole] * 6 + [anywhere] * 3,
        scratch_shapes=[scratch[name] for name in Refs._fields if name in scratch],
        compiler_params=pltpu.CompilerParams(
            collective_id=0, has_side_effects=True, vmem_limit_bytes=62 * 1024 * 1024
        ),
    )(*operands)


def finish_kernel(*refs):
    count = len(refs) // 2
    sources, results = refs[:count], refs[count:]
    for here, there in zip(sources[:5], results[:5]):
        there[...] = here[...].astype(there.dtype)

    @pl.when(pl.program_id(0) == 0)
    def _():
        for here, there in zip(sources[5:], results[5:]):
            there[...] = here[...]


def finish(steps, gc, ge, gr, act, gin, *small):
    arrays = [a.reshape(-1, a.shape[-1]) for a in (gc, ge, gr)]
    blocks = [pl.BlockSpec((a.shape[0] // steps, a.shape[1]), lambda i: (i, 0)) for a in arrays]
    for a in (act, gin):
        blocks.append(pl.BlockSpec((a.shape[0], a.shape[1] // steps), lambda i: (0, i)))
        arrays.append(a)
    whole = [pl.BlockSpec(memory_space=pltpu.VMEM)] * len(small)
    shapes = [jax.ShapeDtypeStruct(a.shape, jnp.float32) for a in arrays[:3]]
    shapes += [jax.ShapeDtypeStruct(a.shape, a.dtype) for a in (act, gin, *small)]
    return pl.pallas_call(
        finish_kernel,
        grid=(steps,),
        out_shape=shapes,
        in_specs=blocks + whole,
        out_specs=blocks + whole,
        compiler_params=pltpu.CompilerParams(vmem_limit_bytes=62 * 1024 * 1024),
    )(*arrays, *small)


def fused(
    frames_in,
    boundary,
    w_reduce,
    gain_inner,
    bias_inner,
    w_conv,
    w_expand,
    gain_outer,
    bias_outer,
    depth_kernels,
    gate_bias,
    cotangent,
):
    n_clip, n_chan = lax.axis_size("clip"), lax.axis_size("chan")
    pixel_total = frames_in.shape[0] * n_clip
    act, gin, ggi, gbi, ggo, gbo, gk, ggb, gc, ge, gr = fused_call(
        n_clip,
        n_chan,
        float(pixel_total),
        frames_in,
        cotangent,
        w_reduce,
        w_conv,
        w_expand,
        boundary,
        gain_inner,
        bias_inner,
        gain_outer,
        bias_outer,
        depth_kernels.transpose(1, 0, 2),
        gate_bias.reshape(1, -1),
    )
    gc, ge, gr, act, gin, ggi, gbi, ggo, gbo, gk, ggb = finish(
        2, gc, ge, gr, act, gin, ggi, gbi, ggo, gbo, gk, ggb
    )
    return (
        act,
        gin,
        gr.reshape(w_reduce.shape),
        ggi,
        gbi,
        gc.reshape(w_conv.shape),
        ge.reshape(w_expand.shape),
        ggo,
        gbo,
        gk.transpose(1, 0, 2),
        ggb.reshape(-1),
    )


def solution(mesh):
    in_specs = (
        P("clip", None),
        P("clip", None),
        P(None, None, "chan"),
        P(None, None, "chan"),
        P(None, None, "chan"),
        P(None, None, None, "chan"),
        P(None, "chan", None),
        P(),
        P(),
        P(None, None, "chan"),
        P("chan"),
        P("clip", None),
    )
    out_specs = (
        P("clip", "chan"),
        P("clip", "chan"),
        P(None, None, "chan"),
        P(None, None, "chan"),
        P(None, None, "chan"),
        P(None, None, None, "chan"),
        P(None, "chan", None),
        P(None, "chan"),
        P(None, "chan"),
        P(None, None, "chan"),
        P("chan"),
    )

    def run(*arguments):
        fits = fused_fits(mesh, arguments[0].shape, arguments[2].shape)
        return jax.shard_map(fused if fits else body, mesh=mesh, in_specs=in_specs, out_specs=out_specs, check_vma=False)(*arguments)

    return run
```
